32 devices in a mesh: dp: 4 (over x, core), ctx: 8 (over z, y).
Axes of the slice: x: 2, y: 2, z: 4, core: 2. Of those that a mesh axis runs over, the one named last changes fastest.
Arguments:
- inputs: float32 [8, 2048, 960], P('dp', 'ctx'), may hold values from -6 to 6
- cotangent: float32 [8, 2048, 960], P('dp', 'ctx'), may hold values from -6 to 6
- weights: bfloat16 [10240, 960], P(('dp', 'ctx')), as said below
- gains: float32 [2, 960], replicated, may hold values from 0.25 to 1.75
- first_moment: float32 [10240, 960], P(('dp', 'ctx')), as said below
- second_moment: float32 [10240, 960], P(('dp', 'ctx')), as said below
- gain_first: float32 [2, 960], replicated, as said below
- gain_second: float32 [2, 960], replicated, as said below
Outputs:
- output: float32 [8, 2048, 960], P('dp', 'ctx')
- input_grad: float32 [8, 2048, 960], P('dp', 'ctx')
- weight_grad: float32 [10240, 960], P(('dp', 'ctx'))
- weight_second: float32 [10240, 960], P(('dp', 'ctx'))
- weight_new: float32 [10240, 960], P(('dp', 'ctx'))
- gain_grad: float32 [2, 960], replicated
- gain_second_new: float32 [2, 960], replicated
- gain_new: float32 [2, 960], replicated
The draws below stay inside these ranges and needn't reach their ends.
Inputs may be any that keep to these rules, and one draw needn't show every extreme that they name: `weights`: independent entries; each of the seven matrices has its own scale of order its fan-in to the minus one half. `first_moment`: both signs, independent entries. `second_moment`: positive entries. `gain_first`: both signs, independent entries. `gain_second`: positive entries.
All inputs are finite; a program needn't handle non-finite values.
Results may differ from the reference program's by a relative error of at most 0.019.
Values may be sent and summed in bfloat16 or wider, within the bound.
No kernel may reach another device: no remote copies, remote signals or barrier semaphores. Data moves between devices by JAX's collectives and lax.ppermute only.
A program may use at most 176 MiB of HBM per device.

```python
import jax
import jax.numpy as jnp
from jax import lax

D = 960
HEADS = 15
KV = 5
HD = 64
FF = 2560
SEQ_LEN = 2048
STEP = 10
SEQS = 8
TL = 256
WCOLS = 10240
N_CTX = 8


def row_table(factors):
    row_index = jnp.arange(WCOLS)[:, None]
    q_cols = HEADS * HD
    kv_cols = KV * HD
    ends = [q_cols, q_cols + kv_cols, q_cols + 2 * kv_cols, 2 * q_cols + 2 * kv_cols, 2 * q_cols + 2 * kv_cols + FF, 2 * q_cols + 2 * kv_cols + 2 * FF]
    table = jnp.full((WCOLS, 1), factors[6], jnp.float32)
    for member in [5, 4, 3, 2, 1, 0]:
        table = jnp.where(row_index < ends[member], factors[member], table)
    return table


def grad_sizes():
    root_tokens = (SEQS * SEQ_LEN) ** 0.5
    return row_table([0.1 * root_tokens, 0.1 * root_tokens, 0.3 * root_tokens, 0.3 * root_tokens, 0.3 * root_tokens, 0.3 * root_tokens, 0.5 * root_tokens])


def draw_weights(key, part):
    key = jax.random.fold_in(key, 11)
    scales = row_table([2.0 * D ** (-0.5), 1.5 * D ** (-0.5), D ** (-0.5), 2.0 * (HEADS * HD) ** (-0.5), D ** (-0.5), D ** (-0.5), FF ** (-0.5)])
    normals = jnp.clip(jax.random.normal(key, (WCOLS, D), jnp.float32), -4.0, 4.0)
    return (normals * scales).astype(jnp.bfloat16)


def draw_first_moment(key, part):
    key = jax.random.fold_in(key, 12)
    normals = jnp.clip(jax.random.normal(key, (WCOLS, D), jnp.float32), -4.0, 4.0)
    return 9.0 * grad_sizes() * normals


def draw_second_moment(key, part):
    key = jax.random.fold_in(key, 13)
    factor = jnp.exp(jax.random.uniform(key, (WCOLS, D), jnp.float32, 0.0, jnp.log(4.0)))
    sizes_now = grad_sizes()
    return 19.0 * sizes_now * sizes_now * factor


def draw_gain_first(key, part):
    key = jax.random.fold_in(key, 14)
    normals = jnp.clip(jax.random.normal(key, (2, D), jnp.float32), -4.0, 4.0)
    return 9.0 * 0.3 * (SEQS * SEQ_LEN) ** 0.5 * normals


def draw_gain_second(key, part):
    key = jax.random.fold_in(key, 15)
    factor = jnp.exp(jax.random.uniform(key, (2, D), jnp.float32, 0.0, jnp.log(4.0)))
    size_now = 0.3 * (SEQS * SEQ_LEN) ** 0.5
    return 19.0 * size_now * size_now * factor


def levels(key, dims, pieces, low, top_value):
    loudness, own = 1.0, jax.random.fold_in(key, 6)
    for position, shards_of in pieces:
        draws = jnp.exp(jax.random.uniform(jax.random.fold_in(own, position), (shards_of,), jnp.float32, low / len(pieces), top_value / len(pieces)))
        loudness = loudness * jnp.repeat(draws, dims[position] // shards_of).reshape([-1 if axis == position else 1 for axis in range(len(dims))])
    return loudness


def gaussian(stream_key, extent, scale, reach, cuts=(), kind=jnp.bfloat16):
    loudness = levels(stream_key, extent, cuts, -0.22, 0.18) if cuts else 1.0
    values = jax.random.normal(stream_key, extent, jnp.float32) * scale * loudness
    return jnp.minimum(jnp.maximum(values, -reach), reach).astype(kind)


def setup_inputs(seed: int = 0) -> dict:
    keys = jax.random.split(jax.random.key(seed), 9)
    inputs = gaussian(keys[0], (SEQS, SEQ_LEN, D), 1.0, 6.0, ((0, 4), (1, 8)), jnp.float32)
    cotangent = gaussian(keys[1], (SEQS, SEQ_LEN, D), 1.0, 6.0, ((0, 4), (1, 8)), jnp.float32)
    weights = draw_weights(jax.random.fold_in(keys[8], 71), 0)
    gains = jnp.clip(1.0 + 0.15 * jax.random.normal(keys[3], (2, D), jnp.float32), 0.25, 1.75)
    first_moment = draw_first_moment(jax.random.fold_in(keys[8], 71), 0)
    second_moment = draw_second_moment(jax.random.fold_in(keys[8], 71), 0)
    gain_first = draw_gain_first(jax.random.fold_in(keys[8], 71), 0)
    gain_second = draw_gain_second(jax.random.fold_in(keys[8], 71), 0)
    return dict(inputs=inputs, cotangent=cotangent, weights=weights, gains=gains, first_moment=first_moment, second_moment=second_moment, gain_first=gain_first, gain_second=gain_second)


SCALE_QK = 0.125
THETA = 10000.0
EPSILON = 1e-05
BETA_ONE = 0.9
BETA_TWO = 0.95
ADAM_EPS = 1e-08
DECAY = 0.1
RATE = 0.02
GAIN_RATE = 0.2
HIGHEST_PREC = lax.Precision.HIGHEST

@jax.custom_vjp
def low(v):
    return lax.optimization_barrier(v.astype(jnp.bfloat16)).astype(jnp.float32)

@jax.custom_vjp
def low_back(v):
    return v

def low_keep(v):
    return (low(v), None)

def low_pass(kept, grad):
    return (grad,)

def back_keep(v):
    return (v, None)

def back_low(kept, grad):
    return (low(grad),)
low.defvjp(low_keep, low_pass)
low_back.defvjp(back_keep, back_low)

def places(row_index, local_rows, ctx_count):
    half_rows = local_rows // 2
    owner_index = row_index // local_rows
    inner_index = row_index % local_rows
    return jnp.where(inner_index < half_rows, owner_index * half_rows + inner_index, (2 * ctx_count - 1 - owner_index) * half_rows + inner_index - half_rows)

def rotate(values, positions_in, sign):
    half_width = values.shape[-1] // 2
    frequency = THETA ** (-jnp.arange(half_width, dtype=jnp.float32) * 2.0 / values.shape[-1])
    angles = positions_in.astype(jnp.float32)[:, None] * frequency[None, :]
    cosine = jnp.cos(angles)[:, None, :]
    sine_part = sign * jnp.sin(angles)[:, None, :]
    first_half = values[..., :half_width]
    second_half = values[..., half_width:]
    return jnp.concatenate([first_half * cosine - second_half * sine_part, second_half * cosine + first_half * sine_part], axis=-1)

def normalize(values):
    return values * lax.rsqrt(lax.optimization_barrier(jnp.mean(values * values, axis=-1, keepdims=True)) + EPSILON)

def matmul_t(left, right):
    return jnp.dot(left, right.T, precision=HIGHEST_PREC)

def attention(queries, key_rows, value_rows, positions_in):
    group_size = HEADS // KV
    key_full = jnp.repeat(key_rows, group_size, axis=1)
    value_full = jnp.repeat(value_rows, group_size, axis=1)
    block_rows = 512 if SEQ_LEN % 512 == 0 else SEQ_LEN
    query_blocks = queries.reshape(SEQ_LEN // block_rows, block_rows, HEADS, HD)
    place_blocks = positions_in.reshape(SEQ_LEN // block_rows, block_rows)

    @jax.checkpoint
    def one_block(block_pair):
        query_part, place_part = block_pair
        scores = low_back(jnp.einsum('qhd,khd->hqk', query_part, key_full, precision=HIGHEST_PREC) * SCALE_QK)
        visible = positions_in[None, None, :] <= place_part[None, :, None]
        masked = jnp.where(visible, scores, -1e+30)
        largest = lax.optimization_barrier(jnp.max(masked, axis=-1, keepdims=True))
        expos = jnp.exp(masked - largest)
        probs = low(expos / lax.optimization_barrier(jnp.sum(expos, axis=-1, keepdims=True)))
        return jnp.einsum('hqk,khd->qhd', probs, value_full, precision=HIGHEST_PREC)
    mixed = lax.map(one_block, (query_blocks, place_blocks))
    return mixed.reshape(SEQ_LEN, HEADS * HD)

def block_forward(wmat, gain_pair, tokens_in, positions_in):
    q_cols = HEADS * HD
    kv_cols = KV * HD
    cut_o = q_cols + 2 * kv_cols
    cut_g = cut_o + q_cols
    cut_d = cut_g + 2 * FF
    a_one = low(normalize(tokens_in) * gain_pair[0])
    qkv = low_back(matmul_t(a_one, wmat[:cut_o]))
    queries = low(rotate(qkv[:, :q_cols].reshape(SEQ_LEN, HEADS, HD), positions_in, 1.0))
    key_rows = low(rotate(qkv[:, q_cols:q_cols + kv_cols].reshape(SEQ_LEN, KV, HD), positions_in, 1.0))
    value_rows = low(qkv[:, q_cols + kv_cols:]).reshape(SEQ_LEN, KV, HD)
    attn = low_back(low(attention(queries, key_rows, value_rows, positions_in)))
    resid = tokens_in + low_back(jnp.dot(attn, wmat[cut_o:cut_g], precision=HIGHEST_PREC))
    a_two = low(normalize(resid) * gain_pair[1])
    gate_up = low_back(matmul_t(a_two, wmat[cut_g:cut_d]))
    gate_pre = gate_up[:, :FF]
    up_pre = gate_up[:, FF:]
    hidden_act = low(gate_pre * jax.nn.sigmoid(gate_pre) * up_pre)
    return resid + low_back(jnp.dot(hidden_act, wmat[cut_d:], precision=HIGHEST_PREC))

def adam_update(param, grad, first, second, rate, decay):
    first_new = BETA_ONE * first + (1.0 - BETA_ONE) * grad
    second_new = BETA_TWO * second + (1.0 - BETA_TWO) * grad * grad
    fix_one = 1.0 - BETA_ONE ** STEP
    fix_two = 1.0 - BETA_TWO ** STEP
    update = first_new / fix_one / (jnp.sqrt(second_new / fix_two) + ADAM_EPS)
    return (first_new, second_new, param - rate * (update + decay * param))

def reference(inputs, cotangent, weights, gains, first_moment, second_moment, gain_first, gain_second):
    weight_full = weights.astype(jnp.float32)
    positions_all = places(jnp.arange(SEQ_LEN, dtype=jnp.int32), TL, N_CTX)

    def micro_step(carry, sequence_pair):
        weight_sum, gain_sum = carry
        tokens_in, cot_in = sequence_pair
        result, pull_back = jax.vjp(lambda wmat, gain_pair, token_arg: block_forward(wmat, gain_pair, token_arg, positions_all), weight_full, gains, tokens_in)
        d_weight, d_gain, d_tokens = pull_back(cot_in)
        return ((weight_sum + d_weight, gain_sum + d_gain), (result, d_tokens))
    start_carry = (jnp.zeros((WCOLS, D), jnp.float32), jnp.zeros((2, D), jnp.float32))
    (weight_grad, gain_grad), (output, input_grad) = lax.scan(micro_step, start_carry, (inputs, cotangent))
    weight_first, weight_second, weight_new = adam_update(weight_full, weight_grad, first_moment, second_moment, RATE, DECAY)
    gain_first_new, gain_second_new, gain_new = adam_update(gains, gain_grad, gain_first, gain_second, GAIN_RATE, 0.0)
    return (output, input_grad, weight_grad, weight_second, weight_new, gain_grad, gain_second_new, gain_new)
```

```python
import jax
import jax.numpy as jnp
from jax import lax
from jax.sharding import PartitionSpec as P

HEADS = 15
KV = 5
HD = 64
FF = 2560
MICRO = 2
STEP = 10


SCALE_QK = 0.125
THETA = 10000.0
EPSILON = 1e-05
BETA_ONE = 0.9
BETA_TWO = 0.95
ADAM_EPS = 1e-08
DECAY = 0.1
RATE = 0.02
GAIN_RATE = 0.2


def places(row_index, local_rows, ctx_count):
    half_rows = local_rows // 2
    owner_index = row_index // local_rows
    inner_index = row_index % local_rows
    return jnp.where(
        inner_index < half_rows,
        owner_index * half_rows + inner_index,
        (2 * ctx_count - 1 - owner_index) * half_rows + inner_index - half_rows,
    )


def rotate(values, positions_in, sign):
    half_width = values.shape[-1] // 2
    frequency = THETA ** (-jnp.arange(half_width, dtype=jnp.float32) * 2.0 / values.shape[-1])
    angles = positions_in.astype(jnp.float32)[:, None] * frequency[None, :]
    cosine = jnp.cos(angles)[:, None, :]
    sine_part = sign * jnp.sin(angles)[:, None, :]
    first_half = values[..., :half_width]
    second_half = values[..., half_width:]
    return jnp.concatenate(
        [
            first_half * cosine - second_half * sine_part,
            second_half * cosine + first_half * sine_part,
        ],
        axis=-1,
    )


def normalize(values):
    return values * lax.rsqrt(jnp.mean(values * values, axis=-1, keepdims=True) + EPSILON)


def norm_back(values, grad_in, gain_row):
    inv_scale = lax.rsqrt(jnp.mean(values * values, axis=-1, keepdims=True) + EPSILON)
    unit_rows = values * inv_scale
    grad_unit = grad_in * gain_row
    grad_values = inv_scale * (
        grad_unit - unit_rows * jnp.mean(grad_unit * unit_rows, axis=-1, keepdims=True)
    )
    return (grad_values, jnp.sum(grad_in * unit_rows, axis=0))


def matmul_n(left, right):
    return jnp.dot(left, right, preferred_element_type=jnp.float32)


def matmul_t(left, right):
    return lax.dot_general(
        left, right, (((1,), (1,)), ((), ())), preferred_element_type=jnp.float32
    )


def matmul_c(left, right):
    return lax.dot_general(
        left, right, (((0,), (0,)), ((), ())), preferred_element_type=jnp.float32
    )


def axis_bits():
    dp_bits = lax.axis_size("dp").bit_length() - 1
    ctx_bits = lax.axis_size("ctx").bit_length() - 1
    low_ctx = ctx_bits // 2
    core = [("dp", 0)]
    along_x = [("dp", bit) for bit in range(1, dp_bits)]
    along_y = [("ctx", bit) for bit in range(low_ctx)]
    along_z = [("ctx", bit) for bit in range(low_ctx, ctx_bits)]
    return core, along_x, along_y, along_z


def swap(values, where):
    axis, bit = where
    size = lax.axis_size(axis)
    return lax.ppermute(values, axis, [(i, i ^ (1 << bit)) for i in range(size)])


def my_bit(where):
    axis, bit = where
    return (lax.axis_index(axis) >> bit) & 1


def halve(values, bits, where, last):
    dim = bits.index(where)
    mine = my_bit(where)
    away = lax.dynamic_index_in_dim(values, 1 - mine, dim, keepdims=False)
    keep = lax.dynamic_index_in_dim(values, mine, dim, keepdims=False)
    total = keep.astype(jnp.float32) + swap(away, where).astype(jnp.float32)
    rest = [b for b in bits if b != where]
    return (total if last else total.astype(jnp.bfloat16)), rest


def scatter_sum(terms):
    core, along_x, along_y, along_z = axis_bits()
    dp_count, ctx_count = lax.axis_size("dp"), lax.axis_size("ctx")
    everything = jnp.concatenate(terms, axis=0)
    rows = everything.shape[0] // (dp_count * ctx_count)
    width = everything.shape[1]
    first = -(-rows // 48) * 16
    cuts = [(0, first), (first, 2 * first), (2 * first, rows)]
    bits = [("dp", b) for b in reversed(range(dp_count.bit_length() - 1))]
    bits += [("ctx", b) for b in reversed(range(ctx_count.bit_length() - 1))]
    values, rest = halve(
        everything.reshape([2] * len(bits) + [rows, width]), bits, core[0], False
    )
    orders = [
        along_x + along_y + along_z,
        along_y + along_z + along_x,
        along_z + along_x + along_y,
    ]
    done = []
    states = [(values[..., low:high, :], rest) for low, high in cuts]
    for step in range(len(orders[0])):
        last = step == len(orders[0]) - 1
        states = [
            halve(part, left, orders[member][step], last)
            for member, (part, left) in enumerate(states)
        ]
    return jnp.concatenate([part for part, _ in states], axis=0)


def butterfly_sum(values):
    core, along_x, along_y, along_z = axis_bits()
    for where in core + along_x + along_y + along_z:
        values = values + swap(values, where)
    return values


def adam_update(param, grad, first, second, rate, decay, step_number):
    first_new = BETA_ONE * first + (1.0 - BETA_ONE) * grad
    second_new = BETA_TWO * second + (1.0 - BETA_TWO) * grad * grad
    fix_one = 1.0 - BETA_ONE**step_number
    fix_two = 1.0 - BETA_TWO**step_number
    update = first_new / fix_one / (jnp.sqrt(second_new / fix_two) + ADAM_EPS)
    return (first_new, second_new, param - rate * (update + decay * param))


def shards(inputs, cotangent, weights, gains, first_moment, second_moment, gain_first, gain_second):
    ctx_count = lax.axis_size("ctx")
    ctx_index = lax.axis_index("ctx")
    local_rows = inputs.shape[1]
    model_width = inputs.shape[2]
    q_cols = HEADS * HD
    kv_cols = KV * HD
    group_size = HEADS // KV
    cut_o = q_cols + 2 * kv_cols
    cut_g = cut_o + q_cols
    cut_d = cut_g + 2 * FF
    local_index = jnp.arange(local_rows, dtype=jnp.int32)
    pos_here = places(ctx_index * local_rows + local_index, local_rows, ctx_count)

    def to_heads(flat_rows):
        return flat_rows.reshape(local_rows, KV, group_size, HD).transpose(1, 2, 0, 3)

    def from_heads(split_rows):
        return split_rows.transpose(2, 0, 1, 3).reshape(local_rows, q_cols)

    outputs_list = []
    grads_list = []
    lefts_all = []
    rights_all = []
    gain_terms = jnp.zeros((2, model_width), jnp.float32)
    gathered = lax.all_gather(weights, ("dp", "ctx"), axis=0, tiled=True)
    for micro_index in range(MICRO):
        tokens_in = inputs[micro_index]
        cot_in = cotangent[micro_index]
        a_one = (normalize(tokens_in) * gains[0]).astype(jnp.bfloat16)
        qkv = matmul_t(a_one, gathered[:cut_o])
        q_rot = rotate(qkv[:, :q_cols].reshape(local_rows, HEADS, HD), pos_here, 1.0).astype(
            jnp.bfloat16
        )
        key_rot = rotate(
            qkv[:, q_cols : q_cols + kv_cols].reshape(local_rows, KV, HD), pos_here, 1.0
        )
        key_rot = key_rot.astype(jnp.bfloat16).reshape(local_rows, kv_cols)
        value_rows = qkv[:, q_cols + kv_cols :].astype(jnp.bfloat16)
        queries = to_heads(q_rot.reshape(local_rows, q_cols))

        def scores_of(key_piece):
            piece_rows = key_piece.shape[0]
            key_pos = places(jnp.arange(piece_rows, dtype=jnp.int32), local_rows, ctx_count)
            raw_scores = (
                jnp.einsum(
                    "kgqd,pkd->kgqp",
                    queries,
                    key_piece.reshape(piece_rows, KV, HD),
                    preferred_element_type=jnp.float32,
                )
                * SCALE_QK
            )
            visible = key_pos[None, None, None, :] <= pos_here[None, None, :, None]
            return (jnp.where(visible, raw_scores, -1e30), visible)

        running_max = jnp.full((KV, group_size, local_rows), -1e30, jnp.float32)
        joined_rows = jnp.concatenate([key_rot, value_rows], axis=1)
        joined_piece = lax.all_gather(joined_rows, "ctx", axis=0, tiled=True)
        attend_key_piece = joined_piece[:, :kv_cols]
        value_piece = joined_piece[:, kv_cols:]
        masked, attend_visible = scores_of(attend_key_piece)
        new_max = jnp.maximum(running_max, jnp.max(masked, axis=-1))
        expos = jnp.where(attend_visible, jnp.exp(masked - new_max[..., None]), 0.0)
        running_sum = jnp.sum(expos, axis=-1)
        weighted = jnp.einsum(
            "kgqp,pkd->kgqd",
            expos.astype(jnp.bfloat16),
            value_piece.reshape(value_piece.shape[0], KV, HD),
            preferred_element_type=jnp.float32,
        )
        running_max, running_sum, weighted = (new_max, running_sum, weighted)
        mixed = weighted / running_sum[..., None]
        log_total = running_max + jnp.log(running_sum)
        attn_low = from_heads(mixed).astype(jnp.bfloat16)
        resid = tokens_in + matmul_n(attn_low, gathered[cut_o:cut_g])
        a_two = (normalize(resid) * gains[1]).astype(jnp.bfloat16)
        gate_up = matmul_t(a_two, gathered[cut_g:cut_d])
        gate_pre = gate_up[:, :FF]
        up_pre = gate_up[:, FF:]
        gate_sigma = jax.nn.sigmoid(gate_pre)
        gate_act = gate_pre * gate_sigma
        hidden_act = (gate_act * up_pre).astype(jnp.bfloat16)
        result = resid + matmul_n(hidden_act, gathered[cut_d:])
        dy_low = cot_in.astype(jnp.bfloat16)
        d_hidden = matmul_t(dy_low, gathered[cut_d:])
        d_gate = d_hidden * up_pre * gate_sigma * (1.0 + gate_pre * (1.0 - gate_sigma))
        d_up = d_hidden * gate_act
        d_gu = jnp.concatenate([d_gate, d_up], axis=1).astype(jnp.bfloat16)
        d_two = matmul_n(d_gu, gathered[cut_g:cut_d])
        d_norm_two, d_gain_two = norm_back(resid, d_two, gains[1])
        d_resid = cot_in + d_norm_two
        d_resid_low = d_resid.astype(jnp.bfloat16)
        d_attn = matmul_t(d_resid_low, gathered[cut_o:cut_g]).astype(jnp.bfloat16)
        d_heads = to_heads(d_attn)
        row_delta = jnp.sum(d_heads.astype(jnp.float32) * mixed, axis=-1)

        def score_grads(key_piece, value_piece):
            piece_rows = key_piece.shape[0]
            masked, visible = scores_of(key_piece)
            probability = jnp.where(visible, jnp.exp(masked - log_total[..., None]), 0.0)
            d_prob = jnp.einsum(
                "kgqd,pkd->kgqp",
                d_heads,
                value_piece.reshape(piece_rows, KV, HD),
                preferred_element_type=jnp.float32,
            )
            d_score = (probability * (d_prob - row_delta[..., None])).astype(jnp.bfloat16)
            return (probability, d_score)

        kv_piece_rows = joined_piece.shape[0]
        kv_probability, kv_d_score = score_grads(attend_key_piece, value_piece)
        d_q = SCALE_QK * jnp.einsum(
            "kgqp,pkd->kgqd",
            kv_d_score,
            attend_key_piece.reshape(kv_piece_rows, KV, HD),
            preferred_element_type=jnp.float32,
        )
        key_part = SCALE_QK * jnp.einsum(
            "kgqp,kgqd->pkd", kv_d_score, queries, preferred_element_type=jnp.float32
        )
        value_part = jnp.einsum(
            "kgqp,kgqd->pkd",
            kv_probability.astype(jnp.bfloat16),
            d_heads,
            preferred_element_type=jnp.float32,
        )
        kv_terms = jnp.concatenate(
            [key_part.reshape(kv_piece_rows, kv_cols), value_part.reshape(kv_piece_rows, kv_cols)],
            axis=1,
        )
        d_kv = lax.psum_scatter(
            kv_terms.astype(jnp.bfloat16), "ctx", scatter_dimension=0, tiled=True
        ).astype(jnp.float32)
        d_k = d_kv[:, :kv_cols]
        d_v = d_kv[:, kv_cols:]
        dq_pre = rotate(from_heads(d_q).reshape(local_rows, HEADS, HD), pos_here, -1.0).reshape(
            local_rows, q_cols
        )
        dk_pre = rotate(d_k.reshape(local_rows, KV, HD), pos_here, -1.0).reshape(
            local_rows, kv_cols
        )
        d_qkv = jnp.concatenate([dq_pre, dk_pre, d_v], axis=1).astype(jnp.bfloat16)
        d_one = matmul_n(d_qkv, gathered[:cut_o])
        d_norm_one, d_gain_one = norm_back(tokens_in, d_one, gains[0])
        d_tokens = d_resid + d_norm_one
        lefts = (d_qkv, attn_low, d_gu, hidden_act)
        rights = (a_one, d_resid_low, a_two, dy_low)
        result, d_tokens, lefts, rights, gain_part = (
            result,
            d_tokens,
            lefts,
            rights,
            jnp.stack([d_gain_one, d_gain_two], axis=0),
        )
        outputs_list.append(result)
        grads_list.append(d_tokens)
        gain_terms = gain_terms + gain_part
        lefts_all.append(lefts)
        rights_all.append(rights)
    lefts_joined = [
        jnp.concatenate([entry[member] for entry in lefts_all], axis=0) for member in range(4)
    ]
    rights_joined = [
        jnp.concatenate([entry[member] for entry in rights_all], axis=0) for member in range(4)
    ]
    weight_share = scatter_sum(
        [
            matmul_c(lefts_joined[member], rights_joined[member]).astype(jnp.bfloat16)
            for member in range(4)
        ]
    )
    gain_grad = butterfly_sum(gain_terms)
    weight_first, weight_second, weight_new = adam_update(
        weights.astype(jnp.float32), weight_share, first_moment, second_moment, RATE, DECAY, STEP
    )
    gain_first_new, gain_second_new, gain_new = adam_update(
        gains, gain_grad, gain_first, gain_second, GAIN_RATE, 0.0, STEP
    )
    return (
        jnp.stack(outputs_list, axis=0),
        jnp.stack(grads_list, axis=0),
        weight_share,
        weight_second,
        weight_new,
        gain_grad,
        gain_second_new,
        gain_new,
    )


def solution(mesh):
    placed = (
        P("dp", "ctx", None),
        P("dp", "ctx", None),
        P(("dp", "ctx"), None),
        P(),
        P(("dp", "ctx"), None),
        P(("dp", "ctx"), None),
        P(),
        P(),
    )
    return jax.shard_map(
        shards,
        mesh=mesh,
        in_specs=placed,
        out_specs=(
            P("dp", "ctx", None),
            P("dp", "ctx", None),
            P(("dp", "ctx"), None),
            P(("dp", "ctx"), None),
            P(("dp", "ctx"), None),
            P(),
            P(),
            P(),
        ),
        check_vma=False,
    )
```

```python
import jax
import jax.numpy as jnp
import numpy as np
from jax import lax
from jax.experimental import pallas as pl
from jax.experimental.pallas import tpu as pltpu
from jax.sharding import PartitionSpec as P

HEADS = 15
KV = 5
HD = 64
FF = 2560
STEP = 10


SCALE_QK = 0.125
THETA = 10000.0
EPSILON = 1e-05
BETA_ONE = 0.9
BETA_TWO = 0.95
ADAM_EPS = 1e-08
DECAY = 0.1
RATE = 0.02
GAIN_RATE = 0.2
GROUP = HEADS // KV
KEY_TILE = 256
HIDDEN = -1e30
VMEM_BYTES = 48 * 1024 * 1024


def places(row_index, local_rows, ctx_count):
    half_rows = local_rows // 2
    owner_index = row_index // local_rows
    inner_index = row_index % local_rows
    return jnp.where(
        inner_index < half_rows,
        owner_index * half_rows + inner_index,
        (2 * ctx_count - 1 - owner_index) * half_rows + inner_index - half_rows,
    )


def angle_tables(positions_in, sign):
    half_width = HD // 2
    frequency = THETA ** (-jnp.arange(half_width, dtype=jnp.float32) * 2.0 / HD)
    angles = frequency[:, None] * positions_in.astype(jnp.float32)[None, :]
    return jnp.cos(angles), sign * jnp.sin(angles)


def rotate(values, tables):
    cosine, sine_part = tables
    heads = values.reshape(-1, HD, values.shape[-1])
    first_half = heads[:, : HD // 2]
    second_half = heads[:, HD // 2 :]
    return jnp.concatenate(
        [
            first_half * cosine - second_half * sine_part,
            second_half * cosine + first_half * sine_part,
        ],
        axis=1,
    ).reshape(values.shape)


def normalize(values):
    return values * lax.rsqrt(jnp.mean(values * values, axis=-1, keepdims=True) + EPSILON)


def norm_back(values, grad_in, gain_row):
    inv_scale = lax.rsqrt(jnp.mean(values * values, axis=-1, keepdims=True) + EPSILON)
    unit_rows = values * inv_scale
    grad_unit = grad_in * gain_row
    grad_values = inv_scale * (
        grad_unit - unit_rows * jnp.mean(grad_unit * unit_rows, axis=-1, keepdims=True)
    )
    return (grad_values, jnp.sum(grad_in * unit_rows, axis=0))


def matmul_n(left, right):
    return jnp.dot(left, right, preferred_element_type=jnp.float32)


def matmul_t(left, right):
    return lax.dot_general(
        left, right, (((1,), (1,)), ((), ())), preferred_element_type=jnp.float32
    )


def matmul_c(left, right):
    return lax.dot_general(
        left, right, (((0,), (0,)), ((), ())), preferred_element_type=jnp.float32
    )


def axis_bits():
    dp_bits = lax.axis_size("dp").bit_length() - 1
    ctx_bits = lax.axis_size("ctx").bit_length() - 1
    low_ctx = ctx_bits // 2
    core = [("dp", 0)]
    along_x = [("dp", bit) for bit in range(1, dp_bits)]
    along_y = [("ctx", bit) for bit in range(low_ctx)]
    along_z = [("ctx", bit) for bit in range(low_ctx, ctx_bits)]
    return core, along_x, along_y, along_z


def swap(values, where):
    axis, bit = where
    size = lax.axis_size(axis)
    return lax.ppermute(values, axis, [(i, i ^ (1 << bit)) for i in range(size)])


def my_bit(where):
    axis, bit = where
    return (lax.axis_index(axis) >> bit) & 1


def rel_offsets(order, axis_sizes):
    dp_count, ctx_count = axis_sizes
    offsets = np.zeros((1,), np.int64)
    for axis, bit in order:
        step = (1 << bit) * (ctx_count if axis == "dp" else 1)
        offsets = np.concatenate([offsets, offsets ^ step])
    return offsets


def spread(values, order):
    values = values[None]
    for where in order:
        values = jnp.concatenate([values, swap(values, where)], axis=0)
    return values


def collect(values, order):
    kept, arrived = values, None
    for where in order:
        half = kept.shape[0] // 2
        if arrived is None:
            away, kept_next = kept[half:], kept[:half]
            arrived = swap(away, where)
        else:
            away = add_low(kept[half:], arrived[half:])
            kept_next = add_low(kept[:half], arrived[:half])
            arrived = swap(away, where)
        kept = kept_next
    return kept[0].astype(jnp.float32) + arrived[0].astype(jnp.float32)


def add_low(left, right):
    return (left.astype(jnp.float32) + right.astype(jnp.float32)).astype(jnp.bfloat16)


def row_groups(rows):
    first = -(-rows // 48) * 16
    return [(0, first), (first, 2 * first), (2 * first, rows)]


def sum_orders():
    core, along_x, along_y, along_z = axis_bits()
    return [
        along_x + along_y + along_z,
        along_y + along_z + along_x,
        along_z + along_x + along_y,
    ]


def lookup(slot, offsets):
    total = jnp.int32(0)
    for bit in range(len(offsets).bit_length() - 1):
        total = total + ((slot >> bit) & 1) * int(offsets[1 << bit])
    return total


def find(offset, offsets):
    total = jnp.int32(0)
    for bit in range(len(offsets).bit_length() - 1):
        place = int(offsets[1 << bit]).bit_length() - 1
        total = total + (((offset >> place) & 1) << bit)
    return total


def gather_weights(weights):
    rows, width = weights.shape
    sizes = (lax.axis_size("dp"), lax.axis_size("ctx"))
    count = sizes[0] * sizes[1]
    core = axis_bits()[0][0]
    me = lax.axis_index("dp") * sizes[1] + lax.axis_index("ctx")
    groups = row_groups(rows)
    orders = [list(reversed(order)) for order in sum_orders()]
    mine = [spread(weights[low:high], order) for (low, high), order in zip(groups, orders)]
    other = [swap(part, core) for part in mine]
    tables = [rel_offsets(order, sizes) for order in orders]

    def body(me_ref, *refs):
        out_ref = refs[-1]
        bit = (me_ref[0] // sizes[1]) & 1
        for (low, high), own, far in zip(groups, refs[:3], refs[3:6]):
            out_ref[0, bit, 0, low:high] = own[0]
            out_ref[0, 1 - bit, 0, low:high] = far[0]

    def place(step, me_ref):
        target = step_offset(step) ^ me_ref[0]
        return (target // (2 * sizes[1]), 0, target % sizes[1], 0, 0)

    def step_offset(step):
        return lookup(step, tables[0])

    in_specs = [
        pl.BlockSpec(
            (1, high - low, width),
            lambda step, me_ref, table=table: (find(step_offset(step), table), 0, 0),
        )
        for (low, high), table in zip(groups, tables)
    ] * 2
    placed = pl.pallas_call(
        body,
        grid_spec=pltpu.PrefetchScalarGridSpec(
            num_scalar_prefetch=1,
            grid=(count // 2,),
            in_specs=in_specs,
            out_specs=pl.BlockSpec((1, 2, 1, rows, width), place),
        ),
        out_shape=jax.ShapeDtypeStruct((sizes[0] // 2, 2, sizes[1], rows, width), weights.dtype),
        compiler_params=pltpu.CompilerParams(vmem_limit_bytes=VMEM_BYTES),
    )(me.reshape(1).astype(jnp.int32), *mine, *other)
    return placed.reshape(count * rows, width)


def scatter_sum(terms):
    sizes = (lax.axis_size("dp"), lax.axis_size("ctx"))
    count = sizes[0] * sizes[1]
    core = axis_bits()[0][0]
    me = (lax.axis_index("dp") * sizes[1] + lax.axis_index("ctx")).reshape(1).astype(jnp.int32)
    blocks, rows, width = terms[0].shape
    groups = row_groups(rows)
    orders = sum_orders()
    tables = [rel_offsets(list(reversed(order)), sizes) for order in orders]

    def sources(flip):
        def chosen(member):
            def index(step, me_ref):
                target = lookup(step, tables[0]) ^ me_ref[0] ^ flip
                return (jnp.where(target // blocks == member, target % blocks, 0), 0, 0)

            return pl.BlockSpec((1, rows, width), index)

        return [chosen(member) for member in range(len(terms))]

    def holder(step, me_ref, flip):
        return (lookup(step, tables[0]) ^ me_ref[0] ^ flip) // blocks

    def pick_body(me_ref, *refs):
        held = holder(pl.program_id(0), me_ref, sizes[1])
        for member in range(len(terms)):

            @pl.when(held == member)
            def _(member=member):
                refs[-1][...] = refs[member][...]

    away = pl.pallas_call(
        pick_body,
        grid_spec=pltpu.PrefetchScalarGridSpec(
            num_scalar_prefetch=1,
            grid=(count // 2,),
            in_specs=sources(sizes[1]),
            out_specs=pl.BlockSpec((1, rows, width), lambda step, me_ref: (step, 0, 0)),
        ),
        out_shape=jax.ShapeDtypeStruct((count // 2, rows, width), jnp.bfloat16),
        compiler_params=pltpu.CompilerParams(vmem_limit_bytes=VMEM_BYTES),
    )(me, *terms)
    arrived = swap(away, core)

    def merge_body(me_ref, *refs):
        held = holder(pl.program_id(0), me_ref, 0)
        outs = refs[-3:]
        far = refs[-4]
        for member in range(len(terms)):

            @pl.when(held == member)
            def _(member=member):
                for (low, high), out in zip(groups, outs):
                    out[0] = (
                        refs[member][0, low:high].astype(jnp.float32)
                        + far[0, low:high].astype(jnp.float32)
                    ).astype(jnp.bfloat16)

    parts = pl.pallas_call(
        merge_body,
        grid_spec=pltpu.PrefetchScalarGridSpec(
            num_scalar_prefetch=1,
            grid=(count // 2,),
            in_specs=sources(0)
            + [pl.BlockSpec((1, rows, width), lambda step, me_ref: (step, 0, 0))],
            out_specs=[
                pl.BlockSpec(
                    (1, high - low, width),
                    lambda step, me_ref, table=table: (
                        find(lookup(step, tables[0]), table),
                        0,
                        0,
                    ),
                )
                for (low, high), table in zip(groups, tables)
            ],
        ),
        out_shape=[
            jax.ShapeDtypeStruct((count // 2, high - low, width), jnp.bfloat16)
            for low, high in groups
        ],
        compiler_params=pltpu.CompilerParams(vmem_limit_bytes=VMEM_BYTES),
    )(me, *terms, arrived)
    return jnp.concatenate([collect(part, order) for part, order in zip(parts, orders)], axis=0)


def butterfly_sum(values):
    core, along_x, along_y, along_z = axis_bits()
    for where in core + along_x + along_y + along_z:
        values = values + swap(values, where)
    return values


def turned(values):
    return jnp.transpose(values)


def attend_body(queries_ref, key_ref, value_ref, key_pos_ref, query_pos_ref, out_ref, total_ref, work):
    low_cols = queries_ref.shape[-1] // 2
    queries = queries_ref[0, 0]
    pieces = []
    largest = jnp.full((1, queries.shape[1]), HIDDEN, jnp.float32)
    largest_high = jnp.full((1, low_cols), HIDDEN, jnp.float32)
    keys_per_half = key_ref.shape[-1]
    for half in range(2):
        picked = queries if half == 0 else queries_ref[0, 0, :, low_cols:]
        places_of = query_pos_ref[...] if half == 0 else query_pos_ref[:, low_cols:]
        for start in range(0, keys_per_half, KEY_TILE):
            keys = turned(key_ref[0, half, :, start : start + KEY_TILE])
            scores = matmul_n(keys, picked)
            seen = key_pos_ref[half, start : start + KEY_TILE] <= places_of
            scores = jnp.where(seen, scores, HIDDEN)
            if half == 0:
                work[start : start + KEY_TILE] = scores
                largest = jnp.maximum(largest, jnp.max(scores, axis=0, keepdims=True))
            else:
                work[keys_per_half + start : keys_per_half + start + KEY_TILE, low_cols:] = scores
                largest_high = jnp.maximum(largest_high, jnp.max(scores, axis=0, keepdims=True))
    low_max = largest[:, :low_cols]
    high_max = jnp.maximum(largest[:, low_cols:], largest_high)
    largest = jnp.concatenate([low_max, high_max], axis=1)
    total = jnp.zeros_like(largest)
    mixed = jnp.zeros((HD, queries.shape[1]), jnp.float32)
    total_high = jnp.zeros_like(largest_high)
    mixed_high = jnp.zeros((HD, low_cols), jnp.float32)
    for half in range(2):
        for start in range(0, keys_per_half, KEY_TILE):
            values = value_ref[0, half, :, start : start + KEY_TILE]
            row = half * keys_per_half + start
            if half == 0:
                expos = jnp.exp(work[row : row + KEY_TILE] - largest)
                total = total + jnp.sum(expos, axis=0, keepdims=True)
                mixed = mixed + matmul_n(values, expos.astype(jnp.bfloat16))
            else:
                expos = jnp.exp(work[row : row + KEY_TILE, low_cols:] - high_max)
                total_high = total_high + jnp.sum(expos, axis=0, keepdims=True)
                mixed_high = mixed_high + matmul_n(values, expos.astype(jnp.bfloat16))
    total = jnp.concatenate([total[:, :low_cols], total[:, low_cols:] + total_high], axis=1)
    mixed = jnp.concatenate([mixed[:, :low_cols], mixed[:, low_cols:] + mixed_high], axis=1)
    out_ref[0, 0] = (mixed / total).astype(jnp.bfloat16)
    total_ref[0, 0] = largest + jnp.log(total)


def attend_back_body(
    queries_ref,
    key_ref,
    value_ref,
    key_pos_ref,
    query_pos_ref,
    out_ref,
    total_ref,
    d_out_ref,
    d_queries_ref,
    d_pair_ref,
):
    low_cols = queries_ref.shape[-1] // 2
    keys_per_half = key_ref.shape[-1]
    delta = jnp.sum(
        d_out_ref[0, 0].astype(jnp.float32) * out_ref[0, 0].astype(jnp.float32),
        axis=0,
        keepdims=True,
    )
    totals = total_ref[0, 0]
    d_queries = []
    for half in range(2):
        if half == 0:
            queries, d_out = queries_ref[0, 0], d_out_ref[0, 0]
            places_of, log_total, row_delta = query_pos_ref[...], totals, delta
        else:
            queries, d_out = queries_ref[0, 0, :, low_cols:], d_out_ref[0, 0, :, low_cols:]
            places_of = query_pos_ref[:, low_cols:]
            log_total, row_delta = totals[:, low_cols:], delta[:, low_cols:]
        part = jnp.zeros((HD, queries.shape[1]), jnp.float32)
        for start in range(0, keys_per_half, KEY_TILE):
            keys_flat = key_ref[0, half, :, start : start + KEY_TILE]
            scores = matmul_n(turned(keys_flat), queries)
            seen = key_pos_ref[half, start : start + KEY_TILE] <= places_of
            probs = jnp.where(seen, jnp.exp(scores - log_total), 0.0)
            values = turned(value_ref[0, half, :, start : start + KEY_TILE])
            d_probs = matmul_n(values, d_out)
            d_scores = (probs * (d_probs - row_delta)).astype(jnp.bfloat16)
            part = part + matmul_n(keys_flat, d_scores)
            d_pair_ref[0, half, 0, start : start + KEY_TILE, :HD] = matmul_t(
                d_scores, queries
            ).astype(jnp.bfloat16)
            d_pair_ref[0, half, 0, start : start + KEY_TILE, HD:] = matmul_t(
                probs.astype(jnp.bfloat16), d_out
            ).astype(jnp.bfloat16)
        d_queries.append(part)
    d_queries_ref[0, 0, :, :low_cols] = d_queries[0][:, :low_cols]
    d_queries_ref[0, 0, :, low_cols:] = d_queries[0][:, low_cols:] + d_queries[1]


def attention_specs(cols, keys_per_half):
    packed = pl.BlockSpec((1, 1, HD, cols), lambda seq, head: (seq, head, 0, 0))
    return packed, [
        packed,
        pl.BlockSpec((1, 2, HD, keys_per_half), lambda seq, head: (seq, 0, head, 0)),
        pl.BlockSpec((1, 2, HD, keys_per_half), lambda seq, head: (seq, 0, KV + head, 0)),
        pl.BlockSpec((2, keys_per_half, 1), lambda seq, head: (0, 0, 0)),
        pl.BlockSpec((1, cols), lambda seq, head: (0, 0)),
    ]


def attend(queries, pairs, key_pos, query_pos):
    seqs, _, _, cols = queries.shape
    keys_per_half = pairs.shape[-1]
    packed, specs = attention_specs(cols, keys_per_half)
    work = seqs * HEADS * keys_per_half * cols // GROUP * 3
    return pl.pallas_call(
        attend_body,
        grid=(seqs, KV),
        in_specs=specs,
        out_specs=[packed, pl.BlockSpec((1, 1, 1, cols), lambda seq, head: (seq, head, 0, 0))],
        out_shape=[
            jax.ShapeDtypeStruct(queries.shape, jnp.bfloat16),
            jax.ShapeDtypeStruct((seqs, KV, 1, cols), jnp.float32),
        ],
        scratch_shapes=[pltpu.VMEM((2 * keys_per_half, cols), jnp.float32)],
        cost_estimate=pl.CostEstimate(
            flops=work * HD, bytes_accessed=8 * 1024 * 1024, transcendentals=work
        ),
        compiler_params=pltpu.CompilerParams(vmem_limit_bytes=VMEM_BYTES),
    )(queries, pairs, pairs, key_pos, query_pos)


def attend_back(queries, pairs, key_pos, query_pos, mixed, log_total, d_mixed):
    seqs, _, _, cols = queries.shape
    keys_per_half = pairs.shape[-1]
    packed, specs = attention_specs(cols, keys_per_half)
    work = seqs * HEADS * keys_per_half * cols // GROUP * 3
    return pl.pallas_call(
        attend_back_body,
        grid=(seqs, KV),
        in_specs=specs
        + [
            packed,
            pl.BlockSpec((1, 1, 1, cols), lambda seq, head: (seq, head, 0, 0)),
            packed,
        ],
        out_specs=[
            packed,
            pl.BlockSpec(
                (1, 2, 1, keys_per_half, 2 * HD), lambda seq, head: (seq, 0, head, 0, 0)
            ),
        ],
        out_shape=[
            jax.ShapeDtypeStruct(queries.shape, jnp.float32),
            jax.ShapeDtypeStruct((seqs, 2, KV, keys_per_half, 2 * HD), jnp.bfloat16),
        ],
        cost_estimate=pl.CostEstimate(
            flops=work * HD * 3, bytes_accessed=16 * 1024 * 1024, transcendentals=work
        ),
        compiler_params=pltpu.CompilerParams(vmem_limit_bytes=VMEM_BYTES),
    )(queries, pairs, pairs, key_pos, query_pos, mixed, log_total, d_mixed)


def feed_body(
    a_two_ref, dy_ref, gate_ref, up_ref, down_ref, out_ref, d_two_ref, d_gate_ref, d_up_ref, d_down_ref
):
    @pl.when(pl.program_id(0) == 0)
    def _():
        out_ref[...] = jnp.zeros_like(out_ref)
        d_two_ref[...] = jnp.zeros_like(d_two_ref)

    a_two, dy_low = a_two_ref[...], dy_ref[...]
    gate_rows, up_rows, down_rows = gate_ref[...], up_ref[...], down_ref[...]
    gate_pre = matmul_t(gate_rows, a_two)
    up_pre = matmul_t(up_rows, a_two)
    d_hidden = matmul_t(down_rows, dy_low)
    sigma = jax.nn.sigmoid(gate_pre)
    gate_act = gate_pre * sigma
    hidden = (gate_act * up_pre).astype(jnp.bfloat16)
    d_gate = (d_hidden * up_pre * sigma * (1.0 + gate_pre * (1.0 - sigma))).astype(jnp.bfloat16)
    d_up = (d_hidden * gate_act).astype(jnp.bfloat16)
    out_ref[...] += matmul_c(hidden, down_rows)
    d_two_ref[...] += matmul_c(d_gate, gate_rows) + matmul_c(d_up, up_rows)
    d_gate_ref[0] = matmul_n(d_gate, a_two).astype(jnp.bfloat16)
    d_up_ref[0] = matmul_n(d_up, a_two).astype(jnp.bfloat16)
    d_down_ref[0] = matmul_n(hidden, dy_low).astype(jnp.bfloat16)


def feed_forward(a_two, dy_low, gathered, rows, cut_g):
    tokens, width = a_two.shape
    blocks = FF // rows
    first = cut_g // rows
    whole = pl.BlockSpec((tokens, width), lambda step: (0, 0))
    grads = pl.BlockSpec((1, rows, width), lambda step: (step, 0, 0))
    return pl.pallas_call(
        feed_body,
        grid=(blocks,),
        in_specs=[whole, whole]
        + [
            pl.BlockSpec((rows, width), lambda step, start=first + member * blocks: (start + step, 0))
            for member in range(3)
        ],
        out_specs=[whole, whole, grads, grads, grads],
        out_shape=[jax.ShapeDtypeStruct((tokens, width), jnp.float32)] * 2
        + [jax.ShapeDtypeStruct((blocks, rows, width), jnp.bfloat16)] * 3,
        cost_estimate=pl.CostEstimate(
            flops=18 * tokens * width * FF, bytes_accessed=12 * FF * width, transcendentals=FF * tokens
        ),
        compiler_params=pltpu.CompilerParams(vmem_limit_bytes=VMEM_BYTES),
    )(a_two, dy_low, gathered, gathered, gathered)


def adam_update(param, grad, first, second, rate, decay, step_number):
    first_new = BETA_ONE * first + (1.0 - BETA_ONE) * grad
    second_new = BETA_TWO * second + (1.0 - BETA_TWO) * grad * grad
    fix_one = 1.0 - BETA_ONE**step_number
    fix_two = 1.0 - BETA_TWO**step_number
    update = first_new / fix_one / (jnp.sqrt(second_new / fix_two) + ADAM_EPS)
    return (first_new, second_new, param - rate * (update + decay * param))


def shards(inputs, cotangent, weights, gains, first_moment, second_moment, gain_first, gain_second):
    sizes = (lax.axis_size("dp"), lax.axis_size("ctx"))
    ctx_count = sizes[1]
    ctx_index = lax.axis_index("ctx")
    seqs, local_rows, model_width = inputs.shape
    half_rows = local_rows // 2
    tokens = seqs * local_rows
    weight_rows = weights.shape[0]
    q_cols = HEADS * HD
    kv_cols = KV * HD
    cut_o = q_cols + 2 * kv_cols
    cut_g = cut_o + q_cols
    along_y, along_z = axis_bits()[2:]
    ctx_order = list(reversed(along_z)) + along_y
    local_index = jnp.arange(local_rows, dtype=jnp.int32)
    pos_here = places(ctx_index * local_rows + local_index, local_rows, ctx_count)
    pos_tokens = jnp.tile(pos_here, seqs)
    turn, turn_back = angle_tables(pos_tokens, 1.0), angle_tables(pos_tokens, -1.0)

    def pack(flat):
        return (
            flat.reshape(KV, GROUP, HD, seqs, 2, half_rows)
            .transpose(3, 0, 2, 4, 1, 5)
            .reshape(seqs, KV, HD, 2 * GROUP * half_rows)
        )

    def unpack(packed):
        return (
            packed.reshape(seqs, KV, HD, 2, GROUP, half_rows)
            .transpose(1, 4, 2, 0, 3, 5)
            .reshape(q_cols, tokens)
        )

    owners = ctx_index ^ jnp.asarray(rel_offsets(ctx_order, sizes), jnp.int32)
    inner = jnp.arange(half_rows, dtype=jnp.int32)
    key_pos = jnp.stack(
        [
            (owners[:, None] * half_rows + inner[None, :]).reshape(-1, 1),
            ((2 * ctx_count - 1 - owners[:, None]) * half_rows + inner[None, :]).reshape(-1, 1),
        ]
    )
    query_pos = jnp.broadcast_to(
        pos_here.reshape(2, 1, half_rows), (2, GROUP, half_rows)
    ).reshape(1, 2 * GROUP * half_rows)

    gathered = gather_weights(weights)
    tokens_in = inputs.reshape(tokens, model_width)
    cot_in = cotangent.reshape(tokens, model_width)
    a_one = (normalize(tokens_in) * gains[0]).astype(jnp.bfloat16)
    qkv = matmul_t(gathered[:cut_o], a_one)
    q_rot = (rotate(qkv[:q_cols], turn).astype(jnp.bfloat16) * SCALE_QK).astype(jnp.bfloat16)
    key_rot = rotate(qkv[q_cols : q_cols + kv_cols], turn).astype(jnp.bfloat16)
    value_rows = qkv[q_cols + kv_cols :].astype(jnp.bfloat16)
    queries = pack(q_rot)
    joined = jnp.concatenate([key_rot, value_rows], axis=0).reshape(2 * kv_cols, seqs, local_rows)

    def lay(slots):
        return (
            slots.reshape(ctx_count, 2 * kv_cols, 2, half_rows)
            .transpose(2, 1, 0, 3)
            .reshape(2, 2 * kv_cols, ctx_count * half_rows)
        )

    pairs = jnp.stack([lay(spread(joined[:, seq], ctx_order)) for seq in range(seqs)])
    mixed, log_total = attend(queries, pairs, key_pos, query_pos)
    attn_low = unpack(mixed)
    resid = tokens_in + matmul_c(attn_low, gathered[cut_o:cut_g])
    a_two = (normalize(resid) * gains[1]).astype(jnp.bfloat16)
    dy_low = cot_in.astype(jnp.bfloat16)
    fed, d_two, d_gate, d_up, d_down = feed_forward(a_two, dy_low, gathered, weight_rows, cut_g)
    result = resid + fed
    d_norm_two, d_gain_two = norm_back(resid, d_two, gains[1])
    d_resid = cot_in + d_norm_two
    d_resid_low = d_resid.astype(jnp.bfloat16)
    d_attn = matmul_t(gathered[cut_o:cut_g], d_resid_low).astype(jnp.bfloat16)
    d_queries, d_pairs = attend_back(
        queries, pairs, key_pos, query_pos, mixed, log_total, pack(d_attn)
    )
    d_pair_slots = d_pairs.reshape(seqs, 2, KV, ctx_count, half_rows, 2 * HD).transpose(
        0, 3, 1, 2, 4, 5
    )
    d_own = jnp.stack(
        [collect(d_pair_slots[seq], list(reversed(ctx_order))) for seq in range(seqs)]
    )
    d_own = d_own.transpose(2, 4, 0, 1, 3).reshape(KV, 2 * HD, tokens)
    d_k = d_own[:, :HD].reshape(kv_cols, tokens)
    d_v = d_own[:, HD:].reshape(kv_cols, tokens)
    d_qkv = jnp.concatenate(
        [
            rotate(unpack(d_queries) * SCALE_QK, turn_back).astype(jnp.bfloat16),
            rotate(d_k, turn_back).astype(jnp.bfloat16),
            d_v.astype(jnp.bfloat16),
        ],
        axis=0,
    )
    d_one = matmul_c(d_qkv, gathered[:cut_o])
    d_norm_one, d_gain_one = norm_back(tokens_in, d_one, gains[0])
    d_tokens = d_resid + d_norm_one
    d_first = jnp.concatenate(
        [
            matmul_n(d_qkv, a_one).astype(jnp.bfloat16),
            matmul_n(attn_low, d_resid_low).astype(jnp.bfloat16),
        ],
        axis=0,
    ).reshape(-1, weight_rows, model_width)
    weight_share = scatter_sum([d_first, d_gate, d_up, d_down])
    gain_grad = butterfly_sum(jnp.stack([d_gain_one, d_gain_two], axis=0))
    weight_first, weight_second, weight_new = adam_update(
        weights.astype(jnp.float32), weight_share, first_moment, second_moment, RATE, DECAY, STEP
    )
    gain_first_new, gain_second_new, gain_new = adam_update(
        gains, gain_grad, gain_first, gain_second, GAIN_RATE, 0.0, STEP
    )
    return (
        result.reshape(inputs.shape),
        d_tokens.reshape(inputs.shape),
        weight_share,
        weight_second,
        weight_new,
        gain_grad,
        gain_second_new,
        gain_new,
    )


def solution(mesh):
    placed = (
        P("dp", "ctx", None),
        P("dp", "ctx", None),
        P(("dp", "ctx"), None),
        P(),
        P(("dp", "ctx"), None),
        P(("dp", "ctx"), None),
        P(),
        P(),
    )
    return jax.shard_map(
        shards,
        mesh=mesh,
        in_specs=placed,
        out_specs=(
            P("dp", "ctx", None),
            P("dp", "ctx", None),
            P(("dp", "ctx"), None),
            P(("dp", "ctx"), None),
            P(("dp", "ctx"), None),
            P(),
            P(),
            P(),
        ),
        check_vma=False,
    )
```

```python
import jax
import jax.numpy as jnp
import numpy as np
from jax import lax
from jax.experimental import pallas as pl
from jax.experimental.pallas import tpu as pltpu
from jax.sharding import Mesh
from jax.sharding import PartitionSpec as P

HEADS = 15
KV = 5
HD = 64
FF = 2560
STEP = 10


SCALE_QK = 0.125
THETA = 10000.0
EPSILON = 1e-05
BETA_ONE = 0.9
BETA_TWO = 0.95
ADAM_EPS = 1e-08
DECAY = 0.1
RATE = 0.02
GAIN_RATE = 0.2
GROUP = HEADS // KV
KEY_TILE = 256
HIDDEN = -1e30
VMEM_BYTES = 48 * 1024 * 1024


def places(row_index, local_rows, ctx_count):
    half_rows = local_rows // 2
    owner_index = row_index // local_rows
    inner_index = row_index % local_rows
    return jnp.where(
        inner_index < half_rows,
        owner_index * half_rows + inner_index,
        (2 * ctx_count - 1 - owner_index) * half_rows + inner_index - half_rows,
    )


def angle_tables(positions_in, sign):
    half_width = HD // 2
    frequency = THETA ** (-jnp.arange(half_width, dtype=jnp.float32) * 2.0 / HD)
    angles = frequency[:, None] * positions_in.astype(jnp.float32)[None, :]
    return jnp.cos(angles), sign * jnp.sin(angles)


def rotate(values, tables):
    cosine, sine_part = tables
    heads = values.reshape(-1, HD, values.shape[-1])
    first_half = heads[:, : HD // 2]
    second_half = heads[:, HD // 2 :]
    return jnp.concatenate(
        [
            first_half * cosine - second_half * sine_part,
            second_half * cosine + first_half * sine_part,
        ],
        axis=1,
    ).reshape(values.shape)


def normalize(values):
    return values * lax.rsqrt(jnp.mean(values * values, axis=-1, keepdims=True) + EPSILON)


def norm_back(values, grad_in, gain_row):
    inv_scale = lax.rsqrt(jnp.mean(values * values, axis=-1, keepdims=True) + EPSILON)
    unit_rows = values * inv_scale
    grad_unit = grad_in * gain_row
    grad_values = inv_scale * (
        grad_unit - unit_rows * jnp.mean(grad_unit * unit_rows, axis=-1, keepdims=True)
    )
    return (grad_values, jnp.sum(grad_in * unit_rows, axis=0))


def matmul_n(left, right):
    return jnp.dot(left, right, preferred_element_type=jnp.float32)


def matmul_t(left, right):
    return lax.dot_general(
        left, right, (((1,), (1,)), ((), ())), preferred_element_type=jnp.float32
    )


def matmul_c(left, right):
    return lax.dot_general(
        left, right, (((0,), (0,)), ((), ())), preferred_element_type=jnp.float32
    )


def bit_groups():
    x_bits = lax.axis_size("x").bit_length() - 1
    ctx_bits = lax.axis_size("ctx").bit_length() - 1
    low_ctx = ctx_bits // 2
    along_x = [("x", bit) for bit in range(x_bits)]
    along_y = [("ctx", bit) for bit in range(low_ctx)]
    along_z = [("ctx", bit) for bit in range(low_ctx, ctx_bits)]
    return along_x, along_y, along_z


def swap_by(values, axis, offset):
    size = lax.axis_size(axis)
    return lax.ppermute(values, axis, [(i, i ^ offset) for i in range(size)])


def swap(values, where):
    return swap_by(values, where[0], 1 << where[1])


def add_low(left, right):
    return (left.astype(jnp.float32) + right.astype(jnp.float32)).astype(jnp.bfloat16)


def rel_offsets(order):
    strides = {"x": 2 * lax.axis_size("ctx"), "ctx": 1}
    offsets = np.zeros((1,), np.int64)
    for axis, bit in order:
        offsets = np.concatenate([offsets, offsets ^ (strides[axis] << bit)])
    return offsets


def lookup(slot, offsets):
    total = jnp.int32(0)
    for bit in range(len(offsets).bit_length() - 1):
        total = total + ((slot >> bit) & 1) * int(offsets[1 << bit])
    return total


def find(offset, offsets):
    total = jnp.int32(0)
    for bit in range(len(offsets).bit_length() - 1):
        place = int(offsets[1 << bit]).bit_length() - 1
        total = total + (((offset >> place) & 1) << bit)
    return total


def collect(values, order):
    kept, arrived = values, None
    for where in order:
        half = kept.shape[0] // 2
        if arrived is None:
            away, kept_next = kept[half:], kept[:half]
        else:
            away = add_low(kept[half:], arrived[half:])
            kept_next = add_low(kept[:half], arrived[:half])
        arrived = swap(away, where)
        kept = kept_next
    return kept[0].astype(jnp.float32) + arrived[0].astype(jnp.float32)


def scatter_whole(terms):
    ctx_count = lax.axis_size("ctx")
    count = 2 * lax.axis_size("x") * ctx_count
    along_x, along_y, along_z = bit_groups()
    core = ("core", 0)
    me = device_index().reshape(1)
    blocks, rows, width = terms[0].shape
    first = -(-rows // 48) * 16
    groups = [(0, first), (first, 2 * first), (2 * first, rows)]
    orders = [
        along_x + along_y + along_z,
        along_y + along_z + along_x,
        along_z + along_x + along_y,
    ]
    tables = [rel_offsets(list(reversed(order))) for order in orders]

    def target(step, me_ref, flip):
        return lookup(step, tables[0]) ^ me_ref[0] ^ flip

    def sources(flip):
        def chosen(member):
            def index(step, me_ref):
                spot = target(step, me_ref, flip)
                return (jnp.where(spot // blocks == member, spot % blocks, 0), 0, 0)

            return pl.BlockSpec((1, rows, width), index)

        return [chosen(member) for member in range(len(terms))]

    def pick_body(me_ref, *refs):
        held = target(pl.program_id(0), me_ref, ctx_count) // blocks
        for member in range(len(terms)):

            @pl.when(held == member)
            def _(member=member):
                refs[-1][...] = refs[member][...]

    away = pl.pallas_call(
        pick_body,
        grid_spec=pltpu.PrefetchScalarGridSpec(
            num_scalar_prefetch=1,
            grid=(count // 2,),
            in_specs=sources(ctx_count),
            out_specs=pl.BlockSpec((1, rows, width), lambda step, me_ref: (step, 0, 0)),
        ),
        out_shape=jax.ShapeDtypeStruct((count // 2, rows, width), jnp.bfloat16),
        compiler_params=pltpu.CompilerParams(vmem_limit_bytes=VMEM_BYTES),
    )(me, *terms)
    arrived = swap(away, core)

    def merge_body(me_ref, *refs):
        held = target(pl.program_id(0), me_ref, 0) // blocks
        for member in range(len(terms)):

            @pl.when(held == member)
            def _(member=member):
                for (low, high), out in zip(groups, refs[-3:]):
                    out[0] = add_low(refs[member][0, low:high], refs[-4][0, low:high])

    parts = pl.pallas_call(
        merge_body,
        grid_spec=pltpu.PrefetchScalarGridSpec(
            num_scalar_prefetch=1,
            grid=(count // 2,),
            in_specs=sources(0)
            + [pl.BlockSpec((1, rows, width), lambda step, me_ref: (step, 0, 0))],
            out_specs=[
                pl.BlockSpec(
                    (1, high - low, width),
                    lambda step, me_ref, table=table: (
                        find(lookup(step, tables[0]), table),
                        0,
                        0,
                    ),
                )
                for (low, high), table in zip(groups, tables)
            ],
        ),
        out_shape=[
            jax.ShapeDtypeStruct((count // 2, high - low, width), jnp.bfloat16)
            for low, high in groups
        ],
        compiler_params=pltpu.CompilerParams(vmem_limit_bytes=VMEM_BYTES),
    )(me, *terms, arrived)
    return jnp.concatenate([collect(part, order) for part, order in zip(parts, orders)], axis=0)


def device_index():
    return (
        (lax.axis_index("x") * 2 + lax.axis_index("core")) * lax.axis_size("ctx")
        + lax.axis_index("ctx")
    ).astype(jnp.int32)


def splits_rows(rows):
    return lax.axis_size("x") == 2 and rows % 32 == 0


def reduce_ctx(keep, away):
    arrived = swap(away, ("core", 0))
    along_x, along_y, along_z = bit_groups()
    rows = keep.shape[2]
    first = -(-rows // 32) * 16
    sums = []
    plain = along_y + along_z
    ctx_bits = len(plain)
    for low, high, order in ((0, first, plain), (first, rows, along_z + along_y)):
        shape = (keep.shape[0],) + (2,) * ctx_bits + (high - low, keep.shape[3])
        held = keep[:, :, low:high].reshape(shape)
        come = arrived[:, :, low:high].reshape(shape)
        left = list(reversed(range(ctx_bits)))
        for where in order:
            dim = 1 + left.index(where[1])
            left.remove(where[1])
            sent = add_low(
                lax.index_in_dim(held, 1, dim, False), lax.index_in_dim(come, 1, dim, False)
            )
            held = add_low(
                lax.index_in_dim(held, 0, dim, False), lax.index_in_dim(come, 0, dim, False)
            )
            come = swap(sent, where)
        sums.append(add_low(held, come))
    return jnp.concatenate(sums, axis=1)


def turned(values):
    return jnp.transpose(values)


def load_packed(ref, aligned):
    if not aligned:
        return ref[0, 0]
    half = ref.shape[1] // 2
    return jnp.concatenate(
        [
            ref[head * HD : (head + 1) * HD, side * half : (side + 1) * half]
            for side in range(2)
            for head in range(GROUP)
        ],
        axis=1,
    )


def store_packed(ref, values, aligned):
    if not aligned:
        ref[0, 0] = values
        return
    half = ref.shape[1] // 2
    for side in range(2):
        for head in range(GROUP):
            start = (side * GROUP + head) * half
            ref[head * HD : (head + 1) * HD, side * half : (side + 1) * half] = values[
                :, start : start + half
            ]


def load_tile(refs, side, tile):
    length = refs[0].shape[1] // 2
    if length >= KEY_TILE:
        start = side * length + tile * KEY_TILE
        return refs[0][:, start : start + KEY_TILE]
    many = KEY_TILE // length
    return jnp.concatenate(
        [
            ref[:, side * length : (side + 1) * length]
            for ref in refs[tile * many : (tile + 1) * many]
        ],
        axis=1,
    )


def attend_body(count, aligned, queries_ref, key_pos_ref, query_pos_ref, *refs):
    key_refs, value_refs = refs[:count], refs[count : 2 * count]
    out_ref, total_ref, work = refs[2 * count :]
    queries = load_packed(queries_ref, aligned)
    low_cols = queries.shape[1] // 2
    queries_high = queries[:, low_cols:]
    tiles = key_pos_ref.shape[1] // KEY_TILE
    largest = jnp.full((1, queries.shape[1]), HIDDEN, jnp.float32)
    largest_high = jnp.full((1, low_cols), HIDDEN, jnp.float32)
    for side in range(2):
        for tile in range(tiles):
            keys = turned(load_tile(key_refs, side, tile))
            row = (side * tiles + tile) * KEY_TILE
            key_places = key_pos_ref[side, tile * KEY_TILE : (tile + 1) * KEY_TILE]
            if side == 0:
                scores = matmul_n(keys, queries)
                scores = jnp.where(key_places <= query_pos_ref[...], scores, HIDDEN)
                work[row : row + KEY_TILE] = scores
                largest = jnp.maximum(largest, jnp.max(scores, axis=0, keepdims=True))
            else:
                scores = matmul_n(keys, queries_high)
                scores = jnp.where(key_places <= query_pos_ref[:, low_cols:], scores, HIDDEN)
                work[row : row + KEY_TILE, low_cols:] = scores
                largest_high = jnp.maximum(largest_high, jnp.max(scores, axis=0, keepdims=True))
    high_max = jnp.maximum(largest[:, low_cols:], largest_high)
    largest = jnp.concatenate([largest[:, :low_cols], high_max], axis=1)
    total = jnp.zeros_like(largest)
    mixed = jnp.zeros((HD, queries.shape[1]), jnp.float32)
    total_high = jnp.zeros_like(largest_high)
    mixed_high = jnp.zeros((HD, low_cols), jnp.float32)
    for side in range(2):
        for tile in range(tiles):
            values = load_tile(value_refs, side, tile)
            row = (side * tiles + tile) * KEY_TILE
            if side == 0:
                expos = jnp.exp(work[row : row + KEY_TILE] - largest)
                total = total + jnp.sum(expos, axis=0, keepdims=True)
                mixed = mixed + matmul_n(values, expos.astype(jnp.bfloat16))
            else:
                expos = jnp.exp(work[row : row + KEY_TILE, low_cols:] - high_max)
                total_high = total_high + jnp.sum(expos, axis=0, keepdims=True)
                mixed_high = mixed_high + matmul_n(values, expos.astype(jnp.bfloat16))
    total = jnp.concatenate([total[:, :low_cols], total[:, low_cols:] + total_high], axis=1)
    mixed = jnp.concatenate([mixed[:, :low_cols], mixed[:, low_cols:] + mixed_high], axis=1)
    store_packed(out_ref, (mixed / total).astype(jnp.bfloat16), aligned)
    total_ref[0, 0] = largest + jnp.log(total)


def attend_back_body(
    count, aligned, queries_ref, key_pos_ref, query_pos_ref, *refs
):
    key_refs, value_refs = refs[:count], refs[count : 2 * count]
    out_ref, total_ref, d_out_ref, cosine_ref, sine_ref = refs[2 * count : 2 * count + 5]
    d_queries_ref, pair_refs = refs[2 * count + 5], refs[2 * count + 6 :]
    all_queries, all_d_out = load_packed(queries_ref, aligned), load_packed(d_out_ref, aligned)
    low_cols = all_queries.shape[1] // 2
    tiles = key_pos_ref.shape[1] // KEY_TILE
    delta = jnp.sum(
        all_d_out.astype(jnp.float32) * load_packed(out_ref, aligned).astype(jnp.float32),
        axis=0,
        keepdims=True,
    )
    totals = total_ref[0, 0]
    parts = []
    for side in range(2):
        if side == 0:
            queries, d_out = all_queries, all_d_out
            query_places, log_total, row_delta = query_pos_ref[...], totals, delta
        else:
            queries, d_out = all_queries[:, low_cols:], all_d_out[:, low_cols:]
            query_places = query_pos_ref[:, low_cols:]
            log_total, row_delta = totals[:, low_cols:], delta[:, low_cols:]
        part = jnp.zeros((HD, queries.shape[1]), jnp.float32)
        for tile in range(tiles):
            keys_flat = load_tile(key_refs, side, tile)
            scores = matmul_n(turned(keys_flat), queries)
            seen = key_pos_ref[side, tile * KEY_TILE : (tile + 1) * KEY_TILE] <= query_places
            probs = jnp.where(seen, jnp.exp(scores - log_total), 0.0)
            d_probs = matmul_n(turned(load_tile(value_refs, side, tile)), d_out)
            d_scores = (probs * (d_probs - row_delta)).astype(jnp.bfloat16)
            part = part + matmul_n(keys_flat, d_scores)
            d_key = matmul_t(d_scores, queries).astype(jnp.bfloat16)
            d_value = matmul_t(probs.astype(jnp.bfloat16), d_out).astype(jnp.bfloat16)
            if aligned:
                length = key_refs[0].shape[1] // 2
                near = pair_refs[0].shape[0]
                for piece in range(KEY_TILE // length):
                    slot = tile * (KEY_TILE // length) + piece
                    ref = pair_refs[slot // near]
                    rows = slice(piece * length, (piece + 1) * length)
                    ref[slot % near, 0, side, :, :HD] = d_key[rows]
                    ref[slot % near, 0, side, :, HD:] = d_value[rows]
            else:
                rows = slice(tile * KEY_TILE, (tile + 1) * KEY_TILE)
                pair_refs[0][side, 0, rows, :HD] = d_key
                pair_refs[0][side, 0, rows, HD:] = d_value
        parts.append(part)
    d_queries = jnp.concatenate(
        [parts[0][:, :low_cols], parts[0][:, low_cols:] + parts[1]], axis=1
    )
    cosine, sine_part = cosine_ref[...], sine_ref[...]
    first_half, second_half = d_queries[: HD // 2], d_queries[HD // 2 :]
    turned_back = jnp.concatenate(
        [
            first_half * cosine + second_half * sine_part,
            second_half * cosine - first_half * sine_part,
        ],
        axis=0,
    )
    store_packed(d_queries_ref, (turned_back * SCALE_QK).astype(jnp.bfloat16), aligned)


def head_specs(count, aligned, cols, keys, local_rows, seq):
    if aligned:
        packed = pl.BlockSpec((GROUP * HD, local_rows), lambda head: (head, seq))
    else:
        packed = pl.BlockSpec((1, 1, HD, cols), lambda head: (seq, head, 0, 0))
    specs = [
        packed,
        pl.BlockSpec((2, keys, 1), lambda head: (0, 0, 0)),
        pl.BlockSpec((1, cols), lambda head: (0, 0)),
    ]
    specs += [pl.BlockSpec((HD, 2 * keys // count), lambda head: (head, seq))] * count
    specs += [pl.BlockSpec((HD, 2 * keys // count), lambda head: (KV + head, seq))] * count
    return packed, specs


def attend(queries, pairs, key_pos, query_pos, local_rows, seq):
    aligned = queries.ndim == 2
    cols, keys, count = query_pos.shape[1], key_pos.shape[1], len(pairs)
    _, specs = head_specs(count, aligned, cols, keys, local_rows, seq)
    work = HEADS * keys * cols // GROUP * 3 // 2
    if aligned:
        out_spec = pl.BlockSpec((GROUP * HD, local_rows), lambda head: (head, 0))
        out_shape = jax.ShapeDtypeStruct((HEADS * HD, local_rows), jnp.bfloat16)
    else:
        out_spec = pl.BlockSpec((1, 1, HD, cols), lambda head: (0, head, 0, 0))
        out_shape = jax.ShapeDtypeStruct((1, KV, HD, cols), jnp.bfloat16)
    return pl.pallas_call(
        lambda *refs: attend_body(count, aligned, *refs),
        grid=(KV,),
        in_specs=specs,
        out_specs=[out_spec, pl.BlockSpec((1, 1, 1, cols), lambda head: (0, head, 0, 0))],
        out_shape=[out_shape, jax.ShapeDtypeStruct((1, KV, 1, cols), jnp.float32)],
        scratch_shapes=[pltpu.VMEM((2 * keys, cols), jnp.float32)],
        cost_estimate=pl.CostEstimate(
            flops=work * HD * 4, bytes_accessed=8 * 1024 * 1024, transcendentals=work
        ),
        compiler_params=pltpu.CompilerParams(vmem_limit_bytes=VMEM_BYTES),
    )(queries, key_pos, query_pos, *pairs, *pairs)


def attend_back(
    queries, pairs, key_pos, query_pos, mixed, log_total, d_mixed, tables, local_rows, seq, near
):
    aligned = queries.ndim == 2
    cols, keys, count = query_pos.shape[1], key_pos.shape[1], len(pairs)
    packed, specs = head_specs(count, aligned, cols, keys, local_rows, seq)
    work = HEADS * keys * cols // GROUP * 3 // 2
    if aligned:
        own = pl.BlockSpec((GROUP * HD, local_rows), lambda head: (head, 0))
        own_shape = jax.ShapeDtypeStruct((HEADS * HD, local_rows), jnp.bfloat16)
        length = keys // count
        pair_specs = [
            pl.BlockSpec((near, 1, 2, length, 2 * HD), lambda head: (0, head, 0, 0, 0))
        ] * (count // near)
        pair_shapes = [jax.ShapeDtypeStruct((near, KV, 2, length, 2 * HD), jnp.bfloat16)] * (
            count // near
        )
    else:
        own = pl.BlockSpec((1, 1, HD, cols), lambda head: (0, head, 0, 0))
        own_shape = jax.ShapeDtypeStruct((1, KV, HD, cols), jnp.bfloat16)
        pair_specs = [pl.BlockSpec((2, 1, keys, 2 * HD), lambda head: (0, head, 0, 0))]
        pair_shapes = [jax.ShapeDtypeStruct((2, KV, keys, 2 * HD), jnp.bfloat16)]
    table_spec = pl.BlockSpec((HD // 2, cols), lambda head: (0, 0))
    return pl.pallas_call(
        lambda *refs: attend_back_body(count, aligned, *refs),
        grid=(KV,),
        in_specs=specs
        + [
            own,
            pl.BlockSpec((1, 1, 1, cols), lambda head: (0, head, 0, 0)),
            packed,
            table_spec,
            table_spec,
        ],
        out_specs=[own] + pair_specs,
        out_shape=[own_shape] + pair_shapes,
        cost_estimate=pl.CostEstimate(
            flops=work * HD * 10, bytes_accessed=16 * 1024 * 1024, transcendentals=work
        ),
        compiler_params=pltpu.CompilerParams(vmem_limit_bytes=VMEM_BYTES),
    )(queries, key_pos, query_pos, *pairs, *pairs, mixed, log_total, d_mixed, *tables)


def put_rows(values, keep_ref, away_ref, member, core):
    half = values.shape[0] // 2
    for mine, low, far in ((0, 0, half), (1, half, 0)):

        @pl.when(core == mine)
        def _(low=low, far=far):
            keep_ref[member, 0] = values[low : low + half]
            away_ref[member, 0] = values[far : far + half]


def feed_body(
    parts, split, me_ref, a_two_ref, dy_ref, *refs
):
    weight_refs, (out_ref, d_two_ref), grad_refs = refs[:6], refs[6:8], refs[8:]
    core = me_ref[0]
    step = pl.program_id(0)

    @pl.when(step == 0)
    def _():
        out_ref[...] = jnp.zeros_like(out_ref)
        d_two_ref[...] = jnp.zeros_like(d_two_ref)

    def rows_of(member):
        wanted = feed_core(member, step, parts)
        return jnp.where(wanted == core, weight_refs[2 * member][...], weight_refs[2 * member + 1][...])

    a_two, dy_low = a_two_ref[...], dy_ref[...]
    gate_rows, up_rows, down_rows = rows_of(0), rows_of(1), rows_of(2)
    gate_pre = matmul_t(gate_rows, a_two)
    up_pre = matmul_t(up_rows, a_two)
    d_hidden = matmul_t(down_rows, dy_low)
    sigma = jax.nn.sigmoid(gate_pre)
    gate_act = gate_pre * sigma
    hidden = (gate_act * up_pre).astype(jnp.bfloat16)
    d_gate = (d_hidden * up_pre * sigma * (1.0 + gate_pre * (1.0 - sigma))).astype(jnp.bfloat16)
    d_up = (d_hidden * gate_act).astype(jnp.bfloat16)
    out_ref[...] += matmul_c(hidden, down_rows)
    d_two_ref[...] += matmul_c(d_gate, gate_rows) + matmul_c(d_up, up_rows)
    for member, (left, right) in enumerate(((d_gate, a_two), (d_up, a_two), (hidden, dy_low))):
        grad = matmul_n(left, right).astype(jnp.bfloat16)
        if split:
            put_rows(grad, grad_refs[0], grad_refs[1], member, core)
        else:
            grad_refs[member][0] = grad


def feed_core(member, step, parts):
    ctx_count, single = parts
    return (member + 1) % 2 if single else step // ctx_count


def feed_forward(a_two, dy_low, mine, far, rows):
    tokens, width = a_two.shape
    ctx_count = lax.axis_size("ctx")
    blocks = FF // rows
    single = blocks == ctx_count
    split = splits_rows(rows)
    parts = (ctx_count, single)
    whole = pl.BlockSpec((tokens, width), lambda step, me_ref: (0, 0))

    def weight_spec(member, own):
        def index(step, me_ref):
            matches = (feed_core(member, step, parts) == me_ref[0]) == own
            return (jnp.where(matches, step % ctx_count, 0), 0)

        return pl.BlockSpec((rows, width), index)

    places_x = [(member + 1) // 2 if single else member + 1 for member in range(3)]
    weight_specs = [weight_spec(member, own) for member in range(3) for own in (True, False)]
    weight_args = [held[places_x[member]] for member in range(3) for held in (mine, far)]
    if split:
        half = pl.BlockSpec(
            (3, 1, rows // 2, width), lambda step, me_ref: (0, step ^ me_ref[1], 0, 0)
        )
        grad_specs = [half, half]
        grad_shapes = [jax.ShapeDtypeStruct((3, blocks, rows // 2, width), jnp.bfloat16)] * 2
    else:
        grad_specs = [pl.BlockSpec((1, rows, width), lambda step, me_ref: (step, 0, 0))] * 3
        grad_shapes = [jax.ShapeDtypeStruct((blocks, rows, width), jnp.bfloat16)] * 3
    me = jnp.stack([lax.axis_index("core"), lax.axis_index("ctx")]).astype(jnp.int32)
    return pl.pallas_call(
        lambda *refs: feed_body(parts, split, *refs),
        grid_spec=pltpu.PrefetchScalarGridSpec(
            num_scalar_prefetch=1,
            grid=(blocks,),
            in_specs=[whole, whole] + weight_specs,
            out_specs=[whole, whole] + grad_specs,
        ),
        out_shape=[jax.ShapeDtypeStruct((tokens, width), jnp.float32)] * 2 + grad_shapes,
        cost_estimate=pl.CostEstimate(
            flops=18 * tokens * width * FF, bytes_accessed=12 * FF * width, transcendentals=FF * tokens
        ),
        compiler_params=pltpu.CompilerParams(vmem_limit_bytes=VMEM_BYTES),
    )(me, a_two, dy_low, *weight_args)


def first_grads(d_qkv, attn_low, a_one, d_resid_low, rows):
    tokens, width = a_one.shape
    split = splits_rows(rows)
    early = d_qkv.shape[0] // rows
    blocks = early + attn_low.shape[0] // rows

    def body(me_ref, qkv_ref, attn_ref, one_ref, resid_ref, *grad_refs):
        first = pl.program_id(0) < early
        left = jnp.where(first, qkv_ref[...], attn_ref[...])
        right = jnp.where(first, one_ref[...], resid_ref[...])
        grad = matmul_n(left, right).astype(jnp.bfloat16)
        if split:
            put_rows(grad, grad_refs[0], grad_refs[1], 0, me_ref[0])
        else:
            grad_refs[0][0] = grad

    whole = pl.BlockSpec((tokens, width), lambda step, me_ref: (0, 0))
    if split:
        half = pl.BlockSpec(
            (1, 1, rows // 2, width), lambda step, me_ref: (0, step ^ me_ref[1], 0, 0)
        )
        grad_specs = [half, half]
        grad_shapes = [jax.ShapeDtypeStruct((1, blocks, rows // 2, width), jnp.bfloat16)] * 2
    else:
        grad_specs = [pl.BlockSpec((1, rows, width), lambda step, me_ref: (step, 0, 0))]
        grad_shapes = [jax.ShapeDtypeStruct((blocks, rows, width), jnp.bfloat16)]
    me = jnp.stack([lax.axis_index("core"), lax.axis_index("ctx")]).astype(jnp.int32)
    return pl.pallas_call(
        body,
        grid_spec=pltpu.PrefetchScalarGridSpec(
            num_scalar_prefetch=1,
            grid=(blocks,),
            in_specs=[
                pl.BlockSpec((rows, tokens), lambda step, me_ref: (jnp.minimum(step, early - 1), 0)),
                pl.BlockSpec((rows, tokens), lambda step, me_ref: (jnp.maximum(step - early, 0), 0)),
                whole,
                whole,
            ],
            out_specs=grad_specs,
        ),
        out_shape=grad_shapes,
        cost_estimate=pl.CostEstimate(
            flops=2 * tokens * width * blocks * rows, bytes_accessed=2 * blocks * rows * width, transcendentals=0
        ),
        compiler_params=pltpu.CompilerParams(vmem_limit_bytes=VMEM_BYTES),
    )(me, d_qkv, attn_low, a_one, d_resid_low)


def adam_update(param, grad, first, second, rate, decay, step_number):
    first_new = BETA_ONE * first + (1.0 - BETA_ONE) * grad
    second_new = BETA_TWO * second + (1.0 - BETA_TWO) * grad * grad
    fix_one = 1.0 - BETA_ONE**step_number
    fix_two = 1.0 - BETA_TWO**step_number
    update = first_new / fix_one / (jnp.sqrt(second_new / fix_two) + ADAM_EPS)
    return (first_new, second_new, param - rate * (update + decay * param))


def shards(inputs, cotangent, weights, gains, first_moment, second_moment, gain_first, gain_second):
    ctx_count = lax.axis_size("ctx")
    x_count = lax.axis_size("x")
    ctx_index, core, x_index = lax.axis_index("ctx"), lax.axis_index("core"), lax.axis_index("x")
    seqs, local_rows, model_width = inputs.shape
    half_rows = local_rows // 2
    tokens = seqs * local_rows
    weight_rows = weights.shape[0]
    q_cols = HEADS * HD
    kv_cols = KV * HD
    cut_o = q_cols + 2 * kv_cols
    along_y, along_z = bit_groups()[1:]
    y_count, z_count = 1 << len(along_y), 1 << len(along_z)
    slot_offsets = [z * y_count + y for y in range(y_count) for z in range(z_count)]
    aligned = half_rows % 128 == 0
    local_index = jnp.arange(local_rows, dtype=jnp.int32)
    pos_here = places(ctx_index * local_rows + local_index, local_rows, ctx_count)
    cosine, sine_part = angle_tables(pos_here, 1.0)
    turn = (jnp.tile(cosine, (1, seqs)), jnp.tile(sine_part, (1, seqs)))
    turn_back = (turn[0], -turn[1])

    def pack(flat):
        if aligned:
            return flat
        return (
            flat.reshape(KV, GROUP, HD, -1, 2, half_rows)
            .transpose(3, 0, 2, 4, 1, 5)
            .reshape(-1, KV, HD, 2 * GROUP * half_rows)
        )

    def unpack(packed):
        if aligned:
            return packed
        return (
            packed.reshape(KV, HD, 2, GROUP, half_rows)
            .transpose(0, 3, 1, 2, 4)
            .reshape(q_cols, local_rows)
        )

    def by_columns(row):
        rows = row.shape[0]
        return jnp.broadcast_to(
            row.reshape(rows, 2, 1, half_rows), (rows, 2, GROUP, half_rows)
        ).reshape(rows, 2 * GROUP * half_rows)

    owners = ctx_index ^ jnp.asarray(slot_offsets, jnp.int32)
    inner = jnp.arange(half_rows, dtype=jnp.int32)
    key_pos = jnp.stack(
        [
            (owners[:, None] * half_rows + inner[None, :]).reshape(-1, 1),
            ((2 * ctx_count - 1 - owners[:, None]) * half_rows + inner[None, :]).reshape(-1, 1),
        ]
    )
    query_pos = by_columns(pos_here[None, :])
    packed_tables = (by_columns(cosine), by_columns(sine_part))

    held = lax.all_gather(weights, ("x", "ctx"), axis=0, tiled=True)
    held = held.reshape(x_count, ctx_count * weight_rows, model_width)
    mine = [held[x] for x in range(x_count)]
    far = [swap(part, ("core", 0)) for part in mine]
    first_rows = jnp.where(core == 0, mine[0], far[0])
    if first_rows.shape[0] < cut_o + q_cols:
        first_rows = jnp.concatenate([first_rows, jnp.where(core == 0, far[0], mine[0])], axis=0)
    qkv_rows, o_rows = first_rows[:cut_o], first_rows[cut_o : cut_o + q_cols]

    tokens_in = inputs.reshape(tokens, model_width)
    cot_in = cotangent.reshape(tokens, model_width)
    dy_low = cot_in.astype(jnp.bfloat16)
    a_one = (normalize(tokens_in) * gains[0]).astype(jnp.bfloat16)
    pair_rows = matmul_t(qkv_rows[q_cols:], a_one)
    joined = jnp.concatenate(
        [rotate(pair_rows[:kv_cols], turn).astype(jnp.bfloat16), pair_rows[kv_cols:].astype(jnp.bfloat16)],
        axis=0,
    )
    near = [joined] + [swap_by(joined, "ctx", z * y_count) for z in range(1, z_count)]
    pairs = list(near)
    for y in range(1, y_count):
        pairs += [swap_by(part, "ctx", y) for part in near]
    if not aligned:
        pairs = [
            jnp.stack(pairs)
            .reshape(ctx_count, 2 * kv_cols, seqs, 2, half_rows)
            .transpose(1, 2, 3, 0, 4)
            .reshape(2 * kv_cols, seqs * 2 * ctx_count * half_rows)
        ]
    q_rot = rotate(matmul_t(qkv_rows[:q_cols], a_one), turn).astype(jnp.bfloat16)
    queries = pack((q_rot * SCALE_QK).astype(jnp.bfloat16))
    attended = [
        attend(queries, pairs, key_pos, query_pos, local_rows, seq) for seq in range(seqs)
    ]
    attn_low = jnp.concatenate([unpack(mixed) for mixed, _ in attended], axis=1)
    resid = tokens_in + matmul_c(attn_low, o_rows)
    a_two = (normalize(resid) * gains[1]).astype(jnp.bfloat16)
    fed, d_two, *feed_grads = feed_forward(a_two, dy_low, mine, far, weight_rows)
    split = splits_rows(weight_rows)
    if split:
        feed_sums = reduce_ctx(*feed_grads)
    result = resid + fed
    d_norm_two, d_gain_two = norm_back(resid, d_two, gains[1])
    d_resid = cot_in + d_norm_two
    d_resid_low = d_resid.astype(jnp.bfloat16)
    d_attn = pack(matmul_t(o_rows, d_resid_low).astype(jnp.bfloat16))
    d_q, d_pair = [], []
    for seq in range(seqs):
        mixed, log_total = attended[seq]
        d_queries, *d_slots = attend_back(
            queries, pairs, key_pos, query_pos, mixed, log_total, d_attn, packed_tables,
            local_rows, seq, z_count,
        )
        d_q.append(unpack(d_queries))
        if not aligned:
            d_slots = (
                d_slots[0]
                .reshape(2, KV, ctx_count, half_rows, 2 * HD)
                .transpose(2, 1, 0, 3, 4)
                .reshape(y_count, z_count, KV, 2, half_rows, 2 * HD)
            )
            d_slots = [d_slots[y] for y in range(y_count)]
        line = d_slots[0].astype(jnp.float32)
        for y in range(1, y_count):
            line = line + swap_by(d_slots[y], "ctx", y).astype(jnp.float32)
        total = line[0]
        for z in range(1, z_count):
            total = total + swap_by(line[z].astype(jnp.bfloat16), "ctx", z * y_count).astype(jnp.float32)
        d_pair.append(total)
    d_own = jnp.stack(d_pair).transpose(1, 4, 0, 2, 3).reshape(KV, 2 * HD, tokens)
    d_qkv = jnp.concatenate(
        [
            jnp.concatenate(d_q, axis=1),
            rotate(d_own[:, :HD].reshape(kv_cols, tokens), turn_back).astype(jnp.bfloat16),
            d_own[:, HD:].reshape(kv_cols, tokens).astype(jnp.bfloat16),
        ],
        axis=0,
    )
    first_terms = first_grads(d_qkv, attn_low, a_one, d_resid_low, weight_rows)
    if split:
        first_sums = reduce_ctx(*first_terms)
        sums = [first_sums[0], feed_sums[0], feed_sums[1], feed_sums[2]]
        own_x = [jnp.where(x_index == 0, sums[core_of], sums[2 + core_of]) for core_of in range(2)]
        other_x = [jnp.where(x_index == 0, sums[2 + core_of], sums[core_of]) for core_of in range(2)]
        halves = [
            own.astype(jnp.float32) + swap(other, ("x", 0)).astype(jnp.float32)
            for own, other in zip(own_x, other_x)
        ]
        own_half = jnp.where(core == 0, halves[0], halves[1])
        other_half = jnp.where(core == 0, halves[1], halves[0]).astype(jnp.bfloat16)
        come = swap(other_half, ("core", 0)).astype(jnp.float32)
        weight_share = jnp.concatenate(
            [jnp.where(core == 0, own_half, come), jnp.where(core == 0, come, own_half)], axis=0
        )
    else:
        weight_share = scatter_whole([first_terms[0], *feed_grads])
    d_one = matmul_c(d_qkv, qkv_rows)
    d_norm_one, d_gain_one = norm_back(tokens_in, d_one, gains[0])
    d_tokens = d_resid + d_norm_one
    gain_parts = lax.all_gather(jnp.stack([d_gain_one, d_gain_two], axis=0), ("x", "core", "ctx"))
    gain_grad = jnp.sum(gain_parts, axis=0)
    weight_first, weight_second, weight_new = adam_update(
        weights.astype(jnp.float32), weight_share, first_moment, second_moment, RATE, DECAY, STEP
    )
    gain_first_new, gain_second_new, gain_new = adam_update(
        gains, gain_grad, gain_first, gain_second, GAIN_RATE, 0.0, STEP
    )
    return (
        result.reshape(inputs.shape),
        d_tokens.reshape(inputs.shape),
        weight_share,
        weight_second,
        weight_new,
        gain_grad,
        gain_second_new,
        gain_new,
    )


def solution(mesh):
    fine = Mesh(
        mesh.devices.reshape(mesh.shape["dp"] // 2, 2, mesh.shape["ctx"]), ("x", "core", "ctx")
    )
    rows = P(("x", "core"), "ctx", None)
    stacked = P(("x", "core", "ctx"), None)
    return jax.shard_map(
        shards,
        mesh=fine,
        in_specs=(rows, rows, stacked, P(), stacked, stacked, P(), P()),
        out_specs=(rows, rows, stacked, stacked, stacked, P(), P(), P()),
        check_vma=False,
    )
```

```python
import jax
import jax.numpy as jnp
import numpy as np
from jax import lax
from jax.experimental import pallas as pl
from jax.experimental.pallas import tpu as pltpu
from jax.sharding import Mesh
from jax.sharding import PartitionSpec as P

HEADS = 15
KV = 5
HD = 64
FF = 2560
STEP = 10


SCALE_QK = 0.125
THETA = 10000.0
EPSILON = 1e-05
BETA_ONE = 0.9
BETA_TWO = 0.95
ADAM_EPS = 1e-08
DECAY = 0.1
RATE = 0.02
GAIN_RATE = 0.2
GROUP = HEADS // KV
KEY_TILE = 256
HIDDEN = -1e30
VMEM_BYTES = 48 * 1024 * 1024


def places(row_index, local_rows, ctx_count):
    half_rows = local_rows // 2
    owner_index = row_index // local_rows
    inner_index = row_index % local_rows
    return jnp.where(
        inner_index < half_rows,
        owner_index * half_rows + inner_index,
        (2 * ctx_count - 1 - owner_index) * half_rows + inner_index - half_rows,
    )


def angle_tables(positions_in, sign):
    half_width = HD // 2
    frequency = THETA ** (-jnp.arange(half_width, dtype=jnp.float32) * 2.0 / HD)
    angles = frequency[:, None] * positions_in.astype(jnp.float32)[None, :]
    return jnp.cos(angles), sign * jnp.sin(angles)


def rotate(values, tables):
    cosine, sine_part = tables
    heads = values.reshape(-1, HD, values.shape[-1])
    first_half = heads[:, : HD // 2]
    second_half = heads[:, HD // 2 :]
    return jnp.concatenate(
        [
            first_half * cosine - second_half * sine_part,
            second_half * cosine + first_half * sine_part,
        ],
        axis=1,
    ).reshape(values.shape)


def normalize(values):
    return values * lax.rsqrt(jnp.mean(values * values, axis=-1, keepdims=True) + EPSILON)


def norm_back(values, grad_in, gain_row):
    inv_scale = lax.rsqrt(jnp.mean(values * values, axis=-1, keepdims=True) + EPSILON)
    unit_rows = values * inv_scale
    grad_unit = grad_in * gain_row
    grad_values = inv_scale * (
        grad_unit - unit_rows * jnp.mean(grad_unit * unit_rows, axis=-1, keepdims=True)
    )
    return (grad_values, jnp.sum(grad_in * unit_rows, axis=0))


def matmul_n(left, right):
    return jnp.dot(left, right, preferred_element_type=jnp.float32)


def matmul_t(left, right):
    return lax.dot_general(
        left, right, (((1,), (1,)), ((), ())), preferred_element_type=jnp.float32
    )


def matmul_c(left, right):
    return lax.dot_general(
        left, right, (((0,), (0,)), ((), ())), preferred_element_type=jnp.float32
    )


def bit_groups():
    x_bits = lax.axis_size("x").bit_length() - 1
    ctx_bits = lax.axis_size("ctx").bit_length() - 1
    low_ctx = ctx_bits // 2
    along_x = [("x", bit) for bit in range(x_bits)]
    along_y = [("ctx", bit) for bit in range(low_ctx)]
    along_z = [("ctx", bit) for bit in range(low_ctx, ctx_bits)]
    return along_x, along_y, along_z


def swap_by(values, axis, offset):
    size = lax.axis_size(axis)
    return lax.ppermute(values, axis, [(i, i ^ offset) for i in range(size)])


def swap(values, where):
    return swap_by(values, where[0], 1 << where[1])


def add_low(left, right):
    return (left.astype(jnp.float32) + right.astype(jnp.float32)).astype(jnp.bfloat16)


def rel_offsets(order):
    strides = {"x": 2 * lax.axis_size("ctx"), "ctx": 1}
    offsets = np.zeros((1,), np.int64)
    for axis, bit in order:
        offsets = np.concatenate([offsets, offsets ^ (strides[axis] << bit)])
    return offsets


def lookup(slot, offsets):
    total = jnp.int32(0)
    for bit in range(len(offsets).bit_length() - 1):
        total = total + ((slot >> bit) & 1) * int(offsets[1 << bit])
    return total


def find(offset, offsets):
    total = jnp.int32(0)
    for bit in range(len(offsets).bit_length() - 1):
        place = int(offsets[1 << bit]).bit_length() - 1
        total = total + (((offset >> place) & 1) << bit)
    return total


def collect(values, order):
    kept, arrived = values, None
    for where in order:
        half = kept.shape[0] // 2
        if arrived is None:
            away, kept_next = kept[half:], kept[:half]
        else:
            away = add_low(kept[half:], arrived[half:])
            kept_next = add_low(kept[:half], arrived[:half])
        arrived = swap(away, where)
        kept = kept_next
    return kept[0].astype(jnp.float32) + arrived[0].astype(jnp.float32)


def scatter_whole(terms):
    ctx_count = lax.axis_size("ctx")
    count = 2 * lax.axis_size("x") * ctx_count
    along_x, along_y, along_z = bit_groups()
    core = ("core", 0)
    me = device_index().reshape(1)
    blocks, rows, width = terms[0].shape
    first = -(-rows // 48) * 16
    groups = [(0, first), (first, 2 * first), (2 * first, rows)]
    orders = [
        along_x + along_y + along_z,
        along_y + along_z + along_x,
        along_z + along_x + along_y,
    ]
    tables = [rel_offsets(list(reversed(order))) for order in orders]

    def target(step, me_ref, flip):
        return lookup(step, tables[0]) ^ me_ref[0] ^ flip

    def sources(flip):
        def chosen(member):
            def index(step, me_ref):
                spot = target(step, me_ref, flip)
                return (jnp.where(spot // blocks == member, spot % blocks, 0), 0, 0)

            return pl.BlockSpec((1, rows, width), index)

        return [chosen(member) for member in range(len(terms))]

    def pick_body(me_ref, *refs):
        held = target(pl.program_id(0), me_ref, ctx_count) // blocks
        for member in range(len(terms)):

            @pl.when(held == member)
            def _(member=member):
                refs[-1][...] = refs[member][...]

    away = pl.pallas_call(
        pick_body,
        grid_spec=pltpu.PrefetchScalarGridSpec(
            num_scalar_prefetch=1,
            grid=(count // 2,),
            in_specs=sources(ctx_count),
            out_specs=pl.BlockSpec((1, rows, width), lambda step, me_ref: (step, 0, 0)),
        ),
        out_shape=jax.ShapeDtypeStruct((count // 2, rows, width), jnp.bfloat16),
        compiler_params=pltpu.CompilerParams(vmem_limit_bytes=VMEM_BYTES),
    )(me, *terms)
    arrived = swap(away, core)

    def merge_body(me_ref, *refs):
        held = target(pl.program_id(0), me_ref, 0) // blocks
        for member in range(len(terms)):

            @pl.when(held == member)
            def _(member=member):
                for (low, high), out in zip(groups, refs[-3:]):
                    out[0] = add_low(refs[member][0, low:high], refs[-4][0, low:high])

    parts = pl.pallas_call(
        merge_body,
        grid_spec=pltpu.PrefetchScalarGridSpec(
            num_scalar_prefetch=1,
            grid=(count // 2,),
            in_specs=sources(0)
            + [pl.BlockSpec((1, rows, width), lambda step, me_ref: (step, 0, 0))],
            out_specs=[
                pl.BlockSpec(
                    (1, high - low, width),
                    lambda step, me_ref, table=table: (
                        find(lookup(step, tables[0]), table),
                        0,
                        0,
                    ),
                )
                for (low, high), table in zip(groups, tables)
            ],
        ),
        out_shape=[
            jax.ShapeDtypeStruct((count // 2, high - low, width), jnp.bfloat16)
            for low, high in groups
        ],
        compiler_params=pltpu.CompilerParams(vmem_limit_bytes=VMEM_BYTES),
    )(me, *terms, arrived)
    return jnp.concatenate([collect(part, order) for part, order in zip(parts, orders)], axis=0)


def device_index():
    return (
        (lax.axis_index("x") * 2 + lax.axis_index("core")) * lax.axis_size("ctx")
        + lax.axis_index("ctx")
    ).astype(jnp.int32)


def splits_rows(rows):
    return lax.axis_size("x") == 2 and rows % 32 == 0


def spread(values, order):
    values = values[None]
    for where in order:
        values = double(values, where)
    return values


def double(values, where):
    return jnp.concatenate([values, swap(values, where)], axis=0)


def ctx_orders():
    along_x, along_y, along_z = bit_groups()
    return [along_y + along_z, along_z + along_y]


def row_cuts(rows):
    first = -(-rows // 32) * 16
    return [(0, first), (first, rows)]


def step_ctx(held, come, left, where):
    dim = 1 + left.index(where[1])
    rest = [bit for bit in left if bit != where[1]]
    pick = lambda values, side: lax.index_in_dim(values, side, dim, False)
    sent = add_low(pick(held, 1), pick(come, 1))
    return add_low(pick(held, 0), pick(come, 0)), sent, rest


def reduce_start(keep, away):
    arrived = swap(away, ("core", 0))
    states = []
    for (low, high), order in zip(row_cuts(keep.shape[2]), ctx_orders()):
        shape = (keep.shape[0],) + (2,) * len(order) + (high - low, keep.shape[3])
        held = keep[:, :, low:high].reshape(shape)
        come = arrived[:, :, low:high].reshape(shape)
        left = list(reversed(range(len(order))))
        states.append(step_ctx(held, come, left, order[0]))
    return states


def ride_parts(ride):
    rounded = lax.reduce_precision(ride, 8, 7)
    return rounded, lax.reduce_precision(ride - rounded, 8, 7)


def with_ride(sent, parts):
    extra = jnp.concatenate([*parts, jnp.zeros((12, parts[0].shape[1]), jnp.float32)])
    return jnp.concatenate([sent.reshape(-1, sent.shape[-1]), extra.astype(jnp.bfloat16)], axis=0)


def swap_with(sent, ride, where):
    parts = ride_parts(ride)
    come, other = off_ride(swap(with_ride(sent, parts), where), sent.shape)
    return come, (parts[0] + parts[1]) + other


def off_ride(come, shape):
    parts = come[-16:].astype(jnp.float32)
    return come[:-16].reshape(shape), parts[0:2] + parts[2:4]


def reduce_finish(states, ride=None):
    sums = []
    for member, ((held, sent, left), order) in enumerate(zip(states, ctx_orders())):
        for position, where in enumerate(order):
            if ride is not None and member == 0:
                come, ride = swap_with(sent, ride, where)
            else:
                come = swap(sent, where)
            if position + 1 < len(order):
                held, sent, left = step_ctx(held, come, left, order[position + 1])
        sums.append(add_low(held, come))
    return jnp.concatenate(sums, axis=1), ride


def gather_halves(weights):
    rows = weights.shape[0]
    x_index, core = lax.axis_index("x"), lax.axis_index("core")
    half = rows // 2
    far = swap(weights, ("x", 0))
    low = jnp.where(x_index == 0, weights, far)
    high = jnp.where(x_index == 0, far, weights)
    both = jnp.stack([low, high])
    keep = jnp.where(core == 0, both[:, :half], both[:, half:])
    come = swap(jnp.where(core == 0, both[:, half:], both[:, :half]), ("core", 0))
    first = jnp.where(core == 0, keep, come)
    second = jnp.where(core == 0, come, keep)
    return first[0], jnp.stack([second[0], first[1], second[1]])


def place_rows(own, far):
    tables = [rel_offsets(list(reversed(order))) for order in ctx_orders()]
    slots, width = own[0].shape[0], own[0].shape[2]
    lengths = [part.shape[1] for part in own]
    half = sum(lengths)

    def body(me_ref, *refs):
        out_ref = refs[-1]
        for core in range(2):

            @pl.when(me_ref[0] == core)
            def _(core=core):
                for source, base in ((0, core * half), (2, (1 - core) * half)):
                    out_ref[0, base : base + lengths[0]] = refs[source][0]
                    out_ref[0, base + lengths[0] : base + half] = refs[source + 1][0]

    specs = [
        pl.BlockSpec(
            (1, length, width),
            lambda step, me_ref, table=table: (find(step ^ me_ref[1], table), 0, 0),
        )
        for length, table in zip(lengths, tables)
    ]
    me = jnp.stack([lax.axis_index("core"), lax.axis_index("ctx")]).astype(jnp.int32)
    return pl.pallas_call(
        body,
        grid_spec=pltpu.PrefetchScalarGridSpec(
            num_scalar_prefetch=1,
            grid=(slots,),
            in_specs=specs * 2,
            out_specs=pl.BlockSpec((1, 2 * half, width), lambda step, me_ref: (step, 0, 0)),
        ),
        out_shape=jax.ShapeDtypeStruct((slots, 2 * half, width), own[0].dtype),
        cost_estimate=pl.CostEstimate(
            flops=0, bytes_accessed=8 * slots * half * width, transcendentals=0
        ),
        compiler_params=pltpu.CompilerParams(vmem_limit_bytes=VMEM_BYTES),
    )(me, *own, *far).reshape(slots * 2 * half, width)


def turned(values):
    return jnp.transpose(values)


def load_packed(ref, aligned):
    if not aligned:
        return ref[0, 0]
    half = ref.shape[1] // 2
    return jnp.concatenate(
        [
            ref[head * HD : (head + 1) * HD, side * half : (side + 1) * half]
            for side in range(2)
            for head in range(GROUP)
        ],
        axis=1,
    )


def store_packed(ref, values, aligned):
    if not aligned:
        ref[0, 0] = values
        return
    half = ref.shape[1] // 2
    for side in range(2):
        for head in range(GROUP):
            start = (side * GROUP + head) * half
            ref[head * HD : (head + 1) * HD, side * half : (side + 1) * half] = values[
                :, start : start + half
            ]


def load_tile(refs, side, tile):
    length = refs[0].shape[1] // 2
    if length >= KEY_TILE:
        start = side * length + tile * KEY_TILE
        return refs[0][:, start : start + KEY_TILE]
    many = KEY_TILE // length
    return jnp.concatenate(
        [
            ref[:, side * length : (side + 1) * length]
            for ref in refs[tile * many : (tile + 1) * many]
        ],
        axis=1,
    )


def attend_body(count, aligned, queries_ref, key_pos_ref, query_pos_ref, *refs):
    key_refs, value_refs = refs[:count], refs[count : 2 * count]
    out_ref, total_ref, work = refs[2 * count :]
    queries = load_packed(queries_ref, aligned)
    low_cols = queries.shape[1] // 2
    queries_high = queries[:, low_cols:]
    tiles = key_pos_ref.shape[1] // KEY_TILE
    largest = jnp.full((1, queries.shape[1]), HIDDEN, jnp.float32)
    largest_high = jnp.full((1, low_cols), HIDDEN, jnp.float32)
    for side in range(2):
        for tile in range(tiles):
            keys = turned(load_tile(key_refs, side, tile))
            row = (side * tiles + tile) * KEY_TILE
            key_places = key_pos_ref[side, tile * KEY_TILE : (tile + 1) * KEY_TILE]
            if side == 0:
                scores = matmul_n(keys, queries)
                scores = jnp.where(key_places <= query_pos_ref[...], scores, HIDDEN)
                work[row : row + KEY_TILE] = scores
                largest = jnp.maximum(largest, jnp.max(scores, axis=0, keepdims=True))
            else:
                scores = matmul_n(keys, queries_high)
                scores = jnp.where(key_places <= query_pos_ref[:, low_cols:], scores, HIDDEN)
                work[row : row + KEY_TILE, low_cols:] = scores
                largest_high = jnp.maximum(largest_high, jnp.max(scores, axis=0, keepdims=True))
    high_max = jnp.maximum(largest[:, low_cols:], largest_high)
    largest = jnp.concatenate([largest[:, :low_cols], high_max], axis=1)
    total = jnp.zeros_like(largest)
    mixed = jnp.zeros((HD, queries.shape[1]), jnp.float32)
    total_high = jnp.zeros_like(largest_high)
    mixed_high = jnp.zeros((HD, low_cols), jnp.float32)
    for side in range(2):
        for tile in range(tiles):
            values = load_tile(value_refs, side, tile)
            row = (side * tiles + tile) * KEY_TILE
            if side == 0:
                expos = jnp.exp(work[row : row + KEY_TILE] - largest)
                total = total + jnp.sum(expos, axis=0, keepdims=True)
                mixed = mixed + matmul_n(values, expos.astype(jnp.bfloat16))
            else:
                expos = jnp.exp(work[row : row + KEY_TILE, low_cols:] - high_max)
                total_high = total_high + jnp.sum(expos, axis=0, keepdims=True)
                mixed_high = mixed_high + matmul_n(values, expos.astype(jnp.bfloat16))
    total = jnp.concatenate([total[:, :low_cols], total[:, low_cols:] + total_high], axis=1)
    mixed = jnp.concatenate([mixed[:, :low_cols], mixed[:, low_cols:] + mixed_high], axis=1)
    store_packed(out_ref, (mixed / total).astype(jnp.bfloat16), aligned)
    total_ref[0, 0] = largest + jnp.log(total)


def attend_back_body(
    count, aligned, queries_ref, key_pos_ref, query_pos_ref, *refs
):
    key_refs, value_refs = refs[:count], refs[count : 2 * count]
    out_ref, total_ref, d_out_ref, cosine_ref, sine_ref = refs[2 * count : 2 * count + 5]
    d_queries_ref, pair_refs = refs[2 * count + 5], refs[2 * count + 6 :]
    all_queries, all_d_out = load_packed(queries_ref, aligned), load_packed(d_out_ref, aligned)
    low_cols = all_queries.shape[1] // 2
    tiles = key_pos_ref.shape[1] // KEY_TILE
    delta = jnp.sum(
        all_d_out.astype(jnp.float32) * load_packed(out_ref, aligned).astype(jnp.float32),
        axis=0,
        keepdims=True,
    )
    totals = total_ref[0, 0]
    parts = []
    for side in range(2):
        if side == 0:
            queries, d_out = all_queries, all_d_out
            query_places, log_total, row_delta = query_pos_ref[...], totals, delta
        else:
            queries, d_out = all_queries[:, low_cols:], all_d_out[:, low_cols:]
            query_places = query_pos_ref[:, low_cols:]
            log_total, row_delta = totals[:, low_cols:], delta[:, low_cols:]
        part = jnp.zeros((HD, queries.shape[1]), jnp.float32)
        for tile in range(tiles):
            keys_flat = load_tile(key_refs, side, tile)
            scores = matmul_n(turned(keys_flat), queries)
            seen = key_pos_ref[side, tile * KEY_TILE : (tile + 1) * KEY_TILE] <= query_places
            probs = jnp.where(seen, jnp.exp(scores - log_total), 0.0)
            d_probs = matmul_n(turned(load_tile(value_refs, side, tile)), d_out)
            d_scores = (probs * (d_probs - row_delta)).astype(jnp.bfloat16)
            part = part + matmul_n(keys_flat, d_scores)
            d_key = matmul_t(d_scores, queries).astype(jnp.bfloat16)
            d_value = matmul_t(probs.astype(jnp.bfloat16), d_out).astype(jnp.bfloat16)
            if aligned:
                length = key_refs[0].shape[1] // 2
                near = pair_refs[0].shape[0]
                for piece in range(KEY_TILE // length):
                    slot = tile * (KEY_TILE // length) + piece
                    ref = pair_refs[slot // near]
                    rows = slice(piece * length, (piece + 1) * length)
                    ref[slot % near, 0, side, :, :HD] = d_key[rows]
                    ref[slot % near, 0, side, :, HD:] = d_value[rows]
            else:
                rows = slice(tile * KEY_TILE, (tile + 1) * KEY_TILE)
                pair_refs[0][side, 0, rows, :HD] = d_key
                pair_refs[0][side, 0, rows, HD:] = d_value
        parts.append(part)
    d_queries = jnp.concatenate(
        [parts[0][:, :low_cols], parts[0][:, low_cols:] + parts[1]], axis=1
    )
    cosine, sine_part = cosine_ref[...], sine_ref[...]
    first_half, second_half = d_queries[: HD // 2], d_queries[HD // 2 :]
    turned_back = jnp.concatenate(
        [
            first_half * cosine + second_half * sine_part,
            second_half * cosine - first_half * sine_part,
        ],
        axis=0,
    )
    store_packed(d_queries_ref, (turned_back * SCALE_QK).astype(jnp.bfloat16), aligned)


def head_specs(count, aligned, cols, keys, local_rows, seq):
    if aligned:
        packed = pl.BlockSpec((GROUP * HD, local_rows), lambda head: (head, seq))
    else:
        packed = pl.BlockSpec((1, 1, HD, cols), lambda head: (seq, head, 0, 0))
    specs = [
        packed,
        pl.BlockSpec((2, keys, 1), lambda head: (0, 0, 0)),
        pl.BlockSpec((1, cols), lambda head: (0, 0)),
    ]
    specs += [pl.BlockSpec((HD, 2 * keys // count), lambda head: (head, seq))] * count
    specs += [pl.BlockSpec((HD, 2 * keys // count), lambda head: (KV + head, seq))] * count
    return packed, specs


def attend(queries, pairs, key_pos, query_pos, local_rows, seq):
    aligned = queries.ndim == 2
    cols, keys, count = query_pos.shape[1], key_pos.shape[1], len(pairs)
    _, specs = head_specs(count, aligned, cols, keys, local_rows, seq)
    work = HEADS * keys * cols // GROUP * 3 // 2
    if aligned:
        out_spec = pl.BlockSpec((GROUP * HD, local_rows), lambda head: (head, 0))
        out_shape = jax.ShapeDtypeStruct((HEADS * HD, local_rows), jnp.bfloat16)
    else:
        out_spec = pl.BlockSpec((1, 1, HD, cols), lambda head: (0, head, 0, 0))
        out_shape = jax.ShapeDtypeStruct((1, KV, HD, cols), jnp.bfloat16)
    return pl.pallas_call(
        lambda *refs: attend_body(count, aligned, *refs),
        grid=(KV,),
        in_specs=specs,
        out_specs=[out_spec, pl.BlockSpec((1, 1, 1, cols), lambda head: (0, head, 0, 0))],
        out_shape=[out_shape, jax.ShapeDtypeStruct((1, KV, 1, cols), jnp.float32)],
        scratch_shapes=[pltpu.VMEM((2 * keys, cols), jnp.float32)],
        cost_estimate=pl.CostEstimate(
            flops=work * HD, bytes_accessed=1024 * 1024, transcendentals=0
        ),
        compiler_params=pltpu.CompilerParams(vmem_limit_bytes=VMEM_BYTES),
    )(queries, key_pos, query_pos, *pairs, *pairs)


def attend_back(
    queries, pairs, key_pos, query_pos, mixed, log_total, d_mixed, tables, local_rows, seq, near
):
    aligned = queries.ndim == 2
    cols, keys, count = query_pos.shape[1], key_pos.shape[1], len(pairs)
    packed, specs = head_specs(count, aligned, cols, keys, local_rows, seq)
    work = HEADS * keys * cols // GROUP * 3 // 2
    if aligned:
        own = pl.BlockSpec((GROUP * HD, local_rows), lambda head: (head, 0))
        own_shape = jax.ShapeDtypeStruct((HEADS * HD, local_rows), jnp.bfloat16)
        length = keys // count
        pair_specs = [
            pl.BlockSpec((near, 1, 2, length, 2 * HD), lambda head: (0, head, 0, 0, 0))
        ] * (count // near)
        pair_shapes = [jax.ShapeDtypeStruct((near, KV, 2, length, 2 * HD), jnp.bfloat16)] * (
            count // near
        )
    else:
        own = pl.BlockSpec((1, 1, HD, cols), lambda head: (0, head, 0, 0))
        own_shape = jax.ShapeDtypeStruct((1, KV, HD, cols), jnp.bfloat16)
        pair_specs = [pl.BlockSpec((2, 1, keys, 2 * HD), lambda head: (0, head, 0, 0))]
        pair_shapes = [jax.ShapeDtypeStruct((2, KV, keys, 2 * HD), jnp.bfloat16)]
    table_spec = pl.BlockSpec((HD // 2, cols), lambda head: (0, 0))
    return pl.pallas_call(
        lambda *refs: attend_back_body(count, aligned, *refs),
        grid=(KV,),
        in_specs=specs
        + [
            own,
            pl.BlockSpec((1, 1, 1, cols), lambda head: (0, head, 0, 0)),
            packed,
            table_spec,
            table_spec,
        ],
        out_specs=[own] + pair_specs,
        out_shape=[own_shape] + pair_shapes,
        cost_estimate=pl.CostEstimate(
            flops=work * HD, bytes_accessed=1024 * 1024, transcendentals=0
        ),
        compiler_params=pltpu.CompilerParams(vmem_limit_bytes=VMEM_BYTES),
    )(queries, key_pos, query_pos, *pairs, *pairs, mixed, log_total, d_mixed, *tables)


def put_rows(values, keep_ref, away_ref, member, core):
    half = values.shape[0] // 2
    for mine, low, far in ((0, 0, half), (1, half, 0)):

        @pl.when(core == mine)
        def _(low=low, far=far):
            keep_ref[member, 0] = values[low : low + half]
            away_ref[member, 0] = values[far : far + half]


def feed_body(
    parts, split, me_ref, a_two_ref, dy_ref, *refs
):
    count = 4 if split else 6
    weight_refs, (out_ref, d_two_ref), grad_refs = (
        refs[:count],
        refs[count : count + 2],
        refs[count + 2 :],
    )
    core = me_ref[0]
    step = pl.program_id(0)

    @pl.when(step == 0)
    def _():
        out_ref[...] = jnp.zeros_like(out_ref)
        d_two_ref[...] = jnp.zeros_like(d_two_ref)

    def rows_of(member):
        if split:
            own = jnp.concatenate([weight_refs[0][0, member], weight_refs[1][0, member]], axis=0)
            far = jnp.concatenate([weight_refs[2][0, member], weight_refs[3][0, member]], axis=0)
            return jnp.concatenate(
                [jnp.where(core == 0, own, far), jnp.where(core == 0, far, own)], axis=0
            )
        wanted = feed_core(member, step, parts)
        return jnp.where(wanted == core, weight_refs[2 * member][0], weight_refs[2 * member + 1][0])

    a_two, dy_low = a_two_ref[...], dy_ref[...]
    gate_rows, up_rows, down_rows = rows_of(0), rows_of(1), rows_of(2)
    gate_pre = matmul_t(gate_rows, a_two)
    up_pre = matmul_t(up_rows, a_two)
    d_hidden = matmul_t(down_rows, dy_low)
    sigma = jax.nn.sigmoid(gate_pre)
    gate_act = gate_pre * sigma
    hidden = (gate_act * up_pre).astype(jnp.bfloat16)
    d_gate = (d_hidden * up_pre * sigma * (1.0 + gate_pre * (1.0 - sigma))).astype(jnp.bfloat16)
    d_up = (d_hidden * gate_act).astype(jnp.bfloat16)
    out_ref[...] += matmul_c(hidden, down_rows)
    d_two_ref[...] += matmul_c(d_gate, gate_rows) + matmul_c(d_up, up_rows)
    for member, (left, right) in enumerate(((d_gate, a_two), (d_up, a_two), (hidden, dy_low))):
        grad = matmul_n(left, right).astype(jnp.bfloat16)
        if split:
            put_rows(grad, grad_refs[0], grad_refs[1], member, core)
        else:
            grad_refs[member][0] = grad


def feed_core(member, step, parts):
    ctx_count, single = parts
    return (member + 1) % 2 if single else step // ctx_count


def feed_forward(a_two, dy_low, mine, far, rows):
    tokens, width = a_two.shape
    ctx_count = lax.axis_size("ctx")
    blocks = FF // rows
    single = blocks == ctx_count
    split = splits_rows(rows)
    parts = (ctx_count, single)
    whole = pl.BlockSpec((tokens, width), lambda step, me_ref: (0, 0))

    def weight_spec(member, own):
        first = (member + 1) * blocks // ctx_count // 2 * ctx_count

        def index(step, me_ref):
            matches = (feed_core(member, step, parts) == me_ref[0]) == own
            return (first + jnp.where(matches, step % ctx_count, 0), 0, 0)

        return pl.BlockSpec((1, rows, width), index)

    if split:
        tables = [rel_offsets(list(reversed(order))) for order in ctx_orders()]
        weight_specs = [
            pl.BlockSpec(
                (1, 3, part.shape[2], width),
                lambda step, me_ref, table=table: (find(step, table), 0, 0, 0),
            )
            for part, table in zip(mine, tables)
        ] * 2
        weight_args = [*mine, *far]
        half = pl.BlockSpec((3, 1, rows // 2, width), lambda step, me_ref: (0, step, 0, 0))
        grad_specs = [half, half]
        grad_shapes = [jax.ShapeDtypeStruct((3, blocks, rows // 2, width), jnp.bfloat16)] * 2
    else:
        weight_specs = [weight_spec(member, own) for member in range(3) for own in (True, False)]
        weight_args = [mine, far] * 3
        grad_specs = [pl.BlockSpec((1, rows, width), lambda step, me_ref: (step, 0, 0))] * 3
        grad_shapes = [jax.ShapeDtypeStruct((blocks, rows, width), jnp.bfloat16)] * 3
    me = jnp.stack([lax.axis_index("core"), lax.axis_index("ctx")]).astype(jnp.int32)
    return pl.pallas_call(
        lambda *refs: feed_body(parts, split, *refs),
        grid_spec=pltpu.PrefetchScalarGridSpec(
            num_scalar_prefetch=1,
            grid=(blocks,),
            in_specs=[whole, whole] + weight_specs,
            out_specs=[whole, whole] + grad_specs,
        ),
        out_shape=[jax.ShapeDtypeStruct((tokens, width), jnp.float32)] * 2 + grad_shapes,
        cost_estimate=pl.CostEstimate(
            flops=18 * tokens * width * FF, bytes_accessed=12 * FF * width, transcendentals=FF * tokens
        ),
        compiler_params=pltpu.CompilerParams(vmem_limit_bytes=VMEM_BYTES),
    )(me, a_two, dy_low, *weight_args)


def first_grads(d_qkv, attn_low, a_one, d_resid_low, rows):
    tokens, width = a_one.shape
    split = splits_rows(rows)
    early = d_qkv.shape[0] // rows
    blocks = early + attn_low.shape[0] // rows

    def body(me_ref, qkv_ref, attn_ref, one_ref, resid_ref, *grad_refs):
        first = pl.program_id(0) < early
        left = jnp.where(first, qkv_ref[...], attn_ref[...])
        right = jnp.where(first, one_ref[...], resid_ref[...])
        grad = matmul_n(left, right).astype(jnp.bfloat16)
        if split:
            put_rows(grad, grad_refs[0], grad_refs[1], 0, me_ref[0])
        else:
            grad_refs[0][0] = grad

    whole = pl.BlockSpec((tokens, width), lambda step, me_ref: (0, 0))
    if split:
        half = pl.BlockSpec(
            (1, 1, rows // 2, width), lambda step, me_ref: (0, step ^ me_ref[1], 0, 0)
        )
        grad_specs = [half, half]
        grad_shapes = [jax.ShapeDtypeStruct((1, blocks, rows // 2, width), jnp.bfloat16)] * 2
    else:
        grad_specs = [pl.BlockSpec((1, rows, width), lambda step, me_ref: (step, 0, 0))]
        grad_shapes = [jax.ShapeDtypeStruct((blocks, rows, width), jnp.bfloat16)]
    me = jnp.stack([lax.axis_index("core"), lax.axis_index("ctx")]).astype(jnp.int32)
    return pl.pallas_call(
        body,
        grid_spec=pltpu.PrefetchScalarGridSpec(
            num_scalar_prefetch=1,
            grid=(blocks,),
            in_specs=[
                pl.BlockSpec((rows, tokens), lambda step, me_ref: (jnp.minimum(step, early - 1), 0)),
                pl.BlockSpec((rows, tokens), lambda step, me_ref: (jnp.maximum(step - early, 0), 0)),
                whole,
                whole,
            ],
            out_specs=grad_specs,
        ),
        out_shape=grad_shapes,
        cost_estimate=pl.CostEstimate(
            flops=2 * tokens * width * blocks * rows, bytes_accessed=2 * blocks * rows * width, transcendentals=0
        ),
        compiler_params=pltpu.CompilerParams(vmem_limit_bytes=VMEM_BYTES),
    )(me, d_qkv, attn_low, a_one, d_resid_low)


def adam_update(param, grad, first, second, rate, decay, step_number):
    first_new = BETA_ONE * first + (1.0 - BETA_ONE) * grad
    second_new = BETA_TWO * second + (1.0 - BETA_TWO) * grad * grad
    fix_one = 1.0 - BETA_ONE**step_number
    fix_two = 1.0 - BETA_TWO**step_number
    update = first_new / fix_one / (jnp.sqrt(second_new / fix_two) + ADAM_EPS)
    return (first_new, second_new, param - rate * (update + decay * param))


def shards(inputs, cotangent, weights, gains, first_moment, second_moment, gain_first, gain_second):
    ctx_count = lax.axis_size("ctx")
    x_count = lax.axis_size("x")
    ctx_index, core, x_index = lax.axis_index("ctx"), lax.axis_index("core"), lax.axis_index("x")
    seqs, local_rows, model_width = inputs.shape
    half_rows = local_rows // 2
    tokens = seqs * local_rows
    weight_rows = weights.shape[0]
    q_cols = HEADS * HD
    kv_cols = KV * HD
    cut_o = q_cols + 2 * kv_cols
    along_y, along_z = bit_groups()[1:]
    y_count, z_count = 1 << len(along_y), 1 << len(along_z)
    slot_offsets = [z * y_count + y for y in range(y_count) for z in range(z_count)]
    aligned = half_rows % 128 == 0
    local_index = jnp.arange(local_rows, dtype=jnp.int32)
    pos_here = places(ctx_index * local_rows + local_index, local_rows, ctx_count)
    cosine, sine_part = angle_tables(pos_here, 1.0)
    turn = (jnp.tile(cosine, (1, seqs)), jnp.tile(sine_part, (1, seqs)))
    turn_back = (turn[0], -turn[1])

    def pack(flat):
        if aligned:
            return flat
        return (
            flat.reshape(KV, GROUP, HD, -1, 2, half_rows)
            .transpose(3, 0, 2, 4, 1, 5)
            .reshape(-1, KV, HD, 2 * GROUP * half_rows)
        )

    def unpack(packed):
        if aligned:
            return packed
        return (
            packed.reshape(KV, HD, 2, GROUP, half_rows)
            .transpose(0, 3, 1, 2, 4)
            .reshape(q_cols, local_rows)
        )

    def by_columns(row):
        rows = row.shape[0]
        return jnp.broadcast_to(
            row.reshape(rows, 2, 1, half_rows), (rows, 2, GROUP, half_rows)
        ).reshape(rows, 2 * GROUP * half_rows)

    owners = ctx_index ^ jnp.asarray(slot_offsets, jnp.int32)
    inner = jnp.arange(half_rows, dtype=jnp.int32)
    key_pos = jnp.stack(
        [
            (owners[:, None] * half_rows + inner[None, :]).reshape(-1, 1),
            ((2 * ctx_count - 1 - owners[:, None]) * half_rows + inner[None, :]).reshape(-1, 1),
        ]
    )
    query_pos = by_columns(pos_here[None, :])
    packed_tables = (by_columns(cosine), by_columns(sine_part))

    split = splits_rows(weight_rows)
    if split:
        first_half, feed_half = gather_halves(weights)
        cuts = row_cuts(weight_rows // 2)
        backward = [list(reversed(order)) for order in ctx_orders()]
        first_own = [spread(first_half[low:high], order) for (low, high), order in zip(cuts, backward)]
        first_far = [swap(part, ("core", 0)) for part in first_own]
        feed_half, first_own = lax.optimization_barrier((feed_half, first_own))
        mine = [feed_half[None, :, low:high] for low, high in cuts]
        mine = [double(part, order[0]) for part, order in zip(mine, backward)]
        first_rows = place_rows(first_own, first_far)
    else:
        mine = lax.all_gather(weights, ("x", "ctx"), axis=0, tiled=True)
        mine = mine.reshape(x_count * ctx_count, weight_rows, model_width)
        far = swap(mine, ("core", 0))
        sides = [
            jnp.where(core == 0, mine[:ctx_count], far[:ctx_count]),
            jnp.where(core == 0, far[:ctx_count], mine[:ctx_count]),
        ]
        first_rows = jnp.concatenate(sides).reshape(-1, model_width)
    qkv_rows, o_rows = first_rows[:cut_o], first_rows[cut_o : cut_o + q_cols]

    tokens_in, cot_in = lax.optimization_barrier(
        (inputs.reshape(tokens, model_width), cotangent.reshape(tokens, model_width))
    )
    dy_low = cot_in.astype(jnp.bfloat16)
    a_one = (normalize(tokens_in) * gains[0]).astype(jnp.bfloat16)
    pair_rows = matmul_t(qkv_rows[q_cols:], a_one)
    joined = jnp.concatenate(
        [rotate(pair_rows[:kv_cols], turn).astype(jnp.bfloat16), pair_rows[kv_cols:].astype(jnp.bfloat16)],
        axis=0,
    )
    if split:
        joined, mine = lax.optimization_barrier((joined, mine))
        for position in range(1, len(backward[0])):
            mine = [double(part, order[position]) for part, order in zip(mine, backward)]
    near = [joined] + [swap_by(joined, "ctx", z * y_count) for z in range(1, z_count)]
    pairs = list(near)
    for y in range(1, y_count):
        pairs += [swap_by(part, "ctx", y) for part in near]
    if not aligned:
        pairs = [
            jnp.stack(pairs)
            .reshape(ctx_count, 2 * kv_cols, seqs, 2, half_rows)
            .transpose(1, 2, 3, 0, 4)
            .reshape(2 * kv_cols, seqs * 2 * ctx_count * half_rows)
        ]
    q_rot = rotate(matmul_t(qkv_rows[:q_cols], a_one), turn).astype(jnp.bfloat16)
    queries = pack((q_rot * SCALE_QK).astype(jnp.bfloat16))
    attended = []
    for seq in range(seqs):
        attended.append(attend(queries, pairs, key_pos, query_pos, local_rows, seq))
        if split and seq == 0:
            attended, mine = lax.optimization_barrier((attended, mine))
            far = [swap(part, ("core", 0)) for part in mine]
    attn_low = jnp.concatenate([unpack(mixed) for mixed, _ in attended], axis=1)
    resid = tokens_in + matmul_c(attn_low, o_rows)
    a_two = (normalize(resid) * gains[1]).astype(jnp.bfloat16)
    fed, d_two, *feed_grads = feed_forward(a_two, dy_low, mine, far, weight_rows)
    result = resid + fed
    d_norm_two, d_gain_two = norm_back(resid, d_two, gains[1])
    d_resid = cot_in + d_norm_two
    d_resid_low = d_resid.astype(jnp.bfloat16)
    d_attn = pack(matmul_t(o_rows, d_resid_low).astype(jnp.bfloat16))
    if split:
        feed_states = reduce_start(*feed_grads)
        feed_states = [list(state) for state in feed_states]
        d_attn, sends = lax.optimization_barrier((d_attn, [state[1] for state in feed_states]))
        for state, sent in zip(feed_states, sends):
            state[1] = sent
        feed_sums, _ = reduce_finish(feed_states)
    d_q, d_pair = [], []
    for seq in range(seqs):
        mixed, log_total = attended[seq]
        d_queries, *d_slots = attend_back(
            queries, pairs, key_pos, query_pos, mixed, log_total, d_attn, packed_tables,
            local_rows, seq, z_count,
        )
        d_q.append(unpack(d_queries))
        if not aligned:
            d_slots = (
                d_slots[0]
                .reshape(2, KV, ctx_count, half_rows, 2 * HD)
                .transpose(2, 1, 0, 3, 4)
                .reshape(y_count, z_count, KV, 2, half_rows, 2 * HD)
            )
            d_slots = [d_slots[y] for y in range(y_count)]
        line = d_slots[0].astype(jnp.float32)
        for y in range(1, y_count):
            line = line + swap_by(d_slots[y], "ctx", y).astype(jnp.float32)
        total = line[0]
        for z in range(1, z_count):
            total = total + swap_by(line[z].astype(jnp.bfloat16), "ctx", z * y_count).astype(jnp.float32)
        d_pair.append(total)
    if split:
        d_pair, feed_sums = lax.optimization_barrier((d_pair, feed_sums))
    d_own = jnp.stack(d_pair).transpose(1, 4, 0, 2, 3).reshape(KV, 2 * HD, tokens)
    d_qkv = jnp.concatenate(
        [
            jnp.concatenate(d_q, axis=1),
            rotate(d_own[:, :HD].reshape(kv_cols, tokens), turn_back).astype(jnp.bfloat16),
            d_own[:, HD:].reshape(kv_cols, tokens).astype(jnp.bfloat16),
        ],
        axis=0,
    )
    first_terms = first_grads(d_qkv, attn_low, a_one, d_resid_low, weight_rows)
    d_one = matmul_c(d_qkv, qkv_rows)
    d_norm_one, d_gain_one = norm_back(tokens_in, d_one, gains[0])
    d_tokens = d_resid + d_norm_one
    gain_grad = jnp.stack([d_gain_one, d_gain_two], axis=0)
    if split:
        first_sums, gain_grad = reduce_finish(reduce_start(*first_terms), gain_grad)
        sums = [first_sums[0], feed_sums[0], feed_sums[1], feed_sums[2]]
        own_x = jnp.stack([jnp.where(x_index == 0, sums[c], sums[2 + c]) for c in range(2)])
        other_x = jnp.stack([jnp.where(x_index == 0, sums[2 + c], sums[c]) for c in range(2)])
        come, gain_grad = swap_with(other_x, gain_grad, ("x", 0))
        halves = own_x.astype(jnp.float32) + come.astype(jnp.float32)
        own_half = jnp.where(core == 0, halves[0], halves[1])
        other_half = jnp.where(core == 0, halves[1], halves[0]).astype(jnp.bfloat16)
        come, gain_grad = swap_with(other_half, gain_grad, ("core", 0))
        come = come.astype(jnp.float32)
        weight_share = jnp.concatenate(
            [jnp.where(core == 0, own_half, come), jnp.where(core == 0, come, own_half)], axis=0
        )
    else:
        weight_share = scatter_whole([first_terms[0], *feed_grads])
        for where in [("core", 0)] + sum(bit_groups(), []):
            gain_grad = gain_grad + swap(gain_grad, where)
    weight_first, weight_second, weight_new = adam_update(
        weights.astype(jnp.float32), weight_share, first_moment, second_moment, RATE, DECAY, STEP
    )
    gain_first_new, gain_second_new, gain_new = adam_update(
        gains, gain_grad, gain_first, gain_second, GAIN_RATE, 0.0, STEP
    )
    return (
        result.reshape(inputs.shape),
        d_tokens.reshape(inputs.shape),
        weight_share,
        weight_second,
        weight_new,
        gain_grad,
        gain_second_new,
        gain_new,
    )


def solution(mesh):
    fine = Mesh(
        mesh.devices.reshape(mesh.shape["dp"] // 2, 2, mesh.shape["ctx"]), ("x", "core", "ctx")
    )
    rows = P(("x", "core"), "ctx", None)
    stacked = P(("x", "core", "ctx"), None)
    return jax.shard_map(
        shards,
        mesh=fine,
        in_specs=(rows, rows, stacked, P(), stacked, stacked, P(), P()),
        out_specs=(rows, rows, stacked, stacked, stacked, P(), P(), P()),
        check_vma=False,
    )
```

```python
import jax
import jax.numpy as jnp
import numpy as np
from jax import lax
from jax.experimental import pallas as pl
from jax.experimental.pallas import tpu as pltpu
from jax.sharding import Mesh
from jax.sharding import PartitionSpec as P

HEADS = 15
KV = 5
HD = 64
FF = 2560
STEP = 10


SCALE_QK = 0.125
THETA = 10000.0
EPSILON = 1e-05
BETA_ONE = 0.9
BETA_TWO = 0.95
ADAM_EPS = 1e-08
DECAY = 0.1
RATE = 0.02
GAIN_RATE = 0.2
GROUP = HEADS // KV
KEY_TILE = 256
HIDDEN = -1e30
VMEM_BYTES = 48 * 1024 * 1024


def places(row_index, local_rows, ctx_count):
    half_rows = local_rows // 2
    owner_index = row_index // local_rows
    inner_index = row_index % local_rows
    return jnp.where(
        inner_index < half_rows,
        owner_index * half_rows + inner_index,
        (2 * ctx_count - 1 - owner_index) * half_rows + inner_index - half_rows,
    )


def angle_tables(positions_in, sign):
    half_width = HD // 2
    frequency = THETA ** (-jnp.arange(half_width, dtype=jnp.float32) * 2.0 / HD)
    angles = frequency[:, None] * positions_in.astype(jnp.float32)[None, :]
    return jnp.cos(angles), sign * jnp.sin(angles)


def rotate(values, tables):
    cosine, sine_part = tables
    heads = values.reshape(-1, HD, values.shape[-1])
    first_half = heads[:, : HD // 2]
    second_half = heads[:, HD // 2 :]
    return jnp.concatenate(
        [
            first_half * cosine - second_half * sine_part,
            second_half * cosine + first_half * sine_part,
        ],
        axis=1,
    ).reshape(values.shape)


def normalize(values):
    return values * lax.rsqrt(jnp.mean(values * values, axis=-1, keepdims=True) + EPSILON)


def norm_back(values, grad_in, gain_row):
    inv_scale = lax.rsqrt(jnp.mean(values * values, axis=-1, keepdims=True) + EPSILON)
    unit_rows = values * inv_scale
    grad_unit = grad_in * gain_row
    grad_values = inv_scale * (
        grad_unit - unit_rows * jnp.mean(grad_unit * unit_rows, axis=-1, keepdims=True)
    )
    return (grad_values, jnp.sum(grad_in * unit_rows, axis=0))


def matmul_n(left, right):
    return jnp.dot(left, right, preferred_element_type=jnp.float32)


def matmul_t(left, right):
    return lax.dot_general(
        left, right, (((1,), (1,)), ((), ())), preferred_element_type=jnp.float32
    )


def matmul_c(left, right):
    return lax.dot_general(
        left, right, (((0,), (0,)), ((), ())), preferred_element_type=jnp.float32
    )


def bit_groups():
    x_bits = lax.axis_size("x").bit_length() - 1
    ctx_bits = lax.axis_size("ctx").bit_length() - 1
    low_ctx = ctx_bits // 2
    along_x = [("x", bit) for bit in range(x_bits)]
    along_y = [("ctx", bit) for bit in range(low_ctx)]
    along_z = [("ctx", bit) for bit in range(low_ctx, ctx_bits)]
    return along_x, along_y, along_z


def swap_by(values, axis, offset):
    size = lax.axis_size(axis)
    return lax.ppermute(values, axis, [(i, i ^ offset) for i in range(size)])


def swap(values, where):
    return swap_by(values, where[0], 1 << where[1])


def add_low(left, right):
    return (left.astype(jnp.float32) + right.astype(jnp.float32)).astype(jnp.bfloat16)


def rel_offsets(order):
    strides = {"x": 2 * lax.axis_size("ctx"), "ctx": 1}
    offsets = np.zeros((1,), np.int64)
    for axis, bit in order:
        offsets = np.concatenate([offsets, offsets ^ (strides[axis] << bit)])
    return offsets


def lookup(slot, offsets):
    total = jnp.int32(0)
    for bit in range(len(offsets).bit_length() - 1):
        total = total + ((slot >> bit) & 1) * int(offsets[1 << bit])
    return total


def find(offset, offsets):
    total = jnp.int32(0)
    for bit in range(len(offsets).bit_length() - 1):
        place = int(offsets[1 << bit]).bit_length() - 1
        total = total + (((offset >> place) & 1) << bit)
    return total


def collect(values, order):
    kept, arrived = values, None
    for where in order:
        half = kept.shape[0] // 2
        if arrived is None:
            away, kept_next = kept[half:], kept[:half]
        else:
            away = add_low(kept[half:], arrived[half:])
            kept_next = add_low(kept[:half], arrived[:half])
        arrived = swap(away, where)
        kept = kept_next
    return kept[0].astype(jnp.float32) + arrived[0].astype(jnp.float32)


def scatter_whole(terms):
    ctx_count = lax.axis_size("ctx")
    count = 2 * lax.axis_size("x") * ctx_count
    along_x, along_y, along_z = bit_groups()
    core = ("core", 0)
    me = device_index().reshape(1)
    blocks, rows, width = terms[0].shape
    first = -(-rows // 48) * 16
    groups = [(0, first), (first, 2 * first), (2 * first, rows)]
    orders = [
        along_x + along_y + along_z,
        along_y + along_z + along_x,
        along_z + along_x + along_y,
    ]
    tables = [rel_offsets(list(reversed(order))) for order in orders]

    def target(step, me_ref, flip):
        return lookup(step, tables[0]) ^ me_ref[0] ^ flip

    def sources(flip):
        def chosen(member):
            def index(step, me_ref):
                spot = target(step, me_ref, flip)
                return (jnp.where(spot // blocks == member, spot % blocks, 0), 0, 0)

            return pl.BlockSpec((1, rows, width), index)

        return [chosen(member) for member in range(len(terms))]

    def pick_body(me_ref, *refs):
        held = target(pl.program_id(0), me_ref, ctx_count) // blocks
        for member in range(len(terms)):

            @pl.when(held == member)
            def _(member=member):
                refs[-1][...] = refs[member][...]

    away = pl.pallas_call(
        pick_body,
        grid_spec=pltpu.PrefetchScalarGridSpec(
            num_scalar_prefetch=1,
            grid=(count // 2,),
            in_specs=sources(ctx_count),
            out_specs=pl.BlockSpec((1, rows, width), lambda step, me_ref: (step, 0, 0)),
        ),
        out_shape=jax.ShapeDtypeStruct((count // 2, rows, width), jnp.bfloat16),
        compiler_params=pltpu.CompilerParams(vmem_limit_bytes=VMEM_BYTES),
    )(me, *terms)
    arrived = swap(away, core)

    def merge_body(me_ref, *refs):
        held = target(pl.program_id(0), me_ref, 0) // blocks
        for member in range(len(terms)):

            @pl.when(held == member)
            def _(member=member):
                for (low, high), out in zip(groups, refs[-3:]):
                    out[0] = add_low(refs[member][0, low:high], refs[-4][0, low:high])

    parts = pl.pallas_call(
        merge_body,
        grid_spec=pltpu.PrefetchScalarGridSpec(
            num_scalar_prefetch=1,
            grid=(count // 2,),
            in_specs=sources(0)
            + [pl.BlockSpec((1, rows, width), lambda step, me_ref: (step, 0, 0))],
            out_specs=[
                pl.BlockSpec(
                    (1, high - low, width),
                    lambda step, me_ref, table=table: (
                        find(lookup(step, tables[0]), table),
                        0,
                        0,
                    ),
                )
                for (low, high), table in zip(groups, tables)
            ],
        ),
        out_shape=[
            jax.ShapeDtypeStruct((count // 2, high - low, width), jnp.bfloat16)
            for low, high in groups
        ],
        compiler_params=pltpu.CompilerParams(vmem_limit_bytes=VMEM_BYTES),
    )(me, *terms, arrived)
    return jnp.concatenate([collect(part, order) for part, order in zip(parts, orders)], axis=0)


def device_index():
    return (
        (lax.axis_index("x") * 2 + lax.axis_index("core")) * lax.axis_size("ctx")
        + lax.axis_index("ctx")
    ).astype(jnp.int32)


def splits_rows(rows):
    along_x, along_y, along_z = bit_groups()
    return (len(along_x), len(along_y), len(along_z)) == (1, 1, 2) and rows % 64 == 0


def spread(values, order):
    values = values[None]
    for where in order:
        values = double(values, where)
    return values


def double(values, where):
    return jnp.concatenate([values, swap(values, where)], axis=0)


def ctx_orders():
    along_x, along_y, along_z = bit_groups()
    return [along_y + along_z, along_z + along_y]


def row_cuts(rows):
    first = -(-rows // 32) * 16
    return [(0, first), (first, rows)]


def slot_bits():
    along_x, along_y, along_z = bit_groups()
    return list(reversed(along_z)) + along_y


def total_low(*terms):
    total = terms[0].astype(jnp.float32)
    for term in terms[1:]:
        total = total + term.astype(jnp.float32)
    return total.astype(jnp.bfloat16)


def reduce_start(keep, away):
    come = swap(away, ("core", 0))
    quarter = keep.shape[2] // 2
    near, far = slice(0, quarter), slice(quarter, 2 * quarter)
    sends = [
        add_low(keep[:, 4:, far], come[:, 4:, far]),
        add_low(keep[:, :4, far], come[:, :4, far]),
    ]
    return sends, (keep[:, :, near], come[:, :, near])


def reduce_y(held, x_upper, ride=None):
    upper = [part[:, 4:] for part in held] + [x_upper]
    return swap_with(total_low(*upper), ride, slot_bits()[2])


def reduce_near(rest, ride=None):
    return swap_with(total_low(*[part[:, 2:] for part in rest]), ride, slot_bits()[1])


def reduce_far(rest, ride=None):
    return swap_with(total_low(*[part[:, 1] for part in rest]), ride, slot_bits()[0])


def reduce_end(rest, z_far):
    total = z_far.astype(jnp.float32)
    for part in rest:
        total = total + part[:, 0].astype(jnp.float32)
    return total


def ride_parts(ride):
    rounded = lax.reduce_precision(ride, 8, 7)
    return rounded, lax.reduce_precision(ride - rounded, 8, 7)


def with_ride(sent, parts):
    extra = jnp.concatenate([*parts, jnp.zeros((12, parts[0].shape[1]), jnp.float32)])
    return jnp.concatenate([sent.reshape(-1, sent.shape[-1]), extra.astype(jnp.bfloat16)], axis=0)


def swap_with(sent, ride, where):
    if ride is None:
        return swap(sent, where), None
    parts = ride_parts(ride)
    come, other = off_ride(swap(with_ride(sent, parts), where), sent.shape)
    return come, (parts[0] + parts[1]) + other


def off_ride(come, shape):
    parts = come[-16:].astype(jnp.float32)
    return come[:-16].reshape(shape), parts[0:2] + parts[2:4]


def gather_halves(weights):
    rows = weights.shape[0]
    x_index, core = lax.axis_index("x"), lax.axis_index("core")
    half = rows // 2
    far = swap(weights, ("x", 0))
    low = jnp.where(x_index == 0, weights, far)
    high = jnp.where(x_index == 0, far, weights)
    both = jnp.stack([low, high])
    keep = jnp.where(core == 0, both[:, :half], both[:, half:])
    come = swap(jnp.where(core == 0, both[:, half:], both[:, :half]), ("core", 0))
    first = jnp.where(core == 0, keep, come)
    second = jnp.where(core == 0, come, keep)
    feed = jnp.stack([second[0], first[1], second[1]])
    return first[0], jnp.where(x_index == 0, feed[:, : half // 2], feed[:, half // 2 :])


def place_rows(own, far):
    tables = [rel_offsets(list(reversed(order))) for order in ctx_orders()]
    slots, width = own[0].shape[0], own[0].shape[2]
    lengths = [part.shape[1] for part in own]
    half = sum(lengths)

    def body(me_ref, *refs):
        out_ref = refs[-1]
        for core in range(2):

            @pl.when(me_ref[0] == core)
            def _(core=core):
                for source, base in ((0, core * half), (2, (1 - core) * half)):
                    out_ref[0, base : base + lengths[0]] = refs[source][0]
                    out_ref[0, base + lengths[0] : base + half] = refs[source + 1][0]

    specs = [
        pl.BlockSpec(
            (1, length, width),
            lambda step, me_ref, table=table: (find(step ^ me_ref[1], table), 0, 0),
        )
        for length, table in zip(lengths, tables)
    ]
    me = jnp.stack([lax.axis_index("core"), lax.axis_index("ctx")]).astype(jnp.int32)
    return pl.pallas_call(
        body,
        grid_spec=pltpu.PrefetchScalarGridSpec(
            num_scalar_prefetch=1,
            grid=(slots,),
            in_specs=specs * 2,
            out_specs=pl.BlockSpec((1, 2 * half, width), lambda step, me_ref: (step, 0, 0)),
        ),
        out_shape=jax.ShapeDtypeStruct((slots, 2 * half, width), own[0].dtype),
        cost_estimate=pl.CostEstimate(
            flops=0, bytes_accessed=8 * slots * half * width, transcendentals=0
        ),
        compiler_params=pltpu.CompilerParams(vmem_limit_bytes=VMEM_BYTES),
    )(me, *own, *far).reshape(slots * 2 * half, width)


def turned(values):
    return jnp.transpose(values)


def load_packed(ref, aligned):
    if not aligned:
        return ref[0, 0]
    half = ref.shape[1] // 2
    return jnp.concatenate(
        [
            ref[head * HD : (head + 1) * HD, side * half : (side + 1) * half]
            for side in range(2)
            for head in range(GROUP)
        ],
        axis=1,
    )


def store_packed(ref, values, aligned):
    if not aligned:
        ref[0, 0] = values
        return
    half = ref.shape[1] // 2
    for side in range(2):
        for head in range(GROUP):
            start = (side * GROUP + head) * half
            ref[head * HD : (head + 1) * HD, side * half : (side + 1) * half] = values[
                :, start : start + half
            ]


def load_tile(refs, side, tile):
    length = refs[0].shape[1] // 2
    if length >= KEY_TILE:
        start = side * length + tile * KEY_TILE
        return refs[0][:, start : start + KEY_TILE]
    many = KEY_TILE // length
    return jnp.concatenate(
        [
            ref[:, side * length : (side + 1) * length]
            for ref in refs[tile * many : (tile + 1) * many]
        ],
        axis=1,
    )


def attend_body(count, aligned, queries_ref, key_pos_ref, query_pos_ref, *refs):
    key_refs, value_refs = refs[:count], refs[count : 2 * count]
    out_ref, total_ref, work = refs[2 * count :]
    queries = load_packed(queries_ref, aligned)
    low_cols = queries.shape[1] // 2
    queries_high = queries[:, low_cols:]
    tiles = key_pos_ref.shape[1] // KEY_TILE
    largest = jnp.full((1, queries.shape[1]), HIDDEN, jnp.float32)
    largest_high = jnp.full((1, low_cols), HIDDEN, jnp.float32)
    for side in range(2):
        for tile in range(tiles):
            keys = turned(load_tile(key_refs, side, tile))
            row = (side * tiles + tile) * KEY_TILE
            key_places = key_pos_ref[side, tile * KEY_TILE : (tile + 1) * KEY_TILE]
            if side == 0:
                scores = matmul_n(keys, queries)
                scores = jnp.where(key_places <= query_pos_ref[...], scores, HIDDEN)
                work[row : row + KEY_TILE] = scores
                largest = jnp.maximum(largest, jnp.max(scores, axis=0, keepdims=True))
            else:
                scores = matmul_n(keys, queries_high)
                scores = jnp.where(key_places <= query_pos_ref[:, low_cols:], scores, HIDDEN)
                work[row : row + KEY_TILE, low_cols:] = scores
                largest_high = jnp.maximum(largest_high, jnp.max(scores, axis=0, keepdims=True))
    high_max = jnp.maximum(largest[:, low_cols:], largest_high)
    largest = jnp.concatenate([largest[:, :low_cols], high_max], axis=1)
    total = jnp.zeros_like(largest)
    mixed = jnp.zeros((HD, queries.shape[1]), jnp.float32)
    total_high = jnp.zeros_like(largest_high)
    mixed_high = jnp.zeros((HD, low_cols), jnp.float32)
    for side in range(2):
        for tile in range(tiles):
            values = load_tile(value_refs, side, tile)
            row = (side * tiles + tile) * KEY_TILE
            if side == 0:
                expos = jnp.exp(work[row : row + KEY_TILE] - largest)
                total = total + jnp.sum(expos, axis=0, keepdims=True)
                mixed = mixed + matmul_n(values, expos.astype(jnp.bfloat16))
            else:
                expos = jnp.exp(work[row : row + KEY_TILE, low_cols:] - high_max)
                total_high = total_high + jnp.sum(expos, axis=0, keepdims=True)
                mixed_high = mixed_high + matmul_n(values, expos.astype(jnp.bfloat16))
    total = jnp.concatenate([total[:, :low_cols], total[:, low_cols:] + total_high], axis=1)
    mixed = jnp.concatenate([mixed[:, :low_cols], mixed[:, low_cols:] + mixed_high], axis=1)
    store_packed(out_ref, (mixed / total).astype(jnp.bfloat16), aligned)
    total_ref[0, 0] = largest + jnp.log(total)


def attend_back_body(
    count, aligned, queries_ref, key_pos_ref, query_pos_ref, *refs
):
    key_refs, value_refs = refs[:count], refs[count : 2 * count]
    out_ref, total_ref, d_out_ref, cosine_ref, sine_ref = refs[2 * count : 2 * count + 5]
    d_queries_ref, pair_refs = refs[2 * count + 5], refs[2 * count + 6 :]
    all_queries, all_d_out = load_packed(queries_ref, aligned), load_packed(d_out_ref, aligned)
    low_cols = all_queries.shape[1] // 2
    tiles = key_pos_ref.shape[1] // KEY_TILE
    delta = jnp.sum(
        all_d_out.astype(jnp.float32) * load_packed(out_ref, aligned).astype(jnp.float32),
        axis=0,
        keepdims=True,
    )
    totals = total_ref[0, 0]
    parts = []
    for side in range(2):
        if side == 0:
            queries, d_out = all_queries, all_d_out
            query_places, log_total, row_delta = query_pos_ref[...], totals, delta
        else:
            queries, d_out = all_queries[:, low_cols:], all_d_out[:, low_cols:]
            query_places = query_pos_ref[:, low_cols:]
            log_total, row_delta = totals[:, low_cols:], delta[:, low_cols:]
        part = jnp.zeros((HD, queries.shape[1]), jnp.float32)
        for tile in range(tiles):
            keys_flat = load_tile(key_refs, side, tile)
            scores = matmul_n(turned(keys_flat), queries)
            seen = key_pos_ref[side, tile * KEY_TILE : (tile + 1) * KEY_TILE] <= query_places
            probs = jnp.where(seen, jnp.exp(scores - log_total), 0.0)
            d_probs = matmul_n(turned(load_tile(value_refs, side, tile)), d_out)
            d_scores = (probs * (d_probs - row_delta)).astype(jnp.bfloat16)
            part = part + matmul_n(keys_flat, d_scores)
            d_key = matmul_t(d_scores, queries).astype(jnp.bfloat16)
            d_value = matmul_t(probs.astype(jnp.bfloat16), d_out).astype(jnp.bfloat16)
            if aligned:
                length = key_refs[0].shape[1] // 2
                places_out = [(ref, slot) for ref in pair_refs for slot in range(ref.shape[0])]
                for piece in range(KEY_TILE // length):
                    ref, slot = places_out[tile * (KEY_TILE // length) + piece]
                    rows = slice(piece * length, (piece + 1) * length)
                    ref[slot, 0, side, :, :HD] = d_key[rows]
                    ref[slot, 0, side, :, HD:] = d_value[rows]
            else:
                rows = slice(tile * KEY_TILE, (tile + 1) * KEY_TILE)
                pair_refs[0][side, 0, rows, :HD] = d_key
                pair_refs[0][side, 0, rows, HD:] = d_value
        parts.append(part)
    d_queries = jnp.concatenate(
        [parts[0][:, :low_cols], parts[0][:, low_cols:] + parts[1]], axis=1
    )
    cosine, sine_part = cosine_ref[...], sine_ref[...]
    first_half, second_half = d_queries[: HD // 2], d_queries[HD // 2 :]
    turned_back = jnp.concatenate(
        [
            first_half * cosine + second_half * sine_part,
            second_half * cosine - first_half * sine_part,
        ],
        axis=0,
    )
    store_packed(d_queries_ref, (turned_back * SCALE_QK).astype(jnp.bfloat16), aligned)


def head_specs(leads, aligned, cols, keys, local_rows, seq):
    count = len(leads)
    if aligned:
        packed = pl.BlockSpec((GROUP * HD, local_rows), lambda head: (head, seq))
    else:
        packed = pl.BlockSpec((1, 1, HD, cols), lambda head: (seq, head, 0, 0))
    specs = [
        packed,
        pl.BlockSpec((2, keys, 1), lambda head: (0, 0, 0)),
        pl.BlockSpec((1, cols), lambda head: (0, 0)),
    ]
    for first in (0, KV):
        specs += [
            pl.BlockSpec(
                (None, HD, 2 * keys // count),
                lambda head, lead=lead, first=first: (lead, first + head, seq),
            )
            for lead in leads
        ]
    return packed, specs


def attend(queries, pairs, key_pos, query_pos, local_rows, seq):
    aligned = queries.ndim == 2
    cols, keys, count = query_pos.shape[1], key_pos.shape[1], len(pairs)
    leads, arrays = [lead for _, lead in pairs], [array for array, _ in pairs]
    _, specs = head_specs(leads, aligned, cols, keys, local_rows, seq)
    work = HEADS * keys * cols // GROUP * 3 // 2
    if aligned:
        out_spec = pl.BlockSpec((GROUP * HD, local_rows), lambda head: (head, 0))
        out_shape = jax.ShapeDtypeStruct((HEADS * HD, local_rows), jnp.bfloat16)
    else:
        out_spec = pl.BlockSpec((1, 1, HD, cols), lambda head: (0, head, 0, 0))
        out_shape = jax.ShapeDtypeStruct((1, KV, HD, cols), jnp.bfloat16)
    return pl.pallas_call(
        lambda *refs: attend_body(count, aligned, *refs),
        grid=(KV,),
        in_specs=specs,
        out_specs=[out_spec, pl.BlockSpec((1, 1, 1, cols), lambda head: (0, head, 0, 0))],
        out_shape=[out_shape, jax.ShapeDtypeStruct((1, KV, 1, cols), jnp.float32)],
        scratch_shapes=[pltpu.VMEM((2 * keys, cols), jnp.float32)],
        cost_estimate=pl.CostEstimate(
            flops=work * HD, bytes_accessed=1024 * 1024, transcendentals=0
        ),
        compiler_params=pltpu.CompilerParams(vmem_limit_bytes=VMEM_BYTES),
    )(queries, key_pos, query_pos, *arrays, *arrays)


def attend_back(
    queries, pairs, key_pos, query_pos, mixed, log_total, d_mixed, tables, local_rows, seq, sets
):
    aligned = queries.ndim == 2
    cols, keys, count = query_pos.shape[1], key_pos.shape[1], len(pairs)
    leads, arrays = [lead for _, lead in pairs], [array for array, _ in pairs]
    packed, specs = head_specs(leads, aligned, cols, keys, local_rows, seq)
    work = HEADS * keys * cols // GROUP * 3 // 2
    if aligned:
        own = pl.BlockSpec((GROUP * HD, local_rows), lambda head: (head, 0))
        own_shape = jax.ShapeDtypeStruct((HEADS * HD, local_rows), jnp.bfloat16)
        length = keys // count
        pair_specs = [
            pl.BlockSpec((slots, 1, 2, length, 2 * HD), lambda head: (0, head, 0, 0, 0))
            for slots in sets
        ]
        pair_shapes = [
            jax.ShapeDtypeStruct((slots, KV, 2, length, 2 * HD), jnp.bfloat16) for slots in sets
        ]
    else:
        own = pl.BlockSpec((1, 1, HD, cols), lambda head: (0, head, 0, 0))
        own_shape = jax.ShapeDtypeStruct((1, KV, HD, cols), jnp.bfloat16)
        pair_specs = [pl.BlockSpec((2, 1, keys, 2 * HD), lambda head: (0, head, 0, 0))]
        pair_shapes = [jax.ShapeDtypeStruct((2, KV, keys, 2 * HD), jnp.bfloat16)]
    table_spec = pl.BlockSpec((HD // 2, cols), lambda head: (0, 0))
    return pl.pallas_call(
        lambda *refs: attend_back_body(count, aligned, *refs),
        grid=(KV,),
        in_specs=specs
        + [
            own,
            pl.BlockSpec((1, 1, 1, cols), lambda head: (0, head, 0, 0)),
            packed,
            table_spec,
            table_spec,
        ],
        out_specs=[own] + pair_specs,
        out_shape=[own_shape] + pair_shapes,
        cost_estimate=pl.CostEstimate(
            flops=work * HD, bytes_accessed=1024 * 1024, transcendentals=0
        ),
        compiler_params=pltpu.CompilerParams(vmem_limit_bytes=VMEM_BYTES),
    )(queries, key_pos, query_pos, *arrays, *arrays, mixed, log_total, d_mixed, *tables)


def put_rows(values, keep_ref, away_ref, member, core, x_index):
    quarter = values.shape[0] // 4
    for mine in range(4):

        @pl.when(2 * core + x_index == mine)
        def _(mine=mine):
            for ref, side in ((keep_ref, mine // 2), (away_ref, 1 - mine // 2)):
                for place, along_x in enumerate((mine % 2, 1 - mine % 2)):
                    start = (2 * side + along_x) * quarter
                    ref[member, 0, place * quarter : (place + 1) * quarter] = values[
                        start : start + quarter
                    ]


def feed_body(
    parts, split, me_ref, a_two_ref, dy_ref, *refs
):
    count = 4 if split else 6
    weight_refs, (out_ref, d_two_ref), grad_refs = (
        refs[:count],
        refs[count : count + 2],
        refs[count + 2 :],
    )
    core, x_index = me_ref[0], me_ref[1]
    step = pl.program_id(0)

    @pl.when(step == 0)
    def _():
        out_ref[...] = jnp.zeros_like(out_ref)
        d_two_ref[...] = jnp.zeros_like(d_two_ref)

    def rows_of(member):
        if split:
            parts_here = [ref[0, member] for ref in weight_refs]
            rows_out = []
            for side in range(2):
                for along_x in range(2):
                    near = jnp.where(x_index == along_x, parts_here[0], parts_here[1])
                    far = jnp.where(x_index == along_x, parts_here[2], parts_here[3])
                    rows_out.append(jnp.where(core == side, near, far))
            return jnp.concatenate(rows_out, axis=0)
        wanted = feed_core(member, step, parts)
        return jnp.where(wanted == core, weight_refs[2 * member][0], weight_refs[2 * member + 1][0])

    a_two, dy_low = a_two_ref[...], dy_ref[...]
    gate_rows, up_rows, down_rows = rows_of(0), rows_of(1), rows_of(2)
    gate_pre = matmul_t(gate_rows, a_two)
    up_pre = matmul_t(up_rows, a_two)
    d_hidden = matmul_t(down_rows, dy_low)
    sigma = jax.nn.sigmoid(gate_pre)
    gate_act = gate_pre * sigma
    hidden = (gate_act * up_pre).astype(jnp.bfloat16)
    d_gate = (d_hidden * up_pre * sigma * (1.0 + gate_pre * (1.0 - sigma))).astype(jnp.bfloat16)
    d_up = (d_hidden * gate_act).astype(jnp.bfloat16)
    out_ref[...] += matmul_c(hidden, down_rows)
    d_two_ref[...] += matmul_c(d_gate, gate_rows) + matmul_c(d_up, up_rows)
    for member, (left, right) in enumerate(((d_gate, a_two), (d_up, a_two), (hidden, dy_low))):
        grad = matmul_n(left, right).astype(jnp.bfloat16)
        if split:
            put_rows(grad, grad_refs[0], grad_refs[1], member, core, x_index)
        else:
            grad_refs[member][0] = grad


def feed_core(member, step, parts):
    ctx_count, single = parts
    return (member + 1) % 2 if single else step // ctx_count


def feed_forward(a_two, dy_low, mine, far, rows):
    tokens, width = a_two.shape
    ctx_count = lax.axis_size("ctx")
    blocks = FF // rows
    single = blocks == ctx_count
    split = splits_rows(rows)
    parts = (ctx_count, single)
    whole = pl.BlockSpec((tokens, width), lambda step, me_ref: (0, 0))

    def weight_spec(member, own):
        first = (member + 1) * blocks // ctx_count // 2 * ctx_count

        def index(step, me_ref):
            matches = (feed_core(member, step, parts) == me_ref[0]) == own
            return (first + jnp.where(matches, step % ctx_count, 0), 0, 0)

        return pl.BlockSpec((1, rows, width), index)

    if split:
        weight_specs = [
            pl.BlockSpec((1, 3, rows // 4, width), lambda step, me_ref: (step, 0, 0, 0))
        ] * 4
        weight_args = [*mine, *far]
        half = pl.BlockSpec((3, 1, rows // 2, width), lambda step, me_ref: (0, step, 0, 0))
        grad_specs = [half, half]
        grad_shapes = [jax.ShapeDtypeStruct((3, blocks, rows // 2, width), jnp.bfloat16)] * 2
    else:
        weight_specs = [weight_spec(member, own) for member in range(3) for own in (True, False)]
        weight_args = [mine, far] * 3
        grad_specs = [pl.BlockSpec((1, rows, width), lambda step, me_ref: (step, 0, 0))] * 3
        grad_shapes = [jax.ShapeDtypeStruct((blocks, rows, width), jnp.bfloat16)] * 3
    me = jnp.stack([lax.axis_index("core"), lax.axis_index("x")]).astype(jnp.int32)
    return pl.pallas_call(
        lambda *refs: feed_body(parts, split, *refs),
        grid_spec=pltpu.PrefetchScalarGridSpec(
            num_scalar_prefetch=1,
            grid=(blocks,),
            in_specs=[whole, whole] + weight_specs,
            out_specs=[whole, whole] + grad_specs,
        ),
        out_shape=[jax.ShapeDtypeStruct((tokens, width), jnp.float32)] * 2 + grad_shapes,
        cost_estimate=pl.CostEstimate(
            flops=18 * tokens * width * FF, bytes_accessed=12 * FF * width, transcendentals=FF * tokens
        ),
        compiler_params=pltpu.CompilerParams(vmem_limit_bytes=VMEM_BYTES),
    )(me, a_two, dy_low, *weight_args)


def first_grads(d_qkv, attn_low, a_one, d_resid_low, rows):
    tokens, width = a_one.shape
    split = splits_rows(rows)
    early = d_qkv.shape[0] // rows
    blocks = early + attn_low.shape[0] // rows

    def body(me_ref, qkv_ref, attn_ref, one_ref, resid_ref, *grad_refs):
        first = pl.program_id(0) < early
        left = jnp.where(first, qkv_ref[...], attn_ref[...])
        right = jnp.where(first, one_ref[...], resid_ref[...])
        grad = matmul_n(left, right).astype(jnp.bfloat16)
        if split:
            put_rows(grad, grad_refs[0], grad_refs[1], 0, me_ref[0], me_ref[2])
        else:
            grad_refs[0][0] = grad

    whole = pl.BlockSpec((tokens, width), lambda step, me_ref: (0, 0))
    if split:
        table = rel_offsets(slot_bits())
        half = pl.BlockSpec(
            (1, 1, rows // 2, width), lambda step, me_ref: (0, find(step ^ me_ref[1], table), 0, 0)
        )
        grad_specs = [half, half]
        grad_shapes = [jax.ShapeDtypeStruct((1, blocks, rows // 2, width), jnp.bfloat16)] * 2
    else:
        grad_specs = [pl.BlockSpec((1, rows, width), lambda step, me_ref: (step, 0, 0))]
        grad_shapes = [jax.ShapeDtypeStruct((blocks, rows, width), jnp.bfloat16)]
    me = jnp.stack([lax.axis_index(name) for name in ("core", "ctx", "x")]).astype(jnp.int32)
    return pl.pallas_call(
        body,
        grid_spec=pltpu.PrefetchScalarGridSpec(
            num_scalar_prefetch=1,
            grid=(blocks,),
            in_specs=[
                pl.BlockSpec((rows, tokens), lambda step, me_ref: (jnp.minimum(step, early - 1), 0)),
                pl.BlockSpec((rows, tokens), lambda step, me_ref: (jnp.maximum(step - early, 0), 0)),
                whole,
                whole,
            ],
            out_specs=grad_specs,
        ),
        out_shape=grad_shapes,
        cost_estimate=pl.CostEstimate(
            flops=2 * tokens * width * blocks * rows, bytes_accessed=2 * blocks * rows * width, transcendentals=0
        ),
        compiler_params=pltpu.CompilerParams(vmem_limit_bytes=VMEM_BYTES),
    )(me, d_qkv, attn_low, a_one, d_resid_low)


def adam_update(param, grad, first, second, rate, decay, step_number):
    first_new = BETA_ONE * first + (1.0 - BETA_ONE) * grad
    second_new = BETA_TWO * second + (1.0 - BETA_TWO) * grad * grad
    fix_one = 1.0 - BETA_ONE**step_number
    fix_two = 1.0 - BETA_TWO**step_number
    update = first_new / fix_one / (jnp.sqrt(second_new / fix_two) + ADAM_EPS)
    return (first_new, second_new, param - rate * (update + decay * param))


def shards(inputs, cotangent, weights, gains, first_moment, second_moment, gain_first, gain_second):
    ctx_count = lax.axis_size("ctx")
    x_count = lax.axis_size("x")
    ctx_index, core, x_index = lax.axis_index("ctx"), lax.axis_index("core"), lax.axis_index("x")
    seqs, local_rows, model_width = inputs.shape
    half_rows = local_rows // 2
    tokens = seqs * local_rows
    weight_rows = weights.shape[0]
    q_cols = HEADS * HD
    kv_cols = KV * HD
    cut_o = q_cols + 2 * kv_cols
    split = splits_rows(weight_rows)
    slots = slot_bits()
    aligned = split and half_rows % 128 == 0
    local_index = jnp.arange(local_rows, dtype=jnp.int32)
    pos_here = places(ctx_index * local_rows + local_index, local_rows, ctx_count)
    cosine, sine_part = angle_tables(pos_here, 1.0)
    turn = (jnp.tile(cosine, (1, seqs)), jnp.tile(sine_part, (1, seqs)))
    turn_back = (turn[0], -turn[1])

    def pack(flat):
        if aligned:
            return flat
        return (
            flat.reshape(KV, GROUP, HD, -1, 2, half_rows)
            .transpose(3, 0, 2, 4, 1, 5)
            .reshape(-1, KV, HD, 2 * GROUP * half_rows)
        )

    def unpack(packed):
        if aligned:
            return packed
        return (
            packed.reshape(KV, HD, 2, GROUP, half_rows)
            .transpose(0, 3, 1, 2, 4)
            .reshape(q_cols, local_rows)
        )

    def by_columns(row):
        rows = row.shape[0]
        return jnp.broadcast_to(
            row.reshape(rows, 2, 1, half_rows), (rows, 2, GROUP, half_rows)
        ).reshape(rows, 2 * GROUP * half_rows)

    owners = ctx_index ^ jnp.asarray(rel_offsets(slots), jnp.int32)
    inner = jnp.arange(half_rows, dtype=jnp.int32)
    key_pos = jnp.stack(
        [
            (owners[:, None] * half_rows + inner[None, :]).reshape(-1, 1),
            ((2 * ctx_count - 1 - owners[:, None]) * half_rows + inner[None, :]).reshape(-1, 1),
        ]
    )
    query_pos = by_columns(pos_here[None, :])
    packed_tables = (by_columns(cosine), by_columns(sine_part))

    if split:
        first_half, feed_quarter = gather_halves(weights)
        cuts = row_cuts(weight_rows // 2)
        backward = [list(reversed(order)) for order in ctx_orders()]
        first_own = [spread(first_half[low:high], order) for (low, high), order in zip(cuts, backward)]
        first_far = [swap(part, ("core", 0)) for part in first_own]
        first_rows = place_rows(first_own, first_far)
        feed_quarter, first_rows = lax.optimization_barrier((feed_quarter, first_rows))
        feed_own = double(feed_quarter[None], slots[0])
    else:
        mine = lax.all_gather(weights, ("x", "ctx"), axis=0, tiled=True)
        mine = mine.reshape(x_count * ctx_count, weight_rows, model_width)
        far = swap(mine, ("core", 0))
        sides = [
            jnp.where(core == 0, mine[:ctx_count], far[:ctx_count]),
            jnp.where(core == 0, far[:ctx_count], mine[:ctx_count]),
        ]
        first_rows = jnp.concatenate(sides).reshape(-1, model_width)
    qkv_rows, o_rows = first_rows[:cut_o], first_rows[cut_o : cut_o + q_cols]

    tokens_in, cot_in = lax.optimization_barrier(
        (inputs.reshape(tokens, model_width), cotangent.reshape(tokens, model_width))
    )
    dy_low = cot_in.astype(jnp.bfloat16)
    a_one = (normalize(tokens_in) * gains[0]).astype(jnp.bfloat16)
    pair_rows = matmul_t(qkv_rows[q_cols:], a_one)
    joined = jnp.concatenate(
        [rotate(pair_rows[:kv_cols], turn).astype(jnp.bfloat16), pair_rows[kv_cols:].astype(jnp.bfloat16)],
        axis=0,
    )
    if split:
        joined, feed_own = lax.optimization_barrier((joined, feed_own))
    if aligned:
        far_z, y_own = swap(joined, slots[0]), swap(joined, slots[2])
    if split:
        feed_near, feed_y = swap(feed_own, slots[1]), swap(feed_own, slots[2])
        feed_x = swap(feed_own, ("x", 0))
    if aligned:
        far_z, y_own, feed_near, feed_y, feed_x = lax.optimization_barrier(
            (far_z, y_own, feed_near, feed_y, feed_x)
        )
        near_z = swap(jnp.stack([joined, far_z]), slots[1])
        y_far = swap(far_z, slots[2])
    if split:
        feed_near_y = swap(feed_near, slots[2])
        x_parts = [feed_x, swap(feed_near, ("x", 0)), swap(feed_y, ("x", 0))]
    if aligned:
        near_z, y_far, feed_near_y, x_parts = lax.optimization_barrier(
            (near_z, y_far, feed_near_y, x_parts)
        )
        y_near = swap(near_z, slots[2])
        pairs = [(joined[None], 0), (far_z[None], 0), (near_z, 0), (near_z, 1)]
        pairs += [(y_own[None], 0), (y_far[None], 0), (y_near, 0), (y_near, 1)]
    else:
        pairs = spread(joined, slots).reshape(ctx_count, 2 * kv_cols, seqs, 2, half_rows)
        pairs = [
            (
                pairs.transpose(1, 2, 3, 0, 4).reshape(
                    1, 2 * kv_cols, seqs * 2 * ctx_count * half_rows
                ),
                0,
            )
        ]
    if split:
        x_parts.append(swap(feed_near_y, ("x", 0)))
        feed_own = jnp.concatenate([feed_own, feed_near, feed_y, feed_near_y], axis=0)
        feed_far = swap(feed_own, ("core", 0))
    q_rot = rotate(matmul_t(qkv_rows[:q_cols], a_one), turn).astype(jnp.bfloat16)
    queries = pack((q_rot * SCALE_QK).astype(jnp.bfloat16))
    attended = []
    for seq in range(seqs):
        attended.append(attend(queries, pairs, key_pos, query_pos, local_rows, seq))
        if split and seq == 0:
            attended, x_parts, feed_far = lax.optimization_barrier((attended, x_parts, feed_far))
            feed_x = jnp.concatenate(x_parts, axis=0)
            mine, far = [feed_own, feed_x], [feed_far, swap(feed_x, ("core", 0))]
    attn_low = jnp.concatenate([unpack(mixed) for mixed, _ in attended], axis=1)
    resid = tokens_in + matmul_c(attn_low, o_rows)
    a_two = (normalize(resid) * gains[1]).astype(jnp.bfloat16)
    fed, d_two, *feed_grads = feed_forward(a_two, dy_low, mine, far, weight_rows)
    result = resid + fed
    d_norm_two, d_gain_two = norm_back(resid, d_two, gains[1])
    d_resid = cot_in + d_norm_two
    d_resid_low = d_resid.astype(jnp.bfloat16)
    d_attn = pack(matmul_t(o_rows, d_resid_low).astype(jnp.bfloat16))
    if split:
        sends, feed_held = reduce_start(*feed_grads)
        d_attn, sends = lax.optimization_barrier((d_attn, sends))
        feed_upper, feed_lower = swap(sends[0], ("x", 0)), swap(sends[1], ("x", 0))
    d_q, d_pair = [], []
    for seq in range(seqs):
        mixed, log_total = attended[seq]
        d_queries, *d_slots = attend_back(
            queries, pairs, key_pos, query_pos, mixed, log_total, d_attn, packed_tables,
            local_rows, seq, (2, 2, 4),
        )
        if split and seq == seqs - 1:
            d_slots, feed_upper, feed_lower = lax.optimization_barrier(
                (d_slots, feed_upper, feed_lower)
            )
            feed_y, _ = reduce_y(feed_held, feed_upper)
        d_q.append(unpack(d_queries))
        if aligned:
            lower, near_part, upper = d_slots
            y_come = swap(upper, slots[2])
            near_come = swap(add_low(near_part, y_come[2:]), slots[1])
            if seq == seqs - 1:
                near_come, feed_y = lax.optimization_barrier((near_come, feed_y))
            far_come = swap(total_low(lower[1], y_come[1], near_come[1]), slots[0])
            total = far_come.astype(jnp.float32)
            for part in (lower, y_come, near_come):
                total = total + part[0].astype(jnp.float32)
        else:
            total = collect(
                d_slots[0]
                .reshape(2, KV, ctx_count, half_rows, 2 * HD)
                .transpose(2, 1, 0, 3, 4),
                list(reversed(slots)),
            )
        d_pair.append(total)
    d_own = jnp.stack(d_pair).transpose(1, 4, 0, 2, 3).reshape(KV, 2 * HD, tokens)
    d_qkv = jnp.concatenate(
        [
            jnp.concatenate(d_q, axis=1),
            rotate(d_own[:, :HD].reshape(kv_cols, tokens), turn_back).astype(jnp.bfloat16),
            d_own[:, HD:].reshape(kv_cols, tokens).astype(jnp.bfloat16),
        ],
        axis=0,
    )
    first_terms = first_grads(d_qkv, attn_low, a_one, d_resid_low, weight_rows)
    if split:
        feed_rest = [part[:, :4] for part in feed_held] + [feed_lower, feed_y]
        feed_near, _ = reduce_near(feed_rest)
        first_terms, feed_near = lax.optimization_barrier((first_terms, feed_near))
        feed_rest = [part[:, :2] for part in feed_rest] + [feed_near]
        feed_far, _ = reduce_far(feed_rest)
    d_one = matmul_c(d_qkv, qkv_rows)
    d_norm_one, d_gain_one = norm_back(tokens_in, d_one, gains[0])
    d_tokens = d_resid + d_norm_one
    gain_grad = jnp.stack([d_gain_one, d_gain_two], axis=0)
    if split:
        sends, first_held = reduce_start(*first_terms)
        first_upper = swap(sends[0], ("x", 0))
        first_lower, gain_grad = swap_with(sends[1], gain_grad, ("x", 0))
        first_upper, feed_far = lax.optimization_barrier((first_upper, feed_far))
        feed_sums = reduce_end(feed_rest, feed_far)
        first_y, gain_grad = reduce_y(first_held, first_upper, gain_grad)
        rest = [part[:, :4] for part in first_held] + [first_lower, first_y]
        first_near, gain_grad = reduce_near(rest, gain_grad)
        rest = [part[:, :2] for part in rest] + [first_near]
        first_far, gain_grad = reduce_far(rest, gain_grad)
        first_sums = reduce_end(rest, first_far)
        sums = [first_sums[0], feed_sums[0], feed_sums[1], feed_sums[2]]
        own_x = jnp.stack([jnp.where(x_index == 0, sums[c], sums[2 + c]) for c in range(2)])
        other_x = jnp.stack([jnp.where(x_index == 0, sums[2 + c], sums[c]) for c in range(2)])
        far_x = swap(other_x.astype(jnp.bfloat16), ("x", 0)).astype(jnp.float32)
        halves = jnp.where(
            x_index == 0,
            jnp.concatenate([own_x, far_x], axis=1),
            jnp.concatenate([far_x, own_x], axis=1),
        )
        own_half = jnp.where(core == 0, halves[0], halves[1])
        other_half = jnp.where(core == 0, halves[1], halves[0]).astype(jnp.bfloat16)
        come, gain_grad = swap_with(other_half, gain_grad, ("core", 0))
        come = come.astype(jnp.float32)
        weight_share = jnp.concatenate(
            [jnp.where(core == 0, own_half, come), jnp.where(core == 0, come, own_half)], axis=0
        )
    else:
        weight_share = scatter_whole([first_terms[0], *feed_grads])
        for where in [("core", 0)] + sum(bit_groups(), []):
            gain_grad = gain_grad + swap(gain_grad, where)
    weight_first, weight_second, weight_new = adam_update(
        weights.astype(jnp.float32), weight_share, first_moment, second_moment, RATE, DECAY, STEP
    )
    gain_first_new, gain_second_new, gain_new = adam_update(
        gains, gain_grad, gain_first, gain_second, GAIN_RATE, 0.0, STEP
    )
    return (
        result.reshape(inputs.shape),
        d_tokens.reshape(inputs.shape),
        weight_share,
        weight_second,
        weight_new,
        gain_grad,
        gain_second_new,
        gain_new,
    )


def solution(mesh):
    fine = Mesh(
        mesh.devices.reshape(mesh.shape["dp"] // 2, 2, mesh.shape["ctx"]), ("x", "core", "ctx")
    )
    rows = P(("x", "core"), "ctx", None)
    stacked = P(("x", "core", "ctx"), None)
    return jax.shard_map(
        shards,
        mesh=fine,
        in_specs=(rows, rows, stacked, P(), stacked, stacked, P(), P()),
        out_specs=(rows, rows, stacked, stacked, stacked, P(), P(), P()),
        check_vma=False,
    )
```

```python
import jax
import jax.numpy as jnp
import numpy as np
from jax import lax
from jax.experimental import pallas as pl
from jax.experimental.pallas import tpu as pltpu
from jax.sharding import Mesh
from jax.sharding import PartitionSpec as P

HEADS = 15
KV = 5
HD = 64
FF = 2560
STEP = 10


SCALE_QK = 0.125
THETA = 10000.0
EPSILON = 1e-05
BETA_ONE = 0.9
BETA_TWO = 0.95
ADAM_EPS = 1e-08
DECAY = 0.1
RATE = 0.02
GAIN_RATE = 0.2
GROUP = HEADS // KV
KEY_TILE = 256
HIDDEN = -1e30
VMEM_BYTES = 48 * 1024 * 1024


def places(row_index, local_rows, ctx_count):
    half_rows = local_rows // 2
    owner_index = row_index // local_rows
    inner_index = row_index % local_rows
    return jnp.where(
        inner_index < half_rows,
        owner_index * half_rows + inner_index,
        (2 * ctx_count - 1 - owner_index) * half_rows + inner_index - half_rows,
    )


def angle_tables(positions_in, sign):
    half_width = HD // 2
    frequency = THETA ** (-jnp.arange(half_width, dtype=jnp.float32) * 2.0 / HD)
    angles = frequency[:, None] * positions_in.astype(jnp.float32)[None, :]
    return jnp.cos(angles), sign * jnp.sin(angles)


def rotate(values, tables):
    cosine, sine_part = tables
    heads = values.reshape(-1, HD, values.shape[-1])
    first_half = heads[:, : HD // 2]
    second_half = heads[:, HD // 2 :]
    return jnp.concatenate(
        [
            first_half * cosine - second_half * sine_part,
            second_half * cosine + first_half * sine_part,
        ],
        axis=1,
    ).reshape(values.shape)


def normalize(values):
    return values * lax.rsqrt(jnp.mean(values * values, axis=-1, keepdims=True) + EPSILON)


def norm_back(values, grad_in, gain_row):
    inv_scale = lax.rsqrt(jnp.mean(values * values, axis=-1, keepdims=True) + EPSILON)
    unit_rows = values * inv_scale
    grad_unit = grad_in * gain_row
    grad_values = inv_scale * (
        grad_unit - unit_rows * jnp.mean(grad_unit * unit_rows, axis=-1, keepdims=True)
    )
    return (grad_values, jnp.sum(grad_in * unit_rows, axis=0))


def matmul_n(left, right):
    return jnp.dot(left, right, preferred_element_type=jnp.float32)


def matmul_t(left, right):
    return lax.dot_general(
        left, right, (((1,), (1,)), ((), ())), preferred_element_type=jnp.float32
    )


def matmul_c(left, right):
    return lax.dot_general(
        left, right, (((0,), (0,)), ((), ())), preferred_element_type=jnp.float32
    )


def bit_groups():
    x_bits = lax.axis_size("x").bit_length() - 1
    ctx_bits = lax.axis_size("ctx").bit_length() - 1
    low_ctx = ctx_bits // 2
    along_x = [("x", bit) for bit in range(x_bits)]
    along_y = [("ctx", bit) for bit in range(low_ctx)]
    along_z = [("ctx", bit) for bit in range(low_ctx, ctx_bits)]
    return along_x, along_y, along_z


def swap_by(values, axis, offset):
    size = lax.axis_size(axis)
    return lax.ppermute(values, axis, [(i, i ^ offset) for i in range(size)])


def swap(values, where):
    return swap_by(values, where[0], 1 << where[1])


def add_low(left, right):
    return (left.astype(jnp.float32) + right.astype(jnp.float32)).astype(jnp.bfloat16)


def rel_offsets(order):
    strides = {"x": 2 * lax.axis_size("ctx"), "ctx": 1}
    offsets = np.zeros((1,), np.int64)
    for axis, bit in order:
        offsets = np.concatenate([offsets, offsets ^ (strides[axis] << bit)])
    return offsets


def lookup(slot, offsets):
    total = jnp.int32(0)
    for bit in range(len(offsets).bit_length() - 1):
        total = total + ((slot >> bit) & 1) * int(offsets[1 << bit])
    return total


def find(offset, offsets):
    total = jnp.int32(0)
    for bit in range(len(offsets).bit_length() - 1):
        place = int(offsets[1 << bit]).bit_length() - 1
        total = total + (((offset >> place) & 1) << bit)
    return total


def collect(values, order):
    kept, arrived = values, None
    for where in order:
        half = kept.shape[0] // 2
        if arrived is None:
            away, kept_next = kept[half:], kept[:half]
        else:
            away = add_low(kept[half:], arrived[half:])
            kept_next = add_low(kept[:half], arrived[:half])
        arrived = swap(away, where)
        kept = kept_next
    return kept[0].astype(jnp.float32) + arrived[0].astype(jnp.float32)


def scatter_whole(terms):
    ctx_count = lax.axis_size("ctx")
    count = 2 * lax.axis_size("x") * ctx_count
    along_x, along_y, along_z = bit_groups()
    core = ("core", 0)
    me = device_index().reshape(1)
    blocks, rows, width = terms[0].shape
    first = -(-rows // 48) * 16
    groups = [(0, first), (first, 2 * first), (2 * first, rows)]
    orders = [
        along_x + along_y + along_z,
        along_y + along_z + along_x,
        along_z + along_x + along_y,
    ]
    tables = [rel_offsets(list(reversed(order))) for order in orders]

    def target(step, me_ref, flip):
        return lookup(step, tables[0]) ^ me_ref[0] ^ flip

    def sources(flip):
        def chosen(member):
            def index(step, me_ref):
                spot = target(step, me_ref, flip)
                return (jnp.where(spot // blocks == member, spot % blocks, 0), 0, 0)

            return pl.BlockSpec((1, rows, width), index)

        return [chosen(member) for member in range(len(terms))]

    def pick_body(me_ref, *refs):
        held = target(pl.program_id(0), me_ref, ctx_count) // blocks
        for member in range(len(terms)):

            @pl.when(held == member)
            def _(member=member):
                refs[-1][...] = refs[member][...]

    away = pl.pallas_call(
        pick_body,
        grid_spec=pltpu.PrefetchScalarGridSpec(
            num_scalar_prefetch=1,
            grid=(count // 2,),
            in_specs=sources(ctx_count),
            out_specs=pl.BlockSpec((1, rows, width), lambda step, me_ref: (step, 0, 0)),
        ),
        out_shape=jax.ShapeDtypeStruct((count // 2, rows, width), jnp.bfloat16),
        compiler_params=pltpu.CompilerParams(vmem_limit_bytes=VMEM_BYTES),
    )(me, *terms)
    arrived = swap(away, core)

    def merge_body(me_ref, *refs):
        held = target(pl.program_id(0), me_ref, 0) // blocks
        for member in range(len(terms)):

            @pl.when(held == member)
            def _(member=member):
                for (low, high), out in zip(groups, refs[-3:]):
                    out[0] = add_low(refs[member][0, low:high], refs[-4][0, low:high])

    parts = pl.pallas_call(
        merge_body,
        grid_spec=pltpu.PrefetchScalarGridSpec(
            num_scalar_prefetch=1,
            grid=(count // 2,),
            in_specs=sources(0)
            + [pl.BlockSpec((1, rows, width), lambda step, me_ref: (step, 0, 0))],
            out_specs=[
                pl.BlockSpec(
                    (1, high - low, width),
                    lambda step, me_ref, table=table: (
                        find(lookup(step, tables[0]), table),
                        0,
                        0,
                    ),
                )
                for (low, high), table in zip(groups, tables)
            ],
        ),
        out_shape=[
            jax.ShapeDtypeStruct((count // 2, high - low, width), jnp.bfloat16)
            for low, high in groups
        ],
        compiler_params=pltpu.CompilerParams(vmem_limit_bytes=VMEM_BYTES),
    )(me, *terms, arrived)
    return jnp.concatenate([collect(part, order) for part, order in zip(parts, orders)], axis=0)


def device_index():
    return (
        (lax.axis_index("x") * 2 + lax.axis_index("core")) * lax.axis_size("ctx")
        + lax.axis_index("ctx")
    ).astype(jnp.int32)


def splits_rows(rows):
    along_x, along_y, along_z = bit_groups()
    return (len(along_x), len(along_y), len(along_z)) == (1, 1, 2) and rows % 64 == 0


def spread(values, order):
    values = values[None]
    for where in order:
        values = double(values, where)
    return values


def double(values, where):
    return jnp.concatenate([values, swap(values, where)], axis=0)


def ctx_orders():
    along_x, along_y, along_z = bit_groups()
    return [along_y + along_z, along_z + along_y]


def row_cuts(rows):
    first = -(-rows // 32) * 16
    return [(0, first), (first, rows)]


def slot_bits():
    along_x, along_y, along_z = bit_groups()
    return list(reversed(along_z)) + along_y


def total_low(*terms):
    total = terms[0].astype(jnp.float32)
    for term in terms[1:]:
        total = total + term.astype(jnp.float32)
    return total.astype(jnp.bfloat16)


def reduce_start(keep, away):
    come = swap(away, ("core", 0))
    quarter = keep.shape[2] // 2
    near, far = slice(0, quarter), slice(quarter, 2 * quarter)
    sends = [
        add_low(keep[4:, :, far], come[4:, :, far]),
        add_low(keep[:4, :, far], come[:4, :, far]),
    ]
    return sends, (keep[:, :, near], come[:, :, near])


def reduce_y(held, x_upper):
    return swap(total_low(*[part[4:] for part in held], x_upper), slot_bits()[2])


def reduce_near(rest):
    return swap(total_low(*[part[2:] for part in rest]), slot_bits()[1])


def reduce_far(rest):
    return swap(total_low(*[part[1] for part in rest]), slot_bits()[0])


def reduce_end(rest, z_far):
    total = z_far.astype(jnp.float32)
    for part in rest:
        total = total + part[0].astype(jnp.float32)
    return total


def reduce_halves(keep, away, ride):
    far_z, near_z, along_y = slot_bits()
    come = swap(away, ("core", 0))
    sums = []
    for (low, high), order in zip(
        row_cuts(keep.shape[1]), ([along_y, near_z, far_z], [near_z, far_z, along_y])
    ):
        shape = (2, 2, 2, high - low, keep.shape[2])
        terms = [keep[:, low:high].reshape(shape), come[:, low:high].reshape(shape)]
        left = [along_y, near_z, far_z]
        for where in order:
            dim = left.index(where)
            left.remove(where)
            sent = total_low(*[lax.index_in_dim(term, 1, dim, False) for term in terms])
            if low == 0:
                arrived, ride = swap_with(sent, ride, where)
            else:
                arrived = swap(sent, where)
            terms = [lax.index_in_dim(term, 0, dim, False) for term in terms] + [arrived]
        total = terms[0].astype(jnp.float32)
        for term in terms[1:]:
            total = total + term.astype(jnp.float32)
        sums.append(total)
    return jnp.concatenate(sums, axis=0), ride


def ride_parts(ride):
    rounded = lax.reduce_precision(ride, 8, 7)
    return rounded, lax.reduce_precision(ride - rounded, 8, 7)


def with_ride(sent, parts):
    extra = jnp.concatenate([*parts, jnp.zeros((12, parts[0].shape[1]), jnp.float32)])
    return jnp.concatenate([sent.reshape(-1, sent.shape[-1]), extra.astype(jnp.bfloat16)], axis=0)


def swap_with(sent, ride, where):
    parts = ride_parts(ride)
    come, other = off_ride(swap(with_ride(sent, parts), where), sent.shape)
    return come, (parts[0] + parts[1]) + other


def off_ride(come, shape):
    parts = come[-16:].astype(jnp.float32)
    return come[:-16].reshape(shape), parts[0:2] + parts[2:4]


def gather_halves(weights):
    rows = weights.shape[0]
    x_index, core = lax.axis_index("x"), lax.axis_index("core")
    half = rows // 2
    far = swap(weights, ("x", 0))
    low = jnp.where(x_index == 0, weights, far)
    high = jnp.where(x_index == 0, far, weights)
    both = jnp.stack([low, high])
    keep = jnp.where(core == 0, both[:, :half], both[:, half:])
    come = swap(jnp.where(core == 0, both[:, half:], both[:, :half]), ("core", 0))
    first = jnp.where(core == 0, keep, come)
    second = jnp.where(core == 0, come, keep)
    feed = jnp.stack([second[0], first[1], second[1]])
    return first[0], jnp.where(x_index == 0, feed[:, : half // 2], feed[:, half // 2 :])


def place_rows(own, far):
    tables = [rel_offsets(list(reversed(order))) for order in ctx_orders()]
    slots, width = own[0].shape[0], own[0].shape[2]
    lengths = [part.shape[1] for part in own]
    half = sum(lengths)

    def body(me_ref, *refs):
        out_ref = refs[-1]
        for core in range(2):

            @pl.when(me_ref[0] == core)
            def _(core=core):
                for source, base in ((0, core * half), (2, (1 - core) * half)):
                    out_ref[0, base : base + lengths[0]] = refs[source][0]
                    out_ref[0, base + lengths[0] : base + half] = refs[source + 1][0]

    specs = [
        pl.BlockSpec(
            (1, length, width),
            lambda step, me_ref, table=table: (find(step ^ me_ref[1], table), 0, 0),
        )
        for length, table in zip(lengths, tables)
    ]
    me = jnp.stack([lax.axis_index("core"), lax.axis_index("ctx")]).astype(jnp.int32)
    return pl.pallas_call(
        body,
        grid_spec=pltpu.PrefetchScalarGridSpec(
            num_scalar_prefetch=1,
            grid=(slots,),
            in_specs=specs * 2,
            out_specs=pl.BlockSpec((1, 2 * half, width), lambda step, me_ref: (step, 0, 0)),
        ),
        out_shape=jax.ShapeDtypeStruct((slots, 2 * half, width), own[0].dtype),
        cost_estimate=pl.CostEstimate(
            flops=0, bytes_accessed=8 * slots * half * width, transcendentals=0
        ),
        compiler_params=pltpu.CompilerParams(vmem_limit_bytes=VMEM_BYTES),
    )(me, *own, *far).reshape(slots * 2 * half, width)


def turned(values):
    return jnp.transpose(values)


def load_packed(ref, aligned):
    if not aligned:
        return ref[0, 0]
    half = ref.shape[1] // 2
    return jnp.concatenate(
        [
            ref[head * HD : (head + 1) * HD, side * half : (side + 1) * half]
            for side in range(2)
            for head in range(GROUP)
        ],
        axis=1,
    )


def store_packed(ref, values, aligned):
    if not aligned:
        ref[0, 0] = values
        return
    half = ref.shape[1] // 2
    for side in range(2):
        for head in range(GROUP):
            start = (side * GROUP + head) * half
            ref[head * HD : (head + 1) * HD, side * half : (side + 1) * half] = values[
                :, start : start + half
            ]


def load_tile(refs, side, tile):
    length = refs[0].shape[1] // 2
    if length >= KEY_TILE:
        start = side * length + tile * KEY_TILE
        return refs[0][:, start : start + KEY_TILE]
    many = KEY_TILE // length
    return jnp.concatenate(
        [
            ref[:, side * length : (side + 1) * length]
            for ref in refs[tile * many : (tile + 1) * many]
        ],
        axis=1,
    )


def attend_body(count, aligned, queries_ref, key_pos_ref, query_pos_ref, *refs):
    key_refs, value_refs = refs[:count], refs[count : 2 * count]
    out_ref, total_ref, work = refs[2 * count :]
    queries = load_packed(queries_ref, aligned)
    low_cols = queries.shape[1] // 2
    queries_high = queries[:, low_cols:]
    tiles = key_pos_ref.shape[1] // KEY_TILE
    largest = jnp.full((1, queries.shape[1]), HIDDEN, jnp.float32)
    largest_high = jnp.full((1, low_cols), HIDDEN, jnp.float32)
    for side in range(2):
        for tile in range(tiles):
            keys = turned(load_tile(key_refs, side, tile))
            row = (side * tiles + tile) * KEY_TILE
            key_places = key_pos_ref[side, tile * KEY_TILE : (tile + 1) * KEY_TILE]
            if side == 0:
                scores = matmul_n(keys, queries)
                scores = jnp.where(key_places <= query_pos_ref[...], scores, HIDDEN)
                work[row : row + KEY_TILE] = scores
                largest = jnp.maximum(largest, jnp.max(scores, axis=0, keepdims=True))
            else:
                scores = matmul_n(keys, queries_high)
                scores = jnp.where(key_places <= query_pos_ref[:, low_cols:], scores, HIDDEN)
                work[row : row + KEY_TILE, low_cols:] = scores
                largest_high = jnp.maximum(largest_high, jnp.max(scores, axis=0, keepdims=True))
    high_max = jnp.maximum(largest[:, low_cols:], largest_high)
    largest = jnp.concatenate([largest[:, :low_cols], high_max], axis=1)
    total = jnp.zeros_like(largest)
    mixed = jnp.zeros((HD, queries.shape[1]), jnp.float32)
    total_high = jnp.zeros_like(largest_high)
    mixed_high = jnp.zeros((HD, low_cols), jnp.float32)
    for side in range(2):
        for tile in range(tiles):
            values = load_tile(value_refs, side, tile)
            row = (side * tiles + tile) * KEY_TILE
            if side == 0:
                expos = jnp.exp(work[row : row + KEY_TILE] - largest)
                total = total + jnp.sum(expos, axis=0, keepdims=True)
                mixed = mixed + matmul_n(values, expos.astype(jnp.bfloat16))
            else:
                expos = jnp.exp(work[row : row + KEY_TILE, low_cols:] - high_max)
                total_high = total_high + jnp.sum(expos, axis=0, keepdims=True)
                mixed_high = mixed_high + matmul_n(values, expos.astype(jnp.bfloat16))
    total = jnp.concatenate([total[:, :low_cols], total[:, low_cols:] + total_high], axis=1)
    mixed = jnp.concatenate([mixed[:, :low_cols], mixed[:, low_cols:] + mixed_high], axis=1)
    store_packed(out_ref, (mixed / total).astype(jnp.bfloat16), aligned)
    total_ref[0, 0] = largest + jnp.log(total)


def attend_back_body(
    count, aligned, queries_ref, key_pos_ref, query_pos_ref, *refs
):
    key_refs, value_refs = refs[:count], refs[count : 2 * count]
    out_ref, total_ref, d_out_ref, cosine_ref, sine_ref = refs[2 * count : 2 * count + 5]
    d_queries_ref, pair_refs = refs[2 * count + 5], refs[2 * count + 6 :]
    all_queries, all_d_out = load_packed(queries_ref, aligned), load_packed(d_out_ref, aligned)
    low_cols = all_queries.shape[1] // 2
    tiles = key_pos_ref.shape[1] // KEY_TILE
    delta = jnp.sum(
        all_d_out.astype(jnp.float32) * load_packed(out_ref, aligned).astype(jnp.float32),
        axis=0,
        keepdims=True,
    )
    totals = total_ref[0, 0]
    parts = []
    for side in range(2):
        if side == 0:
            queries, d_out = all_queries, all_d_out
            query_places, log_total, row_delta = query_pos_ref[...], totals, delta
        else:
            queries, d_out = all_queries[:, low_cols:], all_d_out[:, low_cols:]
            query_places = query_pos_ref[:, low_cols:]
            log_total, row_delta = totals[:, low_cols:], delta[:, low_cols:]
        part = jnp.zeros((HD, queries.shape[1]), jnp.float32)
        for tile in range(tiles):
            keys_flat = load_tile(key_refs, side, tile)
            scores = matmul_n(turned(keys_flat), queries)
            seen = key_pos_ref[side, tile * KEY_TILE : (tile + 1) * KEY_TILE] <= query_places
            probs = jnp.where(seen, jnp.exp(scores - log_total), 0.0)
            d_probs = matmul_n(turned(load_tile(value_refs, side, tile)), d_out)
            d_scores = (probs * (d_probs - row_delta)).astype(jnp.bfloat16)
            part = part + matmul_n(keys_flat, d_scores)
            d_key = matmul_t(d_scores, queries).astype(jnp.bfloat16)
            d_value = matmul_t(probs.astype(jnp.bfloat16), d_out).astype(jnp.bfloat16)
            if aligned:
                length = key_refs[0].shape[1] // 2
                places_out = [(ref, slot) for ref in pair_refs for slot in range(ref.shape[0])]
                for piece in range(KEY_TILE // length):
                    ref, slot = places_out[tile * (KEY_TILE // length) + piece]
                    rows = slice(piece * length, (piece + 1) * length)
                    ref[slot, 0, side, :, :HD] = d_key[rows]
                    ref[slot, 0, side, :, HD:] = d_value[rows]
            else:
                rows = slice(tile * KEY_TILE, (tile + 1) * KEY_TILE)
                pair_refs[0][side, 0, rows, :HD] = d_key
                pair_refs[0][side, 0, rows, HD:] = d_value
        parts.append(part)
    d_queries = jnp.concatenate(
        [parts[0][:, :low_cols], parts[0][:, low_cols:] + parts[1]], axis=1
    )
    cosine, sine_part = cosine_ref[...], sine_ref[...]
    first_half, second_half = d_queries[: HD // 2], d_queries[HD // 2 :]
    turned_back = jnp.concatenate(
        [
            first_half * cosine + second_half * sine_part,
            second_half * cosine - first_half * sine_part,
        ],
        axis=0,
    )
    store_packed(d_queries_ref, (turned_back * SCALE_QK).astype(jnp.bfloat16), aligned)


def own_mask(rows, cols):
    return lax.broadcasted_iota(jnp.int32, (rows, cols), 0) <= (
        lax.broadcasted_iota(jnp.int32, (rows, cols), 1) % rows
    )


def slot_keys(ref, length):
    both = turned(ref[...])
    return both[:length], both[length:]


def attend_slots_body(count, flags_ref, queries_ref, *refs):
    key_refs, value_refs = refs[:count], refs[count : 2 * count]
    out_ref, total_ref, both_queries, work, largest, totals, mixed = refs[2 * count :]
    length = key_refs[0].shape[1] // 2
    cols = GROUP * length
    packed = load_packed(queries_ref, True)
    for side in range(2):
        both_queries[side] = packed[:, side * cols : (side + 1) * cols]
    visible = own_mask(length, cols)
    low_keys, high_keys = zip(*[slot_keys(ref, length) for ref in key_refs])
    row = 0

    def keep_scores(scores, row):
        work[row : row + scores.shape[0]] = scores
        return jnp.max(scores, axis=0, keepdims=True)

    for side, keys in ((0, low_keys[0]), (1, high_keys[0])):
        scores = jnp.where(visible, matmul_n(keys, both_queries[side]), HIDDEN)
        largest[side] = keep_scores(scores, row)
        row += length
    for slot in range(0, count, 2):
        keys = jnp.concatenate([low_keys[slot], low_keys[slot + 1]], axis=0)
        top = keep_scores(matmul_n(keys, both_queries[1]), row)
        largest[1] = jnp.maximum(largest[1], top)
        row += 2 * length
    for slot in range(1, count):
        side = flags_ref[slot]
        keys = jnp.where(side == 0, low_keys[slot], high_keys[slot])
        top = keep_scores(matmul_n(keys, both_queries[side]), row)
        largest[side] = jnp.maximum(largest[side], top)
        row += length
    row = 0
    for side in range(2):
        values = value_refs[0][:, side * length : (side + 1) * length]
        expos = jnp.exp(work[row : row + length] - largest[side])
        totals[side] = jnp.sum(expos, axis=0, keepdims=True)
        mixed[side] = matmul_n(values, expos.astype(jnp.bfloat16))
        row += length
    for slot in range(0, count, 2):
        values = jnp.concatenate(
            [value_refs[slot][:, :length], value_refs[slot + 1][:, :length]], axis=1
        )
        expos = jnp.exp(work[row : row + 2 * length] - largest[1])
        totals[1] += jnp.sum(expos, axis=0, keepdims=True)
        mixed[1] += matmul_n(values, expos.astype(jnp.bfloat16))
        row += 2 * length
    for slot in range(1, count):
        side = flags_ref[slot]
        values = jnp.where(side == 0, value_refs[slot][:, :length], value_refs[slot][:, length:])
        expos = jnp.exp(work[row : row + length] - largest[side])
        totals[side] += jnp.sum(expos, axis=0, keepdims=True)
        mixed[side] += matmul_n(values, expos.astype(jnp.bfloat16))
        row += length
    result = [(mixed[side] / totals[side]).astype(jnp.bfloat16) for side in range(2)]
    store_packed(out_ref, jnp.concatenate(result, axis=1), True)
    logs = [largest[side] + jnp.log(totals[side]) for side in range(2)]
    total_ref[0, 0] = jnp.concatenate(logs, axis=1)


def attend_slots_back_body(count, flags_ref, queries_ref, *refs):
    key_refs, value_refs = refs[:count], refs[count : 2 * count]
    out_ref, total_ref, d_out_ref, cosine_ref, sine_ref = refs[2 * count : 2 * count + 5]
    d_queries_ref = refs[2 * count + 5]
    pair_refs = refs[2 * count + 6 : -5]
    both_queries, both_d_out, log_totals, deltas, sums = refs[-5:]
    length = key_refs[0].shape[1] // 2
    cols = GROUP * length
    queries, d_out = load_packed(queries_ref, True), load_packed(d_out_ref, True)
    delta = jnp.sum(
        d_out.astype(jnp.float32) * load_packed(out_ref, True).astype(jnp.float32),
        axis=0,
        keepdims=True,
    )
    for side in range(2):
        part = slice(side * cols, (side + 1) * cols)
        both_queries[side] = queries[:, part]
        both_d_out[side] = d_out[:, part]
        log_totals[side] = total_ref[0, 0, :, part]
        deltas[side] = delta[:, part]
    sums[...] = jnp.zeros_like(sums)
    visible = own_mask(length, cols)
    low_keys, high_keys = zip(*[slot_keys(ref, length) for ref in key_refs])
    low_values, high_values = zip(*[slot_keys(ref, length) for ref in value_refs])
    places_out = [(ref, slot) for ref in pair_refs for slot in range(ref.shape[0])]

    def block(keys, keys_flat, values, side, mask=None):
        probs = jnp.exp(matmul_n(keys, both_queries[side]) - log_totals[side])
        if mask is not None:
            probs = jnp.where(mask, probs, 0.0)
        d_probs = matmul_n(values, both_d_out[side])
        d_scores = (probs * (d_probs - deltas[side])).astype(jnp.bfloat16)
        sums[side] += matmul_n(keys_flat, d_scores)
        return jnp.concatenate(
            [
                matmul_t(d_scores, both_queries[side]),
                matmul_t(probs.astype(jnp.bfloat16), both_d_out[side]),
            ],
            axis=1,
        )

    low_terms = []
    for slot in range(0, count, 2):
        keys, values = [
            jnp.concatenate([part[slot], part[slot + 1]], axis=0) for part in (low_keys, low_values)
        ]
        flat = jnp.concatenate([key_refs[slot][:, :length], key_refs[slot + 1][:, :length]], axis=1)
        terms = block(keys, flat, values, 1)
        low_terms += [terms[:length], terms[length:]]
    ref, slot = places_out[0]
    own = [
        block(keys, key_refs[0][:, side * length : (side + 1) * length], values, side, visible)
        for side, (keys, values) in enumerate(
            ((low_keys[0], low_values[0]), (high_keys[0], high_values[0]))
        )
    ]
    ref[slot, 0, 0] = (low_terms[0] + own[0]).astype(jnp.bfloat16)
    ref[slot, 0, 1] = own[1].astype(jnp.bfloat16)
    for member in range(1, count):
        side = flags_ref[member]
        low = side == 0
        keys = jnp.where(low, low_keys[member], high_keys[member])
        flat = jnp.where(low, key_refs[member][:, :length], key_refs[member][:, length:])
        values = jnp.where(low, low_values[member], high_values[member])
        terms = block(keys, flat, values, side)
        ref, slot = places_out[member]
        ref[slot, 0, 0] = (low_terms[member] + jnp.where(low, terms, 0.0)).astype(jnp.bfloat16)
        ref[slot, 0, 1] = jnp.where(low, 0.0, terms).astype(jnp.bfloat16)
    d_queries = jnp.concatenate([sums[0], sums[1]], axis=1)
    store_packed(d_queries_ref, turn_queries_back(d_queries, cosine_ref, sine_ref), True)


def turn_queries_back(d_queries, cosine_ref, sine_ref):
    cosine, sine_part = cosine_ref[...], sine_ref[...]
    first_half, second_half = d_queries[: HD // 2], d_queries[HD // 2 :]
    turned_back = jnp.concatenate(
        [
            first_half * cosine + second_half * sine_part,
            second_half * cosine - first_half * sine_part,
        ],
        axis=0,
    )
    return (turned_back * SCALE_QK).astype(jnp.bfloat16)


def slot_specs(leads, local_rows, seq):
    specs = [
        pl.BlockSpec(memory_space=pltpu.SMEM),
        pl.BlockSpec((GROUP * HD, local_rows), lambda head: (head, seq)),
    ]
    for first in (0, KV):
        specs += [
            pl.BlockSpec(
                (None, HD, local_rows),
                lambda head, lead=lead, first=first: (lead, first + head, seq),
            )
            for lead in leads
        ]
    return specs


def attend_slots(queries, pairs, flags, local_rows, seq):
    count, cols = len(pairs), GROUP * local_rows // 2
    leads, arrays = [lead for _, lead in pairs], [array for array, _ in pairs]
    work = HEADS * local_rows * local_rows * count // 2
    return pl.pallas_call(
        lambda *refs: attend_slots_body(count, *refs),
        grid=(KV,),
        in_specs=slot_specs(leads, local_rows, seq),
        out_specs=[
            pl.BlockSpec((GROUP * HD, local_rows), lambda head: (head, 0)),
            pl.BlockSpec((1, 1, 1, 2 * cols), lambda head: (0, head, 0, 0)),
        ],
        out_shape=[
            jax.ShapeDtypeStruct((HEADS * HD, local_rows), jnp.bfloat16),
            jax.ShapeDtypeStruct((1, KV, 1, 2 * cols), jnp.float32),
        ],
        scratch_shapes=[
            pltpu.VMEM((2, HD, cols), jnp.bfloat16),
            pltpu.VMEM(((2 * count + 1) * local_rows // 2, cols), jnp.float32),
            pltpu.VMEM((2, 1, cols), jnp.float32),
            pltpu.VMEM((2, 1, cols), jnp.float32),
            pltpu.VMEM((2, HD, cols), jnp.float32),
        ],
        cost_estimate=pl.CostEstimate(
            flops=work * HD, bytes_accessed=1024 * 1024, transcendentals=0
        ),
        compiler_params=pltpu.CompilerParams(vmem_limit_bytes=VMEM_BYTES),
    )(flags, queries, *arrays, *arrays)


def attend_slots_back(
    queries, pairs, flags, mixed, log_total, d_mixed, tables, local_rows, seq, sets
):
    count, cols = len(pairs), GROUP * local_rows // 2
    leads, arrays = [lead for _, lead in pairs], [array for array, _ in pairs]
    work = HEADS * local_rows * local_rows * count // 2
    own = pl.BlockSpec((GROUP * HD, local_rows), lambda head: (head, 0))
    table_spec = pl.BlockSpec((HD // 2, 2 * cols), lambda head: (0, 0))
    length = local_rows // 2
    return pl.pallas_call(
        lambda *refs: attend_slots_back_body(count, *refs),
        grid=(KV,),
        in_specs=slot_specs(leads, local_rows, seq)
        + [
            own,
            pl.BlockSpec((1, 1, 1, 2 * cols), lambda head: (0, head, 0, 0)),
            pl.BlockSpec((GROUP * HD, local_rows), lambda head: (head, seq)),
            table_spec,
            table_spec,
        ],
        out_specs=[own]
        + [
            pl.BlockSpec((slots, 1, 2, length, 2 * HD), lambda head: (0, head, 0, 0, 0))
            for slots in sets
        ],
        out_shape=[jax.ShapeDtypeStruct((HEADS * HD, local_rows), jnp.bfloat16)]
        + [jax.ShapeDtypeStruct((slots, KV, 2, length, 2 * HD), jnp.bfloat16) for slots in sets],
        scratch_shapes=[
            pltpu.VMEM((2, HD, cols), jnp.bfloat16),
            pltpu.VMEM((2, HD, cols), jnp.bfloat16),
            pltpu.VMEM((2, 1, cols), jnp.float32),
            pltpu.VMEM((2, 1, cols), jnp.float32),
            pltpu.VMEM((2, HD, cols), jnp.float32),
        ],
        cost_estimate=pl.CostEstimate(
            flops=work * HD, bytes_accessed=1024 * 1024, transcendentals=0
        ),
        compiler_params=pltpu.CompilerParams(vmem_limit_bytes=VMEM_BYTES),
    )(flags, queries, *arrays, *arrays, mixed, log_total, d_mixed, *tables)


def head_specs(leads, aligned, cols, keys, local_rows, seq):
    count = len(leads)
    if aligned:
        packed = pl.BlockSpec((GROUP * HD, local_rows), lambda head: (head, seq))
    else:
        packed = pl.BlockSpec((1, 1, HD, cols), lambda head: (seq, head, 0, 0))
    specs = [
        packed,
        pl.BlockSpec((2, keys, 1), lambda head: (0, 0, 0)),
        pl.BlockSpec((1, cols), lambda head: (0, 0)),
    ]
    for first in (0, KV):
        specs += [
            pl.BlockSpec(
                (None, HD, 2 * keys // count),
                lambda head, lead=lead, first=first: (lead, first + head, seq),
            )
            for lead in leads
        ]
    return packed, specs


def attend(queries, pairs, key_pos, query_pos, local_rows, seq):
    aligned = queries.ndim == 2
    cols, keys, count = query_pos.shape[1], key_pos.shape[1], len(pairs)
    leads, arrays = [lead for _, lead in pairs], [array for array, _ in pairs]
    _, specs = head_specs(leads, aligned, cols, keys, local_rows, seq)
    work = HEADS * keys * cols // GROUP * 3 // 2
    if aligned:
        out_spec = pl.BlockSpec((GROUP * HD, local_rows), lambda head: (head, 0))
        out_shape = jax.ShapeDtypeStruct((HEADS * HD, local_rows), jnp.bfloat16)
    else:
        out_spec = pl.BlockSpec((1, 1, HD, cols), lambda head: (0, head, 0, 0))
        out_shape = jax.ShapeDtypeStruct((1, KV, HD, cols), jnp.bfloat16)
    return pl.pallas_call(
        lambda *refs: attend_body(count, aligned, *refs),
        grid=(KV,),
        in_specs=specs,
        out_specs=[out_spec, pl.BlockSpec((1, 1, 1, cols), lambda head: (0, head, 0, 0))],
        out_shape=[out_shape, jax.ShapeDtypeStruct((1, KV, 1, cols), jnp.float32)],
        scratch_shapes=[pltpu.VMEM((2 * keys, cols), jnp.float32)],
        cost_estimate=pl.CostEstimate(
            flops=work * HD, bytes_accessed=1024 * 1024, transcendentals=0
        ),
        compiler_params=pltpu.CompilerParams(vmem_limit_bytes=VMEM_BYTES),
    )(queries, key_pos, query_pos, *arrays, *arrays)


def attend_back(
    queries, pairs, key_pos, query_pos, mixed, log_total, d_mixed, tables, local_rows, seq, sets
):
    aligned = queries.ndim == 2
    cols, keys, count = query_pos.shape[1], key_pos.shape[1], len(pairs)
    leads, arrays = [lead for _, lead in pairs], [array for array, _ in pairs]
    packed, specs = head_specs(leads, aligned, cols, keys, local_rows, seq)
    work = HEADS * keys * cols // GROUP * 3 // 2
    if aligned:
        own = pl.BlockSpec((GROUP * HD, local_rows), lambda head: (head, 0))
        own_shape = jax.ShapeDtypeStruct((HEADS * HD, local_rows), jnp.bfloat16)
        length = keys // count
        pair_specs = [
            pl.BlockSpec((slots, 1, 2, length, 2 * HD), lambda head: (0, head, 0, 0, 0))
            for slots in sets
        ]
        pair_shapes = [
            jax.ShapeDtypeStruct((slots, KV, 2, length, 2 * HD), jnp.bfloat16) for slots in sets
        ]
    else:
        own = pl.BlockSpec((1, 1, HD, cols), lambda head: (0, head, 0, 0))
        own_shape = jax.ShapeDtypeStruct((1, KV, HD, cols), jnp.bfloat16)
        pair_specs = [pl.BlockSpec((2, 1, keys, 2 * HD), lambda head: (0, head, 0, 0))]
        pair_shapes = [jax.ShapeDtypeStruct((2, KV, keys, 2 * HD), jnp.bfloat16)]
    table_spec = pl.BlockSpec((HD // 2, cols), lambda head: (0, 0))
    return pl.pallas_call(
        lambda *refs: attend_back_body(count, aligned, *refs),
        grid=(KV,),
        in_specs=specs
        + [
            own,
            pl.BlockSpec((1, 1, 1, cols), lambda head: (0, head, 0, 0)),
            packed,
            table_spec,
            table_spec,
        ],
        out_specs=[own] + pair_specs,
        out_shape=[own_shape] + pair_shapes,
        cost_estimate=pl.CostEstimate(
            flops=work * HD, bytes_accessed=1024 * 1024, transcendentals=0
        ),
        compiler_params=pltpu.CompilerParams(vmem_limit_bytes=VMEM_BYTES),
    )(queries, key_pos, query_pos, *arrays, *arrays, mixed, log_total, d_mixed, *tables)


def put_rows(values, keep_ref, away_ref, member, core, x_index):
    quarter = values.shape[0] // 4
    for mine in range(4):

        @pl.when(2 * core + x_index == mine)
        def _(mine=mine):
            for ref, side in ((keep_ref, mine // 2), (away_ref, 1 - mine // 2)):
                for place, along_x in enumerate((mine % 2, 1 - mine % 2)):
                    start = (2 * side + along_x) * quarter
                    ref[0, member, place * quarter : (place + 1) * quarter] = values[
                        start : start + quarter
                    ]


def feed_body(
    parts, split, me_ref, a_two_ref, dy_ref, *refs
):
    count = 4 if split else 6
    weight_refs, (out_ref, d_two_ref), grad_refs = (
        refs[:count],
        refs[count : count + 2],
        refs[count + 2 :],
    )
    core, x_index = me_ref[0], me_ref[1]
    step = pl.program_id(0)

    @pl.when(step == 0)
    def _():
        out_ref[...] = jnp.zeros_like(out_ref)
        d_two_ref[...] = jnp.zeros_like(d_two_ref)

    def rows_of(member):
        if split:
            parts_here = [ref[0, member] for ref in weight_refs]
            rows_out = []
            for side in range(2):
                for along_x in range(2):
                    near = jnp.where(x_index == along_x, parts_here[0], parts_here[1])
                    far = jnp.where(x_index == along_x, parts_here[2], parts_here[3])
                    rows_out.append(jnp.where(core == side, near, far))
            return jnp.concatenate(rows_out, axis=0)
        wanted = feed_core(member, step, parts)
        return jnp.where(wanted == core, weight_refs[2 * member][0], weight_refs[2 * member + 1][0])

    a_two, dy_low = a_two_ref[...], dy_ref[...]
    gate_rows, up_rows, down_rows = rows_of(0), rows_of(1), rows_of(2)
    gate_pre = matmul_t(gate_rows, a_two)
    up_pre = matmul_t(up_rows, a_two)
    d_hidden = matmul_t(down_rows, dy_low)
    sigma = jax.nn.sigmoid(gate_pre)
    gate_act = gate_pre * sigma
    hidden = (gate_act * up_pre).astype(jnp.bfloat16)
    d_gate = (d_hidden * up_pre * sigma * (1.0 + gate_pre * (1.0 - sigma))).astype(jnp.bfloat16)
    d_up = (d_hidden * gate_act).astype(jnp.bfloat16)
    out_ref[...] += matmul_c(hidden, down_rows)
    d_two_ref[...] += matmul_c(d_gate, gate_rows) + matmul_c(d_up, up_rows)
    for member, (left, right) in enumerate(((d_gate, a_two), (d_up, a_two), (hidden, dy_low))):
        grad = matmul_n(left, right).astype(jnp.bfloat16)
        if split:
            put_rows(grad, grad_refs[0], grad_refs[1], member, core, x_index)
        else:
            grad_refs[member][0] = grad


def feed_core(member, step, parts):
    ctx_count, single = parts
    return (member + 1) % 2 if single else step // ctx_count


def feed_forward(a_two, dy_low, mine, far, rows):
    tokens, width = a_two.shape
    ctx_count = lax.axis_size("ctx")
    blocks = FF // rows
    single = blocks == ctx_count
    split = splits_rows(rows)
    parts = (ctx_count, single)
    whole = pl.BlockSpec((tokens, width), lambda step, me_ref: (0, 0))

    def weight_spec(member, own):
        first = (member + 1) * blocks // ctx_count // 2 * ctx_count

        def index(step, me_ref):
            matches = (feed_core(member, step, parts) == me_ref[0]) == own
            return (first + jnp.where(matches, step % ctx_count, 0), 0, 0)

        return pl.BlockSpec((1, rows, width), index)

    if split:
        weight_specs = [
            pl.BlockSpec((1, 3, rows // 4, width), lambda step, me_ref: (step, 0, 0, 0))
        ] * 4
        weight_args = [*mine, *far]
        half = pl.BlockSpec((1, 3, rows // 2, width), lambda step, me_ref: (step, 0, 0, 0))
        grad_specs = [half, half]
        grad_shapes = [jax.ShapeDtypeStruct((blocks, 3, rows // 2, width), jnp.bfloat16)] * 2
    else:
        weight_specs = [weight_spec(member, own) for member in range(3) for own in (True, False)]
        weight_args = [mine, far] * 3
        grad_specs = [pl.BlockSpec((1, rows, width), lambda step, me_ref: (step, 0, 0))] * 3
        grad_shapes = [jax.ShapeDtypeStruct((blocks, rows, width), jnp.bfloat16)] * 3
    me = jnp.stack([lax.axis_index("core"), lax.axis_index("x")]).astype(jnp.int32)
    return pl.pallas_call(
        lambda *refs: feed_body(parts, split, *refs),
        grid_spec=pltpu.PrefetchScalarGridSpec(
            num_scalar_prefetch=1,
            grid=(blocks,),
            in_specs=[whole, whole] + weight_specs,
            out_specs=[whole, whole] + grad_specs,
        ),
        out_shape=[jax.ShapeDtypeStruct((tokens, width), jnp.float32)] * 2 + grad_shapes,
        cost_estimate=pl.CostEstimate(
            flops=18 * tokens * width * FF, bytes_accessed=12 * FF * width, transcendentals=FF * tokens
        ),
        compiler_params=pltpu.CompilerParams(vmem_limit_bytes=VMEM_BYTES),
    )(me, a_two, dy_low, *weight_args)


def first_grads(d_qkv, attn_low, a_one, d_resid_low, rows):
    tokens, width = a_one.shape
    split = splits_rows(rows)
    early = d_qkv.shape[0] // rows
    blocks = early + attn_low.shape[0] // rows

    def body(me_ref, qkv_ref, attn_ref, one_ref, resid_ref, *grad_refs):
        first = pl.program_id(0) < early
        left = jnp.where(first, qkv_ref[...], attn_ref[...])
        right = jnp.where(first, one_ref[...], resid_ref[...])
        grad = matmul_n(left, right).astype(jnp.bfloat16)
        if split:
            put_rows(grad, grad_refs[0], grad_refs[1], 0, me_ref[0], 0)
        else:
            grad_refs[0][0] = grad

    whole = pl.BlockSpec((tokens, width), lambda step, me_ref: (0, 0))
    if split:
        table = rel_offsets(slot_bits())
        half = pl.BlockSpec(
            (1, 1, rows // 2, width), lambda step, me_ref: (find(step ^ me_ref[1], table), 0, 0, 0)
        )
        grad_specs = [half, half]
        grad_shapes = [jax.ShapeDtypeStruct((blocks, 1, rows // 2, width), jnp.bfloat16)] * 2
    else:
        grad_specs = [pl.BlockSpec((1, rows, width), lambda step, me_ref: (step, 0, 0))]
        grad_shapes = [jax.ShapeDtypeStruct((blocks, rows, width), jnp.bfloat16)]
    me = jnp.stack([lax.axis_index(name) for name in ("core", "ctx")]).astype(jnp.int32)
    return pl.pallas_call(
        body,
        grid_spec=pltpu.PrefetchScalarGridSpec(
            num_scalar_prefetch=1,
            grid=(blocks,),
            in_specs=[
                pl.BlockSpec((rows, tokens), lambda step, me_ref: (jnp.minimum(step, early - 1), 0)),
                pl.BlockSpec((rows, tokens), lambda step, me_ref: (jnp.maximum(step - early, 0), 0)),
                whole,
                whole,
            ],
            out_specs=grad_specs,
        ),
        out_shape=grad_shapes,
        cost_estimate=pl.CostEstimate(
            flops=2 * tokens * width * blocks * rows, bytes_accessed=2 * blocks * rows * width, transcendentals=0
        ),
        compiler_params=pltpu.CompilerParams(vmem_limit_bytes=VMEM_BYTES),
    )(me, d_qkv, attn_low, a_one, d_resid_low)


def adam_update(param, grad, first, second, rate, decay, step_number):
    first_new = BETA_ONE * first + (1.0 - BETA_ONE) * grad
    second_new = BETA_TWO * second + (1.0 - BETA_TWO) * grad * grad
    fix_one = 1.0 - BETA_ONE**step_number
    fix_two = 1.0 - BETA_TWO**step_number
    update = first_new / fix_one / (jnp.sqrt(second_new / fix_two) + ADAM_EPS)
    return (first_new, second_new, param - rate * (update + decay * param))


def shards(inputs, cotangent, weights, gains, first_moment, second_moment, gain_first, gain_second):
    ctx_count = lax.axis_size("ctx")
    x_count = lax.axis_size("x")
    ctx_index, core, x_index = lax.axis_index("ctx"), lax.axis_index("core"), lax.axis_index("x")
    seqs, local_rows, model_width = inputs.shape
    half_rows = local_rows // 2
    tokens = seqs * local_rows
    weight_rows = weights.shape[0]
    q_cols = HEADS * HD
    kv_cols = KV * HD
    cut_o = q_cols + 2 * kv_cols
    split = splits_rows(weight_rows)
    slots = slot_bits()
    aligned = split and half_rows % 128 == 0
    local_index = jnp.arange(local_rows, dtype=jnp.int32)
    pos_here = places(ctx_index * local_rows + local_index, local_rows, ctx_count)
    cosine, sine_part = angle_tables(pos_here, 1.0)
    turn = (jnp.tile(cosine, (1, seqs)), jnp.tile(sine_part, (1, seqs)))
    turn_back = (turn[0], -turn[1])

    def pack(flat):
        if aligned:
            return flat
        return (
            flat.reshape(KV, GROUP, HD, -1, 2, half_rows)
            .transpose(3, 0, 2, 4, 1, 5)
            .reshape(-1, KV, HD, 2 * GROUP * half_rows)
        )

    def unpack(packed):
        if aligned:
            return packed
        return (
            packed.reshape(KV, HD, 2, GROUP, half_rows)
            .transpose(0, 3, 1, 2, 4)
            .reshape(q_cols, local_rows)
        )

    def by_columns(row):
        rows = row.shape[0]
        return jnp.broadcast_to(
            row.reshape(rows, 2, 1, half_rows), (rows, 2, GROUP, half_rows)
        ).reshape(rows, 2 * GROUP * half_rows)

    owners = ctx_index ^ jnp.asarray(rel_offsets(slots), jnp.int32)
    flags = (owners > ctx_index).astype(jnp.int32)
    inner = jnp.arange(half_rows, dtype=jnp.int32)
    key_pos = jnp.stack(
        [
            (owners[:, None] * half_rows + inner[None, :]).reshape(-1, 1),
            ((2 * ctx_count - 1 - owners[:, None]) * half_rows + inner[None, :]).reshape(-1, 1),
        ]
    )
    query_pos = by_columns(pos_here[None, :])
    packed_tables = (by_columns(cosine), by_columns(sine_part))

    if split:
        first_half, feed_quarter = gather_halves(weights)
        cuts = row_cuts(weight_rows // 2)
        backward = [list(reversed(order)) for order in ctx_orders()]
        first_own = [spread(first_half[low:high], order) for (low, high), order in zip(cuts, backward)]
        feed_quarter, first_own = lax.optimization_barrier((feed_quarter, first_own))
        feed_far_z = swap(feed_quarter[None], slots[0])
        first_far = [swap(part, ("core", 0)) for part in first_own]
        first_rows = place_rows(first_own, first_far)
        first_rows, feed_far_z = lax.optimization_barrier((first_rows, feed_far_z))
    else:
        mine = lax.all_gather(weights, ("x", "ctx"), axis=0, tiled=True)
        mine = mine.reshape(x_count * ctx_count, weight_rows, model_width)
        far = swap(mine, ("core", 0))
        sides = [
            jnp.where(core == 0, mine[:ctx_count], far[:ctx_count]),
            jnp.where(core == 0, far[:ctx_count], mine[:ctx_count]),
        ]
        first_rows = jnp.concatenate(sides).reshape(-1, model_width)
    qkv_rows, o_rows = first_rows[:cut_o], first_rows[cut_o : cut_o + q_cols]

    tokens_in, cot_in = lax.optimization_barrier(
        (inputs.reshape(tokens, model_width), cotangent.reshape(tokens, model_width))
    )
    dy_low = cot_in.astype(jnp.bfloat16)
    a_one = (normalize(tokens_in) * gains[0]).astype(jnp.bfloat16)
    pair_rows = matmul_t(qkv_rows[q_cols:], a_one)
    joined = jnp.concatenate(
        [rotate(pair_rows[:kv_cols], turn).astype(jnp.bfloat16), pair_rows[kv_cols:].astype(jnp.bfloat16)],
        axis=0,
    )
    if split:
        joined, feed_far_z = lax.optimization_barrier((joined, feed_far_z))
        feed_own = jnp.concatenate([feed_quarter[None], feed_far_z], axis=0)
    if aligned:
        far_z, y_own = swap(joined, slots[0]), swap(joined, slots[2])
    if split:
        feed_near, feed_y = swap(feed_own, slots[1]), swap(feed_own, slots[2])
        feed_x = swap(feed_own, ("x", 0))
    if aligned:
        far_z, y_own, feed_near, feed_y = lax.optimization_barrier(
            (far_z, y_own, feed_near, feed_y)
        )
        near_z = swap(jnp.stack([joined, far_z]), slots[1])
        y_far = swap(far_z, slots[2])
    if split:
        feed_near_y = swap(feed_near, slots[2])
        x_parts = [swap(feed_near, ("x", 0)), swap(feed_y, ("x", 0))]
    if aligned:
        near_z, y_far, feed_near_y, feed_x = lax.optimization_barrier(
            (near_z, y_far, feed_near_y, feed_x)
        )
        y_near = swap(near_z, slots[2])
        pairs = [(joined[None], 0), (far_z[None], 0), (near_z, 0), (near_z, 1)]
        pairs += [(y_own[None], 0), (y_far[None], 0), (y_near, 0), (y_near, 1)]
    else:
        pairs = spread(joined, slots).reshape(ctx_count, 2 * kv_cols, seqs, 2, half_rows)
        pairs = [
            (
                pairs.transpose(1, 2, 3, 0, 4).reshape(
                    1, 2 * kv_cols, seqs * 2 * ctx_count * half_rows
                ),
                0,
            )
        ]
    if split:
        x_parts = [feed_x] + x_parts + [swap(feed_near_y, ("x", 0))]
        feed_own = jnp.concatenate([feed_own, feed_near, feed_y, feed_near_y], axis=0)
        feed_far = swap(feed_own, ("core", 0))
    q_rot = rotate(matmul_t(qkv_rows[:q_cols], a_one), turn).astype(jnp.bfloat16)
    queries = pack((q_rot * SCALE_QK).astype(jnp.bfloat16))
    attended = []
    for seq in range(seqs):
        if aligned:
            attended.append(attend_slots(queries, pairs, flags, local_rows, seq))
        else:
            attended.append(attend(queries, pairs, key_pos, query_pos, local_rows, seq))
        if split and seq == 0:
            attended, x_parts, feed_far = lax.optimization_barrier((attended, x_parts, feed_far))
            feed_x = jnp.concatenate(x_parts, axis=0)
            mine, far = [feed_own, feed_x], [feed_far, swap(feed_x, ("core", 0))]
    attn_low = jnp.concatenate([unpack(mixed) for mixed, _ in attended], axis=1)
    resid = tokens_in + matmul_c(attn_low, o_rows)
    a_two = (normalize(resid) * gains[1]).astype(jnp.bfloat16)
    fed, d_two, *feed_grads = feed_forward(a_two, dy_low, mine, far, weight_rows)
    result = resid + fed
    d_norm_two, d_gain_two = norm_back(resid, d_two, gains[1])
    d_resid = cot_in + d_norm_two
    d_resid_low = d_resid.astype(jnp.bfloat16)
    d_attn = pack(matmul_t(o_rows, d_resid_low).astype(jnp.bfloat16))
    if split:
        sends, feed_held = reduce_start(*feed_grads)
        d_attn, sends = lax.optimization_barrier((d_attn, sends))
        feed_upper, feed_lower = swap(sends[0], ("x", 0)), swap(sends[1], ("x", 0))
    d_q, d_pair = [], []
    for seq in range(seqs):
        mixed, log_total = attended[seq]
        if aligned:
            d_queries, *d_slots = attend_slots_back(
                queries, pairs, flags, mixed, log_total, d_attn, packed_tables, local_rows, seq, (2, 2, 4)
            )
        else:
            d_queries, *d_slots = attend_back(
                queries, pairs, key_pos, query_pos, mixed, log_total, d_attn, packed_tables,
                local_rows, seq, (1,),
            )
        if split and seq == seqs - 1:
            d_slots, feed_upper = lax.optimization_barrier((d_slots, feed_upper))
            feed_y = reduce_y(feed_held, feed_upper)
        d_q.append(unpack(d_queries))
        if aligned:
            lower, near_part, upper = d_slots
            y_come = swap(upper, slots[2])
            near_come = swap(add_low(near_part, y_come[2:]), slots[1])
            if seq == seqs - 1:
                near_come, feed_y = lax.optimization_barrier((near_come, feed_y))
            far_come = swap(total_low(lower[1], y_come[1], near_come[1]), slots[0])
            total = far_come.astype(jnp.float32)
            for part in (lower, y_come, near_come):
                total = total + part[0].astype(jnp.float32)
        else:
            total = collect(
                d_slots[0]
                .reshape(2, KV, ctx_count, half_rows, 2 * HD)
                .transpose(2, 1, 0, 3, 4),
                list(reversed(slots)),
            )
        d_pair.append(total)
    d_own = jnp.stack(d_pair).transpose(1, 4, 0, 2, 3).reshape(KV, 2 * HD, tokens)
    d_qkv = jnp.concatenate(
        [
            jnp.concatenate(d_q, axis=1),
            rotate(d_own[:, :HD].reshape(kv_cols, tokens), turn_back).astype(jnp.bfloat16),
            d_own[:, HD:].reshape(kv_cols, tokens).astype(jnp.bfloat16),
        ],
        axis=0,
    )
    first_terms = first_grads(d_qkv, attn_low, a_one, d_resid_low, weight_rows)
    if split:
        feed_rest = [part[:4] for part in feed_held] + [feed_lower, feed_y]
        feed_near = reduce_near(feed_rest)
        first_terms, feed_near = lax.optimization_barrier((first_terms, feed_near))
        feed_rest = [part[:2] for part in feed_rest] + [feed_near]
        feed_sums = reduce_end(feed_rest, reduce_far(feed_rest))
        sent = jnp.where(
            x_index == 0,
            feed_sums[1:],
            jnp.broadcast_to(feed_sums[:1], (2,) + feed_sums.shape[1:]),
        )
        feed_come = swap(sent.astype(jnp.bfloat16), ("x", 0)).astype(jnp.float32)
    d_one = matmul_c(d_qkv, qkv_rows)
    d_norm_one, d_gain_one = norm_back(tokens_in, d_one, gains[0])
    d_tokens = d_resid + d_norm_one
    gain_grad = jnp.stack([d_gain_one, d_gain_two], axis=0)
    if split:
        keep, away = [part[:, 0] for part in first_terms]
        first_half, gain_grad = reduce_halves(keep, away, gain_grad)
        first_half, feed_come = lax.optimization_barrier((first_half, feed_come))
        low_first = first_half.astype(jnp.bfloat16)
        first_come, gain_grad = swap_with(low_first, gain_grad, ("x", 0))
        first_half = first_half + first_come.astype(jnp.float32)
        halves = [
            jnp.where(x_index == 0, first_half, jnp.concatenate([feed_come[0], feed_sums[1]])),
            jnp.where(
                x_index == 0,
                jnp.concatenate([feed_sums[0], feed_come[0]]),
                jnp.concatenate([feed_come[1], feed_sums[2]]),
            ),
        ]
        own_half = jnp.where(core == 0, halves[0], halves[1])
        other_half = jnp.where(core == 0, halves[1], halves[0]).astype(jnp.bfloat16)
        come, gain_grad = swap_with(other_half, gain_grad, ("core", 0))
        come = come.astype(jnp.float32)
        weight_share = jnp.concatenate(
            [jnp.where(core == 0, own_half, come), jnp.where(core == 0, come, own_half)], axis=0
        )
    else:
        weight_share = scatter_whole([first_terms[0], *feed_grads])
        for where in [("core", 0)] + sum(bit_groups(), []):
            gain_grad = gain_grad + swap(gain_grad, where)
    weight_first, weight_second, weight_new = adam_update(
        weights.astype(jnp.float32), weight_share, first_moment, second_moment, RATE, DECAY, STEP
    )
    gain_first_new, gain_second_new, gain_new = adam_update(
        gains, gain_grad, gain_first, gain_second, GAIN_RATE, 0.0, STEP
    )
    return (
        result.reshape(inputs.shape),
        d_tokens.reshape(inputs.shape),
        weight_share,
        weight_second,
        weight_new,
        gain_grad,
        gain_second_new,
        gain_new,
    )


def solution(mesh):
    fine = Mesh(
        mesh.devices.reshape(mesh.shape["dp"] // 2, 2, mesh.shape["ctx"]), ("x", "core", "ctx")
    )
    rows = P(("x", "core"), "ctx", None)
    stacked = P(("x", "core", "ctx"), None)
    return jax.shard_map(
        shards,
        mesh=fine,
        in_specs=(rows, rows, stacked, P(), stacked, stacked, P(), P()),
        out_specs=(rows, rows, stacked, stacked, stacked, P(), P(), P()),
        check_vma=False,
    )
```

```python
import jax
import jax.numpy as jnp
import numpy as np
from jax import lax
from jax.experimental import pallas as pl
from jax.experimental.pallas import tpu as pltpu
from jax.sharding import Mesh
from jax.sharding import PartitionSpec as P

HEADS = 15
KV = 5
HD = 64
FF = 2560
STEP = 10


SCALE_QK = 0.125
THETA = 10000.0
EPSILON = 1e-05
BETA_ONE = 0.9
BETA_TWO = 0.95
ADAM_EPS = 1e-08
DECAY = 0.1
RATE = 0.02
GAIN_RATE = 0.2
GROUP = HEADS // KV
KEY_TILE = 256
HIDDEN = -1e30
VMEM_BYTES = 48 * 1024 * 1024


def places(row_index, local_rows, ctx_count):
    half_rows = local_rows // 2
    owner_index = row_index // local_rows
    inner_index = row_index % local_rows
    return jnp.where(
        inner_index < half_rows,
        owner_index * half_rows + inner_index,
        (2 * ctx_count - 1 - owner_index) * half_rows + inner_index - half_rows,
    )


def angle_tables(positions_in, sign):
    half_width = HD // 2
    frequency = THETA ** (-jnp.arange(half_width, dtype=jnp.float32) * 2.0 / HD)
    angles = frequency[:, None] * positions_in.astype(jnp.float32)[None, :]
    return jnp.cos(angles), sign * jnp.sin(angles)


def rotate(values, tables):
    cosine, sine_part = tables
    heads = values.reshape(-1, HD, values.shape[-1])
    first_half = heads[:, : HD // 2]
    second_half = heads[:, HD // 2 :]
    return jnp.concatenate(
        [
            first_half * cosine - second_half * sine_part,
            second_half * cosine + first_half * sine_part,
        ],
        axis=1,
    ).reshape(values.shape)


def normalize(values):
    return values * lax.rsqrt(jnp.mean(values * values, axis=-1, keepdims=True) + EPSILON)


def norm_back(values, grad_in, gain_row):
    inv_scale = lax.rsqrt(jnp.mean(values * values, axis=-1, keepdims=True) + EPSILON)
    unit_rows = values * inv_scale
    grad_unit = grad_in * gain_row
    grad_values = inv_scale * (
        grad_unit - unit_rows * jnp.mean(grad_unit * unit_rows, axis=-1, keepdims=True)
    )
    return (grad_values, jnp.sum(grad_in * unit_rows, axis=0))


def matmul_n(left, right):
    return jnp.dot(left, right, preferred_element_type=jnp.float32)


def matmul_t(left, right):
    return lax.dot_general(
        left, right, (((1,), (1,)), ((), ())), preferred_element_type=jnp.float32
    )


def matmul_c(left, right):
    return lax.dot_general(
        left, right, (((0,), (0,)), ((), ())), preferred_element_type=jnp.float32
    )


def bit_groups():
    x_bits = lax.axis_size("x").bit_length() - 1
    ctx_bits = lax.axis_size("ctx").bit_length() - 1
    low_ctx = ctx_bits // 2
    along_x = [("x", bit) for bit in range(x_bits)]
    along_y = [("ctx", bit) for bit in range(low_ctx)]
    along_z = [("ctx", bit) for bit in range(low_ctx, ctx_bits)]
    return along_x, along_y, along_z


def swap_by(values, axis, offset):
    size = lax.axis_size(axis)
    return lax.ppermute(values, axis, [(i, i ^ offset) for i in range(size)])


def swap(values, where):
    return swap_by(values, where[0], 1 << where[1])


def add_low(left, right):
    return (left.astype(jnp.float32) + right.astype(jnp.float32)).astype(jnp.bfloat16)


def rel_offsets(order):
    strides = {"x": 2 * lax.axis_size("ctx"), "ctx": 1}
    offsets = np.zeros((1,), np.int64)
    for axis, bit in order:
        offsets = np.concatenate([offsets, offsets ^ (strides[axis] << bit)])
    return offsets


def lookup(slot, offsets):
    total = jnp.int32(0)
    for bit in range(len(offsets).bit_length() - 1):
        total = total + ((slot >> bit) & 1) * int(offsets[1 << bit])
    return total


def find(offset, offsets):
    total = jnp.int32(0)
    for bit in range(len(offsets).bit_length() - 1):
        place = int(offsets[1 << bit]).bit_length() - 1
        total = total + (((offset >> place) & 1) << bit)
    return total


def collect(values, order):
    kept, arrived = values, None
    for where in order:
        half = kept.shape[0] // 2
        if arrived is None:
            away, kept_next = kept[half:], kept[:half]
        else:
            away = add_low(kept[half:], arrived[half:])
            kept_next = add_low(kept[:half], arrived[:half])
        arrived = swap(away, where)
        kept = kept_next
    return kept[0].astype(jnp.float32) + arrived[0].astype(jnp.float32)


def scatter_whole(terms):
    ctx_count = lax.axis_size("ctx")
    count = 2 * lax.axis_size("x") * ctx_count
    along_x, along_y, along_z = bit_groups()
    core = ("core", 0)
    me = device_index().reshape(1)
    blocks, rows, width = terms[0].shape
    first = -(-rows // 48) * 16
    groups = [(0, first), (first, 2 * first), (2 * first, rows)]
    orders = [
        along_x + along_y + along_z,
        along_y + along_z + along_x,
        along_z + along_x + along_y,
    ]
    tables = [rel_offsets(list(reversed(order))) for order in orders]

    def target(step, me_ref, flip):
        return lookup(step, tables[0]) ^ me_ref[0] ^ flip

    def sources(flip):
        def chosen(member):
            def index(step, me_ref):
                spot = target(step, me_ref, flip)
                return (jnp.where(spot // blocks == member, spot % blocks, 0), 0, 0)

            return pl.BlockSpec((1, rows, width), index)

        return [chosen(member) for member in range(len(terms))]

    def pick_body(me_ref, *refs):
        held = target(pl.program_id(0), me_ref, ctx_count) // blocks
        for member in range(len(terms)):

            @pl.when(held == member)
            def _(member=member):
                refs[-1][...] = refs[member][...]

    away = pl.pallas_call(
        pick_body,
        grid_spec=pltpu.PrefetchScalarGridSpec(
            num_scalar_prefetch=1,
            grid=(count // 2,),
            in_specs=sources(ctx_count),
            out_specs=pl.BlockSpec((1, rows, width), lambda step, me_ref: (step, 0, 0)),
        ),
        out_shape=jax.ShapeDtypeStruct((count // 2, rows, width), jnp.bfloat16),
        compiler_params=pltpu.CompilerParams(vmem_limit_bytes=VMEM_BYTES),
    )(me, *terms)
    arrived = swap(away, core)

    def merge_body(me_ref, *refs):
        held = target(pl.program_id(0), me_ref, 0) // blocks
        for member in range(len(terms)):

            @pl.when(held == member)
            def _(member=member):
                for (low, high), out in zip(groups, refs[-3:]):
                    out[0] = add_low(refs[member][0, low:high], refs[-4][0, low:high])

    parts = pl.pallas_call(
        merge_body,
        grid_spec=pltpu.PrefetchScalarGridSpec(
            num_scalar_prefetch=1,
            grid=(count // 2,),
            in_specs=sources(0)
            + [pl.BlockSpec((1, rows, width), lambda step, me_ref: (step, 0, 0))],
            out_specs=[
                pl.BlockSpec(
                    (1, high - low, width),
                    lambda step, me_ref, table=table: (
                        find(lookup(step, tables[0]), table),
                        0,
                        0,
                    ),
                )
                for (low, high), table in zip(groups, tables)
            ],
        ),
        out_shape=[
            jax.ShapeDtypeStruct((count // 2, high - low, width), jnp.bfloat16)
            for low, high in groups
        ],
        compiler_params=pltpu.CompilerParams(vmem_limit_bytes=VMEM_BYTES),
    )(me, *terms, arrived)
    return jnp.concatenate([collect(part, order) for part, order in zip(parts, orders)], axis=0)


def device_index():
    return (
        (lax.axis_index("x") * 2 + lax.axis_index("core")) * lax.axis_size("ctx")
        + lax.axis_index("ctx")
    ).astype(jnp.int32)


def splits_rows(rows):
    along_x, along_y, along_z = bit_groups()
    return (len(along_x), len(along_y), len(along_z)) == (1, 1, 2) and rows % 64 == 0


def spread(values, order):
    values = values[None]
    for where in order:
        values = double(values, where)
    return values


def double(values, where):
    return jnp.concatenate([values, swap(values, where)], axis=0)


def ctx_orders():
    along_x, along_y, along_z = bit_groups()
    return [along_y + along_z, along_z + along_y]


def row_cuts(rows):
    first = -(-rows // 32) * 16
    return [(0, first), (first, rows)]


def slot_bits():
    along_x, along_y, along_z = bit_groups()
    return list(reversed(along_z)) + along_y


def total_low(*terms):
    total = terms[0].astype(jnp.float32)
    for term in terms[1:]:
        total = total + term.astype(jnp.float32)
    return total.astype(jnp.bfloat16)


def reduce_start(keep, away):
    come = swap(away, ("core", 0))
    quarter = keep.shape[2] // 2
    near, far = slice(0, quarter), slice(quarter, 2 * quarter)
    sends = [
        add_low(keep[4:, :, far], come[4:, :, far]),
        add_low(keep[:4, :, far], come[:4, :, far]),
    ]
    return sends, (keep[:, :, near], come[:, :, near])


def reduce_y(held, x_upper):
    return swap(total_low(*[part[4:] for part in held], x_upper), slot_bits()[2])


def reduce_near(rest):
    return swap(total_low(*[part[2:] for part in rest]), slot_bits()[1])


def reduce_far(rest):
    return swap(total_low(*[part[1] for part in rest]), slot_bits()[0])


def reduce_end(rest, z_far):
    total = z_far.astype(jnp.float32)
    for part in rest:
        total = total + part[0].astype(jnp.float32)
    return total


def reduce_halves(keep, away, ride, beside):
    far_z, near_z, along_y = slot_bits()
    come = beside(0, swap(away, ("core", 0)))
    sums = []
    for (low, high), order in zip(
        row_cuts(keep.shape[1]), ([along_y, near_z, far_z], [near_z, far_z, along_y])
    ):
        shape = (2, 2, 2, high - low, keep.shape[2])
        terms = [keep[:, low:high].reshape(shape), come[:, low:high].reshape(shape)]
        left = [along_y, near_z, far_z]
        for position, where in enumerate(order):
            dim = left.index(where)
            left.remove(where)
            sent = total_low(*[lax.index_in_dim(term, 1, dim, False) for term in terms])
            if low == 0:
                arrived, ride = swap_with(sent, ride, where)
                arrived = beside(position + 1, arrived)
            else:
                arrived = swap(sent, where)
            terms = [lax.index_in_dim(term, 0, dim, False) for term in terms] + [arrived]
        total = terms[0].astype(jnp.float32)
        for term in terms[1:]:
            total = total + term.astype(jnp.float32)
        sums.append(total)
    return jnp.concatenate(sums, axis=0), ride


def ride_parts(ride):
    rounded = lax.reduce_precision(ride, 8, 7)
    return rounded, lax.reduce_precision(ride - rounded, 8, 7)


def with_ride(sent, parts):
    extra = jnp.concatenate([*parts, jnp.zeros((12, parts[0].shape[1]), jnp.float32)])
    return jnp.concatenate([sent.reshape(-1, sent.shape[-1]), extra.astype(jnp.bfloat16)], axis=0)


def swap_with(sent, ride, where):
    parts = ride_parts(ride)
    come, other = off_ride(swap(with_ride(sent, parts), where), sent.shape)
    return come, (parts[0] + parts[1]) + other


def off_ride(come, shape):
    parts = come[-16:].astype(jnp.float32)
    return come[:-16].reshape(shape), parts[0:2] + parts[2:4]


def gather_halves(weights):
    rows = weights.shape[0]
    x_index, core = lax.axis_index("x"), lax.axis_index("core")
    half = rows // 2
    far = swap(weights, ("x", 0))
    low = jnp.where(x_index == 0, weights, far)
    high = jnp.where(x_index == 0, far, weights)
    both = jnp.stack([low, high])
    keep = jnp.where(core == 0, both[:, :half], both[:, half:])
    come = swap(jnp.where(core == 0, both[:, half:], both[:, :half]), ("core", 0))
    first = jnp.where(core == 0, keep, come)
    second = jnp.where(core == 0, come, keep)
    feed = jnp.stack([second[0], first[1], second[1]])
    return first[0], jnp.where(x_index == 0, feed[:, : half // 2], feed[:, half // 2 :])


def place_rows(own, far):
    tables = [rel_offsets(list(reversed(order))) for order in ctx_orders()]
    slots, width = own[0].shape[0], own[0].shape[2]
    lengths = [part.shape[1] for part in own]
    half = sum(lengths)

    def body(me_ref, *refs):
        out_ref = refs[-1]
        for core in range(2):

            @pl.when(me_ref[0] == core)
            def _(core=core):
                for source, base in ((0, core * half), (2, (1 - core) * half)):
                    out_ref[0, base : base + lengths[0]] = refs[source][0]
                    out_ref[0, base + lengths[0] : base + half] = refs[source + 1][0]

    specs = [
        pl.BlockSpec(
            (1, length, width),
            lambda step, me_ref, table=table: (find(step ^ me_ref[1], table), 0, 0),
        )
        for length, table in zip(lengths, tables)
    ]
    me = jnp.stack([lax.axis_index("core"), lax.axis_index("ctx")]).astype(jnp.int32)
    return pl.pallas_call(
        body,
        grid_spec=pltpu.PrefetchScalarGridSpec(
            num_scalar_prefetch=1,
            grid=(slots,),
            in_specs=specs * 2,
            out_specs=pl.BlockSpec((1, 2 * half, width), lambda step, me_ref: (step, 0, 0)),
        ),
        out_shape=jax.ShapeDtypeStruct((slots, 2 * half, width), own[0].dtype),
        cost_estimate=pl.CostEstimate(
            flops=0, bytes_accessed=8 * slots * half * width, transcendentals=0
        ),
        compiler_params=pltpu.CompilerParams(vmem_limit_bytes=VMEM_BYTES),
    )(me, *own, *far).reshape(slots * 2 * half, width)


def turned(values):
    return jnp.transpose(values)


def load_packed(ref, aligned):
    if not aligned:
        return ref[0, 0]
    half = ref.shape[1] // 2
    return jnp.concatenate(
        [
            ref[head * HD : (head + 1) * HD, side * half : (side + 1) * half]
            for side in range(2)
            for head in range(GROUP)
        ],
        axis=1,
    )


def store_packed(ref, values, aligned):
    if not aligned:
        ref[0, 0] = values
        return
    half = ref.shape[1] // 2
    for side in range(2):
        for head in range(GROUP):
            start = (side * GROUP + head) * half
            ref[head * HD : (head + 1) * HD, side * half : (side + 1) * half] = values[
                :, start : start + half
            ]


def load_tile(refs, side, tile):
    length = refs[0].shape[1] // 2
    if length >= KEY_TILE:
        start = side * length + tile * KEY_TILE
        return refs[0][:, start : start + KEY_TILE]
    many = KEY_TILE // length
    return jnp.concatenate(
        [
            ref[:, side * length : (side + 1) * length]
            for ref in refs[tile * many : (tile + 1) * many]
        ],
        axis=1,
    )


def attend_body(count, aligned, queries_ref, key_pos_ref, query_pos_ref, *refs):
    key_refs, value_refs = refs[:count], refs[count : 2 * count]
    out_ref, total_ref, work = refs[2 * count :]
    queries = load_packed(queries_ref, aligned)
    low_cols = queries.shape[1] // 2
    queries_high = queries[:, low_cols:]
    tiles = key_pos_ref.shape[1] // KEY_TILE
    largest = jnp.full((1, queries.shape[1]), HIDDEN, jnp.float32)
    largest_high = jnp.full((1, low_cols), HIDDEN, jnp.float32)
    for side in range(2):
        for tile in range(tiles):
            keys = turned(load_tile(key_refs, side, tile))
            row = (side * tiles + tile) * KEY_TILE
            key_places = key_pos_ref[side, tile * KEY_TILE : (tile + 1) * KEY_TILE]
            if side == 0:
                scores = matmul_n(keys, queries)
                scores = jnp.where(key_places <= query_pos_ref[...], scores, HIDDEN)
                work[row : row + KEY_TILE] = scores
                largest = jnp.maximum(largest, jnp.max(scores, axis=0, keepdims=True))
            else:
                scores = matmul_n(keys, queries_high)
                scores = jnp.where(key_places <= query_pos_ref[:, low_cols:], scores, HIDDEN)
                work[row : row + KEY_TILE, low_cols:] = scores
                largest_high = jnp.maximum(largest_high, jnp.max(scores, axis=0, keepdims=True))
    high_max = jnp.maximum(largest[:, low_cols:], largest_high)
    largest = jnp.concatenate([largest[:, :low_cols], high_max], axis=1)
    total = jnp.zeros_like(largest)
    mixed = jnp.zeros((HD, queries.shape[1]), jnp.float32)
    total_high = jnp.zeros_like(largest_high)
    mixed_high = jnp.zeros((HD, low_cols), jnp.float32)
    for side in range(2):
        for tile in range(tiles):
            values = load_tile(value_refs, side, tile)
            row = (side * tiles + tile) * KEY_TILE
            if side == 0:
                expos = jnp.exp(work[row : row + KEY_TILE] - largest)
                total = total + jnp.sum(expos, axis=0, keepdims=True)
                mixed = mixed + matmul_n(values, expos.astype(jnp.bfloat16))
            else:
                expos = jnp.exp(work[row : row + KEY_TILE, low_cols:] - high_max)
                total_high = total_high + jnp.sum(expos, axis=0, keepdims=True)
                mixed_high = mixed_high + matmul_n(values, expos.astype(jnp.bfloat16))
    total = jnp.concatenate([total[:, :low_cols], total[:, low_cols:] + total_high], axis=1)
    mixed = jnp.concatenate([mixed[:, :low_cols], mixed[:, low_cols:] + mixed_high], axis=1)
    store_packed(out_ref, (mixed / total).astype(jnp.bfloat16), aligned)
    total_ref[0, 0] = largest + jnp.log(total)


def attend_back_body(
    count, aligned, queries_ref, key_pos_ref, query_pos_ref, *refs
):
    key_refs, value_refs = refs[:count], refs[count : 2 * count]
    out_ref, total_ref, d_out_ref, cosine_ref, sine_ref = refs[2 * count : 2 * count + 5]
    d_queries_ref, pair_refs = refs[2 * count + 5], refs[2 * count + 6 :]
    all_queries, all_d_out = load_packed(queries_ref, aligned), load_packed(d_out_ref, aligned)
    low_cols = all_queries.shape[1] // 2
    tiles = key_pos_ref.shape[1] // KEY_TILE
    delta = jnp.sum(
        all_d_out.astype(jnp.float32) * load_packed(out_ref, aligned).astype(jnp.float32),
        axis=0,
        keepdims=True,
    )
    totals = total_ref[0, 0]
    parts = []
    for side in range(2):
        if side == 0:
            queries, d_out = all_queries, all_d_out
            query_places, log_total, row_delta = query_pos_ref[...], totals, delta
        else:
            queries, d_out = all_queries[:, low_cols:], all_d_out[:, low_cols:]
            query_places = query_pos_ref[:, low_cols:]
            log_total, row_delta = totals[:, low_cols:], delta[:, low_cols:]
        part = jnp.zeros((HD, queries.shape[1]), jnp.float32)
        for tile in range(tiles):
            keys_flat = load_tile(key_refs, side, tile)
            scores = matmul_n(turned(keys_flat), queries)
            seen = key_pos_ref[side, tile * KEY_TILE : (tile + 1) * KEY_TILE] <= query_places
            probs = jnp.where(seen, jnp.exp(scores - log_total), 0.0)
            d_probs = matmul_n(turned(load_tile(value_refs, side, tile)), d_out)
            d_scores = (probs * (d_probs - row_delta)).astype(jnp.bfloat16)
            part = part + matmul_n(keys_flat, d_scores)
            d_key = matmul_t(d_scores, queries).astype(jnp.bfloat16)
            d_value = matmul_t(probs.astype(jnp.bfloat16), d_out).astype(jnp.bfloat16)
            if aligned:
                length = key_refs[0].shape[1] // 2
                places_out = [(ref, slot) for ref in pair_refs for slot in range(ref.shape[0])]
                for piece in range(KEY_TILE // length):
                    ref, slot = places_out[tile * (KEY_TILE // length) + piece]
                    rows = slice(piece * length, (piece + 1) * length)
                    ref[slot, 0, side, :, :HD] = d_key[rows]
                    ref[slot, 0, side, :, HD:] = d_value[rows]
            else:
                rows = slice(tile * KEY_TILE, (tile + 1) * KEY_TILE)
                pair_refs[0][side, 0, rows, :HD] = d_key
                pair_refs[0][side, 0, rows, HD:] = d_value
        parts.append(part)
    d_queries = jnp.concatenate(
        [parts[0][:, :low_cols], parts[0][:, low_cols:] + parts[1]], axis=1
    )
    cosine, sine_part = cosine_ref[...], sine_ref[...]
    first_half, second_half = d_queries[: HD // 2], d_queries[HD // 2 :]
    turned_back = jnp.concatenate(
        [
            first_half * cosine + second_half * sine_part,
            second_half * cosine - first_half * sine_part,
        ],
        axis=0,
    )
    store_packed(d_queries_ref, (turned_back * SCALE_QK).astype(jnp.bfloat16), aligned)


def own_mask(rows, cols):
    return lax.broadcasted_iota(jnp.int32, (rows, cols), 0) <= (
        lax.broadcasted_iota(jnp.int32, (rows, cols), 1) % rows
    )


def slot_keys(ref, length):
    both = turned(ref[...])
    return both[:length], both[length:]


def attend_slots_body(count, flags_ref, queries_ref, *refs):
    key_refs, value_refs = refs[:count], refs[count : 2 * count]
    out_ref, total_ref, both_queries, work, largest, totals, mixed = refs[2 * count :]
    length = key_refs[0].shape[1] // 2
    cols = GROUP * length
    packed = load_packed(queries_ref, True)
    for side in range(2):
        both_queries[side] = packed[:, side * cols : (side + 1) * cols]
    visible = own_mask(length, cols)
    low_keys, high_keys = zip(*[slot_keys(ref, length) for ref in key_refs])
    row = 0

    def keep_scores(scores, row):
        work[row : row + scores.shape[0]] = scores
        return jnp.max(scores, axis=0, keepdims=True)

    for side, keys in ((0, low_keys[0]), (1, high_keys[0])):
        scores = jnp.where(visible, matmul_n(keys, both_queries[side]), HIDDEN)
        largest[side] = keep_scores(scores, row)
        row += length
    for slot in range(0, count, 2):
        keys = jnp.concatenate([low_keys[slot], low_keys[slot + 1]], axis=0)
        top = keep_scores(matmul_n(keys, both_queries[1]), row)
        largest[1] = jnp.maximum(largest[1], top)
        row += 2 * length
    for slot in range(1, count):
        side = flags_ref[slot]
        keys = jnp.where(side == 0, low_keys[slot], high_keys[slot])
        top = keep_scores(matmul_n(keys, both_queries[side]), row)
        largest[side] = jnp.maximum(largest[side], top)
        row += length
    row = 0
    for side in range(2):
        values = value_refs[0][:, side * length : (side + 1) * length]
        expos = jnp.exp(work[row : row + length] - largest[side])
        totals[side] = jnp.sum(expos, axis=0, keepdims=True)
        mixed[side] = matmul_n(values, expos.astype(jnp.bfloat16))
        row += length
    for slot in range(0, count, 2):
        values = jnp.concatenate(
            [value_refs[slot][:, :length], value_refs[slot + 1][:, :length]], axis=1
        )
        expos = jnp.exp(work[row : row + 2 * length] - largest[1])
        totals[1] += jnp.sum(expos, axis=0, keepdims=True)
        mixed[1] += matmul_n(values, expos.astype(jnp.bfloat16))
        row += 2 * length
    for slot in range(1, count):
        side = flags_ref[slot]
        values = jnp.where(side == 0, value_refs[slot][:, :length], value_refs[slot][:, length:])
        expos = jnp.exp(work[row : row + length] - largest[side])
        totals[side] += jnp.sum(expos, axis=0, keepdims=True)
        mixed[side] += matmul_n(values, expos.astype(jnp.bfloat16))
        row += length
    result = [(mixed[side] / totals[side]).astype(jnp.bfloat16) for side in range(2)]
    store_packed(out_ref, jnp.concatenate(result, axis=1), True)
    logs = [largest[side] + jnp.log(totals[side]) for side in range(2)]
    total_ref[0, 0] = jnp.concatenate(logs, axis=1)


def attend_slots_back_body(count, flags_ref, queries_ref, *refs):
    key_refs, value_refs = refs[:count], refs[count : 2 * count]
    out_ref, total_ref, d_out_ref, cosine_ref, sine_ref = refs[2 * count : 2 * count + 5]
    d_queries_ref = refs[2 * count + 5]
    pair_refs = refs[2 * count + 6 : -7]
    both_queries, both_d_out, turned_queries, turned_d_out, log_totals, deltas, sums = refs[-7:]
    length = key_refs[0].shape[1] // 2
    cols = GROUP * length
    queries, d_out = load_packed(queries_ref, True), load_packed(d_out_ref, True)
    delta = jnp.sum(
        d_out.astype(jnp.float32) * load_packed(out_ref, True).astype(jnp.float32),
        axis=0,
        keepdims=True,
    )
    for side in range(2):
        part = slice(side * cols, (side + 1) * cols)
        both_queries[side] = queries[:, part]
        both_d_out[side] = d_out[:, part]
        turned_queries[side] = turned(queries[:, part])
        turned_d_out[side] = turned(d_out[:, part])
        log_totals[side] = total_ref[0, 0, :, part]
        deltas[side] = delta[:, part]
    sums[...] = jnp.zeros_like(sums)
    visible = own_mask(length, cols)
    low_keys, high_keys = zip(*[slot_keys(ref, length) for ref in key_refs])
    low_values, high_values = zip(*[slot_keys(ref, length) for ref in value_refs])
    places_out = [(ref, slot) for ref in pair_refs for slot in range(ref.shape[0])]

    def block(keys, keys_flat, values, side, mask=None):
        probs = jnp.exp(matmul_n(keys, both_queries[side]) - log_totals[side])
        if mask is not None:
            probs = jnp.where(mask, probs, 0.0)
        d_probs = matmul_n(values, both_d_out[side])
        d_scores = (probs * (d_probs - deltas[side])).astype(jnp.bfloat16)
        sums[side] += matmul_n(keys_flat, d_scores)
        return jnp.concatenate(
            [
                matmul_n(d_scores, turned_queries[side]),
                matmul_n(probs.astype(jnp.bfloat16), turned_d_out[side]),
            ],
            axis=1,
        )

    low_terms = []
    for slot in range(0, count, 2):
        keys, values = [
            jnp.concatenate([part[slot], part[slot + 1]], axis=0) for part in (low_keys, low_values)
        ]
        flat = jnp.concatenate([key_refs[slot][:, :length], key_refs[slot + 1][:, :length]], axis=1)
        terms = block(keys, flat, values, 1)
        low_terms += [terms[:length], terms[length:]]
    ref, slot = places_out[0]
    own = [
        block(keys, key_refs[0][:, side * length : (side + 1) * length], values, side, visible)
        for side, (keys, values) in enumerate(
            ((low_keys[0], low_values[0]), (high_keys[0], high_values[0]))
        )
    ]
    ref[slot, 0, 0] = (low_terms[0] + own[0]).astype(jnp.bfloat16)
    ref[slot, 0, 1] = own[1].astype(jnp.bfloat16)
    for member in range(1, count):
        side = flags_ref[member]
        low = side == 0
        keys = jnp.where(low, low_keys[member], high_keys[member])
        flat = jnp.where(low, key_refs[member][:, :length], key_refs[member][:, length:])
        values = jnp.where(low, low_values[member], high_values[member])
        terms = block(keys, flat, values, side)
        ref, slot = places_out[member]
        ref[slot, 0, 0] = (low_terms[member] + jnp.where(low, terms, 0.0)).astype(jnp.bfloat16)
        ref[slot, 0, 1] = jnp.where(low, 0.0, terms).astype(jnp.bfloat16)
    d_queries = jnp.concatenate([sums[0], sums[1]], axis=1)
    store_packed(d_queries_ref, turn_queries_back(d_queries, cosine_ref, sine_ref), True)


def turn_queries_back(d_queries, cosine_ref, sine_ref):
    cosine, sine_part = cosine_ref[...], sine_ref[...]
    first_half, second_half = d_queries[: HD // 2], d_queries[HD // 2 :]
    turned_back = jnp.concatenate(
        [
            first_half * cosine + second_half * sine_part,
            second_half * cosine - first_half * sine_part,
        ],
        axis=0,
    )
    return (turned_back * SCALE_QK).astype(jnp.bfloat16)


def slot_specs(leads, local_rows, seq):
    specs = [
        pl.BlockSpec(memory_space=pltpu.SMEM),
        pl.BlockSpec((GROUP * HD, local_rows), lambda head: (head, seq)),
    ]
    for first in (0, KV):
        specs += [
            pl.BlockSpec(
                (None, HD, local_rows),
                lambda head, lead=lead, first=first: (lead, first + head, seq),
            )
            for lead in leads
        ]
    return specs


def attend_slots(queries, pairs, flags, local_rows, seq):
    count, cols = len(pairs), GROUP * local_rows // 2
    leads, arrays = [lead for _, lead in pairs], [array for array, _ in pairs]
    work = HEADS * local_rows * local_rows * count // 2
    return pl.pallas_call(
        lambda *refs: attend_slots_body(count, *refs),
        grid=(KV,),
        in_specs=slot_specs(leads, local_rows, seq),
        out_specs=[
            pl.BlockSpec((GROUP * HD, local_rows), lambda head: (head, 0)),
            pl.BlockSpec((1, 1, 1, 2 * cols), lambda head: (0, head, 0, 0)),
        ],
        out_shape=[
            jax.ShapeDtypeStruct((HEADS * HD, local_rows), jnp.bfloat16),
            jax.ShapeDtypeStruct((1, KV, 1, 2 * cols), jnp.float32),
        ],
        scratch_shapes=[
            pltpu.VMEM((2, HD, cols), jnp.bfloat16),
            pltpu.VMEM(((2 * count + 1) * local_rows // 2, cols), jnp.float32),
            pltpu.VMEM((2, 1, cols), jnp.float32),
            pltpu.VMEM((2, 1, cols), jnp.float32),
            pltpu.VMEM((2, HD, cols), jnp.float32),
        ],
        cost_estimate=pl.CostEstimate(
            flops=work * HD, bytes_accessed=1024 * 1024, transcendentals=0
        ),
        compiler_params=pltpu.CompilerParams(vmem_limit_bytes=VMEM_BYTES),
    )(flags, queries, *arrays, *arrays)


def attend_slots_back(
    queries, pairs, flags, mixed, log_total, d_mixed, tables, local_rows, seq, sets
):
    count, cols = len(pairs), GROUP * local_rows // 2
    leads, arrays = [lead for _, lead in pairs], [array for array, _ in pairs]
    work = HEADS * local_rows * local_rows * count // 2
    own = pl.BlockSpec((GROUP * HD, local_rows), lambda head: (head, 0))
    table_spec = pl.BlockSpec((HD // 2, 2 * cols), lambda head: (0, 0))
    length = local_rows // 2
    return pl.pallas_call(
        lambda *refs: attend_slots_back_body(count, *refs),
        grid=(KV,),
        in_specs=slot_specs(leads, local_rows, seq)
        + [
            own,
            pl.BlockSpec((1, 1, 1, 2 * cols), lambda head: (0, head, 0, 0)),
            pl.BlockSpec((GROUP * HD, local_rows), lambda head: (head, seq)),
            table_spec,
            table_spec,
        ],
        out_specs=[own]
        + [
            pl.BlockSpec((slots, 1, 2, length, 2 * HD), lambda head: (0, head, 0, 0, 0))
            for slots in sets
        ],
        out_shape=[jax.ShapeDtypeStruct((HEADS * HD, local_rows), jnp.bfloat16)]
        + [jax.ShapeDtypeStruct((slots, KV, 2, length, 2 * HD), jnp.bfloat16) for slots in sets],
        scratch_shapes=[
            pltpu.VMEM((2, HD, cols), jnp.bfloat16),
            pltpu.VMEM((2, HD, cols), jnp.bfloat16),
            pltpu.VMEM((2, cols, HD), jnp.bfloat16),
            pltpu.VMEM((2, cols, HD), jnp.bfloat16),
            pltpu.VMEM((2, 1, cols), jnp.float32),
            pltpu.VMEM((2, 1, cols), jnp.float32),
            pltpu.VMEM((2, HD, cols), jnp.float32),
        ],
        cost_estimate=pl.CostEstimate(
            flops=work * HD, bytes_accessed=1024 * 1024, transcendentals=0
        ),
        compiler_params=pltpu.CompilerParams(vmem_limit_bytes=VMEM_BYTES),
    )(flags, queries, *arrays, *arrays, mixed, log_total, d_mixed, *tables)


def head_specs(leads, aligned, cols, keys, local_rows, seq):
    count = len(leads)
    if aligned:
        packed = pl.BlockSpec((GROUP * HD, local_rows), lambda head: (head, seq))
    else:
        packed = pl.BlockSpec((1, 1, HD, cols), lambda head: (seq, head, 0, 0))
    specs = [
        packed,
        pl.BlockSpec((2, keys, 1), lambda head: (0, 0, 0)),
        pl.BlockSpec((1, cols), lambda head: (0, 0)),
    ]
    for first in (0, KV):
        specs += [
            pl.BlockSpec(
                (None, HD, 2 * keys // count),
                lambda head, lead=lead, first=first: (lead, first + head, seq),
            )
            for lead in leads
        ]
    return packed, specs


def attend(queries, pairs, key_pos, query_pos, local_rows, seq):
    aligned = queries.ndim == 2
    cols, keys, count = query_pos.shape[1], key_pos.shape[1], len(pairs)
    leads, arrays = [lead for _, lead in pairs], [array for array, _ in pairs]
    _, specs = head_specs(leads, aligned, cols, keys, local_rows, seq)
    work = HEADS * keys * cols // GROUP * 3 // 2
    if aligned:
        out_spec = pl.BlockSpec((GROUP * HD, local_rows), lambda head: (head, 0))
        out_shape = jax.ShapeDtypeStruct((HEADS * HD, local_rows), jnp.bfloat16)
    else:
        out_spec = pl.BlockSpec((1, 1, HD, cols), lambda head: (0, head, 0, 0))
        out_shape = jax.ShapeDtypeStruct((1, KV, HD, cols), jnp.bfloat16)
    return pl.pallas_call(
        lambda *refs: attend_body(count, aligned, *refs),
        grid=(KV,),
        in_specs=specs,
        out_specs=[out_spec, pl.BlockSpec((1, 1, 1, cols), lambda head: (0, head, 0, 0))],
        out_shape=[out_shape, jax.ShapeDtypeStruct((1, KV, 1, cols), jnp.float32)],
        scratch_shapes=[pltpu.VMEM((2 * keys, cols), jnp.float32)],
        cost_estimate=pl.CostEstimate(
            flops=work * HD, bytes_accessed=1024 * 1024, transcendentals=0
        ),
        compiler_params=pltpu.CompilerParams(vmem_limit_bytes=VMEM_BYTES),
    )(queries, key_pos, query_pos, *arrays, *arrays)


def attend_back(
    queries, pairs, key_pos, query_pos, mixed, log_total, d_mixed, tables, local_rows, seq, sets
):
    aligned = queries.ndim == 2
    cols, keys, count = query_pos.shape[1], key_pos.shape[1], len(pairs)
    leads, arrays = [lead for _, lead in pairs], [array for array, _ in pairs]
    packed, specs = head_specs(leads, aligned, cols, keys, local_rows, seq)
    work = HEADS * keys * cols // GROUP * 3 // 2
    if aligned:
        own = pl.BlockSpec((GROUP * HD, local_rows), lambda head: (head, 0))
        own_shape = jax.ShapeDtypeStruct((HEADS * HD, local_rows), jnp.bfloat16)
        length = keys // count
        pair_specs = [
            pl.BlockSpec((slots, 1, 2, length, 2 * HD), lambda head: (0, head, 0, 0, 0))
            for slots in sets
        ]
        pair_shapes = [
            jax.ShapeDtypeStruct((slots, KV, 2, length, 2 * HD), jnp.bfloat16) for slots in sets
        ]
    else:
        own = pl.BlockSpec((1, 1, HD, cols), lambda head: (0, head, 0, 0))
        own_shape = jax.ShapeDtypeStruct((1, KV, HD, cols), jnp.bfloat16)
        pair_specs = [pl.BlockSpec((2, 1, keys, 2 * HD), lambda head: (0, head, 0, 0))]
        pair_shapes = [jax.ShapeDtypeStruct((2, KV, keys, 2 * HD), jnp.bfloat16)]
    table_spec = pl.BlockSpec((HD // 2, cols), lambda head: (0, 0))
    return pl.pallas_call(
        lambda *refs: attend_back_body(count, aligned, *refs),
        grid=(KV,),
        in_specs=specs
        + [
            own,
            pl.BlockSpec((1, 1, 1, cols), lambda head: (0, head, 0, 0)),
            packed,
            table_spec,
            table_spec,
        ],
        out_specs=[own] + pair_specs,
        out_shape=[own_shape] + pair_shapes,
        cost_estimate=pl.CostEstimate(
            flops=work * HD, bytes_accessed=1024 * 1024, transcendentals=0
        ),
        compiler_params=pltpu.CompilerParams(vmem_limit_bytes=VMEM_BYTES),
    )(queries, key_pos, query_pos, *arrays, *arrays, mixed, log_total, d_mixed, *tables)


def put_rows(values, keep_ref, away_ref, place, core, x_index):
    quarter = values.shape[0] // 4
    for mine in range(4):

        @pl.when(2 * core + x_index == mine)
        def _(mine=mine):
            for ref, side in ((keep_ref, mine // 2), (away_ref, 1 - mine // 2)):
                for position, along_x in enumerate((mine % 2, 1 - mine % 2)):
                    start = (2 * side + along_x) * quarter
                    ref[place[0], place[1], position * quarter : (position + 1) * quarter] = values[
                        start : start + quarter
                    ]


def feed_body(
    parts, split, me_ref, a_two_ref, dy_ref, *refs
):
    count = 4 if split else 6
    weight_refs, (out_ref, d_two_ref), grad_refs = (
        refs[:count],
        refs[count : count + 2],
        refs[count + 2 :],
    )
    core, x_index = me_ref[0], me_ref[1]
    step = pl.program_id(0)

    @pl.when(step == 0)
    def _():
        out_ref[...] = jnp.zeros_like(out_ref)
        d_two_ref[...] = jnp.zeros_like(d_two_ref)

    def rows_of(member):
        if split:
            rows_out = []
            for slot in range(weight_refs[0].shape[0]):
                parts_here = [ref[slot, member] for ref in weight_refs]
                for side in range(2):
                    for along_x in range(2):
                        near = jnp.where(x_index == along_x, parts_here[0], parts_here[1])
                        far = jnp.where(x_index == along_x, parts_here[2], parts_here[3])
                        rows_out.append(jnp.where(core == side, near, far))
            return jnp.concatenate(rows_out, axis=0)
        wanted = feed_core(member, step, parts)
        return jnp.where(wanted == core, weight_refs[2 * member][0], weight_refs[2 * member + 1][0])

    a_two, dy_low = a_two_ref[...], dy_ref[...]
    gate_rows, up_rows, down_rows = rows_of(0), rows_of(1), rows_of(2)
    gate_pre = matmul_t(gate_rows, a_two)
    up_pre = matmul_t(up_rows, a_two)
    d_hidden = matmul_t(down_rows, dy_low)
    sigma = jax.nn.sigmoid(gate_pre)
    gate_act = gate_pre * sigma
    hidden = (gate_act * up_pre).astype(jnp.bfloat16)
    d_gate = (d_hidden * up_pre * sigma * (1.0 + gate_pre * (1.0 - sigma))).astype(jnp.bfloat16)
    d_up = (d_hidden * gate_act).astype(jnp.bfloat16)
    out_ref[...] += matmul_c(hidden, down_rows)
    d_two_ref[...] += matmul_c(d_gate, gate_rows) + matmul_c(d_up, up_rows)
    for member, (left, right) in enumerate(((d_gate, a_two), (d_up, a_two), (hidden, dy_low))):
        grad = matmul_n(left, right).astype(jnp.bfloat16)
        if split:
            slots = grad_refs[0].shape[0]
            rows = grad.shape[0] // slots
            for slot in range(slots):
                put_rows(
                    grad[slot * rows : (slot + 1) * rows], *grad_refs, (slot, member), core, x_index
                )
        else:
            grad_refs[member][0] = grad


def feed_core(member, step, parts):
    ctx_count, single = parts
    return (member + 1) % 2 if single else step // ctx_count


def feed_forward(a_two, dy_low, mine, far, rows):
    tokens, width = a_two.shape
    ctx_count = lax.axis_size("ctx")
    blocks = FF // rows
    single = blocks == ctx_count
    split = splits_rows(rows)
    parts = (ctx_count, single)
    whole = pl.BlockSpec((tokens, width), lambda step, me_ref: (0, 0))

    def weight_spec(member, own):
        first = (member + 1) * blocks // ctx_count // 2 * ctx_count

        def index(step, me_ref):
            matches = (feed_core(member, step, parts) == me_ref[0]) == own
            return (first + jnp.where(matches, step % ctx_count, 0), 0, 0)

        return pl.BlockSpec((1, rows, width), index)

    if split:
        weight_specs = [
            pl.BlockSpec((2, 3, rows // 4, width), lambda step, me_ref: (step, 0, 0, 0))
        ] * 4
        weight_args = [*mine, *far]
        half = pl.BlockSpec((2, 3, rows // 2, width), lambda step, me_ref: (step, 0, 0, 0))
        grad_specs = [half, half]
        grad_shapes = [jax.ShapeDtypeStruct((blocks, 3, rows // 2, width), jnp.bfloat16)] * 2
    else:
        weight_specs = [weight_spec(member, own) for member in range(3) for own in (True, False)]
        weight_args = [mine, far] * 3
        grad_specs = [pl.BlockSpec((1, rows, width), lambda step, me_ref: (step, 0, 0))] * 3
        grad_shapes = [jax.ShapeDtypeStruct((blocks, rows, width), jnp.bfloat16)] * 3
    me = jnp.stack([lax.axis_index("core"), lax.axis_index("x")]).astype(jnp.int32)
    return pl.pallas_call(
        lambda *refs: feed_body(parts, split, *refs),
        grid_spec=pltpu.PrefetchScalarGridSpec(
            num_scalar_prefetch=1,
            grid=(blocks // 2 if split else blocks,),
            in_specs=[whole, whole] + weight_specs,
            out_specs=[whole, whole] + grad_specs,
        ),
        out_shape=[jax.ShapeDtypeStruct((tokens, width), jnp.float32)] * 2 + grad_shapes,
        cost_estimate=pl.CostEstimate(
            flops=18 * tokens * width * FF, bytes_accessed=12 * FF * width, transcendentals=FF * tokens
        ),
        compiler_params=pltpu.CompilerParams(vmem_limit_bytes=VMEM_BYTES),
    )(me, a_two, dy_low, *weight_args)


def first_grads(d_qkv, attn_low, a_one, d_resid_low, rows):
    tokens, width = a_one.shape
    split = splits_rows(rows)
    early = d_qkv.shape[0] // rows
    blocks = early + attn_low.shape[0] // rows

    def body(me_ref, qkv_ref, attn_ref, one_ref, resid_ref, *grad_refs):
        first = pl.program_id(0) < early
        left = jnp.where(first, qkv_ref[...], attn_ref[...])
        right = jnp.where(first, one_ref[...], resid_ref[...])
        grad = matmul_n(left, right).astype(jnp.bfloat16)
        if split:
            put_rows(grad, *grad_refs, (0, 0), me_ref[0], 0)
        else:
            grad_refs[0][0] = grad

    whole = pl.BlockSpec((tokens, width), lambda step, me_ref: (0, 0))
    if split:
        table = rel_offsets(slot_bits())
        half = pl.BlockSpec(
            (1, 1, rows // 2, width), lambda step, me_ref: (find(step ^ me_ref[1], table), 0, 0, 0)
        )
        grad_specs = [half, half]
        grad_shapes = [jax.ShapeDtypeStruct((blocks, 1, rows // 2, width), jnp.bfloat16)] * 2
    else:
        grad_specs = [pl.BlockSpec((1, rows, width), lambda step, me_ref: (step, 0, 0))]
        grad_shapes = [jax.ShapeDtypeStruct((blocks, rows, width), jnp.bfloat16)]
    me = jnp.stack([lax.axis_index(name) for name in ("core", "ctx")]).astype(jnp.int32)
    return pl.pallas_call(
        body,
        grid_spec=pltpu.PrefetchScalarGridSpec(
            num_scalar_prefetch=1,
            grid=(blocks,),
            in_specs=[
                pl.BlockSpec((rows, tokens), lambda step, me_ref: (jnp.minimum(step, early - 1), 0)),
                pl.BlockSpec((rows, tokens), lambda step, me_ref: (jnp.maximum(step - early, 0), 0)),
                whole,
                whole,
            ],
            out_specs=grad_specs,
        ),
        out_shape=grad_shapes,
        cost_estimate=pl.CostEstimate(
            flops=2 * tokens * width * blocks * rows, bytes_accessed=2 * blocks * rows * width, transcendentals=0
        ),
        compiler_params=pltpu.CompilerParams(vmem_limit_bytes=VMEM_BYTES),
    )(me, d_qkv, attn_low, a_one, d_resid_low)


def adam_update(param, grad, first, second, rate, decay, step_number):
    first_new = BETA_ONE * first + (1.0 - BETA_ONE) * grad
    second_new = BETA_TWO * second + (1.0 - BETA_TWO) * grad * grad
    fix_one = 1.0 - BETA_ONE**step_number
    fix_two = 1.0 - BETA_TWO**step_number
    update = first_new / fix_one / (jnp.sqrt(second_new / fix_two) + ADAM_EPS)
    return (first_new, second_new, param - rate * (update + decay * param))


def shards(inputs, cotangent, weights, gains, first_moment, second_moment, gain_first, gain_second):
    ctx_count = lax.axis_size("ctx")
    x_count = lax.axis_size("x")
    ctx_index, core, x_index = lax.axis_index("ctx"), lax.axis_index("core"), lax.axis_index("x")
    seqs, local_rows, model_width = inputs.shape
    half_rows = local_rows // 2
    tokens = seqs * local_rows
    weight_rows = weights.shape[0]
    q_cols = HEADS * HD
    kv_cols = KV * HD
    cut_o = q_cols + 2 * kv_cols
    split = splits_rows(weight_rows)
    slots = slot_bits()
    aligned = split and half_rows % 128 == 0
    local_index = jnp.arange(local_rows, dtype=jnp.int32)
    pos_here = places(ctx_index * local_rows + local_index, local_rows, ctx_count)
    cosine, sine_part = angle_tables(pos_here, 1.0)
    turn = (jnp.tile(cosine, (1, seqs)), jnp.tile(sine_part, (1, seqs)))
    turn_back = (turn[0], -turn[1])

    def pack(flat):
        if aligned:
            return flat
        return (
            flat.reshape(KV, GROUP, HD, -1, 2, half_rows)
            .transpose(3, 0, 2, 4, 1, 5)
            .reshape(-1, KV, HD, 2 * GROUP * half_rows)
        )

    def unpack(packed):
        if aligned:
            return packed
        return (
            packed.reshape(KV, HD, 2, GROUP, half_rows)
            .transpose(0, 3, 1, 2, 4)
            .reshape(q_cols, local_rows)
        )

    def by_columns(row):
        rows = row.shape[0]
        return jnp.broadcast_to(
            row.reshape(rows, 2, 1, half_rows), (rows, 2, GROUP, half_rows)
        ).reshape(rows, 2 * GROUP * half_rows)

    owners = ctx_index ^ jnp.asarray(rel_offsets(slots), jnp.int32)
    flags = (owners > ctx_index).astype(jnp.int32)
    inner = jnp.arange(half_rows, dtype=jnp.int32)
    key_pos = jnp.stack(
        [
            (owners[:, None] * half_rows + inner[None, :]).reshape(-1, 1),
            ((2 * ctx_count - 1 - owners[:, None]) * half_rows + inner[None, :]).reshape(-1, 1),
        ]
    )
    query_pos = by_columns(pos_here[None, :])
    packed_tables = (by_columns(cosine), by_columns(sine_part))

    if split:
        first_half, feed_quarter = gather_halves(weights)
        cuts = row_cuts(weight_rows // 2)
        backward = [list(reversed(order)) for order in ctx_orders()]
        first_own = [spread(first_half[low:high], order) for (low, high), order in zip(cuts, backward)]
        feed_quarter, first_own = lax.optimization_barrier((feed_quarter, first_own))
        feed_far_z = swap(feed_quarter[None], slots[0])
        first_far = [swap(part, ("core", 0)) for part in first_own]
        first_rows = place_rows(first_own, first_far)
    else:
        mine = lax.all_gather(weights, ("x", "ctx"), axis=0, tiled=True)
        mine = mine.reshape(x_count * ctx_count, weight_rows, model_width)
        far = swap(mine, ("core", 0))
        sides = [
            jnp.where(core == 0, mine[:ctx_count], far[:ctx_count]),
            jnp.where(core == 0, far[:ctx_count], mine[:ctx_count]),
        ]
        first_rows = jnp.concatenate(sides).reshape(-1, model_width)
    qkv_rows, o_rows = first_rows[:cut_o], first_rows[cut_o : cut_o + q_cols]

    tokens_in, cot_in = lax.optimization_barrier(
        (inputs.reshape(tokens, model_width), cotangent.reshape(tokens, model_width))
    )
    dy_low = cot_in.astype(jnp.bfloat16)
    a_one = (normalize(tokens_in) * gains[0]).astype(jnp.bfloat16)
    pair_rows = matmul_t(qkv_rows[q_cols:], a_one)
    if split:
        pair_rows, feed_far_z = lax.optimization_barrier((pair_rows, feed_far_z))
    joined = jnp.concatenate(
        [rotate(pair_rows[:kv_cols], turn).astype(jnp.bfloat16), pair_rows[kv_cols:].astype(jnp.bfloat16)],
        axis=0,
    )
    if split:
        feed_own = jnp.concatenate([feed_quarter[None], feed_far_z], axis=0)
        joined, feed_own = lax.optimization_barrier((joined, feed_own))
    if aligned:
        far_z, y_own = swap(joined, slots[0]), swap(joined, slots[2])
    if split:
        feed_near, feed_y = swap(feed_own, slots[1]), swap(feed_own, slots[2])
        feed_x = swap(feed_own, ("x", 0))
    if aligned:
        far_z, y_own, feed_near, feed_y, feed_x = lax.optimization_barrier(
            (far_z, y_own, feed_near, feed_y, feed_x)
        )
        near_z = swap(jnp.stack([joined, far_z]), slots[1])
        y_far = swap(far_z, slots[2])
    if split:
        feed_near_y = swap(feed_near, slots[2])
        x_parts = [swap(feed_near, ("x", 0)), swap(feed_y, ("x", 0))]
    if aligned:
        near_z, y_far, feed_near_y, x_parts = lax.optimization_barrier(
            (near_z, y_far, feed_near_y, x_parts)
        )
        y_near = swap(near_z, slots[2])
        pairs = [(joined[None], 0), (far_z[None], 0), (near_z, 0), (near_z, 1)]
        pairs += [(y_own[None], 0), (y_far[None], 0), (y_near, 0), (y_near, 1)]
    else:
        pairs = spread(joined, slots).reshape(ctx_count, 2 * kv_cols, seqs, 2, half_rows)
        pairs = [
            (
                pairs.transpose(1, 2, 3, 0, 4).reshape(
                    1, 2 * kv_cols, seqs * 2 * ctx_count * half_rows
                ),
                0,
            )
        ]
    if split:
        x_parts = [feed_x] + x_parts + [swap(feed_near_y, ("x", 0))]
        feed_own = jnp.concatenate([feed_own, feed_near, feed_y, feed_near_y], axis=0)
        feed_far = swap(feed_own, ("core", 0))
    q_rot = rotate(matmul_t(qkv_rows[:q_cols], a_one), turn).astype(jnp.bfloat16)
    queries = pack((q_rot * SCALE_QK).astype(jnp.bfloat16))
    attended = []
    for seq in range(seqs):
        if aligned:
            attended.append(attend_slots(queries, pairs, flags, local_rows, seq))
        else:
            attended.append(attend(queries, pairs, key_pos, query_pos, local_rows, seq))
        if split and seq == 0:
            attended, x_parts, feed_far = lax.optimization_barrier((attended, x_parts, feed_far))
            feed_x = jnp.concatenate(x_parts, axis=0)
            mine, far = [feed_own, feed_x], [feed_far, swap(feed_x, ("core", 0))]
    attn_low = jnp.concatenate([unpack(mixed) for mixed, _ in attended], axis=1)
    resid = tokens_in + matmul_c(attn_low, o_rows)
    a_two = (normalize(resid) * gains[1]).astype(jnp.bfloat16)
    fed, d_two, *feed_grads = feed_forward(a_two, dy_low, mine, far, weight_rows)
    result = resid + fed
    d_norm_two, d_gain_two = norm_back(resid, d_two, gains[1])
    d_resid = cot_in + d_norm_two
    d_resid_low = d_resid.astype(jnp.bfloat16)
    d_attn = pack(matmul_t(o_rows, d_resid_low).astype(jnp.bfloat16))
    if split:
        sends, feed_held = reduce_start(*feed_grads)
        d_attn, sends = lax.optimization_barrier((d_attn, sends))
        feed_upper, feed_lower = swap(sends[0], ("x", 0)), swap(sends[1], ("x", 0))
    d_q, d_pair = [], []
    for seq in range(seqs):
        mixed, log_total = attended[seq]
        if aligned:
            d_queries, *d_slots = attend_slots_back(
                queries, pairs, flags, mixed, log_total, d_attn, packed_tables, local_rows, seq, (2, 2, 4)
            )
        else:
            d_queries, *d_slots = attend_back(
                queries, pairs, key_pos, query_pos, mixed, log_total, d_attn, packed_tables,
                local_rows, seq, (1,),
            )
        if split and seq == seqs - 1:
            d_slots, feed_upper = lax.optimization_barrier((d_slots, feed_upper))
            feed_y = reduce_y(feed_held, feed_upper)
        d_q.append(unpack(d_queries))
        if aligned:
            lower, near_part, upper = d_slots
            y_come = swap(upper, slots[2])
            near_come = swap(add_low(near_part, y_come[2:]), slots[1])
            if seq == seqs - 1:
                near_come, feed_lower = lax.optimization_barrier((near_come, feed_lower))
            far_come = swap(total_low(lower[1], y_come[1], near_come[1]), slots[0])
            if seq == seqs - 1:
                far_come, feed_y = lax.optimization_barrier((far_come, feed_y))
            total = far_come.astype(jnp.float32)
            for part in (lower, y_come, near_come):
                total = total + part[0].astype(jnp.float32)
        else:
            total = collect(
                d_slots[0]
                .reshape(2, KV, ctx_count, half_rows, 2 * HD)
                .transpose(2, 1, 0, 3, 4),
                list(reversed(slots)),
            )
        d_pair.append(total)
    d_own = jnp.stack(d_pair).transpose(1, 4, 0, 2, 3).reshape(KV, 2 * HD, tokens)
    d_qkv = jnp.concatenate(
        [
            jnp.concatenate(d_q, axis=1),
            rotate(d_own[:, :HD].reshape(kv_cols, tokens), turn_back).astype(jnp.bfloat16),
            d_own[:, HD:].reshape(kv_cols, tokens).astype(jnp.bfloat16),
        ],
        axis=0,
    )
    first_terms = first_grads(d_qkv, attn_low, a_one, d_resid_low, weight_rows)
    if split:
        feed_rest = [part[:4] for part in feed_held] + [feed_lower, feed_y]
        feed_near = reduce_near(feed_rest)
        first_terms, feed_near = lax.optimization_barrier((first_terms, feed_near))
        feed_rest = [part[:2] for part in feed_rest] + [feed_near]
        feed_far = reduce_far(feed_rest)
        feed_later = {}

        def beside(step, value):
            if step == 2:
                value, far_come = lax.optimization_barrier((value, feed_far))
                sums = reduce_end(feed_rest, far_come)
                sent = jnp.where(
                    x_index == 0, sums[1:], jnp.broadcast_to(sums[:1], (2,) + sums.shape[1:])
                )
                feed_later["sums"] = sums
                feed_later["come"] = swap(sent.astype(jnp.bfloat16), ("x", 0))
            return value

    d_one = matmul_c(d_qkv, qkv_rows)
    d_norm_one, d_gain_one = norm_back(tokens_in, d_one, gains[0])
    d_tokens = d_resid + d_norm_one
    gain_grad = jnp.stack([d_gain_one, d_gain_two], axis=0)
    if split:
        keep, away = [part[:, 0] for part in first_terms]
        first_half, gain_grad = reduce_halves(keep, away, gain_grad, beside)
        first_half, feed_come = lax.optimization_barrier((first_half, feed_later["come"]))
        feed_sums, feed_come = feed_later["sums"], feed_come.astype(jnp.float32)
        low_first = first_half.astype(jnp.bfloat16)
        first_come, gain_grad = swap_with(low_first, gain_grad, ("x", 0))
        first_half = first_half + first_come.astype(jnp.float32)
        halves = [
            jnp.where(x_index == 0, first_half, jnp.concatenate([feed_come[0], feed_sums[1]])),
            jnp.where(
                x_index == 0,
                jnp.concatenate([feed_sums[0], feed_come[0]]),
                jnp.concatenate([feed_come[1], feed_sums[2]]),
            ),
        ]
        own_half = jnp.where(core == 0, halves[0], halves[1])
        other_half = jnp.where(core == 0, halves[1], halves[0]).astype(jnp.bfloat16)
        come, gain_grad = swap_with(other_half, gain_grad, ("core", 0))
        come = come.astype(jnp.float32)
        weight_share = jnp.concatenate(
            [jnp.where(core == 0, own_half, come), jnp.where(core == 0, come, own_half)], axis=0
        )
    else:
        weight_share = scatter_whole([first_terms[0], *feed_grads])
        for where in [("core", 0)] + sum(bit_groups(), []):
            gain_grad = gain_grad + swap(gain_grad, where)
    weight_first, weight_second, weight_new = adam_update(
        weights.astype(jnp.float32), weight_share, first_moment, second_moment, RATE, DECAY, STEP
    )
    gain_first_new, gain_second_new, gain_new = adam_update(
        gains, gain_grad, gain_first, gain_second, GAIN_RATE, 0.0, STEP
    )
    return (
        result.reshape(inputs.shape),
        d_tokens.reshape(inputs.shape),
        weight_share,
        weight_second,
        weight_new,
        gain_grad,
        gain_second_new,
        gain_new,
    )


def solution(mesh):
    fine = Mesh(
        mesh.devices.reshape(mesh.shape["dp"] // 2, 2, mesh.shape["ctx"]), ("x", "core", "ctx")
    )
    rows = P(("x", "core"), "ctx", None)
    stacked = P(("x", "core", "ctx"), None)
    return jax.shard_map(
        shards,
        mesh=fine,
        in_specs=(rows, rows, stacked, P(), stacked, stacked, P(), P()),
        out_specs=(rows, rows, stacked, stacked, stacked, P(), P(), P()),
        check_vma=False,
    )
```

```python
import jax
import jax.numpy as jnp
import numpy as np
from jax import lax
from jax.experimental import pallas as pl
from jax.experimental.pallas import tpu as pltpu
from jax.sharding import Mesh
from jax.sharding import PartitionSpec as P

HEADS = 15
KV = 5
HD = 64
FF = 2560
STEP = 10


SCALE_QK = 0.125
THETA = 10000.0
EPSILON = 1e-05
BETA_ONE = 0.9
BETA_TWO = 0.95
ADAM_EPS = 1e-08
DECAY = 0.1
RATE = 0.02
GAIN_RATE = 0.2
GROUP = HEADS // KV
KEY_TILE = 256
HIDDEN = -1e30
VMEM_BYTES = 48 * 1024 * 1024


def places(row_index, local_rows, ctx_count):
    half_rows = local_rows // 2
    owner_index = row_index // local_rows
    inner_index = row_index % local_rows
    return jnp.where(
        inner_index < half_rows,
        owner_index * half_rows + inner_index,
        (2 * ctx_count - 1 - owner_index) * half_rows + inner_index - half_rows,
    )


def angle_tables(positions_in, sign):
    half_width = HD // 2
    frequency = THETA ** (-jnp.arange(half_width, dtype=jnp.float32) * 2.0 / HD)
    angles = frequency[:, None] * positions_in.astype(jnp.float32)[None, :]
    return jnp.cos(angles), sign * jnp.sin(angles)


def rotate(values, tables):
    cosine, sine_part = tables
    heads = values.reshape(-1, HD, values.shape[-1])
    first_half = heads[:, : HD // 2]
    second_half = heads[:, HD // 2 :]
    return jnp.concatenate(
        [
            first_half * cosine - second_half * sine_part,
            second_half * cosine + first_half * sine_part,
        ],
        axis=1,
    ).reshape(values.shape)


def normalize(values):
    return values * lax.rsqrt(jnp.mean(values * values, axis=-1, keepdims=True) + EPSILON)


def norm_back(values, grad_in, gain_row):
    inv_scale = lax.rsqrt(jnp.mean(values * values, axis=-1, keepdims=True) + EPSILON)
    unit_rows = values * inv_scale
    grad_unit = grad_in * gain_row
    grad_values = inv_scale * (
        grad_unit - unit_rows * jnp.mean(grad_unit * unit_rows, axis=-1, keepdims=True)
    )
    return (grad_values, jnp.sum(grad_in * unit_rows, axis=0))


def matmul_n(left, right):
    return jnp.dot(left, right, preferred_element_type=jnp.float32)


def matmul_t(left, right):
    return lax.dot_general(
        left, right, (((1,), (1,)), ((), ())), preferred_element_type=jnp.float32
    )


def matmul_c(left, right):
    return lax.dot_general(
        left, right, (((0,), (0,)), ((), ())), preferred_element_type=jnp.float32
    )


def bit_groups():
    x_bits = lax.axis_size("x").bit_length() - 1
    ctx_bits = lax.axis_size("ctx").bit_length() - 1
    low_ctx = ctx_bits // 2
    along_x = [("x", bit) for bit in range(x_bits)]
    along_y = [("ctx", bit) for bit in range(low_ctx)]
    along_z = [("ctx", bit) for bit in range(low_ctx, ctx_bits)]
    return along_x, along_y, along_z


def swap_by(values, axis, offset):
    size = lax.axis_size(axis)
    return lax.ppermute(values, axis, [(i, i ^ offset) for i in range(size)])


def swap(values, where):
    return swap_by(values, where[0], 1 << where[1])


def add_low(left, right):
    return (left.astype(jnp.float32) + right.astype(jnp.float32)).astype(jnp.bfloat16)


def rel_offsets(order):
    strides = {"x": 2 * lax.axis_size("ctx"), "ctx": 1}
    offsets = np.zeros((1,), np.int64)
    for axis, bit in order:
        offsets = np.concatenate([offsets, offsets ^ (strides[axis] << bit)])
    return offsets


def lookup(slot, offsets):
    total = jnp.int32(0)
    for bit in range(len(offsets).bit_length() - 1):
        total = total + ((slot >> bit) & 1) * int(offsets[1 << bit])
    return total


def find(offset, offsets):
    total = jnp.int32(0)
    for bit in range(len(offsets).bit_length() - 1):
        place = int(offsets[1 << bit]).bit_length() - 1
        total = total + (((offset >> place) & 1) << bit)
    return total


def collect(values, order):
    kept, arrived = values, None
    for where in order:
        half = kept.shape[0] // 2
        if arrived is None:
            away, kept_next = kept[half:], kept[:half]
        else:
            away = add_low(kept[half:], arrived[half:])
            kept_next = add_low(kept[:half], arrived[:half])
        arrived = swap(away, where)
        kept = kept_next
    return kept[0].astype(jnp.float32) + arrived[0].astype(jnp.float32)


def scatter_whole(terms):
    ctx_count = lax.axis_size("ctx")
    count = 2 * lax.axis_size("x") * ctx_count
    along_x, along_y, along_z = bit_groups()
    core = ("core", 0)
    me = device_index().reshape(1)
    blocks, rows, width = terms[0].shape
    first = -(-rows // 48) * 16
    groups = [(0, first), (first, 2 * first), (2 * first, rows)]
    orders = [
        along_x + along_y + along_z,
        along_y + along_z + along_x,
        along_z + along_x + along_y,
    ]
    tables = [rel_offsets(list(reversed(order))) for order in orders]

    def target(step, me_ref, flip):
        return lookup(step, tables[0]) ^ me_ref[0] ^ flip

    def sources(flip):
        def chosen(member):
            def index(step, me_ref):
                spot = target(step, me_ref, flip)
                return (jnp.where(spot // blocks == member, spot % blocks, 0), 0, 0)

            return pl.BlockSpec((1, rows, width), index)

        return [chosen(member) for member in range(len(terms))]

    def pick_body(me_ref, *refs):
        held = target(pl.program_id(0), me_ref, ctx_count) // blocks
        for member in range(len(terms)):

            @pl.when(held == member)
            def _(member=member):
                refs[-1][...] = refs[member][...]

    away = pl.pallas_call(
        pick_body,
        grid_spec=pltpu.PrefetchScalarGridSpec(
            num_scalar_prefetch=1,
            grid=(count // 2,),
            in_specs=sources(ctx_count),
            out_specs=pl.BlockSpec((1, rows, width), lambda step, me_ref: (step, 0, 0)),
        ),
        out_shape=jax.ShapeDtypeStruct((count // 2, rows, width), jnp.bfloat16),
        compiler_params=pltpu.CompilerParams(vmem_limit_bytes=VMEM_BYTES),
    )(me, *terms)
    arrived = swap(away, core)

    def merge_body(me_ref, *refs):
        held = target(pl.program_id(0), me_ref, 0) // blocks
        for member in range(len(terms)):

            @pl.when(held == member)
            def _(member=member):
                for (low, high), out in zip(groups, refs[-3:]):
                    out[0] = add_low(refs[member][0, low:high], refs[-4][0, low:high])

    parts = pl.pallas_call(
        merge_body,
        grid_spec=pltpu.PrefetchScalarGridSpec(
            num_scalar_prefetch=1,
            grid=(count // 2,),
            in_specs=sources(0)
            + [pl.BlockSpec((1, rows, width), lambda step, me_ref: (step, 0, 0))],
            out_specs=[
                pl.BlockSpec(
                    (1, high - low, width),
                    lambda step, me_ref, table=table: (
                        find(lookup(step, tables[0]), table),
                        0,
                        0,
                    ),
                )
                for (low, high), table in zip(groups, tables)
            ],
        ),
        out_shape=[
            jax.ShapeDtypeStruct((count // 2, high - low, width), jnp.bfloat16)
            for low, high in groups
        ],
        compiler_params=pltpu.CompilerParams(vmem_limit_bytes=VMEM_BYTES),
    )(me, *terms, arrived)
    return jnp.concatenate([collect(part, order) for part, order in zip(parts, orders)], axis=0)


def device_index():
    return (
        (lax.axis_index("x") * 2 + lax.axis_index("core")) * lax.axis_size("ctx")
        + lax.axis_index("ctx")
    ).astype(jnp.int32)


def splits_rows(rows):
    along_x, along_y, along_z = bit_groups()
    return (len(along_x), len(along_y), len(along_z)) == (1, 1, 2) and rows % 64 == 0


def spread(values, order):
    values = values[None]
    for where in order:
        values = double(values, where)
    return values


def double(values, where):
    return jnp.concatenate([values, swap(values, where)], axis=0)


def ctx_orders():
    along_x, along_y, along_z = bit_groups()
    return [along_y + along_z, along_z + along_y]


def row_cuts(rows):
    first = -(-rows // 32) * 16
    return [(0, first), (first, rows)]


def slot_bits():
    along_x, along_y, along_z = bit_groups()
    return list(reversed(along_z)) + along_y


def total_low(*terms):
    total = terms[0].astype(jnp.float32)
    for term in terms[1:]:
        total = total + term.astype(jnp.float32)
    return total.astype(jnp.bfloat16)


def reduce_far(rest):
    return swap(total_low(*[part[1] for part in rest]), slot_bits()[0])


def reduce_end(rest, z_far):
    total = z_far.astype(jnp.float32)
    for part in rest:
        total = total + part[0].astype(jnp.float32)
    return total


def reduce_halves(keep, away, ride, beside):
    far_z, near_z, along_y = slot_bits()
    come = beside(0, swap(away, ("core", 0)))
    sums = []
    for (low, high), order in zip(
        row_cuts(keep.shape[1]), ([along_y, near_z, far_z], [near_z, far_z, along_y])
    ):
        shape = (2, 2, 2, high - low, keep.shape[2])
        terms = [keep[:, low:high].reshape(shape), come[:, low:high].reshape(shape)]
        left = [along_y, near_z, far_z]
        for position, where in enumerate(order):
            dim = left.index(where)
            left.remove(where)
            sent = total_low(*[lax.index_in_dim(term, 1, dim, False) for term in terms])
            if low == 0:
                arrived, ride = swap_with(sent, ride, where)
                arrived = beside(position + 1, arrived)
            else:
                arrived = swap(sent, where)
            terms = [lax.index_in_dim(term, 0, dim, False) for term in terms] + [arrived]
        total = terms[0].astype(jnp.float32)
        for term in terms[1:]:
            total = total + term.astype(jnp.float32)
        sums.append(total)
    return jnp.concatenate(sums, axis=0), ride


def ride_parts(ride):
    rounded = lax.reduce_precision(ride, 8, 7)
    return rounded, lax.reduce_precision(ride - rounded, 8, 7)


def with_ride(sent, parts):
    extra = jnp.concatenate([*parts, jnp.zeros((12, parts[0].shape[1]), jnp.float32)])
    return jnp.concatenate([sent.reshape(-1, sent.shape[-1]), extra.astype(jnp.bfloat16)], axis=0)


def swap_with(sent, ride, where):
    parts = ride_parts(ride)
    come, other = off_ride(swap(with_ride(sent, parts), where), sent.shape)
    return come, (parts[0] + parts[1]) + other


def off_ride(come, shape):
    parts = come[-16:].astype(jnp.float32)
    return come[:-16].reshape(shape), parts[0:2] + parts[2:4]


def gather_halves(weights):
    rows = weights.shape[0]
    x_index, core = lax.axis_index("x"), lax.axis_index("core")
    half = rows // 2
    far = swap(weights, ("x", 0))
    low = jnp.where(x_index == 0, weights, far)
    high = jnp.where(x_index == 0, far, weights)
    both = jnp.stack([low, high])
    keep = jnp.where(core == 0, both[:, :half], both[:, half:])
    come = swap(jnp.where(core == 0, both[:, half:], both[:, :half]), ("core", 0))
    first = jnp.where(core == 0, keep, come)
    second = jnp.where(core == 0, come, keep)
    feed = jnp.stack([second[0], first[1], second[1]])
    return first[0], jnp.where(x_index == 0, feed[:, : half // 2], feed[:, half // 2 :])


def place_rows(own, far):
    tables = [rel_offsets(list(reversed(order))) for order in ctx_orders()]
    slots, width = own[0].shape[0], own[0].shape[2]
    lengths = [part.shape[1] for part in own]
    half = sum(lengths)

    def body(me_ref, *refs):
        out_ref = refs[-1]
        for core in range(2):

            @pl.when(me_ref[0] == core)
            def _(core=core):
                for source, base in ((0, core * half), (2, (1 - core) * half)):
                    out_ref[0, base : base + lengths[0]] = refs[source][0]
                    out_ref[0, base + lengths[0] : base + half] = refs[source + 1][0]

    specs = [
        pl.BlockSpec(
            (1, length, width),
            lambda step, me_ref, table=table: (find(step ^ me_ref[1], table), 0, 0),
        )
        for length, table in zip(lengths, tables)
    ]
    me = jnp.stack([lax.axis_index("core"), lax.axis_index("ctx")]).astype(jnp.int32)
    return pl.pallas_call(
        body,
        grid_spec=pltpu.PrefetchScalarGridSpec(
            num_scalar_prefetch=1,
            grid=(slots,),
            in_specs=specs * 2,
            out_specs=pl.BlockSpec((1, 2 * half, width), lambda step, me_ref: (step, 0, 0)),
        ),
        out_shape=jax.ShapeDtypeStruct((slots, 2 * half, width), own[0].dtype),
        cost_estimate=pl.CostEstimate(
            flops=0, bytes_accessed=8 * slots * half * width, transcendentals=0
        ),
        compiler_params=pltpu.CompilerParams(vmem_limit_bytes=VMEM_BYTES),
    )(me, *own, *far).reshape(slots * 2 * half, width)


def turned(values):
    return jnp.transpose(values)


def load_packed(ref, aligned):
    if not aligned:
        return ref[0, 0]
    half = ref.shape[1] // 2
    return jnp.concatenate(
        [
            ref[head * HD : (head + 1) * HD, side * half : (side + 1) * half]
            for side in range(2)
            for head in range(GROUP)
        ],
        axis=1,
    )


def store_packed(ref, values, aligned):
    if not aligned:
        ref[0, 0] = values
        return
    half = ref.shape[1] // 2
    for side in range(2):
        for head in range(GROUP):
            start = (side * GROUP + head) * half
            ref[head * HD : (head + 1) * HD, side * half : (side + 1) * half] = values[
                :, start : start + half
            ]


def load_tile(refs, side, tile):
    length = refs[0].shape[1] // 2
    if length >= KEY_TILE:
        start = side * length + tile * KEY_TILE
        return refs[0][:, start : start + KEY_TILE]
    many = KEY_TILE // length
    return jnp.concatenate(
        [
            ref[:, side * length : (side + 1) * length]
            for ref in refs[tile * many : (tile + 1) * many]
        ],
        axis=1,
    )


def attend_body(count, aligned, queries_ref, key_pos_ref, query_pos_ref, *refs):
    key_refs, value_refs = refs[:count], refs[count : 2 * count]
    out_ref, total_ref, work = refs[2 * count :]
    queries = load_packed(queries_ref, aligned)
    low_cols = queries.shape[1] // 2
    queries_high = queries[:, low_cols:]
    tiles = key_pos_ref.shape[1] // KEY_TILE
    largest = jnp.full((1, queries.shape[1]), HIDDEN, jnp.float32)
    largest_high = jnp.full((1, low_cols), HIDDEN, jnp.float32)
    for side in range(2):
        for tile in range(tiles):
            keys = turned(load_tile(key_refs, side, tile))
            row = (side * tiles + tile) * KEY_TILE
            key_places = key_pos_ref[side, tile * KEY_TILE : (tile + 1) * KEY_TILE]
            if side == 0:
                scores = matmul_n(keys, queries)
                scores = jnp.where(key_places <= query_pos_ref[...], scores, HIDDEN)
                work[row : row + KEY_TILE] = scores
                largest = jnp.maximum(largest, jnp.max(scores, axis=0, keepdims=True))
            else:
                scores = matmul_n(keys, queries_high)
                scores = jnp.where(key_places <= query_pos_ref[:, low_cols:], scores, HIDDEN)
                work[row : row + KEY_TILE, low_cols:] = scores
                largest_high = jnp.maximum(largest_high, jnp.max(scores, axis=0, keepdims=True))
    high_max = jnp.maximum(largest[:, low_cols:], largest_high)
    largest = jnp.concatenate([largest[:, :low_cols], high_max], axis=1)
    total = jnp.zeros_like(largest)
    mixed = jnp.zeros((HD, queries.shape[1]), jnp.float32)
    total_high = jnp.zeros_like(largest_high)
    mixed_high = jnp.zeros((HD, low_cols), jnp.float32)
    for side in range(2):
        for tile in range(tiles):
            values = load_tile(value_refs, side, tile)
            row = (side * tiles + tile) * KEY_TILE
            if side == 0:
                expos = jnp.exp(work[row : row + KEY_TILE] - largest)
                total = total + jnp.sum(expos, axis=0, keepdims=True)
                mixed = mixed + matmul_n(values, expos.astype(jnp.bfloat16))
            else:
                expos = jnp.exp(work[row : row + KEY_TILE, low_cols:] - high_max)
                total_high = total_high + jnp.sum(expos, axis=0, keepdims=True)
                mixed_high = mixed_high + matmul_n(values, expos.astype(jnp.bfloat16))
    total = jnp.concatenate([total[:, :low_cols], total[:, low_cols:] + total_high], axis=1)
    mixed = jnp.concatenate([mixed[:, :low_cols], mixed[:, low_cols:] + mixed_high], axis=1)
    store_packed(out_ref, (mixed / total).astype(jnp.bfloat16), aligned)
    total_ref[0, 0] = largest + jnp.log(total)


def attend_back_body(
    count, aligned, queries_ref, key_pos_ref, query_pos_ref, *refs
):
    key_refs, value_refs = refs[:count], refs[count : 2 * count]
    out_ref, total_ref, d_out_ref, cosine_ref, sine_ref = refs[2 * count : 2 * count + 5]
    d_queries_ref, pair_refs = refs[2 * count + 5], refs[2 * count + 6 :]
    all_queries, all_d_out = load_packed(queries_ref, aligned), load_packed(d_out_ref, aligned)
    low_cols = all_queries.shape[1] // 2
    tiles = key_pos_ref.shape[1] // KEY_TILE
    delta = jnp.sum(
        all_d_out.astype(jnp.float32) * load_packed(out_ref, aligned).astype(jnp.float32),
        axis=0,
        keepdims=True,
    )
    totals = total_ref[0, 0]
    parts = []
    for side in range(2):
        if side == 0:
            queries, d_out = all_queries, all_d_out
            query_places, log_total, row_delta = query_pos_ref[...], totals, delta
        else:
            queries, d_out = all_queries[:, low_cols:], all_d_out[:, low_cols:]
            query_places = query_pos_ref[:, low_cols:]
            log_total, row_delta = totals[:, low_cols:], delta[:, low_cols:]
        part = jnp.zeros((HD, queries.shape[1]), jnp.float32)
        for tile in range(tiles):
            keys_flat = load_tile(key_refs, side, tile)
            scores = matmul_n(turned(keys_flat), queries)
            seen = key_pos_ref[side, tile * KEY_TILE : (tile + 1) * KEY_TILE] <= query_places
            probs = jnp.where(seen, jnp.exp(scores - log_total), 0.0)
            d_probs = matmul_n(turned(load_tile(value_refs, side, tile)), d_out)
            d_scores = (probs * (d_probs - row_delta)).astype(jnp.bfloat16)
            part = part + matmul_n(keys_flat, d_scores)
            d_key = matmul_t(d_scores, queries).astype(jnp.bfloat16)
            d_value = matmul_t(probs.astype(jnp.bfloat16), d_out).astype(jnp.bfloat16)
            if aligned:
                length = key_refs[0].shape[1] // 2
                places_out = [(ref, slot) for ref in pair_refs for slot in range(ref.shape[0])]
                for piece in range(KEY_TILE // length):
                    ref, slot = places_out[tile * (KEY_TILE // length) + piece]
                    rows = slice(piece * length, (piece + 1) * length)
                    ref[slot, 0, side, :, :HD] = d_key[rows]
                    ref[slot, 0, side, :, HD:] = d_value[rows]
            else:
                rows = slice(tile * KEY_TILE, (tile + 1) * KEY_TILE)
                pair_refs[0][side, 0, rows, :HD] = d_key
                pair_refs[0][side, 0, rows, HD:] = d_value
        parts.append(part)
    d_queries = jnp.concatenate(
        [parts[0][:, :low_cols], parts[0][:, low_cols:] + parts[1]], axis=1
    )
    cosine, sine_part = cosine_ref[...], sine_ref[...]
    first_half, second_half = d_queries[: HD // 2], d_queries[HD // 2 :]
    turned_back = jnp.concatenate(
        [
            first_half * cosine + second_half * sine_part,
            second_half * cosine - first_half * sine_part,
        ],
        axis=0,
    )
    store_packed(d_queries_ref, (turned_back * SCALE_QK).astype(jnp.bfloat16), aligned)


def own_mask(rows, cols):
    return lax.broadcasted_iota(jnp.int32, (rows, cols), 0) <= (
        lax.broadcasted_iota(jnp.int32, (rows, cols), 1) % rows
    )


def slot_keys(ref, length):
    both = turned(ref[...])
    return both[:length], both[length:]


def attend_slots_body(count, flags_ref, queries_ref, *refs):
    key_refs, value_refs = refs[:count], refs[count : 2 * count]
    out_ref, total_ref, both_queries, work, largest, totals, mixed = refs[2 * count :]
    length = key_refs[0].shape[1] // 2
    cols = GROUP * length
    packed = load_packed(queries_ref, True)
    for side in range(2):
        both_queries[side] = packed[:, side * cols : (side + 1) * cols]
    visible = own_mask(length, cols)
    low_keys, high_keys = zip(*[slot_keys(ref, length) for ref in key_refs])
    row = 0

    def keep_scores(scores, row):
        work[row : row + scores.shape[0]] = scores
        return jnp.max(scores, axis=0, keepdims=True)

    for side, keys in ((0, low_keys[0]), (1, high_keys[0])):
        scores = jnp.where(visible, matmul_n(keys, both_queries[side]), HIDDEN)
        largest[side] = keep_scores(scores, row)
        row += length
    for slot in range(0, count, 2):
        keys = jnp.concatenate([low_keys[slot], low_keys[slot + 1]], axis=0)
        top = keep_scores(matmul_n(keys, both_queries[1]), row)
        largest[1] = jnp.maximum(largest[1], top)
        row += 2 * length
    for slot in range(1, count):
        side = flags_ref[slot]
        keys = jnp.where(side == 0, low_keys[slot], high_keys[slot])
        top = keep_scores(matmul_n(keys, both_queries[side]), row)
        largest[side] = jnp.maximum(largest[side], top)
        row += length
    row = 0
    for side in range(2):
        values = value_refs[0][:, side * length : (side + 1) * length]
        expos = jnp.exp(work[row : row + length] - largest[side])
        totals[side] = jnp.sum(expos, axis=0, keepdims=True)
        mixed[side] = matmul_n(values, expos.astype(jnp.bfloat16))
        row += length
    for slot in range(0, count, 2):
        values = jnp.concatenate(
            [value_refs[slot][:, :length], value_refs[slot + 1][:, :length]], axis=1
        )
        expos = jnp.exp(work[row : row + 2 * length] - largest[1])
        totals[1] += jnp.sum(expos, axis=0, keepdims=True)
        mixed[1] += matmul_n(values, expos.astype(jnp.bfloat16))
        row += 2 * length
    for slot in range(1, count):
        side = flags_ref[slot]
        values = jnp.where(side == 0, value_refs[slot][:, :length], value_refs[slot][:, length:])
        expos = jnp.exp(work[row : row + length] - largest[side])
        totals[side] += jnp.sum(expos, axis=0, keepdims=True)
        mixed[side] += matmul_n(values, expos.astype(jnp.bfloat16))
        row += length
    result = [(mixed[side] / totals[side]).astype(jnp.bfloat16) for side in range(2)]
    store_packed(out_ref, jnp.concatenate(result, axis=1), True)
    logs = [largest[side] + jnp.log(totals[side]) for side in range(2)]
    total_ref[0, 0] = jnp.concatenate(logs, axis=1)


def attend_slots_back_body(count, flags_ref, queries_ref, *refs):
    key_refs, value_refs = refs[:count], refs[count : 2 * count]
    out_ref, total_ref, d_out_ref, cosine_ref, sine_ref = refs[2 * count : 2 * count + 5]
    d_queries_ref = refs[2 * count + 5]
    pair_refs = refs[2 * count + 6 : -7]
    both_queries, both_d_out, turned_queries, turned_d_out, log_totals, deltas, sums = refs[-7:]
    length = key_refs[0].shape[1] // 2
    cols = GROUP * length
    queries, d_out = load_packed(queries_ref, True), load_packed(d_out_ref, True)
    delta = jnp.sum(
        d_out.astype(jnp.float32) * load_packed(out_ref, True).astype(jnp.float32),
        axis=0,
        keepdims=True,
    )
    for side in range(2):
        part = slice(side * cols, (side + 1) * cols)
        both_queries[side] = queries[:, part]
        both_d_out[side] = d_out[:, part]
        turned_queries[side] = turned(queries[:, part])
        turned_d_out[side] = turned(d_out[:, part])
        log_totals[side] = total_ref[0, 0, :, part]
        deltas[side] = delta[:, part]
    sums[...] = jnp.zeros_like(sums)
    visible = own_mask(length, cols)
    low_keys, high_keys = zip(*[slot_keys(ref, length) for ref in key_refs])
    low_values, high_values = zip(*[slot_keys(ref, length) for ref in value_refs])
    places_out = [(ref, slot) for ref in pair_refs for slot in range(ref.shape[0])]

    def block(keys, keys_flat, values, side, mask=None):
        probs = jnp.exp(matmul_n(keys, both_queries[side]) - log_totals[side])
        if mask is not None:
            probs = jnp.where(mask, probs, 0.0)
        d_probs = matmul_n(values, both_d_out[side])
        d_scores = (probs * (d_probs - deltas[side])).astype(jnp.bfloat16)
        sums[side] += matmul_n(keys_flat, d_scores)
        return jnp.concatenate(
            [
                matmul_n(d_scores, turned_queries[side]),
                matmul_n(probs.astype(jnp.bfloat16), turned_d_out[side]),
            ],
            axis=1,
        )

    low_terms = []
    for slot in range(0, count, 2):
        keys, values = [
            jnp.concatenate([part[slot], part[slot + 1]], axis=0) for part in (low_keys, low_values)
        ]
        flat = jnp.concatenate([key_refs[slot][:, :length], key_refs[slot + 1][:, :length]], axis=1)
        terms = block(keys, flat, values, 1)
        low_terms += [terms[:length], terms[length:]]
    ref, slot = places_out[0]
    own = [
        block(keys, key_refs[0][:, side * length : (side + 1) * length], values, side, visible)
        for side, (keys, values) in enumerate(
            ((low_keys[0], low_values[0]), (high_keys[0], high_values[0]))
        )
    ]
    ref[slot, 0, 0] = (low_terms[0] + own[0]).astype(jnp.bfloat16)
    ref[slot, 0, 1] = own[1].astype(jnp.bfloat16)
    for member in range(1, count):
        side = flags_ref[member]
        low = side == 0
        keys = jnp.where(low, low_keys[member], high_keys[member])
        flat = jnp.where(low, key_refs[member][:, :length], key_refs[member][:, length:])
        values = jnp.where(low, low_values[member], high_values[member])
        terms = block(keys, flat, values, side)
        ref, slot = places_out[member]
        ref[slot, 0, 0] = (low_terms[member] + jnp.where(low, terms, 0.0)).astype(jnp.bfloat16)
        ref[slot, 0, 1] = jnp.where(low, 0.0, terms).astype(jnp.bfloat16)
    d_queries = jnp.concatenate([sums[0], sums[1]], axis=1)
    store_packed(d_queries_ref, turn_queries_back(d_queries, cosine_ref, sine_ref), True)


def turn_queries_back(d_queries, cosine_ref, sine_ref):
    cosine, sine_part = cosine_ref[...], sine_ref[...]
    first_half, second_half = d_queries[: HD // 2], d_queries[HD // 2 :]
    turned_back = jnp.concatenate(
        [
            first_half * cosine + second_half * sine_part,
            second_half * cosine - first_half * sine_part,
        ],
        axis=0,
    )
    return (turned_back * SCALE_QK).astype(jnp.bfloat16)


def slot_specs(leads, local_rows, seq):
    specs = [
        pl.BlockSpec(memory_space=pltpu.SMEM),
        pl.BlockSpec((GROUP * HD, local_rows), lambda head: (head, seq)),
    ]
    for first in (0, KV):
        specs += [
            pl.BlockSpec(
                (None, HD, local_rows),
                lambda head, lead=lead, first=first: (lead, first + head, 0),
            )
            for lead in leads
        ]
    return specs


def attend_slots(queries, pairs, flags, local_rows, seq):
    count, cols = len(pairs), GROUP * local_rows // 2
    leads, arrays = [lead for _, lead in pairs], [array for array, _ in pairs]
    work = HEADS * local_rows * local_rows * count // 2
    return pl.pallas_call(
        lambda *refs: attend_slots_body(count, *refs),
        grid=(KV,),
        in_specs=slot_specs(leads, local_rows, seq),
        out_specs=[
            pl.BlockSpec((GROUP * HD, local_rows), lambda head: (head, 0)),
            pl.BlockSpec((1, 1, 1, 2 * cols), lambda head: (0, head, 0, 0)),
        ],
        out_shape=[
            jax.ShapeDtypeStruct((HEADS * HD, local_rows), jnp.bfloat16),
            jax.ShapeDtypeStruct((1, KV, 1, 2 * cols), jnp.float32),
        ],
        scratch_shapes=[
            pltpu.VMEM((2, HD, cols), jnp.bfloat16),
            pltpu.VMEM(((2 * count + 1) * local_rows // 2, cols), jnp.float32),
            pltpu.VMEM((2, 1, cols), jnp.float32),
            pltpu.VMEM((2, 1, cols), jnp.float32),
            pltpu.VMEM((2, HD, cols), jnp.float32),
        ],
        cost_estimate=pl.CostEstimate(
            flops=work * HD, bytes_accessed=1024 * 1024, transcendentals=0
        ),
        compiler_params=pltpu.CompilerParams(vmem_limit_bytes=VMEM_BYTES),
    )(flags, queries, *arrays, *arrays)


def attend_slots_back(
    queries, pairs, flags, mixed, log_total, d_mixed, tables, local_rows, seq, sets
):
    count, cols = len(pairs), GROUP * local_rows // 2
    leads, arrays = [lead for _, lead in pairs], [array for array, _ in pairs]
    work = HEADS * local_rows * local_rows * count // 2
    own = pl.BlockSpec((GROUP * HD, local_rows), lambda head: (head, 0))
    table_spec = pl.BlockSpec((HD // 2, 2 * cols), lambda head: (0, 0))
    length = local_rows // 2
    return pl.pallas_call(
        lambda *refs: attend_slots_back_body(count, *refs),
        grid=(KV,),
        in_specs=slot_specs(leads, local_rows, seq)
        + [
            own,
            pl.BlockSpec((1, 1, 1, 2 * cols), lambda head: (0, head, 0, 0)),
            pl.BlockSpec((GROUP * HD, local_rows), lambda head: (head, seq)),
            table_spec,
            table_spec,
        ],
        out_specs=[own]
        + [
            pl.BlockSpec((slots, 1, 2, length, 2 * HD), lambda head: (0, head, 0, 0, 0))
            for slots in sets
        ],
        out_shape=[jax.ShapeDtypeStruct((HEADS * HD, local_rows), jnp.bfloat16)]
        + [jax.ShapeDtypeStruct((slots, KV, 2, length, 2 * HD), jnp.bfloat16) for slots in sets],
        scratch_shapes=[
            pltpu.VMEM((2, HD, cols), jnp.bfloat16),
            pltpu.VMEM((2, HD, cols), jnp.bfloat16),
            pltpu.VMEM((2, cols, HD), jnp.bfloat16),
            pltpu.VMEM((2, cols, HD), jnp.bfloat16),
            pltpu.VMEM((2, 1, cols), jnp.float32),
            pltpu.VMEM((2, 1, cols), jnp.float32),
            pltpu.VMEM((2, HD, cols), jnp.float32),
        ],
        cost_estimate=pl.CostEstimate(
            flops=work * HD, bytes_accessed=1024 * 1024, transcendentals=0
        ),
        compiler_params=pltpu.CompilerParams(vmem_limit_bytes=VMEM_BYTES),
    )(flags, queries, *arrays, *arrays, mixed, log_total, d_mixed, *tables)


def head_specs(leads, aligned, cols, keys, local_rows, seq):
    count = len(leads)
    if aligned:
        packed = pl.BlockSpec((GROUP * HD, local_rows), lambda head: (head, seq))
    else:
        packed = pl.BlockSpec((1, 1, HD, cols), lambda head: (seq, head, 0, 0))
    specs = [
        packed,
        pl.BlockSpec((2, keys, 1), lambda head: (0, 0, 0)),
        pl.BlockSpec((1, cols), lambda head: (0, 0)),
    ]
    for first in (0, KV):
        specs += [
            pl.BlockSpec(
                (None, HD, 2 * keys // count),
                lambda head, lead=lead, first=first: (lead, first + head, seq),
            )
            for lead in leads
        ]
    return packed, specs


def attend(queries, pairs, key_pos, query_pos, local_rows, seq):
    aligned = queries.ndim == 2
    cols, keys, count = query_pos.shape[1], key_pos.shape[1], len(pairs)
    leads, arrays = [lead for _, lead in pairs], [array for array, _ in pairs]
    _, specs = head_specs(leads, aligned, cols, keys, local_rows, seq)
    work = HEADS * keys * cols // GROUP * 3 // 2
    if aligned:
        out_spec = pl.BlockSpec((GROUP * HD, local_rows), lambda head: (head, 0))
        out_shape = jax.ShapeDtypeStruct((HEADS * HD, local_rows), jnp.bfloat16)
    else:
        out_spec = pl.BlockSpec((1, 1, HD, cols), lambda head: (0, head, 0, 0))
        out_shape = jax.ShapeDtypeStruct((1, KV, HD, cols), jnp.bfloat16)
    return pl.pallas_call(
        lambda *refs: attend_body(count, aligned, *refs),
        grid=(KV,),
        in_specs=specs,
        out_specs=[out_spec, pl.BlockSpec((1, 1, 1, cols), lambda head: (0, head, 0, 0))],
        out_shape=[out_shape, jax.ShapeDtypeStruct((1, KV, 1, cols), jnp.float32)],
        scratch_shapes=[pltpu.VMEM((2 * keys, cols), jnp.float32)],
        cost_estimate=pl.CostEstimate(
            flops=work * HD, bytes_accessed=1024 * 1024, transcendentals=0
        ),
        compiler_params=pltpu.CompilerParams(vmem_limit_bytes=VMEM_BYTES),
    )(queries, key_pos, query_pos, *arrays, *arrays)


def attend_back(
    queries, pairs, key_pos, query_pos, mixed, log_total, d_mixed, tables, local_rows, seq, sets
):
    aligned = queries.ndim == 2
    cols, keys, count = query_pos.shape[1], key_pos.shape[1], len(pairs)
    leads, arrays = [lead for _, lead in pairs], [array for array, _ in pairs]
    packed, specs = head_specs(leads, aligned, cols, keys, local_rows, seq)
    work = HEADS * keys * cols // GROUP * 3 // 2
    if aligned:
        own = pl.BlockSpec((GROUP * HD, local_rows), lambda head: (head, 0))
        own_shape = jax.ShapeDtypeStruct((HEADS * HD, local_rows), jnp.bfloat16)
        length = keys // count
        pair_specs = [
            pl.BlockSpec((slots, 1, 2, length, 2 * HD), lambda head: (0, head, 0, 0, 0))
            for slots in sets
        ]
        pair_shapes = [
            jax.ShapeDtypeStruct((slots, KV, 2, length, 2 * HD), jnp.bfloat16) for slots in sets
        ]
    else:
        own = pl.BlockSpec((1, 1, HD, cols), lambda head: (0, head, 0, 0))
        own_shape = jax.ShapeDtypeStruct((1, KV, HD, cols), jnp.bfloat16)
        pair_specs = [pl.BlockSpec((2, 1, keys, 2 * HD), lambda head: (0, head, 0, 0))]
        pair_shapes = [jax.ShapeDtypeStruct((2, KV, keys, 2 * HD), jnp.bfloat16)]
    table_spec = pl.BlockSpec((HD // 2, cols), lambda head: (0, 0))
    return pl.pallas_call(
        lambda *refs: attend_back_body(count, aligned, *refs),
        grid=(KV,),
        in_specs=specs
        + [
            own,
            pl.BlockSpec((1, 1, 1, cols), lambda head: (0, head, 0, 0)),
            packed,
            table_spec,
            table_spec,
        ],
        out_specs=[own] + pair_specs,
        out_shape=[own_shape] + pair_shapes,
        cost_estimate=pl.CostEstimate(
            flops=work * HD, bytes_accessed=1024 * 1024, transcendentals=0
        ),
        compiler_params=pltpu.CompilerParams(vmem_limit_bytes=VMEM_BYTES),
    )(queries, key_pos, query_pos, *arrays, *arrays, mixed, log_total, d_mixed, *tables)


def put_rows(values, keep_ref, away_ref, place, core, x_index):
    quarter = values.shape[0] // 4
    for mine in range(4):

        @pl.when(2 * core + x_index == mine)
        def _(mine=mine):
            for ref, side in ((keep_ref, mine // 2), (away_ref, 1 - mine // 2)):
                for position, along_x in enumerate((mine % 2, 1 - mine % 2)):
                    start = (2 * side + along_x) * quarter
                    ref[place[0], place[1], position * quarter : (position + 1) * quarter] = values[
                        start : start + quarter
                    ]


def feed_body(
    parts, split, chained, me_ref, a_two_ref, dy_ref, *refs
):
    count = 4 if split else 6
    before, refs = (refs[:2], refs[2:]) if chained else (None, refs)
    weight_refs, (out_ref, d_two_ref), grad_refs = (
        refs[:count],
        refs[count : count + 2],
        refs[count + 2 :],
    )
    core, x_index = me_ref[0], me_ref[1]
    step = pl.program_id(0)

    @pl.when(step == 0)
    def _():
        for place, ref in enumerate((out_ref, d_two_ref)):
            ref[...] = before[place][...] if chained else jnp.zeros_like(ref)

    def rows_of(member):
        if split:
            rows_out = []
            for slot in range(weight_refs[0].shape[0]):
                parts_here = [ref[slot, member] for ref in weight_refs]
                for side in range(2):
                    for along_x in range(2):
                        near = jnp.where(x_index == along_x, parts_here[0], parts_here[1])
                        far = jnp.where(x_index == along_x, parts_here[2], parts_here[3])
                        rows_out.append(jnp.where(core == side, near, far))
            return jnp.concatenate(rows_out, axis=0)
        wanted = feed_core(member, step, parts)
        return jnp.where(wanted == core, weight_refs[2 * member][0], weight_refs[2 * member + 1][0])

    a_two, dy_low = a_two_ref[...], dy_ref[...]
    gate_rows, up_rows, down_rows = rows_of(0), rows_of(1), rows_of(2)
    gate_pre = matmul_t(gate_rows, a_two)
    up_pre = matmul_t(up_rows, a_two)
    d_hidden = matmul_t(down_rows, dy_low)
    sigma = jax.nn.sigmoid(gate_pre)
    gate_act = gate_pre * sigma
    hidden = (gate_act * up_pre).astype(jnp.bfloat16)
    d_gate = (d_hidden * up_pre * sigma * (1.0 + gate_pre * (1.0 - sigma))).astype(jnp.bfloat16)
    d_up = (d_hidden * gate_act).astype(jnp.bfloat16)
    out_ref[...] += matmul_c(hidden, down_rows)
    d_two_ref[...] += matmul_c(d_gate, gate_rows) + matmul_c(d_up, up_rows)
    for member, (left, right) in enumerate(((d_gate, a_two), (d_up, a_two), (hidden, dy_low))):
        grad = matmul_n(left, right).astype(jnp.bfloat16)
        if split:
            slots = grad_refs[0].shape[0]
            rows = grad.shape[0] // slots
            for slot in range(slots):
                put_rows(
                    grad[slot * rows : (slot + 1) * rows], *grad_refs, (slot, member), core, x_index
                )
        else:
            grad_refs[member][0] = grad


def feed_core(member, step, parts):
    ctx_count, single = parts
    return (member + 1) % 2 if single else step // ctx_count


def feed_forward(a_two, dy_low, mine, far, rows, before=()):
    tokens, width = a_two.shape
    ctx_count = lax.axis_size("ctx")
    blocks = FF // rows
    single = blocks == ctx_count
    split = mine[0].ndim == 4 if isinstance(mine, list) else False
    parts = (ctx_count, single)
    whole = pl.BlockSpec((tokens, width), lambda step, me_ref: (0, 0))

    def weight_spec(member, own):
        first = (member + 1) * blocks // ctx_count // 2 * ctx_count

        def index(step, me_ref):
            matches = (feed_core(member, step, parts) == me_ref[0]) == own
            return (first + jnp.where(matches, step % ctx_count, 0), 0, 0)

        return pl.BlockSpec((1, rows, width), index)

    if split:
        weight_specs = [
            pl.BlockSpec((2, 3, rows // 4, width), lambda step, me_ref: (step, 0, 0, 0))
        ] * 4
        weight_args = [*mine, *far]
        half = pl.BlockSpec((2, 3, rows // 2, width), lambda step, me_ref: (step, 0, 0, 0))
        grad_specs = [half, half]
        blocks = mine[0].shape[0]
        grad_shapes = [jax.ShapeDtypeStruct((blocks, 3, rows // 2, width), jnp.bfloat16)] * 2
    else:
        weight_specs = [weight_spec(member, own) for member in range(3) for own in (True, False)]
        weight_args = [mine, far] * 3
        grad_specs = [pl.BlockSpec((1, rows, width), lambda step, me_ref: (step, 0, 0))] * 3
        grad_shapes = [jax.ShapeDtypeStruct((blocks, rows, width), jnp.bfloat16)] * 3
    me = jnp.stack([lax.axis_index("core"), lax.axis_index("x")]).astype(jnp.int32)
    return pl.pallas_call(
        lambda *refs: feed_body(parts, split, bool(before), *refs),
        grid_spec=pltpu.PrefetchScalarGridSpec(
            num_scalar_prefetch=1,
            grid=(blocks // 2 if split else blocks,),
            in_specs=[whole] * (2 + len(before)) + weight_specs,
            out_specs=[whole, whole] + grad_specs,
        ),
        out_shape=[jax.ShapeDtypeStruct((tokens, width), jnp.float32)] * 2 + grad_shapes,
        cost_estimate=pl.CostEstimate(
            flops=18 * tokens * width * blocks * rows, bytes_accessed=12 * blocks * rows * width,
            transcendentals=0,
        ),
        compiler_params=pltpu.CompilerParams(vmem_limit_bytes=VMEM_BYTES),
    )(me, a_two, dy_low, *before, *weight_args)


def first_grads(d_qkv, attn_low, a_one, d_resid_low, rows, split):
    tokens, width = a_one.shape
    early = d_qkv.shape[0] // rows
    blocks = early + attn_low.shape[0] // rows

    def body(me_ref, qkv_ref, attn_ref, one_ref, resid_ref, *grad_refs):
        first = pl.program_id(0) < early
        left = jnp.where(first, qkv_ref[...], attn_ref[...])
        right = jnp.where(first, one_ref[...], resid_ref[...])
        grad = matmul_n(left, right).astype(jnp.bfloat16)
        if split:
            put_rows(grad, *grad_refs, (0, 0), me_ref[0], 0)
        else:
            grad_refs[0][0] = grad

    whole = pl.BlockSpec((tokens, width), lambda step, me_ref: (0, 0))
    if split:
        table = rel_offsets(slot_bits())
        half = pl.BlockSpec(
            (1, 1, rows // 2, width), lambda step, me_ref: (find(step ^ me_ref[1], table), 0, 0, 0)
        )
        grad_specs = [half, half]
        grad_shapes = [jax.ShapeDtypeStruct((blocks, 1, rows // 2, width), jnp.bfloat16)] * 2
    else:
        grad_specs = [pl.BlockSpec((1, rows, width), lambda step, me_ref: (step, 0, 0))]
        grad_shapes = [jax.ShapeDtypeStruct((blocks, rows, width), jnp.bfloat16)]
    me = jnp.stack([lax.axis_index(name) for name in ("core", "ctx")]).astype(jnp.int32)
    return pl.pallas_call(
        body,
        grid_spec=pltpu.PrefetchScalarGridSpec(
            num_scalar_prefetch=1,
            grid=(blocks,),
            in_specs=[
                pl.BlockSpec((rows, tokens), lambda step, me_ref: (jnp.minimum(step, early - 1), 0)),
                pl.BlockSpec((rows, tokens), lambda step, me_ref: (jnp.maximum(step - early, 0), 0)),
                whole,
                whole,
            ],
            out_specs=grad_specs,
        ),
        out_shape=grad_shapes,
        cost_estimate=pl.CostEstimate(
            flops=2 * tokens * width * blocks * rows, bytes_accessed=2 * blocks * rows * width, transcendentals=0
        ),
        compiler_params=pltpu.CompilerParams(vmem_limit_bytes=VMEM_BYTES),
    )(me, d_qkv, attn_low, a_one, d_resid_low)


def adam_update(param, grad, first, second, rate, decay, step_number):
    first_new = BETA_ONE * first + (1.0 - BETA_ONE) * grad
    second_new = BETA_TWO * second + (1.0 - BETA_TWO) * grad * grad
    fix_one = 1.0 - BETA_ONE**step_number
    fix_two = 1.0 - BETA_TWO**step_number
    update = first_new / fix_one / (jnp.sqrt(second_new / fix_two) + ADAM_EPS)
    return (first_new, second_new, param - rate * (update + decay * param))


def shards(inputs, cotangent, weights, gains, first_moment, second_moment, gain_first, gain_second):
    ctx_count = lax.axis_size("ctx")
    x_count = lax.axis_size("x")
    ctx_index, core, x_index = lax.axis_index("ctx"), lax.axis_index("core"), lax.axis_index("x")
    seqs, local_rows, model_width = inputs.shape
    half_rows = local_rows // 2
    tokens = seqs * local_rows
    weight_rows = weights.shape[0]
    q_cols = HEADS * HD
    kv_cols = KV * HD
    cut_o = q_cols + 2 * kv_cols
    slots = slot_bits()
    aligned = splits_rows(weight_rows) and half_rows % 128 == 0 and seqs == 2
    split = aligned
    local_index = jnp.arange(local_rows, dtype=jnp.int32)
    pos_here = places(ctx_index * local_rows + local_index, local_rows, ctx_count)
    cosine, sine_part = angle_tables(pos_here, 1.0)
    turn = (jnp.tile(cosine, (1, seqs)), jnp.tile(sine_part, (1, seqs)))
    turn_back = (turn[0], -turn[1])

    def pack(flat):
        if aligned:
            return flat
        return (
            flat.reshape(KV, GROUP, HD, -1, 2, half_rows)
            .transpose(3, 0, 2, 4, 1, 5)
            .reshape(-1, KV, HD, 2 * GROUP * half_rows)
        )

    def unpack(packed):
        if aligned:
            return packed
        return (
            packed.reshape(KV, HD, 2, GROUP, half_rows)
            .transpose(0, 3, 1, 2, 4)
            .reshape(q_cols, local_rows)
        )

    def by_columns(row):
        rows = row.shape[0]
        return jnp.broadcast_to(
            row.reshape(rows, 2, 1, half_rows), (rows, 2, GROUP, half_rows)
        ).reshape(rows, 2 * GROUP * half_rows)

    owners = ctx_index ^ jnp.asarray(rel_offsets(slots), jnp.int32)
    flags = (owners > ctx_index).astype(jnp.int32)
    inner = jnp.arange(half_rows, dtype=jnp.int32)
    key_pos = jnp.stack(
        [
            (owners[:, None] * half_rows + inner[None, :]).reshape(-1, 1),
            ((2 * ctx_count - 1 - owners[:, None]) * half_rows + inner[None, :]).reshape(-1, 1),
        ]
    )
    query_pos = by_columns(pos_here[None, :])
    packed_tables = (by_columns(cosine), by_columns(sine_part))

    if split:
        first_half, feed_quarter = gather_halves(weights)
        cuts = row_cuts(weight_rows // 2)
        backward = [list(reversed(order)) for order in ctx_orders()]
        first_own = [spread(first_half[low:high], order) for (low, high), order in zip(cuts, backward)]
        feed_quarter, first_own = lax.optimization_barrier((feed_quarter, first_own))
        feed_far_z = swap(feed_quarter[None], slots[0])
        first_far = [swap(part, ("core", 0)) for part in first_own]
        first_rows = place_rows(first_own, first_far)
    else:
        mine = lax.all_gather(weights, ("x", "ctx"), axis=0, tiled=True)
        mine = mine.reshape(x_count * ctx_count, weight_rows, model_width)
        far = swap(mine, ("core", 0))
        sides = [
            jnp.where(core == 0, mine[:ctx_count], far[:ctx_count]),
            jnp.where(core == 0, far[:ctx_count], mine[:ctx_count]),
        ]
        first_rows = jnp.concatenate(sides).reshape(-1, model_width)
    qkv_rows, o_rows = first_rows[:cut_o], first_rows[cut_o : cut_o + q_cols]

    tokens_in, cot_in = lax.optimization_barrier(
        (inputs.reshape(tokens, model_width), cotangent.reshape(tokens, model_width))
    )
    dy_low = cot_in.astype(jnp.bfloat16)
    a_one = (normalize(tokens_in) * gains[0]).astype(jnp.bfloat16)
    pair_rows = matmul_t(qkv_rows[q_cols:], a_one)
    if split:
        pair_rows, feed_far_z = lax.optimization_barrier((pair_rows, feed_far_z))
    joined = jnp.concatenate(
        [rotate(pair_rows[:kv_cols], turn).astype(jnp.bfloat16), pair_rows[kv_cols:].astype(jnp.bfloat16)],
        axis=0,
    )
    if split:
        feed_own = jnp.concatenate([feed_quarter[None], feed_far_z], axis=0)
        joined, feed_own = lax.optimization_barrier((joined, feed_own))
    if aligned:
        mine_0, mine_1 = [
            joined[:, seq * local_rows : (seq + 1) * local_rows] for seq in range(2)
        ]
        far_0, own_y_0 = swap(mine_0, slots[0]), swap(mine_0, slots[2])
        feed_near, feed_y = swap(feed_own, slots[1]), swap(feed_own, slots[2])
        feed_x = swap(feed_own, ("x", 0))
        far_0, own_y_0, feed_near, feed_y, feed_x, mine_1 = lax.optimization_barrier(
            (far_0, own_y_0, feed_near, feed_y, feed_x, mine_1)
        )
        near_0, far_y_0 = swap(jnp.stack([mine_0, far_0]), slots[1]), swap(far_0, slots[2])
        far_1, own_y_1 = swap(mine_1, slots[0]), swap(mine_1, slots[2])
        near_x = swap(feed_near, ("x", 0))
        near_0, far_y_0, far_1, own_y_1, near_x, feed_y = lax.optimization_barrier(
            (near_0, far_y_0, far_1, own_y_1, near_x, feed_y)
        )
        near_y_0 = swap(near_0, slots[2])
        near_1, far_y_1 = swap(jnp.stack([mine_1, far_1]), slots[1]), swap(far_1, slots[2])
        y_x = swap(feed_y, ("x", 0))
        near_y_0, near_1, far_y_1, y_x, feed_near = lax.optimization_barrier(
            (near_y_0, near_1, far_y_1, y_x, feed_near)
        )
        near_y_1 = swap(near_1, slots[2])
        pairs = [
            [(own[None], 0), (far_z[None], 0), (near, 0), (near, 1)]
            + [(own_y[None], 0), (far_y[None], 0), (near_y, 0), (near_y, 1)]
            for own, far_z, near, own_y, far_y, near_y in (
                (mine_0, far_0, near_0, own_y_0, far_y_0, near_y_0),
                (mine_1, far_1, near_1, own_y_1, far_y_1, near_y_1),
            )
        ]
        feed_lower = [
            jnp.concatenate([feed_own, feed_near], axis=0),
            jnp.concatenate([feed_x, near_x], axis=0),
        ]
        feed_lower_far = [swap(part, ("core", 0)) for part in feed_lower]
        feed_y_far = [swap(part, ("core", 0)) for part in (feed_y, y_x)]
    else:
        pairs = spread(joined, slots).reshape(ctx_count, 2 * kv_cols, seqs, 2, half_rows)
        pairs = [
            (
                pairs.transpose(1, 2, 3, 0, 4).reshape(
                    1, 2 * kv_cols, seqs * 2 * ctx_count * half_rows
                ),
                0,
            )
        ]
    q_rot = rotate(matmul_t(qkv_rows[:q_cols], a_one), turn).astype(jnp.bfloat16)
    queries = pack((q_rot * SCALE_QK).astype(jnp.bfloat16))
    attended = []
    for seq in range(seqs):
        if aligned:
            attended.append(attend_slots(queries, pairs[seq], flags, local_rows, seq))
            if seq == 0:
                attended, feed_near = lax.optimization_barrier((attended, feed_near))
                feed_near_y = swap(feed_near, slots[2])
        else:
            attended.append(attend(queries, pairs, key_pos, query_pos, local_rows, seq))
    attn_low = jnp.concatenate([unpack(mixed) for mixed, _ in attended], axis=1)
    resid = tokens_in + matmul_c(attn_low, o_rows)
    a_two = (normalize(resid) * gains[1]).astype(jnp.bfloat16)
    if aligned:
        a_two, feed_near_y = lax.optimization_barrier((a_two, feed_near_y))
        near_y_x = swap(feed_near_y, ("x", 0))
        near_y_far = swap(feed_near_y, ("core", 0))
        *sums_fed, keep_lower, away_lower = feed_forward(
            a_two, dy_low, feed_lower, feed_lower_far, weight_rows
        )
        sums_fed, near_y_x = lax.optimization_barrier((sums_fed, near_y_x))
        near_y_x_far = swap(near_y_x, ("core", 0))
        come_lower = swap(away_lower, ("core", 0))
        *sums_fed, keep_upper, away_upper = feed_forward(
            a_two, dy_low, [feed_y, y_x], feed_y_far, weight_rows, sums_fed
        )
        come_upper = swap(away_upper, ("core", 0))
        fed, d_two, keep_last, away_last = feed_forward(
            a_two, dy_low, [feed_near_y, near_y_x], [near_y_far, near_y_x_far], weight_rows, sums_fed
        )
        come_last = swap(away_last, ("core", 0))
    else:
        fed, d_two, *feed_grads = feed_forward(a_two, dy_low, mine, far, weight_rows)
    result = resid + fed
    d_norm_two, d_gain_two = norm_back(resid, d_two, gains[1])
    d_resid = cot_in + d_norm_two
    d_resid_low = d_resid.astype(jnp.bfloat16)
    d_attn = pack(matmul_t(o_rows, d_resid_low).astype(jnp.bfloat16))
    if aligned:
        quarter = weight_rows // 4
        held_upper, held_last, held_lower = [
            [(part[:, :, :quarter], part[:, :, quarter:]) for part in parts]
            for parts in (
                (keep_upper, come_upper), (keep_last, come_last), (keep_lower, come_lower)
            )
        ]
        send_upper, send_last, send_lower = [
            total_low(*[far_part for _, far_part in parts])
            for parts in (held_upper, held_last, held_lower)
        ]
        x_upper = swap(send_upper, ("x", 0))
        y_send = total_low(*[part for part, _ in held_upper], x_upper)
        d_attn, y_send, send_last, send_lower = lax.optimization_barrier(
            (d_attn, y_send, send_last, send_lower)
        )
        feed_y_come = swap(y_send, slots[2])
        x_last = swap(send_last, ("x", 0))
        x_lower = swap(send_lower, ("x", 0))
    d_q, d_pair = [], []
    for seq in range(seqs):
        mixed, log_total = attended[seq]
        if aligned:
            d_queries, *d_slots = attend_slots_back(
                queries, pairs[seq], flags, mixed, log_total, d_attn, packed_tables, local_rows, seq, (2, 2, 4)
            )
        else:
            d_queries, *d_slots = attend_back(
                queries, pairs, key_pos, query_pos, mixed, log_total, d_attn, packed_tables,
                local_rows, seq, (1,),
            )
        if aligned and seq == 0:
            d_slots, x_last, feed_y_come = lax.optimization_barrier((d_slots, x_last, feed_y_come))
            last_y_come = swap(total_low(*[part for part, _ in held_last], x_last), slots[2])
        d_q.append(unpack(d_queries))
        if aligned:
            lower, near_part, upper = d_slots
            y_come = swap(upper, slots[2])
            near_come = swap(add_low(near_part, y_come[2:]), slots[1])
            if seq == seqs - 1:
                near_come, x_lower, last_y_come = lax.optimization_barrier(
                    (near_come, x_lower, last_y_come)
                )
                rest = [part for part, _ in held_lower] + [x_lower]
                feed_near_come = swap(
                    total_low(*[part[2:] for part in rest], last_y_come), slots[1]
                )
            far_come = swap(total_low(lower[1], y_come[1], near_come[1]), slots[0])
            if seq == seqs - 1:
                far_come, feed_near_come = lax.optimization_barrier((far_come, feed_near_come))
                feed_rest = [part[:2] for part in rest] + [feed_y_come, feed_near_come]
                feed_far = reduce_far(feed_rest)
            total = far_come.astype(jnp.float32)
            for part in (lower, y_come, near_come):
                total = total + part[0].astype(jnp.float32)
        else:
            total = collect(
                d_slots[0]
                .reshape(2, KV, ctx_count, half_rows, 2 * HD)
                .transpose(2, 1, 0, 3, 4),
                list(reversed(slots)),
            )
        d_pair.append(total)
    d_own = jnp.stack(d_pair).transpose(1, 4, 0, 2, 3).reshape(KV, 2 * HD, tokens)
    d_qkv = jnp.concatenate(
        [
            jnp.concatenate(d_q, axis=1),
            rotate(d_own[:, :HD].reshape(kv_cols, tokens), turn_back).astype(jnp.bfloat16),
            d_own[:, HD:].reshape(kv_cols, tokens).astype(jnp.bfloat16),
        ],
        axis=0,
    )
    first_terms = first_grads(d_qkv, attn_low, a_one, d_resid_low, weight_rows, split)
    if split:
        first_terms, feed_far = lax.optimization_barrier((first_terms, feed_far))
        feed_later = {}

        def beside(step, value):
            if step == 0:
                value, far_come = lax.optimization_barrier((value, feed_far))
                sums = reduce_end(feed_rest, far_come)
                sent = jnp.where(
                    x_index == 0, sums[1:], jnp.broadcast_to(sums[:1], (2,) + sums.shape[1:])
                )
                feed_later["sums"] = sums
                feed_later["come"] = swap(sent.astype(jnp.bfloat16), ("x", 0))
            return value

    d_one = matmul_c(d_qkv, qkv_rows)
    d_norm_one, d_gain_one = norm_back(tokens_in, d_one, gains[0])
    d_tokens = d_resid + d_norm_one
    gain_grad = jnp.stack([d_gain_one, d_gain_two], axis=0)
    if split:
        keep, away = [part[:, 0] for part in first_terms]
        first_half, gain_grad = reduce_halves(keep, away, gain_grad, beside)
        first_half, feed_come = lax.optimization_barrier((first_half, feed_later["come"]))
        feed_sums, feed_come = feed_later["sums"], feed_come.astype(jnp.float32)
        low_first = first_half.astype(jnp.bfloat16)
        first_come, gain_grad = swap_with(low_first, gain_grad, ("x", 0))
        first_half = first_half + first_come.astype(jnp.float32)
        halves = [
            jnp.where(x_index == 0, first_half, jnp.concatenate([feed_come[0], feed_sums[1]])),
            jnp.where(
                x_index == 0,
                jnp.concatenate([feed_sums[0], feed_come[0]]),
                jnp.concatenate([feed_come[1], feed_sums[2]]),
            ),
        ]
        own_half = jnp.where(core == 0, halves[0], halves[1])
        other_half = jnp.where(core == 0, halves[1], halves[0]).astype(jnp.bfloat16)
        come, gain_grad = swap_with(other_half, gain_grad, ("core", 0))
        come = come.astype(jnp.float32)
        weight_share = jnp.concatenate(
            [jnp.where(core == 0, own_half, come), jnp.where(core == 0, come, own_half)], axis=0
        )
    else:
        weight_share = scatter_whole([first_terms[0], *feed_grads])
        for where in [("core", 0)] + sum(bit_groups(), []):
            gain_grad = gain_grad + swap(gain_grad, where)
    weight_first, weight_second, weight_new = adam_update(
        weights.astype(jnp.float32), weight_share, first_moment, second_moment, RATE, DECAY, STEP
    )
    gain_first_new, gain_second_new, gain_new = adam_update(
        gains, gain_grad, gain_first, gain_second, GAIN_RATE, 0.0, STEP
    )
    return (
        result.reshape(inputs.shape),
        d_tokens.reshape(inputs.shape),
        weight_share,
        weight_second,
        weight_new,
        gain_grad,
        gain_second_new,
        gain_new,
    )


def solution(mesh):
    fine = Mesh(
        mesh.devices.reshape(mesh.shape["dp"] // 2, 2, mesh.shape["ctx"]), ("x", "core", "ctx")
    )
    rows = P(("x", "core"), "ctx", None)
    stacked = P(("x", "core", "ctx"), None)
    return jax.shard_map(
        shards,
        mesh=fine,
        in_specs=(rows, rows, stacked, P(), stacked, stacked, P(), P()),
        out_specs=(rows, rows, stacked, stacked, stacked, P(), P(), P()),
        check_vma=False,
    )
```

```python
import jax
import jax.numpy as jnp
import numpy as np
from jax import lax
from jax.experimental import pallas as pl
from jax.experimental.pallas import tpu as pltpu
from jax.sharding import Mesh
from jax.sharding import PartitionSpec as P

HEADS = 15
KV = 5
HD = 64
FF = 2560
STEP = 10


SCALE_QK = 0.125
THETA = 10000.0
EPSILON = 1e-05
BETA_ONE = 0.9
BETA_TWO = 0.95
ADAM_EPS = 1e-08
DECAY = 0.1
RATE = 0.02
GAIN_RATE = 0.2
GROUP = HEADS // KV
KEY_TILE = 256
HIDDEN = -1e30
VMEM_BYTES = 48 * 1024 * 1024


def places(row_index, local_rows, ctx_count):
    half_rows = local_rows // 2
    owner_index = row_index // local_rows
    inner_index = row_index % local_rows
    return jnp.where(
        inner_index < half_rows,
        owner_index * half_rows + inner_index,
        (2 * ctx_count - 1 - owner_index) * half_rows + inner_index - half_rows,
    )


def angle_tables(positions_in, sign):
    half_width = HD // 2
    frequency = THETA ** (-jnp.arange(half_width, dtype=jnp.float32) * 2.0 / HD)
    angles = frequency[:, None] * positions_in.astype(jnp.float32)[None, :]
    return jnp.cos(angles), sign * jnp.sin(angles)


def rotate(values, tables):
    cosine, sine_part = tables
    heads = values.reshape(-1, HD, values.shape[-1])
    first_half = heads[:, : HD // 2]
    second_half = heads[:, HD // 2 :]
    return jnp.concatenate(
        [
            first_half * cosine - second_half * sine_part,
            second_half * cosine + first_half * sine_part,
        ],
        axis=1,
    ).reshape(values.shape)


def normalize(values):
    return values * lax.rsqrt(jnp.mean(values * values, axis=-1, keepdims=True) + EPSILON)


def norm_back(values, grad_in, gain_row):
    inv_scale = lax.rsqrt(jnp.mean(values * values, axis=-1, keepdims=True) + EPSILON)
    unit_rows = values * inv_scale
    grad_unit = grad_in * gain_row
    grad_values = inv_scale * (
        grad_unit - unit_rows * jnp.mean(grad_unit * unit_rows, axis=-1, keepdims=True)
    )
    return (grad_values, jnp.sum(grad_in * unit_rows, axis=0))


def matmul_n(left, right):
    return jnp.dot(left, right, preferred_element_type=jnp.float32)


def matmul_t(left, right):
    return lax.dot_general(
        left, right, (((1,), (1,)), ((), ())), preferred_element_type=jnp.float32
    )


def matmul_c(left, right):
    return lax.dot_general(
        left, right, (((0,), (0,)), ((), ())), preferred_element_type=jnp.float32
    )


def bit_groups():
    x_bits = lax.axis_size("x").bit_length() - 1
    ctx_bits = lax.axis_size("ctx").bit_length() - 1
    low_ctx = ctx_bits // 2
    along_x = [("x", bit) for bit in range(x_bits)]
    along_y = [("ctx", bit) for bit in range(low_ctx)]
    along_z = [("ctx", bit) for bit in range(low_ctx, ctx_bits)]
    return along_x, along_y, along_z


def swap_by(values, axis, offset):
    size = lax.axis_size(axis)
    return lax.ppermute(values, axis, [(i, i ^ offset) for i in range(size)])


def swap(values, where):
    return swap_by(values, where[0], 1 << where[1])


def add_low(left, right):
    return (left.astype(jnp.float32) + right.astype(jnp.float32)).astype(jnp.bfloat16)


def rel_offsets(order):
    strides = {"x": 2 * lax.axis_size("ctx"), "ctx": 1}
    offsets = np.zeros((1,), np.int64)
    for axis, bit in order:
        offsets = np.concatenate([offsets, offsets ^ (strides[axis] << bit)])
    return offsets


def lookup(slot, offsets):
    total = jnp.int32(0)
    for bit in range(len(offsets).bit_length() - 1):
        total = total + ((slot >> bit) & 1) * int(offsets[1 << bit])
    return total


def find(offset, offsets):
    total = jnp.int32(0)
    for bit in range(len(offsets).bit_length() - 1):
        place = int(offsets[1 << bit]).bit_length() - 1
        total = total + (((offset >> place) & 1) << bit)
    return total


def collect(values, order):
    kept, arrived = values, None
    for where in order:
        half = kept.shape[0] // 2
        if arrived is None:
            away, kept_next = kept[half:], kept[:half]
        else:
            away = add_low(kept[half:], arrived[half:])
            kept_next = add_low(kept[:half], arrived[:half])
        arrived = swap(away, where)
        kept = kept_next
    return kept[0].astype(jnp.float32) + arrived[0].astype(jnp.float32)


def scatter_whole(terms):
    ctx_count = lax.axis_size("ctx")
    count = 2 * lax.axis_size("x") * ctx_count
    along_x, along_y, along_z = bit_groups()
    core = ("core", 0)
    me = device_index().reshape(1)
    blocks, rows, width = terms[0].shape
    first = -(-rows // 48) * 16
    groups = [(0, first), (first, 2 * first), (2 * first, rows)]
    orders = [
        along_x + along_y + along_z,
        along_y + along_z + along_x,
        along_z + along_x + along_y,
    ]
    tables = [rel_offsets(list(reversed(order))) for order in orders]

    def target(step, me_ref, flip):
        return lookup(step, tables[0]) ^ me_ref[0] ^ flip

    def sources(flip):
        def chosen(member):
            def index(step, me_ref):
                spot = target(step, me_ref, flip)
                return (jnp.where(spot // blocks == member, spot % blocks, 0), 0, 0)

            return pl.BlockSpec((1, rows, width), index)

        return [chosen(member) for member in range(len(terms))]

    def pick_body(me_ref, *refs):
        held = target(pl.program_id(0), me_ref, ctx_count) // blocks
        for member in range(len(terms)):

            @pl.when(held == member)
            def _(member=member):
                refs[-1][...] = refs[member][...]

    away = pl.pallas_call(
        pick_body,
        grid_spec=pltpu.PrefetchScalarGridSpec(
            num_scalar_prefetch=1,
            grid=(count // 2,),
            in_specs=sources(ctx_count),
            out_specs=pl.BlockSpec((1, rows, width), lambda step, me_ref: (step, 0, 0)),
        ),
        out_shape=jax.ShapeDtypeStruct((count // 2, rows, width), jnp.bfloat16),
        compiler_params=pltpu.CompilerParams(vmem_limit_bytes=VMEM_BYTES),
    )(me, *terms)
    arrived = swap(away, core)

    def merge_body(me_ref, *refs):
        held = target(pl.program_id(0), me_ref, 0) // blocks
        for member in range(len(terms)):

            @pl.when(held == member)
            def _(member=member):
                for (low, high), out in zip(groups, refs[-3:]):
                    out[0] = add_low(refs[member][0, low:high], refs[-4][0, low:high])

    parts = pl.pallas_call(
        merge_body,
        grid_spec=pltpu.PrefetchScalarGridSpec(
            num_scalar_prefetch=1,
            grid=(count // 2,),
            in_specs=sources(0)
            + [pl.BlockSpec((1, rows, width), lambda step, me_ref: (step, 0, 0))],
            out_specs=[
                pl.BlockSpec(
                    (1, high - low, width),
                    lambda step, me_ref, table=table: (
                        find(lookup(step, tables[0]), table),
                        0,
                        0,
                    ),
                )
                for (low, high), table in zip(groups, tables)
            ],
        ),
        out_shape=[
            jax.ShapeDtypeStruct((count // 2, high - low, width), jnp.bfloat16)
            for low, high in groups
        ],
        compiler_params=pltpu.CompilerParams(vmem_limit_bytes=VMEM_BYTES),
    )(me, *terms, arrived)
    return jnp.concatenate([collect(part, order) for part, order in zip(parts, orders)], axis=0)


def device_index():
    return (
        (lax.axis_index("x") * 2 + lax.axis_index("core")) * lax.axis_size("ctx")
        + lax.axis_index("ctx")
    ).astype(jnp.int32)


def splits_rows(rows):
    along_x, along_y, along_z = bit_groups()
    return (len(along_x), len(along_y), len(along_z)) == (1, 1, 2) and rows % 64 == 0


def spread(values, order):
    values = values[None]
    for where in order:
        values = double(values, where)
    return values


def double(values, where):
    return jnp.concatenate([values, swap(values, where)], axis=0)


def ctx_orders():
    along_x, along_y, along_z = bit_groups()
    return [along_y + along_z, along_z + along_y]


def row_cuts(rows):
    first = -(-rows // 32) * 16
    return [(0, first), (first, rows)]


def slot_bits():
    along_x, along_y, along_z = bit_groups()
    return list(reversed(along_z)) + along_y


def total_low(*terms):
    total = terms[0].astype(jnp.float32)
    for term in terms[1:]:
        total = total + term.astype(jnp.float32)
    return total.astype(jnp.bfloat16)


def reduce_far(rest):
    return swap(total_low(*[part[1] for part in rest]), slot_bits()[0])


def reduce_end(rest, z_far):
    total = z_far.astype(jnp.float32)
    for part in rest:
        total = total + part[0].astype(jnp.float32)
    return total


def reduce_halves(keep, away, ride, beside):
    far_z, near_z, along_y = slot_bits()
    come = beside(0, swap(away, ("core", 0)))
    sums = []
    for (low, high), order in zip(
        row_cuts(keep.shape[1]), ([along_y, near_z, far_z], [near_z, far_z, along_y])
    ):
        shape = (2, 2, 2, high - low, keep.shape[2])
        terms = [keep[:, low:high].reshape(shape), come[:, low:high].reshape(shape)]
        left = [along_y, near_z, far_z]
        for position, where in enumerate(order):
            dim = left.index(where)
            left.remove(where)
            sent = total_low(*[lax.index_in_dim(term, 1, dim, False) for term in terms])
            if low == 0:
                arrived, ride = swap_with(sent, ride, where)
                arrived = beside(position + 1, arrived)
            else:
                arrived = swap(sent, where)
            terms = [lax.index_in_dim(term, 0, dim, False) for term in terms] + [arrived]
        total = terms[0].astype(jnp.float32)
        for term in terms[1:]:
            total = total + term.astype(jnp.float32)
        sums.append(total)
    return jnp.concatenate(sums, axis=0), ride


def ride_parts(ride):
    rounded = lax.reduce_precision(ride, 8, 7)
    return rounded, lax.reduce_precision(ride - rounded, 8, 7)


def with_ride(sent, parts):
    extra = jnp.concatenate([*parts, jnp.zeros((12, parts[0].shape[1]), jnp.float32)])
    return jnp.concatenate([sent.reshape(-1, sent.shape[-1]), extra.astype(jnp.bfloat16)], axis=0)


def swap_with(sent, ride, where):
    parts = ride_parts(ride)
    come, other = off_ride(swap(with_ride(sent, parts), where), sent.shape)
    return come, (parts[0] + parts[1]) + other


def off_ride(come, shape):
    parts = come[-16:].astype(jnp.float32)
    return come[:-16].reshape(shape), parts[0:2] + parts[2:4]


def gather_halves(weights):
    rows = weights.shape[0]
    x_index, core = lax.axis_index("x"), lax.axis_index("core")
    half = rows // 2
    far = swap(weights, ("x", 0))
    low = jnp.where(x_index == 0, weights, far)
    high = jnp.where(x_index == 0, far, weights)
    both = jnp.stack([low, high])
    keep = jnp.where(core == 0, both[:, :half], both[:, half:])
    come = swap(jnp.where(core == 0, both[:, half:], both[:, :half]), ("core", 0))
    first = jnp.where(core == 0, keep, come)
    second = jnp.where(core == 0, come, keep)
    feed = jnp.stack([second[0], first[1], second[1]])
    return first[0], jnp.where(x_index == 0, feed[:, : half // 2], feed[:, half // 2 :])


def place_rows(own, far):
    tables = [rel_offsets(list(reversed(order))) for order in ctx_orders()]
    slots, width = own[0].shape[0], own[0].shape[2]
    lengths = [part.shape[1] for part in own]
    half = sum(lengths)

    def body(me_ref, *refs):
        out_ref = refs[-1]
        for core in range(2):

            @pl.when(me_ref[0] == core)
            def _(core=core):
                for source, base in ((0, core * half), (2, (1 - core) * half)):
                    out_ref[0, base : base + lengths[0]] = refs[source][0]
                    out_ref[0, base + lengths[0] : base + half] = refs[source + 1][0]

    specs = [
        pl.BlockSpec(
            (1, length, width),
            lambda step, me_ref, table=table: (find(step ^ me_ref[1], table), 0, 0),
        )
        for length, table in zip(lengths, tables)
    ]
    me = jnp.stack([lax.axis_index("core"), lax.axis_index("ctx")]).astype(jnp.int32)
    return pl.pallas_call(
        body,
        grid_spec=pltpu.PrefetchScalarGridSpec(
            num_scalar_prefetch=1,
            grid=(slots,),
            in_specs=specs * 2,
            out_specs=pl.BlockSpec((1, 2 * half, width), lambda step, me_ref: (step, 0, 0)),
        ),
        out_shape=jax.ShapeDtypeStruct((slots, 2 * half, width), own[0].dtype),
        cost_estimate=pl.CostEstimate(
            flops=0, bytes_accessed=8 * slots * half * width, transcendentals=0
        ),
        compiler_params=pltpu.CompilerParams(vmem_limit_bytes=VMEM_BYTES),
    )(me, *own, *far).reshape(slots * 2 * half, width)


def turned(values):
    return jnp.transpose(values)


def load_packed(ref, aligned):
    if not aligned:
        return ref[0, 0]
    half = ref.shape[1] // 2
    return jnp.concatenate(
        [
            ref[head * HD : (head + 1) * HD, side * half : (side + 1) * half]
            for side in range(2)
            for head in range(GROUP)
        ],
        axis=1,
    )


def store_packed(ref, values, aligned):
    if not aligned:
        ref[0, 0] = values
        return
    half = ref.shape[1] // 2
    for side in range(2):
        for head in range(GROUP):
            start = (side * GROUP + head) * half
            ref[head * HD : (head + 1) * HD, side * half : (side + 1) * half] = values[
                :, start : start + half
            ]


def load_tile(refs, side, tile):
    length = refs[0].shape[1] // 2
    if length >= KEY_TILE:
        start = side * length + tile * KEY_TILE
        return refs[0][:, start : start + KEY_TILE]
    many = KEY_TILE // length
    return jnp.concatenate(
        [
            ref[:, side * length : (side + 1) * length]
            for ref in refs[tile * many : (tile + 1) * many]
        ],
        axis=1,
    )


def attend_body(count, aligned, queries_ref, key_pos_ref, query_pos_ref, *refs):
    key_refs, value_refs = refs[:count], refs[count : 2 * count]
    out_ref, total_ref, work = refs[2 * count :]
    queries = load_packed(queries_ref, aligned)
    low_cols = queries.shape[1] // 2
    queries_high = queries[:, low_cols:]
    tiles = key_pos_ref.shape[1] // KEY_TILE
    largest = jnp.full((1, queries.shape[1]), HIDDEN, jnp.float32)
    largest_high = jnp.full((1, low_cols), HIDDEN, jnp.float32)
    for side in range(2):
        for tile in range(tiles):
            keys = turned(load_tile(key_refs, side, tile))
            row = (side * tiles + tile) * KEY_TILE
            key_places = key_pos_ref[side, tile * KEY_TILE : (tile + 1) * KEY_TILE]
            if side == 0:
                scores = matmul_n(keys, queries)
                scores = jnp.where(key_places <= query_pos_ref[...], scores, HIDDEN)
                work[row : row + KEY_TILE] = scores
                largest = jnp.maximum(largest, jnp.max(scores, axis=0, keepdims=True))
            else:
                scores = matmul_n(keys, queries_high)
                scores = jnp.where(key_places <= query_pos_ref[:, low_cols:], scores, HIDDEN)
                work[row : row + KEY_TILE, low_cols:] = scores
                largest_high = jnp.maximum(largest_high, jnp.max(scores, axis=0, keepdims=True))
    high_max = jnp.maximum(largest[:, low_cols:], largest_high)
    largest = jnp.concatenate([largest[:, :low_cols], high_max], axis=1)
    total = jnp.zeros_like(largest)
    mixed = jnp.zeros((HD, queries.shape[1]), jnp.float32)
    total_high = jnp.zeros_like(largest_high)
    mixed_high = jnp.zeros((HD, low_cols), jnp.float32)
    for side in range(2):
        for tile in range(tiles):
            values = load_tile(value_refs, side, tile)
            row = (side * tiles + tile) * KEY_TILE
            if side == 0:
                expos = jnp.exp(work[row : row + KEY_TILE] - largest)
                total = total + jnp.sum(expos, axis=0, keepdims=True)
                mixed = mixed + matmul_n(values, expos.astype(jnp.bfloat16))
            else:
                expos = jnp.exp(work[row : row + KEY_TILE, low_cols:] - high_max)
                total_high = total_high + jnp.sum(expos, axis=0, keepdims=True)
                mixed_high = mixed_high + matmul_n(values, expos.astype(jnp.bfloat16))
    total = jnp.concatenate([total[:, :low_cols], total[:, low_cols:] + total_high], axis=1)
    mixed = jnp.concatenate([mixed[:, :low_cols], mixed[:, low_cols:] + mixed_high], axis=1)
    store_packed(out_ref, (mixed / total).astype(jnp.bfloat16), aligned)
    total_ref[0, 0] = largest + jnp.log(total)


def attend_back_body(
    count, aligned, queries_ref, key_pos_ref, query_pos_ref, *refs
):
    key_refs, value_refs = refs[:count], refs[count : 2 * count]
    out_ref, total_ref, d_out_ref, cosine_ref, sine_ref = refs[2 * count : 2 * count + 5]
    d_queries_ref, pair_refs = refs[2 * count + 5], refs[2 * count + 6 :]
    all_queries, all_d_out = load_packed(queries_ref, aligned), load_packed(d_out_ref, aligned)
    low_cols = all_queries.shape[1] // 2
    tiles = key_pos_ref.shape[1] // KEY_TILE
    delta = jnp.sum(
        all_d_out.astype(jnp.float32) * load_packed(out_ref, aligned).astype(jnp.float32),
        axis=0,
        keepdims=True,
    )
    totals = total_ref[0, 0]
    parts = []
    for side in range(2):
        if side == 0:
            queries, d_out = all_queries, all_d_out
            query_places, log_total, row_delta = query_pos_ref[...], totals, delta
        else:
            queries, d_out = all_queries[:, low_cols:], all_d_out[:, low_cols:]
            query_places = query_pos_ref[:, low_cols:]
            log_total, row_delta = totals[:, low_cols:], delta[:, low_cols:]
        part = jnp.zeros((HD, queries.shape[1]), jnp.float32)
        for tile in range(tiles):
            keys_flat = load_tile(key_refs, side, tile)
            scores = matmul_n(turned(keys_flat), queries)
            seen = key_pos_ref[side, tile * KEY_TILE : (tile + 1) * KEY_TILE] <= query_places
            probs = jnp.where(seen, jnp.exp(scores - log_total), 0.0)
            d_probs = matmul_n(turned(load_tile(value_refs, side, tile)), d_out)
            d_scores = (probs * (d_probs - row_delta)).astype(jnp.bfloat16)
            part = part + matmul_n(keys_flat, d_scores)
            d_key = matmul_t(d_scores, queries).astype(jnp.bfloat16)
            d_value = matmul_t(probs.astype(jnp.bfloat16), d_out).astype(jnp.bfloat16)
            if aligned:
                length = key_refs[0].shape[1] // 2
                places_out = [(ref, slot) for ref in pair_refs for slot in range(ref.shape[0])]
                for piece in range(KEY_TILE // length):
                    ref, slot = places_out[tile * (KEY_TILE // length) + piece]
                    rows = slice(piece * length, (piece + 1) * length)
                    ref[slot, 0, side, :, :HD] = d_key[rows]
                    ref[slot, 0, side, :, HD:] = d_value[rows]
            else:
                rows = slice(tile * KEY_TILE, (tile + 1) * KEY_TILE)
                pair_refs[0][side, 0, rows, :HD] = d_key
                pair_refs[0][side, 0, rows, HD:] = d_value
        parts.append(part)
    d_queries = jnp.concatenate(
        [parts[0][:, :low_cols], parts[0][:, low_cols:] + parts[1]], axis=1
    )
    cosine, sine_part = cosine_ref[...], sine_ref[...]
    first_half, second_half = d_queries[: HD // 2], d_queries[HD // 2 :]
    turned_back = jnp.concatenate(
        [
            first_half * cosine + second_half * sine_part,
            second_half * cosine - first_half * sine_part,
        ],
        axis=0,
    )
    store_packed(d_queries_ref, (turned_back * SCALE_QK).astype(jnp.bfloat16), aligned)


def own_mask(rows, cols):
    return lax.broadcasted_iota(jnp.int32, (rows, cols), 0) <= (
        lax.broadcasted_iota(jnp.int32, (rows, cols), 1) % rows
    )


def slot_keys(ref, length):
    both = turned(ref[...])
    return both[:length], both[length:]


def attend_slots_body(count, flags_ref, queries_ref, *refs):
    key_refs, value_refs = refs[:count], refs[count : 2 * count]
    out_ref, total_ref, both_queries, work, largest, totals, mixed = refs[2 * count :]
    length = key_refs[0].shape[1] // 2
    cols = GROUP * length
    packed = load_packed(queries_ref, True)
    for side in range(2):
        both_queries[side] = packed[:, side * cols : (side + 1) * cols]
    visible = own_mask(length, cols)
    low_keys, high_keys = zip(*[slot_keys(ref, length) for ref in key_refs])
    row = 0

    def keep_scores(scores, row):
        work[row : row + scores.shape[0]] = scores
        return jnp.max(scores, axis=0, keepdims=True)

    for side, keys in ((0, low_keys[0]), (1, high_keys[0])):
        scores = jnp.where(visible, matmul_n(keys, both_queries[side]), HIDDEN)
        largest[side] = keep_scores(scores, row)
        row += length
    for slot in range(0, count, 2):
        keys = jnp.concatenate([low_keys[slot], low_keys[slot + 1]], axis=0)
        top = keep_scores(matmul_n(keys, both_queries[1]), row)
        largest[1] = jnp.maximum(largest[1], top)
        row += 2 * length
    for slot in range(1, count):
        side = flags_ref[slot]
        keys = jnp.where(side == 0, low_keys[slot], high_keys[slot])
        top = keep_scores(matmul_n(keys, both_queries[side]), row)
        largest[side] = jnp.maximum(largest[side], top)
        row += length
    row = 0
    for side in range(2):
        values = value_refs[0][:, side * length : (side + 1) * length]
        expos = jnp.exp(work[row : row + length] - largest[side])
        totals[side] = jnp.sum(expos, axis=0, keepdims=True)
        mixed[side] = matmul_n(values, expos.astype(jnp.bfloat16))
        row += length
    for slot in range(0, count, 2):
        values = jnp.concatenate(
            [value_refs[slot][:, :length], value_refs[slot + 1][:, :length]], axis=1
        )
        expos = jnp.exp(work[row : row + 2 * length] - largest[1])
        totals[1] += jnp.sum(expos, axis=0, keepdims=True)
        mixed[1] += matmul_n(values, expos.astype(jnp.bfloat16))
        row += 2 * length
    for slot in range(1, count):
        side = flags_ref[slot]
        values = jnp.where(side == 0, value_refs[slot][:, :length], value_refs[slot][:, length:])
        expos = jnp.exp(work[row : row + length] - largest[side])
        totals[side] += jnp.sum(expos, axis=0, keepdims=True)
        mixed[side] += matmul_n(values, expos.astype(jnp.bfloat16))
        row += length
    result = [(mixed[side] / totals[side]).astype(jnp.bfloat16) for side in range(2)]
    store_packed(out_ref, jnp.concatenate(result, axis=1), True)
    logs = [largest[side] + jnp.log(totals[side]) for side in range(2)]
    total_ref[0, 0] = jnp.concatenate(logs, axis=1)


def attend_slots_back_body(count, flags_ref, queries_ref, *refs):
    key_refs, value_refs = refs[:count], refs[count : 2 * count]
    out_ref, total_ref, d_out_ref, cosine_ref, sine_ref = refs[2 * count : 2 * count + 5]
    d_queries_ref = refs[2 * count + 5]
    pair_refs = refs[2 * count + 6 : -7]
    both_queries, both_d_out, turned_queries, turned_d_out, log_totals, deltas, sums = refs[-7:]
    length = key_refs[0].shape[1] // 2
    cols = GROUP * length
    queries, d_out = load_packed(queries_ref, True), load_packed(d_out_ref, True)
    delta = jnp.sum(
        d_out.astype(jnp.float32) * load_packed(out_ref, True).astype(jnp.float32),
        axis=0,
        keepdims=True,
    )
    for side in range(2):
        part = slice(side * cols, (side + 1) * cols)
        both_queries[side] = queries[:, part]
        both_d_out[side] = d_out[:, part]
        turned_queries[side] = turned(queries[:, part])
        turned_d_out[side] = turned(d_out[:, part])
        log_totals[side] = total_ref[0, 0, :, part]
        deltas[side] = delta[:, part]
    sums[...] = jnp.zeros_like(sums)
    visible = own_mask(length, cols)
    low_keys, high_keys = zip(*[slot_keys(ref, length) for ref in key_refs])
    low_values, high_values = zip(*[slot_keys(ref, length) for ref in value_refs])
    places_out = [(ref, slot) for ref in pair_refs for slot in range(ref.shape[0])]

    def block(keys, keys_flat, values, side, mask=None):
        probs = jnp.exp(matmul_n(keys, both_queries[side]) - log_totals[side])
        if mask is not None:
            probs = jnp.where(mask, probs, 0.0)
        d_probs = matmul_n(values, both_d_out[side])
        d_scores = (probs * (d_probs - deltas[side])).astype(jnp.bfloat16)
        sums[side] += matmul_n(keys_flat, d_scores)
        return jnp.concatenate(
            [
                matmul_n(d_scores, turned_queries[side]),
                matmul_n(probs.astype(jnp.bfloat16), turned_d_out[side]),
            ],
            axis=1,
        )

    low_terms = []
    for slot in range(0, count, 2):
        keys, values = [
            jnp.concatenate([part[slot], part[slot + 1]], axis=0) for part in (low_keys, low_values)
        ]
        flat = jnp.concatenate([key_refs[slot][:, :length], key_refs[slot + 1][:, :length]], axis=1)
        terms = block(keys, flat, values, 1)
        low_terms += [terms[:length], terms[length:]]
    ref, slot = places_out[0]
    own = [
        block(keys, key_refs[0][:, side * length : (side + 1) * length], values, side, visible)
        for side, (keys, values) in enumerate(
            ((low_keys[0], low_values[0]), (high_keys[0], high_values[0]))
        )
    ]
    ref[slot, 0, 0] = (low_terms[0] + own[0]).astype(jnp.bfloat16)
    ref[slot, 0, 1] = own[1].astype(jnp.bfloat16)
    for member in range(1, count):
        side = flags_ref[member]
        low = side == 0
        keys = jnp.where(low, low_keys[member], high_keys[member])
        flat = jnp.where(low, key_refs[member][:, :length], key_refs[member][:, length:])
        values = jnp.where(low, low_values[member], high_values[member])
        terms = block(keys, flat, values, side)
        ref, slot = places_out[member]
        ref[slot, 0, 0] = (low_terms[member] + jnp.where(low, terms, 0.0)).astype(jnp.bfloat16)
        ref[slot, 0, 1] = jnp.where(low, 0.0, terms).astype(jnp.bfloat16)
    d_queries = jnp.concatenate([sums[0], sums[1]], axis=1)
    store_packed(d_queries_ref, turn_queries_back(d_queries, cosine_ref, sine_ref), True)


def turn_queries_back(d_queries, cosine_ref, sine_ref):
    cosine, sine_part = cosine_ref[...], sine_ref[...]
    first_half, second_half = d_queries[: HD // 2], d_queries[HD // 2 :]
    turned_back = jnp.concatenate(
        [
            first_half * cosine + second_half * sine_part,
            second_half * cosine - first_half * sine_part,
        ],
        axis=0,
    )
    return (turned_back * SCALE_QK).astype(jnp.bfloat16)


def slot_specs(leads, local_rows, seq):
    specs = [
        pl.BlockSpec(memory_space=pltpu.SMEM),
        pl.BlockSpec((GROUP * HD, local_rows), lambda head: (head, seq)),
    ]
    for first in (0, KV):
        specs += [
            pl.BlockSpec(
                (None, HD, local_rows),
                lambda head, lead=lead, first=first: (lead, first + head, 0),
            )
            for lead in leads
        ]
    return specs


def attend_slots(queries, pairs, flags, local_rows, seq):
    count, cols = len(pairs), GROUP * local_rows // 2
    leads, arrays = [lead for _, lead in pairs], [array for array, _ in pairs]
    work = HEADS * local_rows * local_rows * count // 2
    return pl.pallas_call(
        lambda *refs: attend_slots_body(count, *refs),
        grid=(KV,),
        in_specs=slot_specs(leads, local_rows, seq),
        out_specs=[
            pl.BlockSpec((GROUP * HD, local_rows), lambda head: (head, 0)),
            pl.BlockSpec((1, 1, 1, 2 * cols), lambda head: (0, head, 0, 0)),
        ],
        out_shape=[
            jax.ShapeDtypeStruct((HEADS * HD, local_rows), jnp.bfloat16),
            jax.ShapeDtypeStruct((1, KV, 1, 2 * cols), jnp.float32),
        ],
        scratch_shapes=[
            pltpu.VMEM((2, HD, cols), jnp.bfloat16),
            pltpu.VMEM(((2 * count + 1) * local_rows // 2, cols), jnp.float32),
            pltpu.VMEM((2, 1, cols), jnp.float32),
            pltpu.VMEM((2, 1, cols), jnp.float32),
            pltpu.VMEM((2, HD, cols), jnp.float32),
        ],
        cost_estimate=pl.CostEstimate(
            flops=work * HD, bytes_accessed=1024 * 1024, transcendentals=0
        ),
        compiler_params=pltpu.CompilerParams(vmem_limit_bytes=VMEM_BYTES),
    )(flags, queries, *arrays, *arrays)


def attend_slots_back(
    queries, pairs, flags, mixed, log_total, d_mixed, tables, local_rows, seq, sets
):
    count, cols = len(pairs), GROUP * local_rows // 2
    leads, arrays = [lead for _, lead in pairs], [array for array, _ in pairs]
    work = HEADS * local_rows * local_rows * count // 2
    own = pl.BlockSpec((GROUP * HD, local_rows), lambda head: (head, 0))
    table_spec = pl.BlockSpec((HD // 2, 2 * cols), lambda head: (0, 0))
    length = local_rows // 2
    return pl.pallas_call(
        lambda *refs: attend_slots_back_body(count, *refs),
        grid=(KV,),
        in_specs=slot_specs(leads, local_rows, seq)
        + [
            own,
            pl.BlockSpec((1, 1, 1, 2 * cols), lambda head: (0, head, 0, 0)),
            pl.BlockSpec((GROUP * HD, local_rows), lambda head: (head, seq)),
            table_spec,
            table_spec,
        ],
        out_specs=[own]
        + [
            pl.BlockSpec((slots, 1, 2, length, 2 * HD), lambda head: (0, head, 0, 0, 0))
            for slots in sets
        ],
        out_shape=[jax.ShapeDtypeStruct((HEADS * HD, local_rows), jnp.bfloat16)]
        + [jax.ShapeDtypeStruct((slots, KV, 2, length, 2 * HD), jnp.bfloat16) for slots in sets],
        scratch_shapes=[
            pltpu.VMEM((2, HD, cols), jnp.bfloat16),
            pltpu.VMEM((2, HD, cols), jnp.bfloat16),
            pltpu.VMEM((2, cols, HD), jnp.bfloat16),
            pltpu.VMEM((2, cols, HD), jnp.bfloat16),
            pltpu.VMEM((2, 1, cols), jnp.float32),
            pltpu.VMEM((2, 1, cols), jnp.float32),
            pltpu.VMEM((2, HD, cols), jnp.float32),
        ],
        cost_estimate=pl.CostEstimate(
            flops=work * HD, bytes_accessed=1024 * 1024, transcendentals=0
        ),
        compiler_params=pltpu.CompilerParams(vmem_limit_bytes=VMEM_BYTES),
    )(flags, queries, *arrays, *arrays, mixed, log_total, d_mixed, *tables)


def head_specs(leads, aligned, cols, keys, local_rows, seq):
    count = len(leads)
    if aligned:
        packed = pl.BlockSpec((GROUP * HD, local_rows), lambda head: (head, seq))
    else:
        packed = pl.BlockSpec((1, 1, HD, cols), lambda head: (seq, head, 0, 0))
    specs = [
        packed,
        pl.BlockSpec((2, keys, 1), lambda head: (0, 0, 0)),
        pl.BlockSpec((1, cols), lambda head: (0, 0)),
    ]
    for first in (0, KV):
        specs += [
            pl.BlockSpec(
                (None, HD, 2 * keys // count),
                lambda head, lead=lead, first=first: (lead, first + head, seq),
            )
            for lead in leads
        ]
    return packed, specs


def attend(queries, pairs, key_pos, query_pos, local_rows, seq):
    aligned = queries.ndim == 2
    cols, keys, count = query_pos.shape[1], key_pos.shape[1], len(pairs)
    leads, arrays = [lead for _, lead in pairs], [array for array, _ in pairs]
    _, specs = head_specs(leads, aligned, cols, keys, local_rows, seq)
    work = HEADS * keys * cols // GROUP * 3 // 2
    if aligned:
        out_spec = pl.BlockSpec((GROUP * HD, local_rows), lambda head: (head, 0))
        out_shape = jax.ShapeDtypeStruct((HEADS * HD, local_rows), jnp.bfloat16)
    else:
        out_spec = pl.BlockSpec((1, 1, HD, cols), lambda head: (0, head, 0, 0))
        out_shape = jax.ShapeDtypeStruct((1, KV, HD, cols), jnp.bfloat16)
    return pl.pallas_call(
        lambda *refs: attend_body(count, aligned, *refs),
        grid=(KV,),
        in_specs=specs,
        out_specs=[out_spec, pl.BlockSpec((1, 1, 1, cols), lambda head: (0, head, 0, 0))],
        out_shape=[out_shape, jax.ShapeDtypeStruct((1, KV, 1, cols), jnp.float32)],
        scratch_shapes=[pltpu.VMEM((2 * keys, cols), jnp.float32)],
        cost_estimate=pl.CostEstimate(
            flops=work * HD, bytes_accessed=1024 * 1024, transcendentals=0
        ),
        compiler_params=pltpu.CompilerParams(vmem_limit_bytes=VMEM_BYTES),
    )(queries, key_pos, query_pos, *arrays, *arrays)


def attend_back(
    queries, pairs, key_pos, query_pos, mixed, log_total, d_mixed, tables, local_rows, seq, sets
):
    aligned = queries.ndim == 2
    cols, keys, count = query_pos.shape[1], key_pos.shape[1], len(pairs)
    leads, arrays = [lead for _, lead in pairs], [array for array, _ in pairs]
    packed, specs = head_specs(leads, aligned, cols, keys, local_rows, seq)
    work = HEADS * keys * cols // GROUP * 3 // 2
    if aligned:
        own = pl.BlockSpec((GROUP * HD, local_rows), lambda head: (head, 0))
        own_shape = jax.ShapeDtypeStruct((HEADS * HD, local_rows), jnp.bfloat16)
        length = keys // count
        pair_specs = [
            pl.BlockSpec((slots, 1, 2, length, 2 * HD), lambda head: (0, head, 0, 0, 0))
            for slots in sets
        ]
        pair_shapes = [
            jax.ShapeDtypeStruct((slots, KV, 2, length, 2 * HD), jnp.bfloat16) for slots in sets
        ]
    else:
        own = pl.BlockSpec((1, 1, HD, cols), lambda head: (0, head, 0, 0))
        own_shape = jax.ShapeDtypeStruct((1, KV, HD, cols), jnp.bfloat16)
        pair_specs = [pl.BlockSpec((2, 1, keys, 2 * HD), lambda head: (0, head, 0, 0))]
        pair_shapes = [jax.ShapeDtypeStruct((2, KV, keys, 2 * HD), jnp.bfloat16)]
    table_spec = pl.BlockSpec((HD // 2, cols), lambda head: (0, 0))
    return pl.pallas_call(
        lambda *refs: attend_back_body(count, aligned, *refs),
        grid=(KV,),
        in_specs=specs
        + [
            own,
            pl.BlockSpec((1, 1, 1, cols), lambda head: (0, head, 0, 0)),
            packed,
            table_spec,
            table_spec,
        ],
        out_specs=[own] + pair_specs,
        out_shape=[own_shape] + pair_shapes,
        cost_estimate=pl.CostEstimate(
            flops=work * HD, bytes_accessed=1024 * 1024, transcendentals=0
        ),
        compiler_params=pltpu.CompilerParams(vmem_limit_bytes=VMEM_BYTES),
    )(queries, key_pos, query_pos, *arrays, *arrays, mixed, log_total, d_mixed, *tables)


def put_rows(values, keep_ref, away_ref, place, core, x_index):
    quarter = values.shape[0] // 4
    for mine in range(4):

        @pl.when(2 * core + x_index == mine)
        def _(mine=mine):
            for ref, side in ((keep_ref, mine // 2), (away_ref, 1 - mine // 2)):
                for position, along_x in enumerate((mine % 2, 1 - mine % 2)):
                    start = (2 * side + along_x) * quarter
                    ref[place[0], place[1], position * quarter : (position + 1) * quarter] = values[
                        start : start + quarter
                    ]


def feed_body(
    parts, split, chained, me_ref, a_two_ref, dy_ref, *refs
):
    count = 4 if split else 6
    before, refs = (refs[:2], refs[2:]) if chained else (None, refs)
    weight_refs, (out_ref, d_two_ref), grad_refs = (
        refs[:count],
        refs[count : count + 2],
        refs[count + 2 :],
    )
    core, x_index = me_ref[0], me_ref[1]
    step = pl.program_id(0)

    @pl.when(step == 0)
    def _():
        for place, ref in enumerate((out_ref, d_two_ref)):
            ref[...] = before[place][...] if chained else jnp.zeros_like(ref)

    def rows_of(member):
        if split:
            rows_out = []
            for slot in range(weight_refs[0].shape[0]):
                parts_here = [ref[slot, member] for ref in weight_refs]
                for side in range(2):
                    for along_x in range(2):
                        near = jnp.where(x_index == along_x, parts_here[0], parts_here[1])
                        far = jnp.where(x_index == along_x, parts_here[2], parts_here[3])
                        rows_out.append(jnp.where(core == side, near, far))
            return jnp.concatenate(rows_out, axis=0)
        wanted = feed_core(member, step, parts)
        return jnp.where(wanted == core, weight_refs[2 * member][0], weight_refs[2 * member + 1][0])

    a_two, dy_low = a_two_ref[...], dy_ref[...]
    gate_rows, up_rows, down_rows = rows_of(0), rows_of(1), rows_of(2)
    gate_pre = matmul_t(gate_rows, a_two)
    up_pre = matmul_t(up_rows, a_two)
    d_hidden = matmul_t(down_rows, dy_low)
    sigma = jax.nn.sigmoid(gate_pre)
    gate_act = gate_pre * sigma
    hidden = (gate_act * up_pre).astype(jnp.bfloat16)
    d_gate = (d_hidden * up_pre * sigma * (1.0 + gate_pre * (1.0 - sigma))).astype(jnp.bfloat16)
    d_up = (d_hidden * gate_act).astype(jnp.bfloat16)
    out_ref[...] += matmul_c(hidden, down_rows)
    d_two_ref[...] += matmul_c(d_gate, gate_rows) + matmul_c(d_up, up_rows)
    for member, (left, right) in enumerate(((d_gate, a_two), (d_up, a_two), (hidden, dy_low))):
        grad = matmul_n(left, right).astype(jnp.bfloat16)
        if split:
            slots = grad_refs[0].shape[0]
            rows = grad.shape[0] // slots
            for slot in range(slots):
                put_rows(
                    grad[slot * rows : (slot + 1) * rows], *grad_refs, (slot, member), core, x_index
                )
        else:
            grad_refs[member][0] = grad


def feed_core(member, step, parts):
    ctx_count, single = parts
    return (member + 1) % 2 if single else step // ctx_count


def feed_forward(a_two, dy_low, mine, far, rows, before=()):
    tokens, width = a_two.shape
    ctx_count = lax.axis_size("ctx")
    blocks = FF // rows
    single = blocks == ctx_count
    split = mine[0].ndim == 4 if isinstance(mine, list) else False
    parts = (ctx_count, single)
    whole = pl.BlockSpec((tokens, width), lambda step, me_ref: (0, 0))

    def weight_spec(member, own):
        first = (member + 1) * blocks // ctx_count // 2 * ctx_count

        def index(step, me_ref):
            matches = (feed_core(member, step, parts) == me_ref[0]) == own
            return (first + jnp.where(matches, step % ctx_count, 0), 0, 0)

        return pl.BlockSpec((1, rows, width), index)

    if split:
        weight_specs = [
            pl.BlockSpec((2, 3, rows // 4, width), lambda step, me_ref: (step, 0, 0, 0))
        ] * 4
        weight_args = [*mine, *far]
        half = pl.BlockSpec((2, 3, rows // 2, width), lambda step, me_ref: (step, 0, 0, 0))
        grad_specs = [half, half]
        blocks = mine[0].shape[0]
        grad_shapes = [jax.ShapeDtypeStruct((blocks, 3, rows // 2, width), jnp.bfloat16)] * 2
    else:
        weight_specs = [weight_spec(member, own) for member in range(3) for own in (True, False)]
        weight_args = [mine, far] * 3
        grad_specs = [pl.BlockSpec((1, rows, width), lambda step, me_ref: (step, 0, 0))] * 3
        grad_shapes = [jax.ShapeDtypeStruct((blocks, rows, width), jnp.bfloat16)] * 3
    me = jnp.stack([lax.axis_index("core"), lax.axis_index("x")]).astype(jnp.int32)
    return pl.pallas_call(
        lambda *refs: feed_body(parts, split, bool(before), *refs),
        grid_spec=pltpu.PrefetchScalarGridSpec(
            num_scalar_prefetch=1,
            grid=(blocks // 2 if split else blocks,),
            in_specs=[whole] * (2 + len(before)) + weight_specs,
            out_specs=[whole, whole] + grad_specs,
        ),
        out_shape=[jax.ShapeDtypeStruct((tokens, width), jnp.float32)] * 2 + grad_shapes,
        cost_estimate=pl.CostEstimate(
            flops=18 * tokens * width * blocks * rows, bytes_accessed=12 * blocks * rows * width,
            transcendentals=0,
        ),
        compiler_params=pltpu.CompilerParams(vmem_limit_bytes=VMEM_BYTES),
    )(me, a_two, dy_low, *before, *weight_args)


def first_grads(d_qkv, attn_low, a_one, d_resid_low, rows, split):
    tokens, width = a_one.shape
    early = d_qkv.shape[0] // rows
    blocks = early + attn_low.shape[0] // rows

    def body(me_ref, qkv_ref, attn_ref, one_ref, resid_ref, *grad_refs):
        first = pl.program_id(0) < early
        left = jnp.where(first, qkv_ref[...], attn_ref[...])
        right = jnp.where(first, one_ref[...], resid_ref[...])
        grad = matmul_n(left, right).astype(jnp.bfloat16)
        if split:
            put_rows(grad, *grad_refs, (0, 0), me_ref[0], 0)
        else:
            grad_refs[0][0] = grad

    whole = pl.BlockSpec((tokens, width), lambda step, me_ref: (0, 0))
    if split:
        table = rel_offsets(slot_bits())
        half = pl.BlockSpec(
            (1, 1, rows // 2, width), lambda step, me_ref: (find(step ^ me_ref[1], table), 0, 0, 0)
        )
        grad_specs = [half, half]
        grad_shapes = [jax.ShapeDtypeStruct((blocks, 1, rows // 2, width), jnp.bfloat16)] * 2
    else:
        grad_specs = [pl.BlockSpec((1, rows, width), lambda step, me_ref: (step, 0, 0))]
        grad_shapes = [jax.ShapeDtypeStruct((blocks, rows, width), jnp.bfloat16)]
    me = jnp.stack([lax.axis_index(name) for name in ("core", "ctx")]).astype(jnp.int32)
    return pl.pallas_call(
        body,
        grid_spec=pltpu.PrefetchScalarGridSpec(
            num_scalar_prefetch=1,
            grid=(blocks,),
            in_specs=[
                pl.BlockSpec((rows, tokens), lambda step, me_ref: (jnp.minimum(step, early - 1), 0)),
                pl.BlockSpec((rows, tokens), lambda step, me_ref: (jnp.maximum(step - early, 0), 0)),
                whole,
                whole,
            ],
            out_specs=grad_specs,
        ),
        out_shape=grad_shapes,
        cost_estimate=pl.CostEstimate(
            flops=2 * tokens * width * blocks * rows, bytes_accessed=2 * blocks * rows * width, transcendentals=0
        ),
        compiler_params=pltpu.CompilerParams(vmem_limit_bytes=VMEM_BYTES),
    )(me, d_qkv, attn_low, a_one, d_resid_low)


def adam_update(param, grad, first, second, rate, decay, step_number):
    first_new = BETA_ONE * first + (1.0 - BETA_ONE) * grad
    second_new = BETA_TWO * second + (1.0 - BETA_TWO) * grad * grad
    fix_one = 1.0 - BETA_ONE**step_number
    fix_two = 1.0 - BETA_TWO**step_number
    update = first_new / fix_one / (jnp.sqrt(second_new / fix_two) + ADAM_EPS)
    return (first_new, second_new, param - rate * (update + decay * param))


def shards(inputs, cotangent, weights, gains, first_moment, second_moment, gain_first, gain_second):
    ctx_count = lax.axis_size("ctx")
    x_count = lax.axis_size("x")
    ctx_index, core, x_index = lax.axis_index("ctx"), lax.axis_index("core"), lax.axis_index("x")
    seqs, local_rows, model_width = inputs.shape
    half_rows = local_rows // 2
    tokens = seqs * local_rows
    weight_rows = weights.shape[0]
    q_cols = HEADS * HD
    kv_cols = KV * HD
    cut_o = q_cols + 2 * kv_cols
    slots = slot_bits()
    aligned = splits_rows(weight_rows) and half_rows % 128 == 0 and seqs == 2
    split = aligned
    local_index = jnp.arange(local_rows, dtype=jnp.int32)
    pos_here = places(ctx_index * local_rows + local_index, local_rows, ctx_count)
    cosine, sine_part = angle_tables(pos_here, 1.0)
    turn = (jnp.tile(cosine, (1, seqs)), jnp.tile(sine_part, (1, seqs)))
    turn_back = (turn[0], -turn[1])

    def pack(flat):
        if aligned:
            return flat
        return (
            flat.reshape(KV, GROUP, HD, -1, 2, half_rows)
            .transpose(3, 0, 2, 4, 1, 5)
            .reshape(-1, KV, HD, 2 * GROUP * half_rows)
        )

    def unpack(packed):
        if aligned:
            return packed
        return (
            packed.reshape(KV, HD, 2, GROUP, half_rows)
            .transpose(0, 3, 1, 2, 4)
            .reshape(q_cols, local_rows)
        )

    def by_columns(row):
        rows = row.shape[0]
        return jnp.broadcast_to(
            row.reshape(rows, 2, 1, half_rows), (rows, 2, GROUP, half_rows)
        ).reshape(rows, 2 * GROUP * half_rows)

    owners = ctx_index ^ jnp.asarray(rel_offsets(slots), jnp.int32)
    flags = (owners > ctx_index).astype(jnp.int32)
    inner = jnp.arange(half_rows, dtype=jnp.int32)
    key_pos = jnp.stack(
        [
            (owners[:, None] * half_rows + inner[None, :]).reshape(-1, 1),
            ((2 * ctx_count - 1 - owners[:, None]) * half_rows + inner[None, :]).reshape(-1, 1),
        ]
    )
    query_pos = by_columns(pos_here[None, :])
    packed_tables = (by_columns(cosine), by_columns(sine_part))

    if split:
        first_half, feed_quarter = gather_halves(weights)
        cuts = row_cuts(weight_rows // 2)
        backward = [list(reversed(order)) for order in ctx_orders()]
        first_own = [spread(first_half[low:high], order) for (low, high), order in zip(cuts, backward)]
        feed_quarter, first_own = lax.optimization_barrier((feed_quarter, first_own))
        feed_far_z = swap(feed_quarter[None], slots[0])
        first_far = [swap(part, ("core", 0)) for part in first_own]
        first_rows = place_rows(first_own, first_far)
    else:
        mine = lax.all_gather(weights, ("x", "ctx"), axis=0, tiled=True)
        mine = mine.reshape(x_count * ctx_count, weight_rows, model_width)
        far = swap(mine, ("core", 0))
        sides = [
            jnp.where(core == 0, mine[:ctx_count], far[:ctx_count]),
            jnp.where(core == 0, far[:ctx_count], mine[:ctx_count]),
        ]
        first_rows = jnp.concatenate(sides).reshape(-1, model_width)
    qkv_rows, o_rows = first_rows[:cut_o], first_rows[cut_o : cut_o + q_cols]

    tokens_in, cot_in = lax.optimization_barrier(
        (inputs.reshape(tokens, model_width), cotangent.reshape(tokens, model_width))
    )
    dy_low = cot_in.astype(jnp.bfloat16)
    a_one = (normalize(tokens_in) * gains[0]).astype(jnp.bfloat16)
    pair_rows = matmul_t(qkv_rows[q_cols:], a_one)
    if split:
        pair_rows, feed_far_z = lax.optimization_barrier((pair_rows, feed_far_z))
    joined = jnp.concatenate(
        [rotate(pair_rows[:kv_cols], turn).astype(jnp.bfloat16), pair_rows[kv_cols:].astype(jnp.bfloat16)],
        axis=0,
    )
    if split:
        feed_own = jnp.concatenate([feed_quarter[None], feed_far_z], axis=0)
        joined, feed_own = lax.optimization_barrier((joined, feed_own))
    if aligned:
        mine_0, mine_1 = [
            joined[:, seq * local_rows : (seq + 1) * local_rows] for seq in range(2)
        ]
        far_0, own_y_0 = swap(mine_0, slots[0]), swap(mine_0, slots[2])
        feed_near, feed_y = swap(feed_own, slots[1]), swap(feed_own, slots[2])
        feed_x = swap(feed_own, ("x", 0))
        far_0, own_y_0, feed_near, feed_y, feed_x, mine_1 = lax.optimization_barrier(
            (far_0, own_y_0, feed_near, feed_y, feed_x, mine_1)
        )
        near_0, far_y_0 = swap(jnp.stack([mine_0, far_0]), slots[1]), swap(far_0, slots[2])
        far_1, own_y_1 = swap(mine_1, slots[0]), swap(mine_1, slots[2])
        near_x = swap(feed_near, ("x", 0))
        near_0, far_y_0, far_1, own_y_1, near_x, feed_y = lax.optimization_barrier(
            (near_0, far_y_0, far_1, own_y_1, near_x, feed_y)
        )
        near_y_0 = swap(near_0, slots[2])
        near_1, far_y_1 = swap(jnp.stack([mine_1, far_1]), slots[1]), swap(far_1, slots[2])
        y_x = swap(feed_y, ("x", 0))
        near_y_0, near_1, far_y_1, y_x, feed_near = lax.optimization_barrier(
            (near_y_0, near_1, far_y_1, y_x, feed_near)
        )
        near_y_1 = swap(near_1, slots[2])
        pairs = [
            [(own[None], 0), (far_z[None], 0), (near, 0), (near, 1)]
            + [(own_y[None], 0), (far_y[None], 0), (near_y, 0), (near_y, 1)]
            for own, far_z, near, own_y, far_y, near_y in (
                (mine_0, far_0, near_0, own_y_0, far_y_0, near_y_0),
                (mine_1, far_1, near_1, own_y_1, far_y_1, near_y_1),
            )
        ]
        feed_lower = [
            jnp.concatenate([feed_own, feed_near], axis=0),
            jnp.concatenate([feed_x, near_x], axis=0),
        ]
        feed_lower_far = [swap(part, ("core", 0)) for part in feed_lower]
    else:
        pairs = spread(joined, slots).reshape(ctx_count, 2 * kv_cols, seqs, 2, half_rows)
        pairs = [
            (
                pairs.transpose(1, 2, 3, 0, 4).reshape(
                    1, 2 * kv_cols, seqs * 2 * ctx_count * half_rows
                ),
                0,
            )
        ]
    q_rot = rotate(matmul_t(qkv_rows[:q_cols], a_one), turn).astype(jnp.bfloat16)
    queries = pack((q_rot * SCALE_QK).astype(jnp.bfloat16))
    attended = []
    for seq in range(seqs):
        if aligned:
            attended.append(attend_slots(queries, pairs[seq], flags, local_rows, seq))
            if seq == 0:
                attended, feed_near = lax.optimization_barrier((attended, feed_near))
                feed_near_y = swap(feed_near, slots[2])
        else:
            attended.append(attend(queries, pairs, key_pos, query_pos, local_rows, seq))
    attn_low = jnp.concatenate([unpack(mixed) for mixed, _ in attended], axis=1)
    resid = tokens_in + matmul_c(attn_low, o_rows)
    a_two = (normalize(resid) * gains[1]).astype(jnp.bfloat16)
    if aligned:
        a_two, feed_near_y = lax.optimization_barrier((a_two, feed_near_y))
        near_y_x = swap(feed_near_y, ("x", 0))
        upper_own = jnp.concatenate([feed_y, feed_near_y], axis=0)
        upper_far = swap(upper_own, ("core", 0))
        *sums_fed, keep_lower, away_lower = feed_forward(
            a_two, dy_low, feed_lower, feed_lower_far, weight_rows
        )
        sums_fed, near_y_x, upper_far = lax.optimization_barrier((sums_fed, near_y_x, upper_far))
        upper_x = jnp.concatenate([y_x, near_y_x], axis=0)
        come_lower = swap(away_lower, ("core", 0))
        fed, d_two, keep_upper, away_upper = feed_forward(
            a_two,
            dy_low,
            [upper_own, upper_x],
            [upper_far, swap(upper_x, ("core", 0))],
            weight_rows,
            sums_fed,
        )
        come_upper = swap(away_upper, ("core", 0))
    else:
        fed, d_two, *feed_grads = feed_forward(a_two, dy_low, mine, far, weight_rows)
    result = resid + fed
    d_norm_two, d_gain_two = norm_back(resid, d_two, gains[1])
    d_resid = cot_in + d_norm_two
    d_resid_low = d_resid.astype(jnp.bfloat16)
    d_attn = pack(matmul_t(o_rows, d_resid_low).astype(jnp.bfloat16))
    if aligned:
        quarter = weight_rows // 4
        held_upper, held_lower = [
            [(part[:, :, :quarter], part[:, :, quarter:]) for part in parts]
            for parts in ((keep_upper, come_upper), (keep_lower, come_lower))
        ]
        send_upper, send_lower = [
            total_low(*[far_part for _, far_part in parts]) for parts in (held_upper, held_lower)
        ]
        x_lower = swap(send_lower, ("x", 0))
        d_attn, send_upper = lax.optimization_barrier((d_attn, send_upper))
        x_upper = swap(send_upper, ("x", 0))
    d_q, d_pair = [], []
    for seq in range(seqs):
        mixed, log_total = attended[seq]
        if aligned:
            d_queries, *d_slots = attend_slots_back(
                queries, pairs[seq], flags, mixed, log_total, d_attn, packed_tables, local_rows, seq, (2, 2, 4)
            )
        else:
            d_queries, *d_slots = attend_back(
                queries, pairs, key_pos, query_pos, mixed, log_total, d_attn, packed_tables,
                local_rows, seq, (1,),
            )
        if aligned and seq == 0:
            d_slots, d_attn, x_lower = lax.optimization_barrier((d_slots, d_attn, x_lower))
        if aligned and seq == 1:
            d_slots, x_upper = lax.optimization_barrier((d_slots, x_upper))
            feed_y_come = swap(total_low(*[part for part, _ in held_upper], x_upper), slots[2])
        d_q.append(unpack(d_queries))
        if aligned:
            lower, near_part, upper = d_slots
            y_come = swap(upper, slots[2])
            near_come = swap(add_low(near_part, y_come[2:]), slots[1])
            far_come = swap(total_low(lower[1], y_come[1], near_come[1]), slots[0])
            if seq == 1:
                far_come, feed_y_come = lax.optimization_barrier((far_come, feed_y_come))
                rest = [part for part, _ in held_lower] + [x_lower, feed_y_come]
                feed_near_come = swap(total_low(*[part[2:] for part in rest]), slots[1])
            total = far_come.astype(jnp.float32)
            for part in (lower, y_come, near_come):
                total = total + part[0].astype(jnp.float32)
        else:
            total = collect(
                d_slots[0]
                .reshape(2, KV, ctx_count, half_rows, 2 * HD)
                .transpose(2, 1, 0, 3, 4),
                list(reversed(slots)),
            )
        d_pair.append(total)
    d_own = jnp.stack(d_pair).transpose(1, 4, 0, 2, 3).reshape(KV, 2 * HD, tokens)
    d_qkv = jnp.concatenate(
        [
            jnp.concatenate(d_q, axis=1),
            rotate(d_own[:, :HD].reshape(kv_cols, tokens), turn_back).astype(jnp.bfloat16),
            d_own[:, HD:].reshape(kv_cols, tokens).astype(jnp.bfloat16),
        ],
        axis=0,
    )
    first_terms = first_grads(d_qkv, attn_low, a_one, d_resid_low, weight_rows, split)
    if split:
        first_terms, feed_near_come = lax.optimization_barrier((first_terms, feed_near_come))
        feed_rest = [part[:2] for part in rest] + [feed_near_come]
        feed_far = reduce_far(feed_rest)
        feed_later = {}

        def beside(step, value):
            if step == 2:
                value, far_come = lax.optimization_barrier((value, feed_far))
                sums = reduce_end(feed_rest, far_come)
                sent = jnp.where(
                    x_index == 0, sums[1:], jnp.broadcast_to(sums[:1], (2,) + sums.shape[1:])
                )
                feed_later["sums"] = sums
                feed_later["come"] = swap(sent.astype(jnp.bfloat16), ("x", 0))
            return value

    d_one = matmul_c(d_qkv, qkv_rows)
    d_norm_one, d_gain_one = norm_back(tokens_in, d_one, gains[0])
    d_tokens = d_resid + d_norm_one
    gain_grad = jnp.stack([d_gain_one, d_gain_two], axis=0)
    if split:
        keep, away = [part[:, 0] for part in first_terms]
        first_half, gain_grad = reduce_halves(keep, away, gain_grad, beside)
        first_half, feed_come = lax.optimization_barrier((first_half, feed_later["come"]))
        feed_sums, feed_come = feed_later["sums"], feed_come.astype(jnp.float32)
        low_first = first_half.astype(jnp.bfloat16)
        first_come, gain_grad = swap_with(low_first, gain_grad, ("x", 0))
        first_half = first_half + first_come.astype(jnp.float32)
        halves = [
            jnp.where(x_index == 0, first_half, jnp.concatenate([feed_come[0], feed_sums[1]])),
            jnp.where(
                x_index == 0,
                jnp.concatenate([feed_sums[0], feed_come[0]]),
                jnp.concatenate([feed_come[1], feed_sums[2]]),
            ),
        ]
        own_half = jnp.where(core == 0, halves[0], halves[1])
        other_half = jnp.where(core == 0, halves[1], halves[0]).astype(jnp.bfloat16)
        come, gain_grad = swap_with(other_half, gain_grad, ("core", 0))
        come = come.astype(jnp.float32)
        weight_share = jnp.concatenate(
            [jnp.where(core == 0, own_half, come), jnp.where(core == 0, come, own_half)], axis=0
        )
    else:
        weight_share = scatter_whole([first_terms[0], *feed_grads])
        for where in [("core", 0)] + sum(bit_groups(), []):
            gain_grad = gain_grad + swap(gain_grad, where)
    weight_first, weight_second, weight_new = adam_update(
        weights.astype(jnp.float32), weight_share, first_moment, second_moment, RATE, DECAY, STEP
    )
    gain_first_new, gain_second_new, gain_new = adam_update(
        gains, gain_grad, gain_first, gain_second, GAIN_RATE, 0.0, STEP
    )
    return (
        result.reshape(inputs.shape),
        d_tokens.reshape(inputs.shape),
        weight_share,
        weight_second,
        weight_new,
        gain_grad,
        gain_second_new,
        gain_new,
    )


def solution(mesh):
    fine = Mesh(
        mesh.devices.reshape(mesh.shape["dp"] // 2, 2, mesh.shape["ctx"]), ("x", "core", "ctx")
    )
    rows = P(("x", "core"), "ctx", None)
    stacked = P(("x", "core", "ctx"), None)
    return jax.shard_map(
        shards,
        mesh=fine,
        in_specs=(rows, rows, stacked, P(), stacked, stacked, P(), P()),
        out_specs=(rows, rows, stacked, stacked, stacked, P(), P(), P()),
        check_vma=False,
    )
```

```python
import jax
import jax.numpy as jnp
import numpy as np
from jax import lax
from jax.experimental import pallas as pl
from jax.experimental.pallas import tpu as pltpu
from jax.sharding import Mesh
from jax.sharding import PartitionSpec as P

HEADS = 15
KV = 5
HD = 64
FF = 2560
STEP = 10


SCALE_QK = 0.125
THETA = 10000.0
EPSILON = 1e-05
BETA_ONE = 0.9
BETA_TWO = 0.95
ADAM_EPS = 1e-08
DECAY = 0.1
RATE = 0.02
GAIN_RATE = 0.2
GROUP = HEADS // KV
KEY_TILE = 256
HIDDEN = -1e30
VMEM_BYTES = 48 * 1024 * 1024


def places(row_index, local_rows, ctx_count):
    half_rows = local_rows // 2
    owner_index = row_index // local_rows
    inner_index = row_index % local_rows
    return jnp.where(
        inner_index < half_rows,
        owner_index * half_rows + inner_index,
        (2 * ctx_count - 1 - owner_index) * half_rows + inner_index - half_rows,
    )


def angle_tables(positions_in, sign):
    half_width = HD // 2
    frequency = THETA ** (-jnp.arange(half_width, dtype=jnp.float32) * 2.0 / HD)
    angles = frequency[:, None] * positions_in.astype(jnp.float32)[None, :]
    return jnp.cos(angles), sign * jnp.sin(angles)


def rotate(values, tables):
    cosine, sine_part = tables
    heads = values.reshape(-1, HD, values.shape[-1])
    first_half = heads[:, : HD // 2]
    second_half = heads[:, HD // 2 :]
    return jnp.concatenate(
        [
            first_half * cosine - second_half * sine_part,
            second_half * cosine + first_half * sine_part,
        ],
        axis=1,
    ).reshape(values.shape)


def normalize(values):
    return values * lax.rsqrt(jnp.mean(values * values, axis=-1, keepdims=True) + EPSILON)


def norm_back(values, grad_in, gain_row):
    inv_scale = lax.rsqrt(jnp.mean(values * values, axis=-1, keepdims=True) + EPSILON)
    unit_rows = values * inv_scale
    grad_unit = grad_in * gain_row
    grad_values = inv_scale * (
        grad_unit - unit_rows * jnp.mean(grad_unit * unit_rows, axis=-1, keepdims=True)
    )
    return (grad_values, jnp.sum(grad_in * unit_rows, axis=0))


def matmul_n(left, right):
    return jnp.dot(left, right, preferred_element_type=jnp.float32)


def matmul_t(left, right):
    return lax.dot_general(
        left, right, (((1,), (1,)), ((), ())), preferred_element_type=jnp.float32
    )


def matmul_c(left, right):
    return lax.dot_general(
        left, right, (((0,), (0,)), ((), ())), preferred_element_type=jnp.float32
    )


def bit_groups():
    x_bits = lax.axis_size("x").bit_length() - 1
    ctx_bits = lax.axis_size("ctx").bit_length() - 1
    low_ctx = ctx_bits // 2
    along_x = [("x", bit) for bit in range(x_bits)]
    along_y = [("ctx", bit) for bit in range(low_ctx)]
    along_z = [("ctx", bit) for bit in range(low_ctx, ctx_bits)]
    return along_x, along_y, along_z


def swap_by(values, axis, offset):
    size = lax.axis_size(axis)
    return lax.ppermute(values, axis, [(i, i ^ offset) for i in range(size)])


def swap(values, where):
    return swap_by(values, where[0], 1 << where[1])


def add_low(left, right):
    return (left.astype(jnp.float32) + right.astype(jnp.float32)).astype(jnp.bfloat16)


def rel_offsets(order):
    strides = {"x": 2 * lax.axis_size("ctx"), "ctx": 1}
    offsets = np.zeros((1,), np.int64)
    for axis, bit in order:
        offsets = np.concatenate([offsets, offsets ^ (strides[axis] << bit)])
    return offsets


def lookup(slot, offsets):
    total = jnp.int32(0)
    for bit in range(len(offsets).bit_length() - 1):
        total = total + ((slot >> bit) & 1) * int(offsets[1 << bit])
    return total


def find(offset, offsets):
    total = jnp.int32(0)
    for bit in range(len(offsets).bit_length() - 1):
        place = int(offsets[1 << bit]).bit_length() - 1
        total = total + (((offset >> place) & 1) << bit)
    return total


def collect(values, order):
    kept, arrived = values, None
    for where in order:
        half = kept.shape[0] // 2
        if arrived is None:
            away, kept_next = kept[half:], kept[:half]
        else:
            away = add_low(kept[half:], arrived[half:])
            kept_next = add_low(kept[:half], arrived[:half])
        arrived = swap(away, where)
        kept = kept_next
    return kept[0].astype(jnp.float32) + arrived[0].astype(jnp.float32)


def scatter_whole(terms):
    ctx_count = lax.axis_size("ctx")
    count = 2 * lax.axis_size("x") * ctx_count
    along_x, along_y, along_z = bit_groups()
    core = ("core", 0)
    me = device_index().reshape(1)
    blocks, rows, width = terms[0].shape
    first = -(-rows // 48) * 16
    groups = [(0, first), (first, 2 * first), (2 * first, rows)]
    orders = [
        along_x + along_y + along_z,
        along_y + along_z + along_x,
        along_z + along_x + along_y,
    ]
    tables = [rel_offsets(list(reversed(order))) for order in orders]

    def target(step, me_ref, flip):
        return lookup(step, tables[0]) ^ me_ref[0] ^ flip

    def sources(flip):
        def chosen(member):
            def index(step, me_ref):
                spot = target(step, me_ref, flip)
                return (jnp.where(spot // blocks == member, spot % blocks, 0), 0, 0)

            return pl.BlockSpec((1, rows, width), index)

        return [chosen(member) for member in range(len(terms))]

    def pick_body(me_ref, *refs):
        held = target(pl.program_id(0), me_ref, ctx_count) // blocks
        for member in range(len(terms)):

            @pl.when(held == member)
            def _(member=member):
                refs[-1][...] = refs[member][...]

    away = pl.pallas_call(
        pick_body,
        grid_spec=pltpu.PrefetchScalarGridSpec(
            num_scalar_prefetch=1,
            grid=(count // 2,),
            in_specs=sources(ctx_count),
            out_specs=pl.BlockSpec((1, rows, width), lambda step, me_ref: (step, 0, 0)),
        ),
        out_shape=jax.ShapeDtypeStruct((count // 2, rows, width), jnp.bfloat16),
        compiler_params=pltpu.CompilerParams(vmem_limit_bytes=VMEM_BYTES),
    )(me, *terms)
    arrived = swap(away, core)

    def merge_body(me_ref, *refs):
        held = target(pl.program_id(0), me_ref, 0) // blocks
        for member in range(len(terms)):

            @pl.when(held == member)
            def _(member=member):
                for (low, high), out in zip(groups, refs[-3:]):
                    out[0] = add_low(refs[member][0, low:high], refs[-4][0, low:high])

    parts = pl.pallas_call(
        merge_body,
        grid_spec=pltpu.PrefetchScalarGridSpec(
            num_scalar_prefetch=1,
            grid=(count // 2,),
            in_specs=sources(0)
            + [pl.BlockSpec((1, rows, width), lambda step, me_ref: (step, 0, 0))],
            out_specs=[
                pl.BlockSpec(
                    (1, high - low, width),
                    lambda step, me_ref, table=table: (
                        find(lookup(step, tables[0]), table),
                        0,
                        0,
                    ),
                )
                for (low, high), table in zip(groups, tables)
            ],
        ),
        out_shape=[
            jax.ShapeDtypeStruct((count // 2, high - low, width), jnp.bfloat16)
            for low, high in groups
        ],
        compiler_params=pltpu.CompilerParams(vmem_limit_bytes=VMEM_BYTES),
    )(me, *terms, arrived)
    return jnp.concatenate([collect(part, order) for part, order in zip(parts, orders)], axis=0)


def device_index():
    return (
        (lax.axis_index("x") * 2 + lax.axis_index("core")) * lax.axis_size("ctx")
        + lax.axis_index("ctx")
    ).astype(jnp.int32)


def splits_rows(rows):
    along_x, along_y, along_z = bit_groups()
    return (len(along_x), len(along_y), len(along_z)) == (1, 1, 2) and rows % 64 == 0


def spread(values, order):
    values = values[None]
    for where in order:
        values = double(values, where)
    return values


def double(values, where):
    return jnp.concatenate([values, swap(values, where)], axis=0)


def ctx_orders():
    along_x, along_y, along_z = bit_groups()
    return [along_y + along_z, along_z + along_y]


def row_cuts(rows):
    first = -(-rows // 32) * 16
    return [(0, first), (first, rows)]


def slot_bits():
    along_x, along_y, along_z = bit_groups()
    return list(reversed(along_z)) + along_y


def total_low(*terms):
    total = terms[0].astype(jnp.float32)
    for term in terms[1:]:
        total = total + term.astype(jnp.float32)
    return total.astype(jnp.bfloat16)


def reduce_end(rest, z_far):
    total = z_far.astype(jnp.float32)
    for part in rest:
        total = total + part[0].astype(jnp.float32)
    return total


def reduce_halves(keep, away, ride, beside):
    far_z, near_z, along_y = slot_bits()
    come = beside(0, swap(away, ("core", 0)))
    sums = []
    for (low, high), order in zip(
        row_cuts(keep.shape[1]), ([along_y, near_z, far_z], [near_z, far_z, along_y])
    ):
        shape = (2, 2, 2, high - low, keep.shape[2])
        terms = [keep[:, low:high].reshape(shape), come[:, low:high].reshape(shape)]
        left = [along_y, near_z, far_z]
        for position, where in enumerate(order):
            dim = left.index(where)
            left.remove(where)
            sent = total_low(*[lax.index_in_dim(term, 1, dim, False) for term in terms])
            if low == 0:
                arrived, ride = swap_with(sent, ride, where)
                arrived = beside(position + 1, arrived)
            else:
                arrived = swap(sent, where)
            terms = [lax.index_in_dim(term, 0, dim, False) for term in terms] + [arrived]
        total = terms[0].astype(jnp.float32)
        for term in terms[1:]:
            total = total + term.astype(jnp.float32)
        sums.append(total)
    return jnp.concatenate(sums, axis=0), ride


def ride_parts(ride):
    rounded = lax.reduce_precision(ride, 8, 7)
    return rounded, lax.reduce_precision(ride - rounded, 8, 7)


def with_ride(sent, parts):
    extra = jnp.concatenate([*parts, jnp.zeros((12, parts[0].shape[1]), jnp.float32)])
    return jnp.concatenate([sent.reshape(-1, sent.shape[-1]), extra.astype(jnp.bfloat16)], axis=0)


def swap_with(sent, ride, where):
    parts = ride_parts(ride)
    come, other = off_ride(swap(with_ride(sent, parts), where), sent.shape)
    return come, (parts[0] + parts[1]) + other


def off_ride(come, shape):
    parts = come[-16:].astype(jnp.float32)
    return come[:-16].reshape(shape), parts[0:2] + parts[2:4]


def gather_halves(weights):
    rows = weights.shape[0]
    x_index, core = lax.axis_index("x"), lax.axis_index("core")
    half = rows // 2
    far = swap(weights, ("x", 0))
    low = jnp.where(x_index == 0, weights, far)
    high = jnp.where(x_index == 0, far, weights)
    both = jnp.stack([low, high])
    keep = jnp.where(core == 0, both[:, :half], both[:, half:])
    come = swap(jnp.where(core == 0, both[:, half:], both[:, :half]), ("core", 0))
    first = jnp.where(core == 0, keep, come)
    second = jnp.where(core == 0, come, keep)
    feed = jnp.stack([second[0], first[1], second[1]])
    return first[0], jnp.where(x_index == 0, feed[:, : half // 2], feed[:, half // 2 :])


def place_rows(own, far):
    tables = [rel_offsets(list(reversed(order))) for order in ctx_orders()]
    slots, width = own[0].shape[0], own[0].shape[2]
    lengths = [part.shape[1] for part in own]
    half = sum(lengths)

    def body(me_ref, *refs):
        out_ref = refs[-1]
        for core in range(2):

            @pl.when(me_ref[0] == core)
            def _(core=core):
                for source, base in ((0, core * half), (2, (1 - core) * half)):
                    out_ref[0, base : base + lengths[0]] = refs[source][0]
                    out_ref[0, base + lengths[0] : base + half] = refs[source + 1][0]

    specs = [
        pl.BlockSpec(
            (1, length, width),
            lambda step, me_ref, table=table: (find(step ^ me_ref[1], table), 0, 0),
        )
        for length, table in zip(lengths, tables)
    ]
    me = jnp.stack([lax.axis_index("core"), lax.axis_index("ctx")]).astype(jnp.int32)
    return pl.pallas_call(
        body,
        grid_spec=pltpu.PrefetchScalarGridSpec(
            num_scalar_prefetch=1,
            grid=(slots,),
            in_specs=specs * 2,
            out_specs=pl.BlockSpec((1, 2 * half, width), lambda step, me_ref: (step, 0, 0)),
        ),
        out_shape=jax.ShapeDtypeStruct((slots, 2 * half, width), own[0].dtype),
        cost_estimate=pl.CostEstimate(
            flops=0, bytes_accessed=8 * slots * half * width, transcendentals=0
        ),
        compiler_params=pltpu.CompilerParams(vmem_limit_bytes=VMEM_BYTES),
    )(me, *own, *far).reshape(slots * 2 * half, width)


def turned(values):
    return jnp.transpose(values)


def load_packed(ref, aligned):
    if not aligned:
        return ref[0, 0]
    half = ref.shape[1] // 2
    return jnp.concatenate(
        [
            ref[head * HD : (head + 1) * HD, side * half : (side + 1) * half]
            for side in range(2)
            for head in range(GROUP)
        ],
        axis=1,
    )


def store_packed(ref, values, aligned):
    if not aligned:
        ref[0, 0] = values
        return
    half = ref.shape[1] // 2
    for side in range(2):
        for head in range(GROUP):
            start = (side * GROUP + head) * half
            ref[head * HD : (head + 1) * HD, side * half : (side + 1) * half] = values[
                :, start : start + half
            ]


def load_tile(refs, side, tile):
    length = refs[0].shape[1] // 2
    if length >= KEY_TILE:
        start = side * length + tile * KEY_TILE
        return refs[0][:, start : start + KEY_TILE]
    many = KEY_TILE // length
    return jnp.concatenate(
        [
            ref[:, side * length : (side + 1) * length]
            for ref in refs[tile * many : (tile + 1) * many]
        ],
        axis=1,
    )


def attend_body(count, aligned, queries_ref, key_pos_ref, query_pos_ref, *refs):
    key_refs, value_refs = refs[:count], refs[count : 2 * count]
    out_ref, total_ref, work = refs[2 * count :]
    queries = load_packed(queries_ref, aligned)
    low_cols = queries.shape[1] // 2
    queries_high = queries[:, low_cols:]
    tiles = key_pos_ref.shape[1] // KEY_TILE
    largest = jnp.full((1, queries.shape[1]), HIDDEN, jnp.float32)
    largest_high = jnp.full((1, low_cols), HIDDEN, jnp.float32)
    for side in range(2):
        for tile in range(tiles):
            keys = turned(load_tile(key_refs, side, tile))
            row = (side * tiles + tile) * KEY_TILE
            key_places = key_pos_ref[side, tile * KEY_TILE : (tile + 1) * KEY_TILE]
            if side == 0:
                scores = matmul_n(keys, queries)
                scores = jnp.where(key_places <= query_pos_ref[...], scores, HIDDEN)
                work[row : row + KEY_TILE] = scores
                largest = jnp.maximum(largest, jnp.max(scores, axis=0, keepdims=True))
            else:
                scores = matmul_n(keys, queries_high)
                scores = jnp.where(key_places <= query_pos_ref[:, low_cols:], scores, HIDDEN)
                work[row : row + KEY_TILE, low_cols:] = scores
                largest_high = jnp.maximum(largest_high, jnp.max(scores, axis=0, keepdims=True))
    high_max = jnp.maximum(largest[:, low_cols:], largest_high)
    largest = jnp.concatenate([largest[:, :low_cols], high_max], axis=1)
    total = jnp.zeros_like(largest)
    mixed = jnp.zeros((HD, queries.shape[1]), jnp.float32)
    total_high = jnp.zeros_like(largest_high)
    mixed_high = jnp.zeros((HD, low_cols), jnp.float32)
    for side in range(2):
        for tile in range(tiles):
            values = load_tile(value_refs, side, tile)
            row = (side * tiles + tile) * KEY_TILE
            if side == 0:
                expos = jnp.exp(work[row : row + KEY_TILE] - largest)
                total = total + jnp.sum(expos, axis=0, keepdims=True)
                mixed = mixed + matmul_n(values, expos.astype(jnp.bfloat16))
            else:
                expos = jnp.exp(work[row : row + KEY_TILE, low_cols:] - high_max)
                total_high = total_high + jnp.sum(expos, axis=0, keepdims=True)
                mixed_high = mixed_high + matmul_n(values, expos.astype(jnp.bfloat16))
    total = jnp.concatenate([total[:, :low_cols], total[:, low_cols:] + total_high], axis=1)
    mixed = jnp.concatenate([mixed[:, :low_cols], mixed[:, low_cols:] + mixed_high], axis=1)
    store_packed(out_ref, (mixed / total).astype(jnp.bfloat16), aligned)
    total_ref[0, 0] = largest + jnp.log(total)


def attend_back_body(
    count, aligned, queries_ref, key_pos_ref, query_pos_ref, *refs
):
    key_refs, value_refs = refs[:count], refs[count : 2 * count]
    out_ref, total_ref, d_out_ref, cosine_ref, sine_ref = refs[2 * count : 2 * count + 5]
    d_queries_ref, pair_refs = refs[2 * count + 5], refs[2 * count + 6 :]
    all_queries, all_d_out = load_packed(queries_ref, aligned), load_packed(d_out_ref, aligned)
    low_cols = all_queries.shape[1] // 2
    tiles = key_pos_ref.shape[1] // KEY_TILE
    delta = jnp.sum(
        all_d_out.astype(jnp.float32) * load_packed(out_ref, aligned).astype(jnp.float32),
        axis=0,
        keepdims=True,
    )
    totals = total_ref[0, 0]
    parts = []
    for side in range(2):
        if side == 0:
            queries, d_out = all_queries, all_d_out
            query_places, log_total, row_delta = query_pos_ref[...], totals, delta
        else:
            queries, d_out = all_queries[:, low_cols:], all_d_out[:, low_cols:]
            query_places = query_pos_ref[:, low_cols:]
            log_total, row_delta = totals[:, low_cols:], delta[:, low_cols:]
        part = jnp.zeros((HD, queries.shape[1]), jnp.float32)
        for tile in range(tiles):
            keys_flat = load_tile(key_refs, side, tile)
            scores = matmul_n(turned(keys_flat), queries)
            seen = key_pos_ref[side, tile * KEY_TILE : (tile + 1) * KEY_TILE] <= query_places
            probs = jnp.where(seen, jnp.exp(scores - log_total), 0.0)
            d_probs = matmul_n(turned(load_tile(value_refs, side, tile)), d_out)
            d_scores = (probs * (d_probs - row_delta)).astype(jnp.bfloat16)
            part = part + matmul_n(keys_flat, d_scores)
            d_key = matmul_t(d_scores, queries).astype(jnp.bfloat16)
            d_value = matmul_t(probs.astype(jnp.bfloat16), d_out).astype(jnp.bfloat16)
            if aligned:
                length = key_refs[0].shape[1] // 2
                places_out = [(ref, slot) for ref in pair_refs for slot in range(ref.shape[0])]
                for piece in range(KEY_TILE // length):
                    ref, slot = places_out[tile * (KEY_TILE // length) + piece]
                    rows = slice(piece * length, (piece + 1) * length)
                    ref[slot, 0, side, :, :HD] = d_key[rows]
                    ref[slot, 0, side, :, HD:] = d_value[rows]
            else:
                rows = slice(tile * KEY_TILE, (tile + 1) * KEY_TILE)
                pair_refs[0][side, 0, rows, :HD] = d_key
                pair_refs[0][side, 0, rows, HD:] = d_value
        parts.append(part)
    d_queries = jnp.concatenate(
        [parts[0][:, :low_cols], parts[0][:, low_cols:] + parts[1]], axis=1
    )
    cosine, sine_part = cosine_ref[...], sine_ref[...]
    first_half, second_half = d_queries[: HD // 2], d_queries[HD // 2 :]
    turned_back = jnp.concatenate(
        [
            first_half * cosine + second_half * sine_part,
            second_half * cosine - first_half * sine_part,
        ],
        axis=0,
    )
    store_packed(d_queries_ref, (turned_back * SCALE_QK).astype(jnp.bfloat16), aligned)


def own_mask(rows, cols):
    return lax.broadcasted_iota(jnp.int32, (rows, cols), 0) <= (
        lax.broadcasted_iota(jnp.int32, (rows, cols), 1) % rows
    )


def slot_keys(ref, length):
    both = turned(ref[...])
    return both[:length], both[length:]


def attend_slots_body(count, flags_ref, queries_ref, *refs):
    key_refs, value_refs = refs[:count], refs[count : 2 * count]
    out_ref, total_ref, both_queries, work, largest, totals, mixed = refs[2 * count :]
    length = key_refs[0].shape[1] // 2
    cols = GROUP * length
    packed = load_packed(queries_ref, True)
    for side in range(2):
        both_queries[side] = packed[:, side * cols : (side + 1) * cols]
    visible = own_mask(length, cols)
    low_keys, high_keys = zip(*[slot_keys(ref, length) for ref in key_refs])
    row = 0

    def keep_scores(scores, row):
        work[row : row + scores.shape[0]] = scores
        return jnp.max(scores, axis=0, keepdims=True)

    for side, keys in ((0, low_keys[0]), (1, high_keys[0])):
        scores = jnp.where(visible, matmul_n(keys, both_queries[side]), HIDDEN)
        largest[side] = keep_scores(scores, row)
        row += length
    for slot in range(0, count, 2):
        keys = jnp.concatenate([low_keys[slot], low_keys[slot + 1]], axis=0)
        top = keep_scores(matmul_n(keys, both_queries[1]), row)
        largest[1] = jnp.maximum(largest[1], top)
        row += 2 * length
    for slot in range(1, count):
        side = flags_ref[slot]
        keys = jnp.where(side == 0, low_keys[slot], high_keys[slot])
        top = keep_scores(matmul_n(keys, both_queries[side]), row)
        largest[side] = jnp.maximum(largest[side], top)
        row += length
    row = 0
    for side in range(2):
        values = value_refs[0][:, side * length : (side + 1) * length]
        expos = jnp.exp(work[row : row + length] - largest[side])
        totals[side] = jnp.sum(expos, axis=0, keepdims=True)
        mixed[side] = matmul_n(values, expos.astype(jnp.bfloat16))
        row += length
    for slot in range(0, count, 2):
        values = jnp.concatenate(
            [value_refs[slot][:, :length], value_refs[slot + 1][:, :length]], axis=1
        )
        expos = jnp.exp(work[row : row + 2 * length] - largest[1])
        totals[1] += jnp.sum(expos, axis=0, keepdims=True)
        mixed[1] += matmul_n(values, expos.astype(jnp.bfloat16))
        row += 2 * length
    for slot in range(1, count):
        side = flags_ref[slot]
        values = jnp.where(side == 0, value_refs[slot][:, :length], value_refs[slot][:, length:])
        expos = jnp.exp(work[row : row + length] - largest[side])
        totals[side] += jnp.sum(expos, axis=0, keepdims=True)
        mixed[side] += matmul_n(values, expos.astype(jnp.bfloat16))
        row += length
    result = [(mixed[side] / totals[side]).astype(jnp.bfloat16) for side in range(2)]
    store_packed(out_ref, jnp.concatenate(result, axis=1), True)
    logs = [largest[side] + jnp.log(totals[side]) for side in range(2)]
    total_ref[0, 0] = jnp.concatenate(logs, axis=1)


def attend_slots_back_body(count, flags_ref, queries_ref, *refs):
    key_refs, value_refs = refs[:count], refs[count : 2 * count]
    out_ref, total_ref, d_out_ref, cosine_ref, sine_ref = refs[2 * count : 2 * count + 5]
    d_queries_ref = refs[2 * count + 5]
    pair_refs = refs[2 * count + 6 : -7]
    both_queries, both_d_out, turned_queries, turned_d_out, log_totals, deltas, sums = refs[-7:]
    length = key_refs[0].shape[1] // 2
    cols = GROUP * length
    queries, d_out = load_packed(queries_ref, True), load_packed(d_out_ref, True)
    delta = jnp.sum(
        d_out.astype(jnp.float32) * load_packed(out_ref, True).astype(jnp.float32),
        axis=0,
        keepdims=True,
    )
    for side in range(2):
        part = slice(side * cols, (side + 1) * cols)
        both_queries[side] = queries[:, part]
        both_d_out[side] = d_out[:, part]
        turned_queries[side] = turned(queries[:, part])
        turned_d_out[side] = turned(d_out[:, part])
        log_totals[side] = total_ref[0, 0, :, part]
        deltas[side] = delta[:, part]
    sums[...] = jnp.zeros_like(sums)
    visible = own_mask(length, cols)
    low_keys, high_keys = zip(*[slot_keys(ref, length) for ref in key_refs])
    low_values, high_values = zip(*[slot_keys(ref, length) for ref in value_refs])
    places_out = [(ref, slot) for ref in pair_refs for slot in range(ref.shape[0])]

    def block(keys, keys_flat, values, side, mask=None):
        probs = jnp.exp(matmul_n(keys, both_queries[side]) - log_totals[side])
        if mask is not None:
            probs = jnp.where(mask, probs, 0.0)
        d_probs = matmul_n(values, both_d_out[side])
        d_scores = (probs * (d_probs - deltas[side])).astype(jnp.bfloat16)
        sums[side] += matmul_n(keys_flat, d_scores)
        return jnp.concatenate(
            [
                matmul_n(d_scores, turned_queries[side]),
                matmul_n(probs.astype(jnp.bfloat16), turned_d_out[side]),
            ],
            axis=1,
        )

    low_terms = []
    for slot in range(0, count, 2):
        keys, values = [
            jnp.concatenate([part[slot], part[slot + 1]], axis=0) for part in (low_keys, low_values)
        ]
        flat = jnp.concatenate([key_refs[slot][:, :length], key_refs[slot + 1][:, :length]], axis=1)
        terms = block(keys, flat, values, 1)
        low_terms += [terms[:length], terms[length:]]
    ref, slot = places_out[0]
    own = [
        block(keys, key_refs[0][:, side * length : (side + 1) * length], values, side, visible)
        for side, (keys, values) in enumerate(
            ((low_keys[0], low_values[0]), (high_keys[0], high_values[0]))
        )
    ]
    ref[slot, 0, 0] = (low_terms[0] + own[0]).astype(jnp.bfloat16)
    ref[slot, 0, 1] = own[1].astype(jnp.bfloat16)
    for member in range(1, count):
        side = flags_ref[member]
        low = side == 0
        keys = jnp.where(low, low_keys[member], high_keys[member])
        flat = jnp.where(low, key_refs[member][:, :length], key_refs[member][:, length:])
        values = jnp.where(low, low_values[member], high_values[member])
        terms = block(keys, flat, values, side)
        ref, slot = places_out[member]
        ref[slot, 0, 0] = (low_terms[member] + jnp.where(low, terms, 0.0)).astype(jnp.bfloat16)
        ref[slot, 0, 1] = jnp.where(low, 0.0, terms).astype(jnp.bfloat16)
    d_queries = jnp.concatenate([sums[0], sums[1]], axis=1)
    store_packed(d_queries_ref, turn_queries_back(d_queries, cosine_ref, sine_ref), True)


def turn_queries_back(d_queries, cosine_ref, sine_ref):
    cosine, sine_part = cosine_ref[...], sine_ref[...]
    first_half, second_half = d_queries[: HD // 2], d_queries[HD // 2 :]
    turned_back = jnp.concatenate(
        [
            first_half * cosine + second_half * sine_part,
            second_half * cosine - first_half * sine_part,
        ],
        axis=0,
    )
    return (turned_back * SCALE_QK).astype(jnp.bfloat16)


def slot_specs(leads, local_rows, seq):
    specs = [
        pl.BlockSpec(memory_space=pltpu.SMEM),
        pl.BlockSpec((GROUP * HD, local_rows), lambda head: (head, seq)),
    ]
    for first in (0, KV):
        specs += [
            pl.BlockSpec(
                (None, HD, local_rows),
                lambda head, lead=lead, first=first: (lead, first + head, 0),
            )
            for lead in leads
        ]
    return specs


def attend_slots(queries, pairs, flags, local_rows, seq):
    count, cols = len(pairs), GROUP * local_rows // 2
    leads, arrays = [lead for _, lead in pairs], [array for array, _ in pairs]
    work = HEADS * local_rows * local_rows * count // 2
    return pl.pallas_call(
        lambda *refs: attend_slots_body(count, *refs),
        grid=(KV,),
        in_specs=slot_specs(leads, local_rows, seq),
        out_specs=[
            pl.BlockSpec((GROUP * HD, local_rows), lambda head: (head, 0)),
            pl.BlockSpec((1, 1, 1, 2 * cols), lambda head: (0, head, 0, 0)),
        ],
        out_shape=[
            jax.ShapeDtypeStruct((HEADS * HD, local_rows), jnp.bfloat16),
            jax.ShapeDtypeStruct((1, KV, 1, 2 * cols), jnp.float32),
        ],
        scratch_shapes=[
            pltpu.VMEM((2, HD, cols), jnp.bfloat16),
            pltpu.VMEM(((2 * count + 1) * local_rows // 2, cols), jnp.float32),
            pltpu.VMEM((2, 1, cols), jnp.float32),
            pltpu.VMEM((2, 1, cols), jnp.float32),
            pltpu.VMEM((2, HD, cols), jnp.float32),
        ],
        cost_estimate=pl.CostEstimate(
            flops=work * HD, bytes_accessed=1024 * 1024, transcendentals=0
        ),
        compiler_params=pltpu.CompilerParams(vmem_limit_bytes=VMEM_BYTES),
    )(flags, queries, *arrays, *arrays)


def attend_slots_back(
    queries, pairs, flags, mixed, log_total, d_mixed, tables, local_rows, seq, sets
):
    count, cols = len(pairs), GROUP * local_rows // 2
    leads, arrays = [lead for _, lead in pairs], [array for array, _ in pairs]
    work = HEADS * local_rows * local_rows * count // 2
    own = pl.BlockSpec((GROUP * HD, local_rows), lambda head: (head, 0))
    table_spec = pl.BlockSpec((HD // 2, 2 * cols), lambda head: (0, 0))
    length = local_rows // 2
    return pl.pallas_call(
        lambda *refs: attend_slots_back_body(count, *refs),
        grid=(KV,),
        in_specs=slot_specs(leads, local_rows, seq)
        + [
            own,
            pl.BlockSpec((1, 1, 1, 2 * cols), lambda head: (0, head, 0, 0)),
            pl.BlockSpec((GROUP * HD, local_rows), lambda head: (head, seq)),
            table_spec,
            table_spec,
        ],
        out_specs=[own]
        + [
            pl.BlockSpec((slots, 1, 2, length, 2 * HD), lambda head: (0, head, 0, 0, 0))
            for slots in sets
        ],
        out_shape=[jax.ShapeDtypeStruct((HEADS * HD, local_rows), jnp.bfloat16)]
        + [jax.ShapeDtypeStruct((slots, KV, 2, length, 2 * HD), jnp.bfloat16) for slots in sets],
        scratch_shapes=[
            pltpu.VMEM((2, HD, cols), jnp.bfloat16),
            pltpu.VMEM((2, HD, cols), jnp.bfloat16),
            pltpu.VMEM((2, cols, HD), jnp.bfloat16),
            pltpu.VMEM((2, cols, HD), jnp.bfloat16),
            pltpu.VMEM((2, 1, cols), jnp.float32),
            pltpu.VMEM((2, 1, cols), jnp.float32),
            pltpu.VMEM((2, HD, cols), jnp.float32),
        ],
        cost_estimate=pl.CostEstimate(
            flops=work * HD, bytes_accessed=1024 * 1024, transcendentals=0
        ),
        compiler_params=pltpu.CompilerParams(vmem_limit_bytes=VMEM_BYTES),
    )(flags, queries, *arrays, *arrays, mixed, log_total, d_mixed, *tables)


def head_specs(leads, aligned, cols, keys, local_rows, seq):
    count = len(leads)
    if aligned:
        packed = pl.BlockSpec((GROUP * HD, local_rows), lambda head: (head, seq))
    else:
        packed = pl.BlockSpec((1, 1, HD, cols), lambda head: (seq, head, 0, 0))
    specs = [
        packed,
        pl.BlockSpec((2, keys, 1), lambda head: (0, 0, 0)),
        pl.BlockSpec((1, cols), lambda head: (0, 0)),
    ]
    for first in (0, KV):
        specs += [
            pl.BlockSpec(
                (None, HD, 2 * keys // count),
                lambda head, lead=lead, first=first: (lead, first + head, seq),
            )
            for lead in leads
        ]
    return packed, specs


def attend(queries, pairs, key_pos, query_pos, local_rows, seq):
    aligned = queries.ndim == 2
    cols, keys, count = query_pos.shape[1], key_pos.shape[1], len(pairs)
    leads, arrays = [lead for _, lead in pairs], [array for array, _ in pairs]
    _, specs = head_specs(leads, aligned, cols, keys, local_rows, seq)
    work = HEADS * keys * cols // GROUP * 3 // 2
    if aligned:
        out_spec = pl.BlockSpec((GROUP * HD, local_rows), lambda head: (head, 0))
        out_shape = jax.ShapeDtypeStruct((HEADS * HD, local_rows), jnp.bfloat16)
    else:
        out_spec = pl.BlockSpec((1, 1, HD, cols), lambda head: (0, head, 0, 0))
        out_shape = jax.ShapeDtypeStruct((1, KV, HD, cols), jnp.bfloat16)
    return pl.pallas_call(
        lambda *refs: attend_body(count, aligned, *refs),
        grid=(KV,),
        in_specs=specs,
        out_specs=[out_spec, pl.BlockSpec((1, 1, 1, cols), lambda head: (0, head, 0, 0))],
        out_shape=[out_shape, jax.ShapeDtypeStruct((1, KV, 1, cols), jnp.float32)],
        scratch_shapes=[pltpu.VMEM((2 * keys, cols), jnp.float32)],
        cost_estimate=pl.CostEstimate(
            flops=work * HD, bytes_accessed=1024 * 1024, transcendentals=0
        ),
        compiler_params=pltpu.CompilerParams(vmem_limit_bytes=VMEM_BYTES),
    )(queries, key_pos, query_pos, *arrays, *arrays)


def attend_back(
    queries, pairs, key_pos, query_pos, mixed, log_total, d_mixed, tables, local_rows, seq, sets
):
    aligned = queries.ndim == 2
    cols, keys, count = query_pos.shape[1], key_pos.shape[1], len(pairs)
    leads, arrays = [lead for _, lead in pairs], [array for array, _ in pairs]
    packed, specs = head_specs(leads, aligned, cols, keys, local_rows, seq)
    work = HEADS * keys * cols // GROUP * 3 // 2
    if aligned:
        own = pl.BlockSpec((GROUP * HD, local_rows), lambda head: (head, 0))
        own_shape = jax.ShapeDtypeStruct((HEADS * HD, local_rows), jnp.bfloat16)
        length = keys // count
        pair_specs = [
            pl.BlockSpec((slots, 1, 2, length, 2 * HD), lambda head: (0, head, 0, 0, 0))
            for slots in sets
        ]
        pair_shapes = [
            jax.ShapeDtypeStruct((slots, KV, 2, length, 2 * HD), jnp.bfloat16) for slots in sets
        ]
    else:
        own = pl.BlockSpec((1, 1, HD, cols), lambda head: (0, head, 0, 0))
        own_shape = jax.ShapeDtypeStruct((1, KV, HD, cols), jnp.bfloat16)
        pair_specs = [pl.BlockSpec((2, 1, keys, 2 * HD), lambda head: (0, head, 0, 0))]
        pair_shapes = [jax.ShapeDtypeStruct((2, KV, keys, 2 * HD), jnp.bfloat16)]
    table_spec = pl.BlockSpec((HD // 2, cols), lambda head: (0, 0))
    return pl.pallas_call(
        lambda *refs: attend_back_body(count, aligned, *refs),
        grid=(KV,),
        in_specs=specs
        + [
            own,
            pl.BlockSpec((1, 1, 1, cols), lambda head: (0, head, 0, 0)),
            packed,
            table_spec,
            table_spec,
        ],
        out_specs=[own] + pair_specs,
        out_shape=[own_shape] + pair_shapes,
        cost_estimate=pl.CostEstimate(
            flops=work * HD, bytes_accessed=1024 * 1024, transcendentals=0
        ),
        compiler_params=pltpu.CompilerParams(vmem_limit_bytes=VMEM_BYTES),
    )(queries, key_pos, query_pos, *arrays, *arrays, mixed, log_total, d_mixed, *tables)


def put_rows(values, keep_ref, away_ref, place, core, x_index):
    quarter = values.shape[0] // 4
    for mine in range(4):

        @pl.when(2 * core + x_index == mine)
        def _(mine=mine):
            for ref, side in ((keep_ref, mine // 2), (away_ref, 1 - mine // 2)):
                for position, along_x in enumerate((mine % 2, 1 - mine % 2)):
                    start = (2 * side + along_x) * quarter
                    ref[place[0], place[1], position * quarter : (position + 1) * quarter] = values[
                        start : start + quarter
                    ]


def feed_body(
    parts, split, chained, me_ref, a_two_ref, dy_ref, *refs
):
    count = 4 if split else 6
    before, refs = (refs[:2], refs[2:]) if chained else (None, refs)
    weight_refs, (out_ref, d_two_ref), grad_refs = (
        refs[:count],
        refs[count : count + 2],
        refs[count + 2 :],
    )
    core, x_index = me_ref[0], me_ref[1]
    step = pl.program_id(0)

    @pl.when(step == 0)
    def _():
        for place, ref in enumerate((out_ref, d_two_ref)):
            ref[...] = before[place][...] if chained else jnp.zeros_like(ref)

    def rows_of(member):
        if split:
            rows_out = []
            for slot in range(weight_refs[0].shape[0]):
                parts_here = [ref[slot, member] for ref in weight_refs]
                for side in range(2):
                    for along_x in range(2):
                        near = jnp.where(x_index == along_x, parts_here[0], parts_here[1])
                        far = jnp.where(x_index == along_x, parts_here[2], parts_here[3])
                        rows_out.append(jnp.where(core == side, near, far))
            return jnp.concatenate(rows_out, axis=0)
        wanted = feed_core(member, step, parts)
        return jnp.where(wanted == core, weight_refs[2 * member][0], weight_refs[2 * member + 1][0])

    a_two, dy_low = a_two_ref[...], dy_ref[...]
    gate_rows, up_rows, down_rows = rows_of(0), rows_of(1), rows_of(2)
    gate_pre = matmul_t(gate_rows, a_two)
    up_pre = matmul_t(up_rows, a_two)
    d_hidden = matmul_t(down_rows, dy_low)
    sigma = jax.nn.sigmoid(gate_pre)
    gate_act = gate_pre * sigma
    hidden = (gate_act * up_pre).astype(jnp.bfloat16)
    d_gate = (d_hidden * up_pre * sigma * (1.0 + gate_pre * (1.0 - sigma))).astype(jnp.bfloat16)
    d_up = (d_hidden * gate_act).astype(jnp.bfloat16)
    out_ref[...] += matmul_c(hidden, down_rows)
    d_two_ref[...] += matmul_c(d_gate, gate_rows) + matmul_c(d_up, up_rows)
    for member, (left, right) in enumerate(((d_gate, a_two), (d_up, a_two), (hidden, dy_low))):
        grad = matmul_n(left, right).astype(jnp.bfloat16)
        if split:
            slots = grad_refs[0].shape[0]
            rows = grad.shape[0] // slots
            for slot in range(slots):
                put_rows(
                    grad[slot * rows : (slot + 1) * rows], *grad_refs, (slot, member), core, x_index
                )
        else:
            grad_refs[member][0] = grad


def feed_core(member, step, parts):
    ctx_count, single = parts
    return (member + 1) % 2 if single else step // ctx_count


def feed_forward(a_two, dy_low, mine, far, rows, before=()):
    tokens, width = a_two.shape
    ctx_count = lax.axis_size("ctx")
    blocks = FF // rows
    single = blocks == ctx_count
    split = mine[0].ndim == 4 if isinstance(mine, list) else False
    parts = (ctx_count, single)
    whole = pl.BlockSpec((tokens, width), lambda step, me_ref: (0, 0))

    def weight_spec(member, own):
        first = (member + 1) * blocks // ctx_count // 2 * ctx_count

        def index(step, me_ref):
            matches = (feed_core(member, step, parts) == me_ref[0]) == own
            return (first + jnp.where(matches, step % ctx_count, 0), 0, 0)

        return pl.BlockSpec((1, rows, width), index)

    if split:
        weight_specs = [
            pl.BlockSpec((2, 3, rows // 4, width), lambda step, me_ref: (step, 0, 0, 0))
        ] * 4
        weight_args = [*mine, *far]
        half = pl.BlockSpec((2, 3, rows // 2, width), lambda step, me_ref: (step, 0, 0, 0))
        grad_specs = [half, half]
        blocks = mine[0].shape[0]
        grad_shapes = [jax.ShapeDtypeStruct((blocks, 3, rows // 2, width), jnp.bfloat16)] * 2
    else:
        weight_specs = [weight_spec(member, own) for member in range(3) for own in (True, False)]
        weight_args = [mine, far] * 3
        grad_specs = [pl.BlockSpec((1, rows, width), lambda step, me_ref: (step, 0, 0))] * 3
        grad_shapes = [jax.ShapeDtypeStruct((blocks, rows, width), jnp.bfloat16)] * 3
    me = jnp.stack([lax.axis_index("core"), lax.axis_index("x")]).astype(jnp.int32)
    return pl.pallas_call(
        lambda *refs: feed_body(parts, split, bool(before), *refs),
        grid_spec=pltpu.PrefetchScalarGridSpec(
            num_scalar_prefetch=1,
            grid=(blocks // 2 if split else blocks,),
            in_specs=[whole] * (2 + len(before)) + weight_specs,
            out_specs=[whole, whole] + grad_specs,
        ),
        out_shape=[jax.ShapeDtypeStruct((tokens, width), jnp.float32)] * 2 + grad_shapes,
        cost_estimate=pl.CostEstimate(
            flops=18 * tokens * width * blocks * rows, bytes_accessed=12 * blocks * rows * width,
            transcendentals=0,
        ),
        compiler_params=pltpu.CompilerParams(vmem_limit_bytes=VMEM_BYTES),
    )(me, a_two, dy_low, *before, *weight_args)


def first_grads(d_qkv, attn_low, a_one, d_resid_low, rows, split):
    tokens, width = a_one.shape
    early = d_qkv.shape[0] // rows
    blocks = early + attn_low.shape[0] // rows

    def body(me_ref, qkv_ref, attn_ref, one_ref, resid_ref, *grad_refs):
        first = pl.program_id(0) < early
        left = jnp.where(first, qkv_ref[...], attn_ref[...])
        right = jnp.where(first, one_ref[...], resid_ref[...])
        grad = matmul_n(left, right).astype(jnp.bfloat16)
        if split:
            put_rows(grad, *grad_refs, (0, 0), me_ref[0], 0)
        else:
            grad_refs[0][0] = grad

    whole = pl.BlockSpec((tokens, width), lambda step, me_ref: (0, 0))
    if split:
        table = rel_offsets(slot_bits())
        half = pl.BlockSpec(
            (1, 1, rows // 2, width), lambda step, me_ref: (find(step ^ me_ref[1], table), 0, 0, 0)
        )
        grad_specs = [half, half]
        grad_shapes = [jax.ShapeDtypeStruct((blocks, 1, rows // 2, width), jnp.bfloat16)] * 2
    else:
        grad_specs = [pl.BlockSpec((1, rows, width), lambda step, me_ref: (step, 0, 0))]
        grad_shapes = [jax.ShapeDtypeStruct((blocks, rows, width), jnp.bfloat16)]
    me = jnp.stack([lax.axis_index(name) for name in ("core", "ctx")]).astype(jnp.int32)
    return pl.pallas_call(
        body,
        grid_spec=pltpu.PrefetchScalarGridSpec(
            num_scalar_prefetch=1,
            grid=(blocks,),
            in_specs=[
                pl.BlockSpec((rows, tokens), lambda step, me_ref: (jnp.minimum(step, early - 1), 0)),
                pl.BlockSpec((rows, tokens), lambda step, me_ref: (jnp.maximum(step - early, 0), 0)),
                whole,
                whole,
            ],
            out_specs=grad_specs,
        ),
        out_shape=grad_shapes,
        cost_estimate=pl.CostEstimate(
            flops=2 * tokens * width * blocks * rows, bytes_accessed=2 * blocks * rows * width, transcendentals=0
        ),
        compiler_params=pltpu.CompilerParams(vmem_limit_bytes=VMEM_BYTES),
    )(me, d_qkv, attn_low, a_one, d_resid_low)


def adam_update(param, grad, first, second, rate, decay, step_number):
    first_new = BETA_ONE * first + (1.0 - BETA_ONE) * grad
    second_new = BETA_TWO * second + (1.0 - BETA_TWO) * grad * grad
    fix_one = 1.0 - BETA_ONE**step_number
    fix_two = 1.0 - BETA_TWO**step_number
    update = first_new / fix_one / (jnp.sqrt(second_new / fix_two) + ADAM_EPS)
    return (first_new, second_new, param - rate * (update + decay * param))


def shards(inputs, cotangent, weights, gains, first_moment, second_moment, gain_first, gain_second):
    ctx_count = lax.axis_size("ctx")
    x_count = lax.axis_size("x")
    ctx_index, core, x_index = lax.axis_index("ctx"), lax.axis_index("core"), lax.axis_index("x")
    seqs, local_rows, model_width = inputs.shape
    half_rows = local_rows // 2
    tokens = seqs * local_rows
    weight_rows = weights.shape[0]
    q_cols = HEADS * HD
    kv_cols = KV * HD
    cut_o = q_cols + 2 * kv_cols
    slots = slot_bits()
    aligned = splits_rows(weight_rows) and half_rows % 128 == 0 and seqs == 2
    split = aligned
    local_index = jnp.arange(local_rows, dtype=jnp.int32)
    pos_here = places(ctx_index * local_rows + local_index, local_rows, ctx_count)
    cosine, sine_part = angle_tables(pos_here, 1.0)
    turn = (jnp.tile(cosine, (1, seqs)), jnp.tile(sine_part, (1, seqs)))
    turn_back = (turn[0], -turn[1])

    def pack(flat):
        if aligned:
            return flat
        return (
            flat.reshape(KV, GROUP, HD, -1, 2, half_rows)
            .transpose(3, 0, 2, 4, 1, 5)
            .reshape(-1, KV, HD, 2 * GROUP * half_rows)
        )

    def unpack(packed):
        if aligned:
            return packed
        return (
            packed.reshape(KV, HD, 2, GROUP, half_rows)
            .transpose(0, 3, 1, 2, 4)
            .reshape(q_cols, local_rows)
        )

    def by_columns(row):
        rows = row.shape[0]
        return jnp.broadcast_to(
            row.reshape(rows, 2, 1, half_rows), (rows, 2, GROUP, half_rows)
        ).reshape(rows, 2 * GROUP * half_rows)

    owners = ctx_index ^ jnp.asarray(rel_offsets(slots), jnp.int32)
    flags = (owners > ctx_index).astype(jnp.int32)
    inner = jnp.arange(half_rows, dtype=jnp.int32)
    key_pos = jnp.stack(
        [
            (owners[:, None] * half_rows + inner[None, :]).reshape(-1, 1),
            ((2 * ctx_count - 1 - owners[:, None]) * half_rows + inner[None, :]).reshape(-1, 1),
        ]
    )
    query_pos = by_columns(pos_here[None, :])
    packed_tables = (by_columns(cosine), by_columns(sine_part))

    if split:
        first_half, feed_quarter = gather_halves(weights)
        cuts = row_cuts(weight_rows // 2)
        backward = [list(reversed(order)) for order in ctx_orders()]
        first_own = [spread(first_half[low:high], order) for (low, high), order in zip(cuts, backward)]
        feed_quarter, first_own = lax.optimization_barrier((feed_quarter, first_own))
        feed_far_z = swap(feed_quarter[None], slots[0])
        first_far = [swap(part, ("core", 0)) for part in first_own]
        first_rows = place_rows(first_own, first_far)
    else:
        mine = lax.all_gather(weights, ("x", "ctx"), axis=0, tiled=True)
        mine = mine.reshape(x_count * ctx_count, weight_rows, model_width)
        far = swap(mine, ("core", 0))
        sides = [
            jnp.where(core == 0, mine[:ctx_count], far[:ctx_count]),
            jnp.where(core == 0, far[:ctx_count], mine[:ctx_count]),
        ]
        first_rows = jnp.concatenate(sides).reshape(-1, model_width)
    qkv_rows, o_rows = first_rows[:cut_o], first_rows[cut_o : cut_o + q_cols]

    tokens_in, cot_in = lax.optimization_barrier(
        (inputs.reshape(tokens, model_width), cotangent.reshape(tokens, model_width))
    )
    dy_low = cot_in.astype(jnp.bfloat16)
    a_one = (normalize(tokens_in) * gains[0]).astype(jnp.bfloat16)
    pair_rows = matmul_t(qkv_rows[q_cols:], a_one)
    if split:
        pair_rows, feed_far_z = lax.optimization_barrier((pair_rows, feed_far_z))
    joined = jnp.concatenate(
        [rotate(pair_rows[:kv_cols], turn).astype(jnp.bfloat16), pair_rows[kv_cols:].astype(jnp.bfloat16)],
        axis=0,
    )
    if split:
        feed_own = jnp.concatenate([feed_quarter[None], feed_far_z], axis=0)
        joined, feed_own = lax.optimization_barrier((joined, feed_own))
    if aligned:
        mine_0, mine_1 = [
            joined[:, seq * local_rows : (seq + 1) * local_rows] for seq in range(2)
        ]
        far_0, own_y_0 = swap(mine_0, slots[0]), swap(mine_0, slots[2])
        feed_near, feed_y = swap(feed_own, slots[1]), swap(feed_own, slots[2])
        feed_x = swap(feed_own, ("x", 0))
        far_0, own_y_0, feed_near, feed_y, feed_x, mine_1 = lax.optimization_barrier(
            (far_0, own_y_0, feed_near, feed_y, feed_x, mine_1)
        )
        near_0, far_y_0 = swap(jnp.stack([mine_0, far_0]), slots[1]), swap(far_0, slots[2])
        far_1, own_y_1 = swap(mine_1, slots[0]), swap(mine_1, slots[2])
        near_x = swap(feed_near, ("x", 0))
        near_0, far_y_0, far_1, own_y_1, near_x, feed_y = lax.optimization_barrier(
            (near_0, far_y_0, far_1, own_y_1, near_x, feed_y)
        )
        near_y_0 = swap(near_0, slots[2])
        near_1, far_y_1 = swap(jnp.stack([mine_1, far_1]), slots[1]), swap(far_1, slots[2])
        y_x = swap(feed_y, ("x", 0))
        near_y_0, near_1, far_y_1, y_x, feed_near = lax.optimization_barrier(
            (near_y_0, near_1, far_y_1, y_x, feed_near)
        )
        near_y_1 = swap(near_1, slots[2])
        pairs = [
            [(own[None], 0), (far_z[None], 0), (near, 0), (near, 1)]
            + [(own_y[None], 0), (far_y[None], 0), (near_y, 0), (near_y, 1)]
            for own, far_z, near, own_y, far_y, near_y in (
                (mine_0, far_0, near_0, own_y_0, far_y_0, near_y_0),
                (mine_1, far_1, near_1, own_y_1, far_y_1, near_y_1),
            )
        ]
        feed_lower = [
            jnp.concatenate([feed_own, feed_near], axis=0),
            jnp.concatenate([feed_x, near_x], axis=0),
        ]
        feed_lower_far = [swap(part, ("core", 0)) for part in feed_lower]
    else:
        pairs = spread(joined, slots).reshape(ctx_count, 2 * kv_cols, seqs, 2, half_rows)
        pairs = [
            (
                pairs.transpose(1, 2, 3, 0, 4).reshape(
                    1, 2 * kv_cols, seqs * 2 * ctx_count * half_rows
                ),
                0,
            )
        ]
    q_rot = rotate(matmul_t(qkv_rows[:q_cols], a_one), turn).astype(jnp.bfloat16)
    queries = pack((q_rot * SCALE_QK).astype(jnp.bfloat16))
    attended = []
    for seq in range(seqs):
        if aligned:
            attended.append(attend_slots(queries, pairs[seq], flags, local_rows, seq))
            if seq == 0:
                attended, feed_near = lax.optimization_barrier((attended, feed_near))
                feed_near_y = swap(feed_near, slots[2])
        else:
            attended.append(attend(queries, pairs, key_pos, query_pos, local_rows, seq))
    attn_low = jnp.concatenate([unpack(mixed) for mixed, _ in attended], axis=1)
    resid = tokens_in + matmul_c(attn_low, o_rows)
    a_two = (normalize(resid) * gains[1]).astype(jnp.bfloat16)
    if aligned:
        a_two, feed_near_y = lax.optimization_barrier((a_two, feed_near_y))
        near_y_x = swap(feed_near_y, ("x", 0))
        upper_own = jnp.concatenate([feed_y, feed_near_y], axis=0)
        upper_far = swap(upper_own, ("core", 0))
        *sums_fed, keep_lower, away_lower = feed_forward(
            a_two, dy_low, feed_lower, feed_lower_far, weight_rows
        )
        sums_fed, near_y_x, upper_far = lax.optimization_barrier((sums_fed, near_y_x, upper_far))
        upper_x = jnp.concatenate([y_x, near_y_x], axis=0)
        come_lower = swap(away_lower, ("core", 0))
        fed, d_two, keep_upper, away_upper = feed_forward(
            a_two,
            dy_low,
            [upper_own, upper_x],
            [upper_far, swap(upper_x, ("core", 0))],
            weight_rows,
            sums_fed,
        )
        come_upper = swap(away_upper, ("core", 0))
    else:
        fed, d_two, *feed_grads = feed_forward(a_two, dy_low, mine, far, weight_rows)
    result = resid + fed
    d_norm_two, d_gain_two = norm_back(resid, d_two, gains[1])
    d_resid = cot_in + d_norm_two
    d_resid_low = d_resid.astype(jnp.bfloat16)
    d_attn = pack(matmul_t(o_rows, d_resid_low).astype(jnp.bfloat16))
    if aligned:
        quarter = weight_rows // 4
        held_upper, held_lower = [
            [(part[:, :, :quarter], part[:, :, quarter:]) for part in parts]
            for parts in ((keep_upper, come_upper), (keep_lower, come_lower))
        ]
        send_upper, send_lower = [
            total_low(*[far_part for _, far_part in parts]) for parts in (held_upper, held_lower)
        ]
        d_attn, send_upper, send_lower = lax.optimization_barrier((d_attn, send_upper, send_lower))
        x_upper = swap(send_upper, ("x", 0))
        x_lower = swap(send_lower, ("x", 0))
    d_q, d_pair = [], []
    for seq in range(seqs):
        mixed, log_total = attended[seq]
        if aligned:
            d_queries, *d_slots = attend_slots_back(
                queries, pairs[seq], flags, mixed, log_total, d_attn, packed_tables, local_rows, seq, (2, 2, 4)
            )
        else:
            d_queries, *d_slots = attend_back(
                queries, pairs, key_pos, query_pos, mixed, log_total, d_attn, packed_tables,
                local_rows, seq, (1,),
            )
        if aligned and seq == 1:
            d_slots, x_upper = lax.optimization_barrier((d_slots, x_upper))
            feed_y_come = swap(total_low(*[part for part, _ in held_upper], x_upper), slots[2])
        d_q.append(unpack(d_queries))
        if aligned:
            lower, near_part, upper = d_slots
            y_come = swap(upper, slots[2])
            near_come = swap(add_low(near_part, y_come[2:]), slots[1])
            if seq == 1:
                near_come, x_lower = lax.optimization_barrier((near_come, x_lower))
            far_come = swap(total_low(lower[1], y_come[1], near_come[1]), slots[0])
            if seq == 1:
                far_come, feed_y_come = lax.optimization_barrier((far_come, feed_y_come))
                rest = [part for part, _ in held_lower] + [x_lower, feed_y_come]
                feed_near_come = swap(total_low(*[part[2:] for part in rest]), slots[1])
            total = far_come.astype(jnp.float32)
            for part in (lower, y_come, near_come):
                total = total + part[0].astype(jnp.float32)
        else:
            total = collect(
                d_slots[0]
                .reshape(2, KV, ctx_count, half_rows, 2 * HD)
                .transpose(2, 1, 0, 3, 4),
                list(reversed(slots)),
            )
        d_pair.append(total)
    d_own = jnp.stack(d_pair).transpose(1, 4, 0, 2, 3).reshape(KV, 2 * HD, tokens)
    d_qkv = jnp.concatenate(
        [
            jnp.concatenate(d_q, axis=1),
            rotate(d_own[:, :HD].reshape(kv_cols, tokens), turn_back).astype(jnp.bfloat16),
            d_own[:, HD:].reshape(kv_cols, tokens).astype(jnp.bfloat16),
        ],
        axis=0,
    )
    first_terms = first_grads(d_qkv, attn_low, a_one, d_resid_low, weight_rows, split)
    if split:
        first_terms, feed_near_come = lax.optimization_barrier((first_terms, feed_near_come))
        feed_rest = [part[:2] for part in rest] + [feed_near_come]
        far_send = total_low(*[part[1] for part in feed_rest])
        feed_later = {}

        def beside(step, value):
            if step == 0:
                value, sent = lax.optimization_barrier((value, far_send))
                feed_later["far"] = swap(sent, slots[0])
            if step == 1:
                value, far_come = lax.optimization_barrier((value, feed_later["far"]))
                sums = reduce_end(feed_rest, far_come)
                sent = jnp.where(
                    x_index == 0, sums[1:], jnp.broadcast_to(sums[:1], (2,) + sums.shape[1:])
                )
                feed_later["sums"] = sums
                feed_later["come"] = swap(sent.astype(jnp.bfloat16), ("x", 0))
            return value

    d_one = matmul_c(d_qkv, qkv_rows)
    d_norm_one, d_gain_one = norm_back(tokens_in, d_one, gains[0])
    d_tokens = d_resid + d_norm_one
    gain_grad = jnp.stack([d_gain_one, d_gain_two], axis=0)
    if split:
        keep, away = [part[:, 0] for part in first_terms]
        first_half, gain_grad = reduce_halves(keep, away, gain_grad, beside)
        first_half, feed_come = lax.optimization_barrier((first_half, feed_later["come"]))
        feed_sums, feed_come = feed_later["sums"], feed_come.astype(jnp.float32)
        low_first = first_half.astype(jnp.bfloat16)
        first_come, gain_grad = swap_with(low_first, gain_grad, ("x", 0))
        first_half = first_half + first_come.astype(jnp.float32)
        halves = [
            jnp.where(x_index == 0, first_half, jnp.concatenate([feed_come[0], feed_sums[1]])),
            jnp.where(
                x_index == 0,
                jnp.concatenate([feed_sums[0], feed_come[0]]),
                jnp.concatenate([feed_come[1], feed_sums[2]]),
            ),
        ]
        own_half = jnp.where(core == 0, halves[0], halves[1])
        other_half = jnp.where(core == 0, halves[1], halves[0]).astype(jnp.bfloat16)
        come, gain_grad = swap_with(other_half, gain_grad, ("core", 0))
        come = come.astype(jnp.float32)
        weight_share = jnp.concatenate(
            [jnp.where(core == 0, own_half, come), jnp.where(core == 0, come, own_half)], axis=0
        )
    else:
        weight_share = scatter_whole([first_terms[0], *feed_grads])
        for where in [("core", 0)] + sum(bit_groups(), []):
            gain_grad = gain_grad + swap(gain_grad, where)
    weight_first, weight_second, weight_new = adam_update(
        weights.astype(jnp.float32), weight_share, first_moment, second_moment, RATE, DECAY, STEP
    )
    gain_first_new, gain_second_new, gain_new = adam_update(
        gains, gain_grad, gain_first, gain_second, GAIN_RATE, 0.0, STEP
    )
    return (
        result.reshape(inputs.shape),
        d_tokens.reshape(inputs.shape),
        weight_share,
        weight_second,
        weight_new,
        gain_grad,
        gain_second_new,
        gain_new,
    )


def solution(mesh):
    fine = Mesh(
        mesh.devices.reshape(mesh.shape["dp"] // 2, 2, mesh.shape["ctx"]), ("x", "core", "ctx")
    )
    rows = P(("x", "core"), "ctx", None)
    stacked = P(("x", "core", "ctx"), None)
    return jax.shard_map(
        shards,
        mesh=fine,
        in_specs=(rows, rows, stacked, P(), stacked, stacked, P(), P()),
        out_specs=(rows, rows, stacked, stacked, stacked, P(), P(), P()),
        check_vma=False,
    )
```

```python
import jax
import jax.numpy as jnp
import numpy as np
from jax import lax
from jax.experimental import pallas as pl
from jax.experimental.pallas import tpu as pltpu
from jax.sharding import Mesh
from jax.sharding import PartitionSpec as P

HEADS = 15
KV = 5
HD = 64
FF = 2560
STEP = 10


SCALE_QK = 0.125
THETA = 10000.0
EPSILON = 1e-05
BETA_ONE = 0.9
BETA_TWO = 0.95
ADAM_EPS = 1e-08
DECAY = 0.1
RATE = 0.02
GAIN_RATE = 0.2
GROUP = HEADS // KV
KEY_TILE = 256
HIDDEN = -1e30
VMEM_BYTES = 48 * 1024 * 1024


def places(row_index, local_rows, ctx_count):
    half_rows = local_rows // 2
    owner_index = row_index // local_rows
    inner_index = row_index % local_rows
    return jnp.where(
        inner_index < half_rows,
        owner_index * half_rows + inner_index,
        (2 * ctx_count - 1 - owner_index) * half_rows + inner_index - half_rows,
    )


def angle_tables(positions_in, sign):
    half_width = HD // 2
    frequency = THETA ** (-jnp.arange(half_width, dtype=jnp.float32) * 2.0 / HD)
    angles = frequency[:, None] * positions_in.astype(jnp.float32)[None, :]
    return jnp.cos(angles), sign * jnp.sin(angles)


def rotate(values, tables):
    cosine, sine_part = tables
    heads = values.reshape(-1, HD, values.shape[-1])
    first_half = heads[:, : HD // 2]
    second_half = heads[:, HD // 2 :]
    return jnp.concatenate(
        [
            first_half * cosine - second_half * sine_part,
            second_half * cosine + first_half * sine_part,
        ],
        axis=1,
    ).reshape(values.shape)


def normalize(values):
    return values * lax.rsqrt(jnp.mean(values * values, axis=-1, keepdims=True) + EPSILON)


def norm_back(values, grad_in, gain_row):
    inv_scale = lax.rsqrt(jnp.mean(values * values, axis=-1, keepdims=True) + EPSILON)
    unit_rows = values * inv_scale
    grad_unit = grad_in * gain_row
    grad_values = inv_scale * (
        grad_unit - unit_rows * jnp.mean(grad_unit * unit_rows, axis=-1, keepdims=True)
    )
    return (grad_values, jnp.sum(grad_in * unit_rows, axis=0))


def matmul_n(left, right):
    return jnp.dot(left, right, preferred_element_type=jnp.float32)


def matmul_t(left, right):
    return lax.dot_general(
        left, right, (((1,), (1,)), ((), ())), preferred_element_type=jnp.float32
    )


def matmul_c(left, right):
    return lax.dot_general(
        left, right, (((0,), (0,)), ((), ())), preferred_element_type=jnp.float32
    )


def bit_groups():
    x_bits = lax.axis_size("x").bit_length() - 1
    ctx_bits = lax.axis_size("ctx").bit_length() - 1
    low_ctx = ctx_bits // 2
    along_x = [("x", bit) for bit in range(x_bits)]
    along_y = [("ctx", bit) for bit in range(low_ctx)]
    along_z = [("ctx", bit) for bit in range(low_ctx, ctx_bits)]
    return along_x, along_y, along_z


def swap_by(values, axis, offset):
    size = lax.axis_size(axis)
    return lax.ppermute(values, axis, [(i, i ^ offset) for i in range(size)])


def swap(values, where):
    return swap_by(values, where[0], 1 << where[1])


def add_low(left, right):
    return (left.astype(jnp.float32) + right.astype(jnp.float32)).astype(jnp.bfloat16)


def rel_offsets(order):
    strides = {"x": 2 * lax.axis_size("ctx"), "ctx": 1}
    offsets = np.zeros((1,), np.int64)
    for axis, bit in order:
        offsets = np.concatenate([offsets, offsets ^ (strides[axis] << bit)])
    return offsets


def lookup(slot, offsets):
    total = jnp.int32(0)
    for bit in range(len(offsets).bit_length() - 1):
        total = total + ((slot >> bit) & 1) * int(offsets[1 << bit])
    return total


def find(offset, offsets):
    total = jnp.int32(0)
    for bit in range(len(offsets).bit_length() - 1):
        place = int(offsets[1 << bit]).bit_length() - 1
        total = total + (((offset >> place) & 1) << bit)
    return total


def collect(values, order):
    kept, arrived = values, None
    for where in order:
        half = kept.shape[0] // 2
        if arrived is None:
            away, kept_next = kept[half:], kept[:half]
        else:
            away = add_low(kept[half:], arrived[half:])
            kept_next = add_low(kept[:half], arrived[:half])
        arrived = swap(away, where)
        kept = kept_next
    return kept[0].astype(jnp.float32) + arrived[0].astype(jnp.float32)


def scatter_whole(terms):
    ctx_count = lax.axis_size("ctx")
    count = 2 * lax.axis_size("x") * ctx_count
    along_x, along_y, along_z = bit_groups()
    core = ("core", 0)
    me = device_index().reshape(1)
    blocks, rows, width = terms[0].shape
    first = -(-rows // 48) * 16
    groups = [(0, first), (first, 2 * first), (2 * first, rows)]
    orders = [
        along_x + along_y + along_z,
        along_y + along_z + along_x,
        along_z + along_x + along_y,
    ]
    tables = [rel_offsets(list(reversed(order))) for order in orders]

    def target(step, me_ref, flip):
        return lookup(step, tables[0]) ^ me_ref[0] ^ flip

    def sources(flip):
        def chosen(member):
            def index(step, me_ref):
                spot = target(step, me_ref, flip)
                return (jnp.where(spot // blocks == member, spot % blocks, 0), 0, 0)

            return pl.BlockSpec((1, rows, width), index)

        return [chosen(member) for member in range(len(terms))]

    def pick_body(me_ref, *refs):
        held = target(pl.program_id(0), me_ref, ctx_count) // blocks
        for member in range(len(terms)):

            @pl.when(held == member)
            def _(member=member):
                refs[-1][...] = refs[member][...]

    away = pl.pallas_call(
        pick_body,
        grid_spec=pltpu.PrefetchScalarGridSpec(
            num_scalar_prefetch=1,
            grid=(count // 2,),
            in_specs=sources(ctx_count),
            out_specs=pl.BlockSpec((1, rows, width), lambda step, me_ref: (step, 0, 0)),
        ),
        out_shape=jax.ShapeDtypeStruct((count // 2, rows, width), jnp.bfloat16),
        compiler_params=pltpu.CompilerParams(vmem_limit_bytes=VMEM_BYTES),
    )(me, *terms)
    arrived = swap(away, core)

    def merge_body(me_ref, *refs):
        held = target(pl.program_id(0), me_ref, 0) // blocks
        for member in range(len(terms)):

            @pl.when(held == member)
            def _(member=member):
                for (low, high), out in zip(groups, refs[-3:]):
                    out[0] = add_low(refs[member][0, low:high], refs[-4][0, low:high])

    parts = pl.pallas_call(
        merge_body,
        grid_spec=pltpu.PrefetchScalarGridSpec(
            num_scalar_prefetch=1,
            grid=(count // 2,),
            in_specs=sources(0)
            + [pl.BlockSpec((1, rows, width), lambda step, me_ref: (step, 0, 0))],
            out_specs=[
                pl.BlockSpec(
                    (1, high - low, width),
                    lambda step, me_ref, table=table: (
                        find(lookup(step, tables[0]), table),
                        0,
                        0,
                    ),
                )
                for (low, high), table in zip(groups, tables)
            ],
        ),
        out_shape=[
            jax.ShapeDtypeStruct((count // 2, high - low, width), jnp.bfloat16)
            for low, high in groups
        ],
        compiler_params=pltpu.CompilerParams(vmem_limit_bytes=VMEM_BYTES),
    )(me, *terms, arrived)
    return jnp.concatenate([collect(part, order) for part, order in zip(parts, orders)], axis=0)


def device_index():
    return (
        (lax.axis_index("x") * 2 + lax.axis_index("core")) * lax.axis_size("ctx")
        + lax.axis_index("ctx")
    ).astype(jnp.int32)


def splits_rows(rows):
    along_x, along_y, along_z = bit_groups()
    return (len(along_x), len(along_y), len(along_z)) == (1, 1, 2) and rows % 64 == 0


def spread(values, order):
    values = values[None]
    for where in order:
        values = double(values, where)
    return values


def double(values, where):
    return jnp.concatenate([values, swap(values, where)], axis=0)


def ctx_orders():
    along_x, along_y, along_z = bit_groups()
    return [along_y + along_z, along_z + along_y]


def row_cuts(rows):
    first = -(-rows // 32) * 16
    return [(0, first), (first, rows)]


def slot_bits():
    along_x, along_y, along_z = bit_groups()
    return list(reversed(along_z)) + along_y


def total_low(*terms):
    total = terms[0].astype(jnp.float32)
    for term in terms[1:]:
        total = total + term.astype(jnp.float32)
    return total.astype(jnp.bfloat16)


def reduce_end(rest, z_far):
    total = z_far.astype(jnp.float32)
    for part in rest:
        total = total + part[0].astype(jnp.float32)
    return total


def reduce_halves(keep, away, ride, beside):
    far_z, near_z, along_y = slot_bits()
    come = beside(0, swap(away, ("core", 0)))
    sums = []
    for (low, high), order in zip(
        row_cuts(keep.shape[1]), ([along_y, near_z, far_z], [near_z, far_z, along_y])
    ):
        shape = (2, 2, 2, high - low, keep.shape[2])
        terms = [keep[:, low:high].reshape(shape), come[:, low:high].reshape(shape)]
        left = [along_y, near_z, far_z]
        for position, where in enumerate(order):
            dim = left.index(where)
            left.remove(where)
            sent = total_low(*[lax.index_in_dim(term, 1, dim, False) for term in terms])
            if low == 0:
                arrived, ride = swap_with(sent, ride, where)
                arrived = beside(position + 1, arrived)
            else:
                arrived = swap(sent, where)
            terms = [lax.index_in_dim(term, 0, dim, False) for term in terms] + [arrived]
        total = terms[0].astype(jnp.float32)
        for term in terms[1:]:
            total = total + term.astype(jnp.float32)
        sums.append(total)
    return jnp.concatenate(sums, axis=0), ride


def ride_parts(ride):
    rounded = lax.reduce_precision(ride, 8, 7)
    return rounded, lax.reduce_precision(ride - rounded, 8, 7)


def with_ride(sent, parts):
    extra = jnp.concatenate([*parts, jnp.zeros((12, parts[0].shape[1]), jnp.float32)])
    return jnp.concatenate([sent.reshape(-1, sent.shape[-1]), extra.astype(jnp.bfloat16)], axis=0)


def swap_with(sent, ride, where):
    parts = ride_parts(ride)
    come, other = off_ride(swap(with_ride(sent, parts), where), sent.shape)
    return come, (parts[0] + parts[1]) + other


def off_ride(come, shape):
    parts = come[-16:].astype(jnp.float32)
    return come[:-16].reshape(shape), parts[0:2] + parts[2:4]


def gather_first(weights):
    half = weights.shape[0] // 2
    far = lax.ppermute(weights, ("x", "core"), [(0, 2)])
    rows = jnp.where(lax.axis_index("x") == 0, weights, far)
    come = swap(rows[half:], ("core", 0))
    return jnp.where(lax.axis_index("core") == 0, rows[:half], come), far


def gather_quarters(weights, first_far):
    half = weights.shape[0] // 2
    x_index, core = lax.axis_index("x"), lax.axis_index("core")
    far = lax.ppermute(weights, ("x", "core"), [(2, 0), (1, 3), (3, 1)])
    far = jnp.where((x_index == 1) & (core == 0), first_far, far)
    both = jnp.stack([jnp.where(x_index == 0, weights, far), jnp.where(x_index == 0, far, weights)])
    keep = jnp.where(core == 0, both[:, :half], both[:, half:])
    come = swap(jnp.where(core == 0, both[:, half:], both[:, :half]), ("core", 0))
    first = jnp.where(core == 0, keep, come)
    second = jnp.where(core == 0, come, keep)
    feed = jnp.stack([second[0], first[1], second[1]])
    return jnp.where(x_index == 0, feed[:, : half // 2], feed[:, half // 2 :])


def place_rows(own, far):
    tables = [rel_offsets(list(reversed(order))) for order in ctx_orders()]
    slots, width = own[0].shape[0], own[0].shape[2]
    lengths = [part.shape[1] for part in own]
    half = sum(lengths)

    def body(me_ref, *refs):
        out_ref = refs[-1]
        for core in range(2):

            @pl.when(me_ref[0] == core)
            def _(core=core):
                for source, base in ((0, core * half), (2, (1 - core) * half)):
                    out_ref[0, base : base + lengths[0]] = refs[source][0]
                    out_ref[0, base + lengths[0] : base + half] = refs[source + 1][0]

    specs = [
        pl.BlockSpec(
            (1, length, width),
            lambda step, me_ref, table=table: (find(step ^ me_ref[1], table), 0, 0),
        )
        for length, table in zip(lengths, tables)
    ]
    me = jnp.stack([lax.axis_index("core"), lax.axis_index("ctx")]).astype(jnp.int32)
    return pl.pallas_call(
        body,
        grid_spec=pltpu.PrefetchScalarGridSpec(
            num_scalar_prefetch=1,
            grid=(slots,),
            in_specs=specs * 2,
            out_specs=pl.BlockSpec((1, 2 * half, width), lambda step, me_ref: (step, 0, 0)),
        ),
        out_shape=jax.ShapeDtypeStruct((slots, 2 * half, width), own[0].dtype),
        cost_estimate=pl.CostEstimate(
            flops=0, bytes_accessed=8 * slots * half * width, transcendentals=0
        ),
        compiler_params=pltpu.CompilerParams(vmem_limit_bytes=VMEM_BYTES),
    )(me, *own, *far).reshape(slots * 2 * half, width)


def turned(values):
    return jnp.transpose(values)


def load_packed(ref, aligned):
    if not aligned:
        return ref[0, 0]
    half = ref.shape[1] // 2
    return jnp.concatenate(
        [
            ref[head * HD : (head + 1) * HD, side * half : (side + 1) * half]
            for side in range(2)
            for head in range(GROUP)
        ],
        axis=1,
    )


def store_packed(ref, values, aligned):
    if not aligned:
        ref[0, 0] = values
        return
    half = ref.shape[1] // 2
    for side in range(2):
        for head in range(GROUP):
            start = (side * GROUP + head) * half
            ref[head * HD : (head + 1) * HD, side * half : (side + 1) * half] = values[
                :, start : start + half
            ]


def load_tile(refs, side, tile):
    length = refs[0].shape[1] // 2
    if length >= KEY_TILE:
        start = side * length + tile * KEY_TILE
        return refs[0][:, start : start + KEY_TILE]
    many = KEY_TILE // length
    return jnp.concatenate(
        [
            ref[:, side * length : (side + 1) * length]
            for ref in refs[tile * many : (tile + 1) * many]
        ],
        axis=1,
    )


def attend_body(count, aligned, queries_ref, key_pos_ref, query_pos_ref, *refs):
    key_refs, value_refs = refs[:count], refs[count : 2 * count]
    out_ref, total_ref, work = refs[2 * count :]
    queries = load_packed(queries_ref, aligned)
    low_cols = queries.shape[1] // 2
    queries_high = queries[:, low_cols:]
    tiles = key_pos_ref.shape[1] // KEY_TILE
    largest = jnp.full((1, queries.shape[1]), HIDDEN, jnp.float32)
    largest_high = jnp.full((1, low_cols), HIDDEN, jnp.float32)
    for side in range(2):
        for tile in range(tiles):
            keys = turned(load_tile(key_refs, side, tile))
            row = (side * tiles + tile) * KEY_TILE
            key_places = key_pos_ref[side, tile * KEY_TILE : (tile + 1) * KEY_TILE]
            if side == 0:
                scores = matmul_n(keys, queries)
                scores = jnp.where(key_places <= query_pos_ref[...], scores, HIDDEN)
                work[row : row + KEY_TILE] = scores
                largest = jnp.maximum(largest, jnp.max(scores, axis=0, keepdims=True))
            else:
                scores = matmul_n(keys, queries_high)
                scores = jnp.where(key_places <= query_pos_ref[:, low_cols:], scores, HIDDEN)
                work[row : row + KEY_TILE, low_cols:] = scores
                largest_high = jnp.maximum(largest_high, jnp.max(scores, axis=0, keepdims=True))
    high_max = jnp.maximum(largest[:, low_cols:], largest_high)
    largest = jnp.concatenate([largest[:, :low_cols], high_max], axis=1)
    total = jnp.zeros_like(largest)
    mixed = jnp.zeros((HD, queries.shape[1]), jnp.float32)
    total_high = jnp.zeros_like(largest_high)
    mixed_high = jnp.zeros((HD, low_cols), jnp.float32)
    for side in range(2):
        for tile in range(tiles):
            values = load_tile(value_refs, side, tile)
            row = (side * tiles + tile) * KEY_TILE
            if side == 0:
                expos = jnp.exp(work[row : row + KEY_TILE] - largest)
                total = total + jnp.sum(expos, axis=0, keepdims=True)
                mixed = mixed + matmul_n(values, expos.astype(jnp.bfloat16))
            else:
                expos = jnp.exp(work[row : row + KEY_TILE, low_cols:] - high_max)
                total_high = total_high + jnp.sum(expos, axis=0, keepdims=True)
                mixed_high = mixed_high + matmul_n(values, expos.astype(jnp.bfloat16))
    total = jnp.concatenate([total[:, :low_cols], total[:, low_cols:] + total_high], axis=1)
    mixed = jnp.concatenate([mixed[:, :low_cols], mixed[:, low_cols:] + mixed_high], axis=1)
    store_packed(out_ref, (mixed / total).astype(jnp.bfloat16), aligned)
    total_ref[0, 0] = largest + jnp.log(total)


def attend_back_body(
    count, aligned, queries_ref, key_pos_ref, query_pos_ref, *refs
):
    key_refs, value_refs = refs[:count], refs[count : 2 * count]
    out_ref, total_ref, d_out_ref, cosine_ref, sine_ref = refs[2 * count : 2 * count + 5]
    d_queries_ref, pair_refs = refs[2 * count + 5], refs[2 * count + 6 :]
    all_queries, all_d_out = load_packed(queries_ref, aligned), load_packed(d_out_ref, aligned)
    low_cols = all_queries.shape[1] // 2
    tiles = key_pos_ref.shape[1] // KEY_TILE
    delta = jnp.sum(
        all_d_out.astype(jnp.float32) * load_packed(out_ref, aligned).astype(jnp.float32),
        axis=0,
        keepdims=True,
    )
    totals = total_ref[0, 0]
    parts = []
    for side in range(2):
        if side == 0:
            queries, d_out = all_queries, all_d_out
            query_places, log_total, row_delta = query_pos_ref[...], totals, delta
        else:
            queries, d_out = all_queries[:, low_cols:], all_d_out[:, low_cols:]
            query_places = query_pos_ref[:, low_cols:]
            log_total, row_delta = totals[:, low_cols:], delta[:, low_cols:]
        part = jnp.zeros((HD, queries.shape[1]), jnp.float32)
        for tile in range(tiles):
            keys_flat = load_tile(key_refs, side, tile)
            scores = matmul_n(turned(keys_flat), queries)
            seen = key_pos_ref[side, tile * KEY_TILE : (tile + 1) * KEY_TILE] <= query_places
            probs = jnp.where(seen, jnp.exp(scores - log_total), 0.0)
            d_probs = matmul_n(turned(load_tile(value_refs, side, tile)), d_out)
            d_scores = (probs * (d_probs - row_delta)).astype(jnp.bfloat16)
            part = part + matmul_n(keys_flat, d_scores)
            d_key = matmul_t(d_scores, queries).astype(jnp.bfloat16)
            d_value = matmul_t(probs.astype(jnp.bfloat16), d_out).astype(jnp.bfloat16)
            if aligned:
                length = key_refs[0].shape[1] // 2
                places_out = [(ref, slot) for ref in pair_refs for slot in range(ref.shape[0])]
                for piece in range(KEY_TILE // length):
                    ref, slot = places_out[tile * (KEY_TILE // length) + piece]
                    rows = slice(piece * length, (piece + 1) * length)
                    ref[slot, 0, side, :, :HD] = d_key[rows]
                    ref[slot, 0, side, :, HD:] = d_value[rows]
            else:
                rows = slice(tile * KEY_TILE, (tile + 1) * KEY_TILE)
                pair_refs[0][side, 0, rows, :HD] = d_key
                pair_refs[0][side, 0, rows, HD:] = d_value
        parts.append(part)
    d_queries = jnp.concatenate(
        [parts[0][:, :low_cols], parts[0][:, low_cols:] + parts[1]], axis=1
    )
    cosine, sine_part = cosine_ref[...], sine_ref[...]
    first_half, second_half = d_queries[: HD // 2], d_queries[HD // 2 :]
    turned_back = jnp.concatenate(
        [
            first_half * cosine + second_half * sine_part,
            second_half * cosine - first_half * sine_part,
        ],
        axis=0,
    )
    store_packed(d_queries_ref, (turned_back * SCALE_QK).astype(jnp.bfloat16), aligned)


def own_mask(rows, cols):
    return lax.broadcasted_iota(jnp.int32, (rows, cols), 0) <= (
        lax.broadcasted_iota(jnp.int32, (rows, cols), 1) % rows
    )


def slot_keys(ref, length):
    both = turned(ref[...])
    return both[:length], both[length:]


def attend_slots_body(count, flags_ref, queries_ref, *refs):
    key_refs, value_refs = refs[:count], refs[count : 2 * count]
    out_ref, total_ref, both_queries, work, largest, totals, mixed = refs[2 * count :]
    length = key_refs[0].shape[1] // 2
    cols = GROUP * length
    packed = load_packed(queries_ref, True)
    for side in range(2):
        both_queries[side] = packed[:, side * cols : (side + 1) * cols]
    visible = own_mask(length, cols)
    low_keys, high_keys = zip(*[slot_keys(ref, length) for ref in key_refs])
    row = 0

    def keep_scores(scores, row):
        work[row : row + scores.shape[0]] = scores
        return jnp.max(scores, axis=0, keepdims=True)

    for side, keys in ((0, low_keys[0]), (1, high_keys[0])):
        scores = jnp.where(visible, matmul_n(keys, both_queries[side]), HIDDEN)
        largest[side] = keep_scores(scores, row)
        row += length
    for slot in range(0, count, 2):
        keys = jnp.concatenate([low_keys[slot], low_keys[slot + 1]], axis=0)
        top = keep_scores(matmul_n(keys, both_queries[1]), row)
        largest[1] = jnp.maximum(largest[1], top)
        row += 2 * length
    for slot in range(1, count):
        side = flags_ref[slot]
        keys = jnp.where(side == 0, low_keys[slot], high_keys[slot])
        top = keep_scores(matmul_n(keys, both_queries[side]), row)
        largest[side] = jnp.maximum(largest[side], top)
        row += length
    row = 0
    for side in range(2):
        values = value_refs[0][:, side * length : (side + 1) * length]
        expos = jnp.exp(work[row : row + length] - largest[side])
        totals[side] = jnp.sum(expos, axis=0, keepdims=True)
        mixed[side] = matmul_n(values, expos.astype(jnp.bfloat16))
        row += length
    for slot in range(0, count, 2):
        values = jnp.concatenate(
            [value_refs[slot][:, :length], value_refs[slot + 1][:, :length]], axis=1
        )
        expos = jnp.exp(work[row : row + 2 * length] - largest[1])
        totals[1] += jnp.sum(expos, axis=0, keepdims=True)
        mixed[1] += matmul_n(values, expos.astype(jnp.bfloat16))
        row += 2 * length
    for slot in range(1, count):
        side = flags_ref[slot]
        values = jnp.where(side == 0, value_refs[slot][:, :length], value_refs[slot][:, length:])
        expos = jnp.exp(work[row : row + length] - largest[side])
        totals[side] += jnp.sum(expos, axis=0, keepdims=True)
        mixed[side] += matmul_n(values, expos.astype(jnp.bfloat16))
        row += length
    result = [(mixed[side] / totals[side]).astype(jnp.bfloat16) for side in range(2)]
    store_packed(out_ref, jnp.concatenate(result, axis=1), True)
    logs = [largest[side] + jnp.log(totals[side]) for side in range(2)]
    total_ref[0, 0] = jnp.concatenate(logs, axis=1)


def attend_slots_back_body(count, flags_ref, queries_ref, *refs):
    key_refs, value_refs = refs[:count], refs[count : 2 * count]
    out_ref, total_ref, d_out_ref, cosine_ref, sine_ref = refs[2 * count : 2 * count + 5]
    d_queries_ref = refs[2 * count + 5]
    pair_refs = refs[2 * count + 6 : -7]
    both_queries, both_d_out, turned_queries, turned_d_out, log_totals, deltas, sums = refs[-7:]
    length = key_refs[0].shape[1] // 2
    cols = GROUP * length
    queries, d_out = load_packed(queries_ref, True), load_packed(d_out_ref, True)
    delta = jnp.sum(
        d_out.astype(jnp.float32) * load_packed(out_ref, True).astype(jnp.float32),
        axis=0,
        keepdims=True,
    )
    for side in range(2):
        part = slice(side * cols, (side + 1) * cols)
        both_queries[side] = queries[:, part]
        both_d_out[side] = d_out[:, part]
        turned_queries[side] = turned(queries[:, part])
        turned_d_out[side] = turned(d_out[:, part])
        log_totals[side] = total_ref[0, 0, :, part]
        deltas[side] = delta[:, part]
    sums[...] = jnp.zeros_like(sums)
    visible = own_mask(length, cols)
    low_keys, high_keys = zip(*[slot_keys(ref, length) for ref in key_refs])
    low_values, high_values = zip(*[slot_keys(ref, length) for ref in value_refs])
    places_out = [(ref, slot) for ref in pair_refs for slot in range(ref.shape[0])]

    def block(keys, keys_flat, values, side, mask=None):
        probs = jnp.exp(matmul_n(keys, both_queries[side]) - log_totals[side])
        if mask is not None:
            probs = jnp.where(mask, probs, 0.0)
        d_probs = matmul_n(values, both_d_out[side])
        d_scores = (probs * (d_probs - deltas[side])).astype(jnp.bfloat16)
        sums[side] += matmul_n(keys_flat, d_scores)
        return jnp.concatenate(
            [
                matmul_n(d_scores, turned_queries[side]),
                matmul_n(probs.astype(jnp.bfloat16), turned_d_out[side]),
            ],
            axis=1,
        )

    low_terms = []
    for slot in range(0, count, 2):
        keys, values = [
            jnp.concatenate([part[slot], part[slot + 1]], axis=0) for part in (low_keys, low_values)
        ]
        flat = jnp.concatenate([key_refs[slot][:, :length], key_refs[slot + 1][:, :length]], axis=1)
        terms = block(keys, flat, values, 1)
        low_terms += [terms[:length], terms[length:]]
    ref, slot = places_out[0]
    own = [
        block(keys, key_refs[0][:, side * length : (side + 1) * length], values, side, visible)
        for side, (keys, values) in enumerate(
            ((low_keys[0], low_values[0]), (high_keys[0], high_values[0]))
        )
    ]
    ref[slot, 0, 0] = (low_terms[0] + own[0]).astype(jnp.bfloat16)
    ref[slot, 0, 1] = own[1].astype(jnp.bfloat16)
    for member in range(1, count):
        side = flags_ref[member]
        low = side == 0
        keys = jnp.where(low, low_keys[member], high_keys[member])
        flat = jnp.where(low, key_refs[member][:, :length], key_refs[member][:, length:])
        values = jnp.where(low, low_values[member], high_values[member])
        terms = block(keys, flat, values, side)
        ref, slot = places_out[member]
        ref[slot, 0, 0] = (low_terms[member] + jnp.where(low, terms, 0.0)).astype(jnp.bfloat16)
        ref[slot, 0, 1] = jnp.where(low, 0.0, terms).astype(jnp.bfloat16)
    d_queries = jnp.concatenate([sums[0], sums[1]], axis=1)
    store_packed(d_queries_ref, turn_queries_back(d_queries, cosine_ref, sine_ref), True)


def turn_queries_back(d_queries, cosine_ref, sine_ref):
    cosine, sine_part = cosine_ref[...], sine_ref[...]
    first_half, second_half = d_queries[: HD // 2], d_queries[HD // 2 :]
    turned_back = jnp.concatenate(
        [
            first_half * cosine + second_half * sine_part,
            second_half * cosine - first_half * sine_part,
        ],
        axis=0,
    )
    return (turned_back * SCALE_QK).astype(jnp.bfloat16)


def slot_specs(leads, local_rows, seq):
    specs = [
        pl.BlockSpec(memory_space=pltpu.SMEM),
        pl.BlockSpec((GROUP * HD, local_rows), lambda head: (head, seq)),
    ]
    for first in (0, KV):
        specs += [
            pl.BlockSpec(
                (None, HD, local_rows),
                lambda head, lead=lead, first=first: (lead, first + head, 0),
            )
            for lead in leads
        ]
    return specs


def attend_slots(queries, pairs, flags, local_rows, seq):
    count, cols = len(pairs), GROUP * local_rows // 2
    leads, arrays = [lead for _, lead in pairs], [array for array, _ in pairs]
    work = HEADS * local_rows * local_rows * count // 2
    return pl.pallas_call(
        lambda *refs: attend_slots_body(count, *refs),
        grid=(KV,),
        in_specs=slot_specs(leads, local_rows, seq),
        out_specs=[
            pl.BlockSpec((GROUP * HD, local_rows), lambda head: (head, 0)),
            pl.BlockSpec((1, 1, 1, 2 * cols), lambda head: (0, head, 0, 0)),
        ],
        out_shape=[
            jax.ShapeDtypeStruct((HEADS * HD, local_rows), jnp.bfloat16),
            jax.ShapeDtypeStruct((1, KV, 1, 2 * cols), jnp.float32),
        ],
        scratch_shapes=[
            pltpu.VMEM((2, HD, cols), jnp.bfloat16),
            pltpu.VMEM(((2 * count + 1) * local_rows // 2, cols), jnp.float32),
            pltpu.VMEM((2, 1, cols), jnp.float32),
            pltpu.VMEM((2, 1, cols), jnp.float32),
            pltpu.VMEM((2, HD, cols), jnp.float32),
        ],
        cost_estimate=pl.CostEstimate(
            flops=work * HD, bytes_accessed=1024 * 1024, transcendentals=0
        ),
        compiler_params=pltpu.CompilerParams(vmem_limit_bytes=VMEM_BYTES),
    )(flags, queries, *arrays, *arrays)


def attend_slots_back(
    queries, pairs, flags, mixed, log_total, d_mixed, tables, local_rows, seq, sets
):
    count, cols = len(pairs), GROUP * local_rows // 2
    leads, arrays = [lead for _, lead in pairs], [array for array, _ in pairs]
    work = HEADS * local_rows * local_rows * count // 2
    own = pl.BlockSpec((GROUP * HD, local_rows), lambda head: (head, 0))
    table_spec = pl.BlockSpec((HD // 2, 2 * cols), lambda head: (0, 0))
    length = local_rows // 2
    return pl.pallas_call(
        lambda *refs: attend_slots_back_body(count, *refs),
        grid=(KV,),
        in_specs=slot_specs(leads, local_rows, seq)
        + [
            own,
            pl.BlockSpec((1, 1, 1, 2 * cols), lambda head: (0, head, 0, 0)),
            pl.BlockSpec((GROUP * HD, local_rows), lambda head: (head, seq)),
            table_spec,
            table_spec,
        ],
        out_specs=[own]
        + [
            pl.BlockSpec((slots, 1, 2, length, 2 * HD), lambda head: (0, head, 0, 0, 0))
            for slots in sets
        ],
        out_shape=[jax.ShapeDtypeStruct((HEADS * HD, local_rows), jnp.bfloat16)]
        + [jax.ShapeDtypeStruct((slots, KV, 2, length, 2 * HD), jnp.bfloat16) for slots in sets],
        scratch_shapes=[
            pltpu.VMEM((2, HD, cols), jnp.bfloat16),
            pltpu.VMEM((2, HD, cols), jnp.bfloat16),
            pltpu.VMEM((2, cols, HD), jnp.bfloat16),
            pltpu.VMEM((2, cols, HD), jnp.bfloat16),
            pltpu.VMEM((2, 1, cols), jnp.float32),
            pltpu.VMEM((2, 1, cols), jnp.float32),
            pltpu.VMEM((2, HD, cols), jnp.float32),
        ],
        cost_estimate=pl.CostEstimate(
            flops=work * HD, bytes_accessed=1024 * 1024, transcendentals=0
        ),
        compiler_params=pltpu.CompilerParams(vmem_limit_bytes=VMEM_BYTES),
    )(flags, queries, *arrays, *arrays, mixed, log_total, d_mixed, *tables)


def head_specs(leads, aligned, cols, keys, local_rows, seq):
    count = len(leads)
    if aligned:
        packed = pl.BlockSpec((GROUP * HD, local_rows), lambda head: (head, seq))
    else:
        packed = pl.BlockSpec((1, 1, HD, cols), lambda head: (seq, head, 0, 0))
    specs = [
        packed,
        pl.BlockSpec((2, keys, 1), lambda head: (0, 0, 0)),
        pl.BlockSpec((1, cols), lambda head: (0, 0)),
    ]
    for first in (0, KV):
        specs += [
            pl.BlockSpec(
                (None, HD, 2 * keys // count),
                lambda head, lead=lead, first=first: (lead, first + head, seq),
            )
            for lead in leads
        ]
    return packed, specs


def attend(queries, pairs, key_pos, query_pos, local_rows, seq):
    aligned = queries.ndim == 2
    cols, keys, count = query_pos.shape[1], key_pos.shape[1], len(pairs)
    leads, arrays = [lead for _, lead in pairs], [array for array, _ in pairs]
    _, specs = head_specs(leads, aligned, cols, keys, local_rows, seq)
    work = HEADS * keys * cols // GROUP * 3 // 2
    if aligned:
        out_spec = pl.BlockSpec((GROUP * HD, local_rows), lambda head: (head, 0))
        out_shape = jax.ShapeDtypeStruct((HEADS * HD, local_rows), jnp.bfloat16)
    else:
        out_spec = pl.BlockSpec((1, 1, HD, cols), lambda head: (0, head, 0, 0))
        out_shape = jax.ShapeDtypeStruct((1, KV, HD, cols), jnp.bfloat16)
    return pl.pallas_call(
        lambda *refs: attend_body(count, aligned, *refs),
        grid=(KV,),
        in_specs=specs,
        out_specs=[out_spec, pl.BlockSpec((1, 1, 1, cols), lambda head: (0, head, 0, 0))],
        out_shape=[out_shape, jax.ShapeDtypeStruct((1, KV, 1, cols), jnp.float32)],
        scratch_shapes=[pltpu.VMEM((2 * keys, cols), jnp.float32)],
        cost_estimate=pl.CostEstimate(
            flops=work * HD, bytes_accessed=1024 * 1024, transcendentals=0
        ),
        compiler_params=pltpu.CompilerParams(vmem_limit_bytes=VMEM_BYTES),
    )(queries, key_pos, query_pos, *arrays, *arrays)


def attend_back(
    queries, pairs, key_pos, query_pos, mixed, log_total, d_mixed, tables, local_rows, seq, sets
):
    aligned = queries.ndim == 2
    cols, keys, count = query_pos.shape[1], key_pos.shape[1], len(pairs)
    leads, arrays = [lead for _, lead in pairs], [array for array, _ in pairs]
    packed, specs = head_specs(leads, aligned, cols, keys, local_rows, seq)
    work = HEADS * keys * cols // GROUP * 3 // 2
    if aligned:
        own = pl.BlockSpec((GROUP * HD, local_rows), lambda head: (head, 0))
        own_shape = jax.ShapeDtypeStruct((HEADS * HD, local_rows), jnp.bfloat16)
        length = keys // count
        pair_specs = [
            pl.BlockSpec((slots, 1, 2, length, 2 * HD), lambda head: (0, head, 0, 0, 0))
            for slots in sets
        ]
        pair_shapes = [
            jax.ShapeDtypeStruct((slots, KV, 2, length, 2 * HD), jnp.bfloat16) for slots in sets
        ]
    else:
        own = pl.BlockSpec((1, 1, HD, cols), lambda head: (0, head, 0, 0))
        own_shape = jax.ShapeDtypeStruct((1, KV, HD, cols), jnp.bfloat16)
        pair_specs = [pl.BlockSpec((2, 1, keys, 2 * HD), lambda head: (0, head, 0, 0))]
        pair_shapes = [jax.ShapeDtypeStruct((2, KV, keys, 2 * HD), jnp.bfloat16)]
    table_spec = pl.BlockSpec((HD // 2, cols), lambda head: (0, 0))
    return pl.pallas_call(
        lambda *refs: attend_back_body(count, aligned, *refs),
        grid=(KV,),
        in_specs=specs
        + [
            own,
            pl.BlockSpec((1, 1, 1, cols), lambda head: (0, head, 0, 0)),
            packed,
            table_spec,
            table_spec,
        ],
        out_specs=[own] + pair_specs,
        out_shape=[own_shape] + pair_shapes,
        cost_estimate=pl.CostEstimate(
            flops=work * HD, bytes_accessed=1024 * 1024, transcendentals=0
        ),
        compiler_params=pltpu.CompilerParams(vmem_limit_bytes=VMEM_BYTES),
    )(queries, key_pos, query_pos, *arrays, *arrays, mixed, log_total, d_mixed, *tables)


def put_rows(values, keep_ref, away_ref, place, core, x_index):
    quarter = values.shape[0] // 4
    for mine in range(4):

        @pl.when(2 * core + x_index == mine)
        def _(mine=mine):
            for ref, side in ((keep_ref, mine // 2), (away_ref, 1 - mine // 2)):
                for position, along_x in enumerate((mine % 2, 1 - mine % 2)):
                    start = (2 * side + along_x) * quarter
                    ref[place[0], place[1], position * quarter : (position + 1) * quarter] = values[
                        start : start + quarter
                    ]


def feed_body(
    parts, split, chained, me_ref, a_two_ref, dy_ref, *refs
):
    count = 4 if split else 6
    before, refs = (refs[:2], refs[2:]) if chained else (None, refs)
    weight_refs, (out_ref, d_two_ref), grad_refs = (
        refs[:count],
        refs[count : count + 2],
        refs[count + 2 :],
    )
    core, x_index = me_ref[0], me_ref[1]
    step = pl.program_id(0)

    @pl.when(step == 0)
    def _():
        for place, ref in enumerate((out_ref, d_two_ref)):
            ref[...] = before[place][...] if chained else jnp.zeros_like(ref)

    def rows_of(member):
        if split:
            rows_out = []
            for slot in range(weight_refs[0].shape[0]):
                parts_here = [ref[slot, member] for ref in weight_refs]
                for side in range(2):
                    for along_x in range(2):
                        near = jnp.where(x_index == along_x, parts_here[0], parts_here[1])
                        far = jnp.where(x_index == along_x, parts_here[2], parts_here[3])
                        rows_out.append(jnp.where(core == side, near, far))
            return jnp.concatenate(rows_out, axis=0)
        wanted = feed_core(member, step, parts)
        return jnp.where(wanted == core, weight_refs[2 * member][0], weight_refs[2 * member + 1][0])

    a_two, dy_low = a_two_ref[...], dy_ref[...]
    gate_rows, up_rows, down_rows = rows_of(0), rows_of(1), rows_of(2)
    gate_pre = matmul_t(gate_rows, a_two)
    up_pre = matmul_t(up_rows, a_two)
    d_hidden = matmul_t(down_rows, dy_low)
    sigma = jax.nn.sigmoid(gate_pre)
    gate_act = gate_pre * sigma
    hidden = (gate_act * up_pre).astype(jnp.bfloat16)
    d_gate = (d_hidden * up_pre * sigma * (1.0 + gate_pre * (1.0 - sigma))).astype(jnp.bfloat16)
    d_up = (d_hidden * gate_act).astype(jnp.bfloat16)
    out_ref[...] += matmul_c(hidden, down_rows)
    d_two_ref[...] += matmul_c(d_gate, gate_rows) + matmul_c(d_up, up_rows)
    for member, (left, right) in enumerate(((d_gate, a_two), (d_up, a_two), (hidden, dy_low))):
        grad = matmul_n(left, right).astype(jnp.bfloat16)
        if split:
            slots = grad_refs[0].shape[0]
            rows = grad.shape[0] // slots
            for slot in range(slots):
                put_rows(
                    grad[slot * rows : (slot + 1) * rows], *grad_refs, (slot, member), core, x_index
                )
        else:
            grad_refs[member][0] = grad


def feed_core(member, step, parts):
    ctx_count, single = parts
    return (member + 1) % 2 if single else step // ctx_count


def feed_forward(a_two, dy_low, mine, far, rows, before=()):
    tokens, width = a_two.shape
    ctx_count = lax.axis_size("ctx")
    blocks = FF // rows
    single = blocks == ctx_count
    split = mine[0].ndim == 4 if isinstance(mine, list) else False
    parts = (ctx_count, single)
    whole = pl.BlockSpec((tokens, width), lambda step, me_ref: (0, 0))

    def weight_spec(member, own):
        first = (member + 1) * blocks // ctx_count // 2 * ctx_count

        def index(step, me_ref):
            matches = (feed_core(member, step, parts) == me_ref[0]) == own
            return (first + jnp.where(matches, step % ctx_count, 0), 0, 0)

        return pl.BlockSpec((1, rows, width), index)

    if split:
        weight_specs = [
            pl.BlockSpec((2, 3, rows // 4, width), lambda step, me_ref: (step, 0, 0, 0))
        ] * 4
        weight_args = [*mine, *far]
        half = pl.BlockSpec((2, 3, rows // 2, width), lambda step, me_ref: (step, 0, 0, 0))
        grad_specs = [half, half]
        blocks = mine[0].shape[0]
        grad_shapes = [jax.ShapeDtypeStruct((blocks, 3, rows // 2, width), jnp.bfloat16)] * 2
    else:
        weight_specs = [weight_spec(member, own) for member in range(3) for own in (True, False)]
        weight_args = [mine, far] * 3
        grad_specs = [pl.BlockSpec((1, rows, width), lambda step, me_ref: (step, 0, 0))] * 3
        grad_shapes = [jax.ShapeDtypeStruct((blocks, rows, width), jnp.bfloat16)] * 3
    me = jnp.stack([lax.axis_index("core"), lax.axis_index("x")]).astype(jnp.int32)
    return pl.pallas_call(
        lambda *refs: feed_body(parts, split, bool(before), *refs),
        grid_spec=pltpu.PrefetchScalarGridSpec(
            num_scalar_prefetch=1,
            grid=(blocks // 2 if split else blocks,),
            in_specs=[whole] * (2 + len(before)) + weight_specs,
            out_specs=[whole, whole] + grad_specs,
        ),
        out_shape=[jax.ShapeDtypeStruct((tokens, width), jnp.float32)] * 2 + grad_shapes,
        cost_estimate=pl.CostEstimate(
            flops=18 * tokens * width * blocks * rows, bytes_accessed=12 * blocks * rows * width,
            transcendentals=0,
        ),
        compiler_params=pltpu.CompilerParams(vmem_limit_bytes=VMEM_BYTES),
    )(me, a_two, dy_low, *before, *weight_args)


def first_grads(d_qkv, attn_low, a_one, d_resid_low, rows, split):
    tokens, width = a_one.shape
    early = d_qkv.shape[0] // rows
    blocks = early + attn_low.shape[0] // rows

    def body(me_ref, qkv_ref, attn_ref, one_ref, resid_ref, *grad_refs):
        first = pl.program_id(0) < early
        left = jnp.where(first, qkv_ref[...], attn_ref[...])
        right = jnp.where(first, one_ref[...], resid_ref[...])
        grad = matmul_n(left, right).astype(jnp.bfloat16)
        if split:
            put_rows(grad, *grad_refs, (0, 0), me_ref[0], 0)
        else:
            grad_refs[0][0] = grad

    whole = pl.BlockSpec((tokens, width), lambda step, me_ref: (0, 0))
    if split:
        table = rel_offsets(slot_bits())
        half = pl.BlockSpec(
            (1, 1, rows // 2, width), lambda step, me_ref: (find(step ^ me_ref[1], table), 0, 0, 0)
        )
        grad_specs = [half, half]
        grad_shapes = [jax.ShapeDtypeStruct((blocks, 1, rows // 2, width), jnp.bfloat16)] * 2
    else:
        grad_specs = [pl.BlockSpec((1, rows, width), lambda step, me_ref: (step, 0, 0))]
        grad_shapes = [jax.ShapeDtypeStruct((blocks, rows, width), jnp.bfloat16)]
    me = jnp.stack([lax.axis_index(name) for name in ("core", "ctx")]).astype(jnp.int32)
    return pl.pallas_call(
        body,
        grid_spec=pltpu.PrefetchScalarGridSpec(
            num_scalar_prefetch=1,
            grid=(blocks,),
            in_specs=[
                pl.BlockSpec((rows, tokens), lambda step, me_ref: (jnp.minimum(step, early - 1), 0)),
                pl.BlockSpec((rows, tokens), lambda step, me_ref: (jnp.maximum(step - early, 0), 0)),
                whole,
                whole,
            ],
            out_specs=grad_specs,
        ),
        out_shape=grad_shapes,
        cost_estimate=pl.CostEstimate(
            flops=2 * tokens * width * blocks * rows, bytes_accessed=2 * blocks * rows * width, transcendentals=0
        ),
        compiler_params=pltpu.CompilerParams(vmem_limit_bytes=VMEM_BYTES),
    )(me, d_qkv, attn_low, a_one, d_resid_low)


def adam_update(param, grad, first, second, rate, decay, step_number):
    first_new = BETA_ONE * first + (1.0 - BETA_ONE) * grad
    second_new = BETA_TWO * second + (1.0 - BETA_TWO) * grad * grad
    fix_one = 1.0 - BETA_ONE**step_number
    fix_two = 1.0 - BETA_TWO**step_number
    update = first_new / fix_one / (jnp.sqrt(second_new / fix_two) + ADAM_EPS)
    return (first_new, second_new, param - rate * (update + decay * param))


def shards(inputs, cotangent, weights, gains, first_moment, second_moment, gain_first, gain_second):
    ctx_count = lax.axis_size("ctx")
    x_count = lax.axis_size("x")
    ctx_index, core, x_index = lax.axis_index("ctx"), lax.axis_index("core"), lax.axis_index("x")
    seqs, local_rows, model_width = inputs.shape
    half_rows = local_rows // 2
    tokens = seqs * local_rows
    weight_rows = weights.shape[0]
    q_cols = HEADS * HD
    kv_cols = KV * HD
    cut_o = q_cols + 2 * kv_cols
    slots = slot_bits()
    aligned = splits_rows(weight_rows) and half_rows % 128 == 0 and seqs == 2
    split = aligned
    local_index = jnp.arange(local_rows, dtype=jnp.int32)
    pos_here = places(ctx_index * local_rows + local_index, local_rows, ctx_count)
    cosine, sine_part = angle_tables(pos_here, 1.0)
    turn = (jnp.tile(cosine, (1, seqs)), jnp.tile(sine_part, (1, seqs)))

    def pack(flat):
        if aligned:
            return flat
        return (
            flat.reshape(KV, GROUP, HD, -1, 2, half_rows)
            .transpose(3, 0, 2, 4, 1, 5)
            .reshape(-1, KV, HD, 2 * GROUP * half_rows)
        )

    def unpack(packed):
        if aligned:
            return packed
        return (
            packed.reshape(KV, HD, 2, GROUP, half_rows)
            .transpose(0, 3, 1, 2, 4)
            .reshape(q_cols, local_rows)
        )

    def by_columns(row):
        rows = row.shape[0]
        return jnp.broadcast_to(
            row.reshape(rows, 2, 1, half_rows), (rows, 2, GROUP, half_rows)
        ).reshape(rows, 2 * GROUP * half_rows)

    owners = ctx_index ^ jnp.asarray(rel_offsets(slots), jnp.int32)
    flags = (owners > ctx_index).astype(jnp.int32)
    inner = jnp.arange(half_rows, dtype=jnp.int32)
    key_pos = jnp.stack(
        [
            (owners[:, None] * half_rows + inner[None, :]).reshape(-1, 1),
            ((2 * ctx_count - 1 - owners[:, None]) * half_rows + inner[None, :]).reshape(-1, 1),
        ]
    )
    query_pos = by_columns(pos_here[None, :])
    packed_tables = (by_columns(cosine), by_columns(sine_part))

    if split:
        first_half, first_far_x = gather_first(weights)
        cuts = row_cuts(weight_rows // 2)
        backward = [list(reversed(order)) for order in ctx_orders()]
        first_own = [
            double(first_half[None, low:high], order[0])
            for (low, high), order in zip(cuts, backward)
        ]
        later_weights, first_far_x, first_own = lax.optimization_barrier(
            (weights, first_far_x, first_own)
        )
        feed_quarter = gather_quarters(later_weights, first_far_x)
        for position in (1, 2):
            first_own = [
                double(part, order[position]) for part, order in zip(first_own, backward)
            ]
        feed_quarter, first_own, packed_tables, flags, turn = lax.optimization_barrier(
            (feed_quarter, first_own, packed_tables, flags, turn)
        )
        feed_far_z = swap(feed_quarter[None], slots[0])
        first_far = [swap(part, ("core", 0)) for part in first_own]
        first_rows = place_rows(first_own, first_far)
    else:
        mine = lax.all_gather(weights, ("x", "ctx"), axis=0, tiled=True)
        mine = mine.reshape(x_count * ctx_count, weight_rows, model_width)
        far = swap(mine, ("core", 0))
        sides = [
            jnp.where(core == 0, mine[:ctx_count], far[:ctx_count]),
            jnp.where(core == 0, far[:ctx_count], mine[:ctx_count]),
        ]
        first_rows = jnp.concatenate(sides).reshape(-1, model_width)
    qkv_rows, o_rows = first_rows[:cut_o], first_rows[cut_o : cut_o + q_cols]

    tokens_in, cot_in = lax.optimization_barrier(
        (inputs.reshape(tokens, model_width), cotangent.reshape(tokens, model_width))
    )
    dy_low = cot_in.astype(jnp.bfloat16)
    a_one = (normalize(tokens_in) * gains[0]).astype(jnp.bfloat16)
    pair_rows = matmul_t(qkv_rows[q_cols:], a_one)
    if split:
        pair_rows, feed_far_z = lax.optimization_barrier((pair_rows, feed_far_z))
    joined = jnp.concatenate(
        [rotate(pair_rows[:kv_cols], turn).astype(jnp.bfloat16), pair_rows[kv_cols:].astype(jnp.bfloat16)],
        axis=0,
    )
    if split:
        feed_own = jnp.concatenate([feed_quarter[None], feed_far_z], axis=0)
        joined, feed_own = lax.optimization_barrier((joined, feed_own))
    if aligned:
        mine_0, mine_1 = [
            joined[:, seq * local_rows : (seq + 1) * local_rows] for seq in range(2)
        ]
        far_0, own_y_0 = swap(mine_0, slots[0]), swap(mine_0, slots[2])
        feed_near, feed_y = swap(feed_own, slots[1]), swap(feed_own, slots[2])
        feed_x = swap(feed_own, ("x", 0))
        far_0, own_y_0, feed_near, feed_y, feed_x, mine_1 = lax.optimization_barrier(
            (far_0, own_y_0, feed_near, feed_y, feed_x, mine_1)
        )
        near_0, far_y_0 = swap(jnp.stack([mine_0, far_0]), slots[1]), swap(far_0, slots[2])
        far_1, own_y_1 = swap(mine_1, slots[0]), swap(mine_1, slots[2])
        near_x = swap(feed_near, ("x", 0))
        near_0, far_y_0, far_1, own_y_1, near_x, feed_y = lax.optimization_barrier(
            (near_0, far_y_0, far_1, own_y_1, near_x, feed_y)
        )
        near_y_0 = swap(near_0, slots[2])
        near_1, far_y_1 = swap(jnp.stack([mine_1, far_1]), slots[1]), swap(far_1, slots[2])
        y_x = swap(feed_y, ("x", 0))
        near_y_0, near_1, far_y_1, y_x, feed_near = lax.optimization_barrier(
            (near_y_0, near_1, far_y_1, y_x, feed_near)
        )
        near_y_1 = swap(near_1, slots[2])
        pairs = [
            [(own[None], 0), (far_z[None], 0), (near, 0), (near, 1)]
            + [(own_y[None], 0), (far_y[None], 0), (near_y, 0), (near_y, 1)]
            for own, far_z, near, own_y, far_y, near_y in (
                (mine_0, far_0, near_0, own_y_0, far_y_0, near_y_0),
                (mine_1, far_1, near_1, own_y_1, far_y_1, near_y_1),
            )
        ]
        feed_lower = [
            jnp.concatenate([feed_own, feed_near], axis=0),
            jnp.concatenate([feed_x, near_x], axis=0),
        ]
        feed_lower_far = [swap(part, ("core", 0)) for part in feed_lower]
    else:
        pairs = spread(joined, slots).reshape(ctx_count, 2 * kv_cols, seqs, 2, half_rows)
        pairs = [
            (
                pairs.transpose(1, 2, 3, 0, 4).reshape(
                    1, 2 * kv_cols, seqs * 2 * ctx_count * half_rows
                ),
                0,
            )
        ]
    q_rot = rotate(matmul_t(qkv_rows[:q_cols], a_one), turn).astype(jnp.bfloat16)
    queries = pack((q_rot * SCALE_QK).astype(jnp.bfloat16))
    attended = []
    for seq in range(seqs):
        if aligned:
            attended.append(attend_slots(queries, pairs[seq], flags, local_rows, seq))
            if seq == 0:
                attended, feed_near = lax.optimization_barrier((attended, feed_near))
                feed_near_y = swap(feed_near, slots[2])
        else:
            attended.append(attend(queries, pairs, key_pos, query_pos, local_rows, seq))
    attn_low = jnp.concatenate([unpack(mixed) for mixed, _ in attended], axis=1)
    resid = tokens_in + matmul_c(attn_low, o_rows)
    a_two = (normalize(resid) * gains[1]).astype(jnp.bfloat16)
    if aligned:
        a_two, feed_near_y = lax.optimization_barrier((a_two, feed_near_y))
        near_y_x = swap(feed_near_y, ("x", 0))
        upper_own = jnp.concatenate([feed_y, feed_near_y], axis=0)
        upper_far = swap(upper_own, ("core", 0))
        *sums_fed, keep_lower, away_lower = feed_forward(
            a_two, dy_low, feed_lower, feed_lower_far, weight_rows
        )
        sums_fed, near_y_x, upper_far = lax.optimization_barrier((sums_fed, near_y_x, upper_far))
        upper_x = jnp.concatenate([y_x, near_y_x], axis=0)
        come_lower = swap(away_lower, ("core", 0))
        fed, d_two, keep_upper, away_upper = feed_forward(
            a_two,
            dy_low,
            [upper_own, upper_x],
            [upper_far, swap(upper_x, ("core", 0))],
            weight_rows,
            sums_fed,
        )
        come_upper = swap(away_upper, ("core", 0))
    else:
        fed, d_two, *feed_grads = feed_forward(a_two, dy_low, mine, far, weight_rows)
    result = resid + fed
    d_norm_two, d_gain_two = norm_back(resid, d_two, gains[1])
    d_resid = cot_in + d_norm_two
    d_resid_low = d_resid.astype(jnp.bfloat16)
    d_attn = pack(matmul_t(o_rows, d_resid_low).astype(jnp.bfloat16))
    if aligned:
        quarter = weight_rows // 4
        held_upper, held_lower = [
            [(part[:, :, :quarter], part[:, :, quarter:]) for part in parts]
            for parts in ((keep_upper, come_upper), (keep_lower, come_lower))
        ]
        send_upper, send_lower = [
            total_low(*[far_part for _, far_part in parts]) for parts in (held_upper, held_lower)
        ]
        d_attn, send_upper = lax.optimization_barrier((d_attn, send_upper))
        x_upper = swap(send_upper, ("x", 0))
        x_lower = swap(send_lower, ("x", 0))
    d_q, d_pair = [], []
    for seq in range(seqs):
        mixed, log_total = attended[seq]
        if aligned:
            d_queries, *d_slots = attend_slots_back(
                queries, pairs[seq], flags, mixed, log_total, d_attn, packed_tables, local_rows, seq, (2, 2, 4)
            )
        else:
            d_queries, *d_slots = attend_back(
                queries, pairs, key_pos, query_pos, mixed, log_total, d_attn, packed_tables,
                local_rows, seq, (1,),
            )
        if aligned and seq == 1:
            d_slots, x_upper = lax.optimization_barrier((d_slots, x_upper))
            feed_y_come = swap(total_low(*[part for part, _ in held_upper], x_upper), slots[2])
        d_q.append(unpack(d_queries))
        if aligned:
            lower, near_part, upper = d_slots
            y_come = swap(upper, slots[2])
            near_come = swap(add_low(near_part, y_come[2:]), slots[1])
            if seq == 1:
                near_come, x_lower = lax.optimization_barrier((near_come, x_lower))
            far_come = swap(total_low(lower[1], y_come[1], near_come[1]), slots[0])
            if seq == 1:
                far_come, feed_y_come = lax.optimization_barrier((far_come, feed_y_come))
                rest = [part for part, _ in held_lower] + [x_lower, feed_y_come]
                feed_near_come = swap(total_low(*[part[2:] for part in rest]), slots[1])
            total = far_come.astype(jnp.float32)
            for part in (lower, y_come, near_come):
                total = total + part[0].astype(jnp.float32)
        else:
            total = collect(
                d_slots[0]
                .reshape(2, KV, ctx_count, half_rows, 2 * HD)
                .transpose(2, 1, 0, 3, 4),
                list(reversed(slots)),
            )
        d_pair.append(total)
    d_own = jnp.stack(d_pair).transpose(1, 4, 0, 2, 3).reshape(KV, 2 * HD, tokens)
    d_qkv = jnp.concatenate(
        [
            jnp.concatenate(d_q, axis=1),
            rotate(d_own[:, :HD].reshape(kv_cols, tokens), (turn[0], -turn[1])).astype(jnp.bfloat16),
            d_own[:, HD:].reshape(kv_cols, tokens).astype(jnp.bfloat16),
        ],
        axis=0,
    )
    d_one = matmul_c(d_qkv, qkv_rows)
    first_terms = first_grads(d_qkv, attn_low, a_one, d_resid_low, weight_rows, split)
    if split:
        first_terms, feed_near_come = lax.optimization_barrier((first_terms, feed_near_come))
        feed_rest = [part[:2] for part in rest] + [feed_near_come]
        far_send = total_low(*[part[1] for part in feed_rest])
        feed_later = {}

        def beside(step, value):
            if step == 0:
                value, sent = lax.optimization_barrier((value, far_send))
                feed_later["far"] = swap(sent, slots[0])
            if step == 1:
                value, far_come = lax.optimization_barrier((value, feed_later["far"]))
                sums = reduce_end(feed_rest, far_come)
                sent = jnp.where(
                    x_index == 0, sums[1:], jnp.broadcast_to(sums[:1], (2,) + sums.shape[1:])
                )
                feed_later["sums"] = sums
                feed_later["come"] = swap(sent.astype(jnp.bfloat16), ("x", 0))
            return value

    d_norm_one, d_gain_one = norm_back(tokens_in, d_one, gains[0])
    d_tokens = d_resid + d_norm_one
    gain_grad = jnp.stack([d_gain_one, d_gain_two], axis=0)
    if split:
        keep, away = [part[:, 0] for part in first_terms]
        first_half, gain_grad = reduce_halves(keep, away, gain_grad, beside)
        first_half, feed_come = lax.optimization_barrier((first_half, feed_later["come"]))
        feed_sums, feed_come = feed_later["sums"], feed_come.astype(jnp.float32)
        low_first = first_half.astype(jnp.bfloat16)
        first_come, gain_grad = swap_with(low_first, gain_grad, ("x", 0))
        first_half = first_half + first_come.astype(jnp.float32)
        halves = [
            jnp.where(x_index == 0, first_half, jnp.concatenate([feed_come[0], feed_sums[1]])),
            jnp.where(
                x_index == 0,
                jnp.concatenate([feed_sums[0], feed_come[0]]),
                jnp.concatenate([feed_come[1], feed_sums[2]]),
            ),
        ]
        own_half = jnp.where(core == 0, halves[0], halves[1])
        other_half = jnp.where(core == 0, halves[1], halves[0]).astype(jnp.bfloat16)
        come, gain_grad = swap_with(other_half, gain_grad, ("core", 0))
        come = come.astype(jnp.float32)
        weight_share = jnp.concatenate(
            [jnp.where(core == 0, own_half, come), jnp.where(core == 0, come, own_half)], axis=0
        )
    else:
        weight_share = scatter_whole([first_terms[0], *feed_grads])
        for where in [("core", 0)] + sum(bit_groups(), []):
            gain_grad = gain_grad + swap(gain_grad, where)
    weight_first, weight_second, weight_new = adam_update(
        weights.astype(jnp.float32), weight_share, first_moment, second_moment, RATE, DECAY, STEP
    )
    gain_first_new, gain_second_new, gain_new = adam_update(
        gains, gain_grad, gain_first, gain_second, GAIN_RATE, 0.0, STEP
    )
    return (
        result.reshape(inputs.shape),
        d_tokens.reshape(inputs.shape),
        weight_share,
        weight_second,
        weight_new,
        gain_grad,
        gain_second_new,
        gain_new,
    )


def solution(mesh):
    fine = Mesh(
        mesh.devices.reshape(mesh.shape["dp"] // 2, 2, mesh.shape["ctx"]), ("x", "core", "ctx")
    )
    rows = P(("x", "core"), "ctx", None)
    stacked = P(("x", "core", "ctx"), None)
    return jax.shard_map(
        shards,
        mesh=fine,
        in_specs=(rows, rows, stacked, P(), stacked, stacked, P(), P()),
        out_specs=(rows, rows, stacked, stacked, stacked, P(), P(), P()),
        check_vma=False,
    )
```

```python
import jax
import jax.numpy as jnp
import numpy as np
from jax import lax
from jax.experimental import pallas as pl
from jax.experimental.pallas import tpu as pltpu
from jax.sharding import Mesh
from jax.sharding import PartitionSpec as P

HEADS = 15
KV = 5
HD = 64
FF = 2560
STEP = 10


SCALE_QK = 0.125
THETA = 10000.0
EPSILON = 1e-05
BETA_ONE = 0.9
BETA_TWO = 0.95
ADAM_EPS = 1e-08
DECAY = 0.1
RATE = 0.02
GAIN_RATE = 0.2
GROUP = HEADS // KV
KEY_TILE = 256
HIDDEN = -1e30
VMEM_BYTES = 48 * 1024 * 1024


def places(row_index, local_rows, ctx_count):
    half_rows = local_rows // 2
    owner_index = row_index // local_rows
    inner_index = row_index % local_rows
    return jnp.where(
        inner_index < half_rows,
        owner_index * half_rows + inner_index,
        (2 * ctx_count - 1 - owner_index) * half_rows + inner_index - half_rows,
    )


def angle_tables(positions_in, sign):
    half_width = HD // 2
    frequency = THETA ** (-jnp.arange(half_width, dtype=jnp.float32) * 2.0 / HD)
    angles = frequency[:, None] * positions_in.astype(jnp.float32)[None, :]
    return jnp.cos(angles), sign * jnp.sin(angles)


def rotate(values, tables):
    cosine, sine_part = tables
    heads = values.reshape(-1, HD, values.shape[-1])
    first_half = heads[:, : HD // 2]
    second_half = heads[:, HD // 2 :]
    return jnp.concatenate(
        [
            first_half * cosine - second_half * sine_part,
            second_half * cosine + first_half * sine_part,
        ],
        axis=1,
    ).reshape(values.shape)


def normalize(values):
    return values * lax.rsqrt(jnp.mean(values * values, axis=-1, keepdims=True) + EPSILON)


def norm_back(values, grad_in, gain_row):
    inv_scale = lax.rsqrt(jnp.mean(values * values, axis=-1, keepdims=True) + EPSILON)
    unit_rows = values * inv_scale
    grad_unit = grad_in * gain_row
    grad_values = inv_scale * (
        grad_unit - unit_rows * jnp.mean(grad_unit * unit_rows, axis=-1, keepdims=True)
    )
    return (grad_values, jnp.sum(grad_in * unit_rows, axis=0))


def matmul_n(left, right):
    return jnp.dot(left, right, preferred_element_type=jnp.float32)


def matmul_t(left, right):
    return lax.dot_general(
        left, right, (((1,), (1,)), ((), ())), preferred_element_type=jnp.float32
    )


def matmul_c(left, right):
    return lax.dot_general(
        left, right, (((0,), (0,)), ((), ())), preferred_element_type=jnp.float32
    )


def bit_groups():
    x_bits = lax.axis_size("x").bit_length() - 1
    ctx_bits = lax.axis_size("ctx").bit_length() - 1
    low_ctx = ctx_bits // 2
    along_x = [("x", bit) for bit in range(x_bits)]
    along_y = [("ctx", bit) for bit in range(low_ctx)]
    along_z = [("ctx", bit) for bit in range(low_ctx, ctx_bits)]
    return along_x, along_y, along_z


def swap_by(values, axis, offset):
    size = lax.axis_size(axis)
    return lax.ppermute(values, axis, [(i, i ^ offset) for i in range(size)])


def swap(values, where):
    return swap_by(values, where[0], 1 << where[1])


def add_low(left, right):
    return (left.astype(jnp.float32) + right.astype(jnp.float32)).astype(jnp.bfloat16)


def rel_offsets(order):
    strides = {"x": 2 * lax.axis_size("ctx"), "ctx": 1}
    offsets = np.zeros((1,), np.int64)
    for axis, bit in order:
        offsets = np.concatenate([offsets, offsets ^ (strides[axis] << bit)])
    return offsets


def lookup(slot, offsets):
    total = jnp.int32(0)
    for bit in range(len(offsets).bit_length() - 1):
        total = total + ((slot >> bit) & 1) * int(offsets[1 << bit])
    return total


def find(offset, offsets):
    total = jnp.int32(0)
    for bit in range(len(offsets).bit_length() - 1):
        place = int(offsets[1 << bit]).bit_length() - 1
        total = total + (((offset >> place) & 1) << bit)
    return total


def collect(values, order):
    kept, arrived = values, None
    for where in order:
        half = kept.shape[0] // 2
        if arrived is None:
            away, kept_next = kept[half:], kept[:half]
        else:
            away = add_low(kept[half:], arrived[half:])
            kept_next = add_low(kept[:half], arrived[:half])
        arrived = swap(away, where)
        kept = kept_next
    return kept[0].astype(jnp.float32) + arrived[0].astype(jnp.float32)


def scatter_whole(terms):
    ctx_count = lax.axis_size("ctx")
    count = 2 * lax.axis_size("x") * ctx_count
    along_x, along_y, along_z = bit_groups()
    core = ("core", 0)
    me = device_index().reshape(1)
    blocks, rows, width = terms[0].shape
    first = -(-rows // 48) * 16
    groups = [(0, first), (first, 2 * first), (2 * first, rows)]
    orders = [
        along_x + along_y + along_z,
        along_y + along_z + along_x,
        along_z + along_x + along_y,
    ]
    tables = [rel_offsets(list(reversed(order))) for order in orders]

    def target(step, me_ref, flip):
        return lookup(step, tables[0]) ^ me_ref[0] ^ flip

    def sources(flip):
        def chosen(member):
            def index(step, me_ref):
                spot = target(step, me_ref, flip)
                return (jnp.where(spot // blocks == member, spot % blocks, 0), 0, 0)

            return pl.BlockSpec((1, rows, width), index)

        return [chosen(member) for member in range(len(terms))]

    def pick_body(me_ref, *refs):
        held = target(pl.program_id(0), me_ref, ctx_count) // blocks
        for member in range(len(terms)):

            @pl.when(held == member)
            def _(member=member):
                refs[-1][...] = refs[member][...]

    away = pl.pallas_call(
        pick_body,
        grid_spec=pltpu.PrefetchScalarGridSpec(
            num_scalar_prefetch=1,
            grid=(count // 2,),
            in_specs=sources(ctx_count),
            out_specs=pl.BlockSpec((1, rows, width), lambda step, me_ref: (step, 0, 0)),
        ),
        out_shape=jax.ShapeDtypeStruct((count // 2, rows, width), jnp.bfloat16),
        compiler_params=pltpu.CompilerParams(vmem_limit_bytes=VMEM_BYTES),
    )(me, *terms)
    arrived = swap(away, core)

    def merge_body(me_ref, *refs):
        held = target(pl.program_id(0), me_ref, 0) // blocks
        for member in range(len(terms)):

            @pl.when(held == member)
            def _(member=member):
                for (low, high), out in zip(groups, refs[-3:]):
                    out[0] = add_low(refs[member][0, low:high], refs[-4][0, low:high])

    parts = pl.pallas_call(
        merge_body,
        grid_spec=pltpu.PrefetchScalarGridSpec(
            num_scalar_prefetch=1,
            grid=(count // 2,),
            in_specs=sources(0)
            + [pl.BlockSpec((1, rows, width), lambda step, me_ref: (step, 0, 0))],
            out_specs=[
                pl.BlockSpec(
                    (1, high - low, width),
                    lambda step, me_ref, table=table: (
                        find(lookup(step, tables[0]), table),
                        0,
                        0,
                    ),
                )
                for (low, high), table in zip(groups, tables)
            ],
        ),
        out_shape=[
            jax.ShapeDtypeStruct((count // 2, high - low, width), jnp.bfloat16)
            for low, high in groups
        ],
        compiler_params=pltpu.CompilerParams(vmem_limit_bytes=VMEM_BYTES),
    )(me, *terms, arrived)
    return jnp.concatenate([collect(part, order) for part, order in zip(parts, orders)], axis=0)


def device_index():
    return (
        (lax.axis_index("x") * 2 + lax.axis_index("core")) * lax.axis_size("ctx")
        + lax.axis_index("ctx")
    ).astype(jnp.int32)


def splits_rows(rows):
    along_x, along_y, along_z = bit_groups()
    return (len(along_x), len(along_y), len(along_z)) == (1, 1, 2) and rows % 64 == 0


def spread(values, order):
    values = values[None]
    for where in order:
        values = double(values, where)
    return values


def double(values, where):
    return jnp.concatenate([values, swap(values, where)], axis=0)


def ctx_orders():
    along_x, along_y, along_z = bit_groups()
    return [along_y + along_z, along_z + along_y]


def row_cuts(rows):
    first = -(-rows // 32) * 16
    return [(0, first), (first, rows)]


def slot_bits():
    along_x, along_y, along_z = bit_groups()
    return list(reversed(along_z)) + along_y


def total_low(*terms):
    total = terms[0].astype(jnp.float32)
    for term in terms[1:]:
        total = total + term.astype(jnp.float32)
    return total.astype(jnp.bfloat16)


def reduce_end(rest, z_far):
    total = z_far.astype(jnp.float32)
    for part in rest:
        total = total + part[0].astype(jnp.float32)
    return total


def reduce_halves(keep, away, ride, beside):
    far_z, near_z, along_y = slot_bits()
    come = beside(0, swap(away, ("core", 0)))
    sums = []
    for (low, high), order in zip(
        row_cuts(keep.shape[1]), ([along_y, near_z, far_z], [near_z, far_z, along_y])
    ):
        shape = (2, 2, 2, high - low, keep.shape[2])
        terms = [keep[:, low:high].reshape(shape), come[:, low:high].reshape(shape)]
        left = [along_y, near_z, far_z]
        for position, where in enumerate(order):
            dim = left.index(where)
            left.remove(where)
            sent = total_low(*[lax.index_in_dim(term, 1, dim, False) for term in terms])
            if low == 0:
                arrived, ride = swap_with(sent, ride, where)
                arrived = beside(position + 1, arrived)
            else:
                arrived = swap(sent, where)
            terms = [lax.index_in_dim(term, 0, dim, False) for term in terms] + [arrived]
        total = terms[0].astype(jnp.float32)
        for term in terms[1:]:
            total = total + term.astype(jnp.float32)
        sums.append(total)
    return jnp.concatenate(sums, axis=0), ride


def ride_parts(ride):
    rounded = lax.reduce_precision(ride, 8, 7)
    return rounded, lax.reduce_precision(ride - rounded, 8, 7)


def with_ride(sent, parts):
    extra = jnp.concatenate([*parts, jnp.zeros((12, parts[0].shape[1]), jnp.float32)])
    return jnp.concatenate([sent.reshape(-1, sent.shape[-1]), extra.astype(jnp.bfloat16)], axis=0)


def swap_with(sent, ride, where):
    parts = ride_parts(ride)
    come, other = off_ride(swap(with_ride(sent, parts), where), sent.shape)
    return come, (parts[0] + parts[1]) + other


def off_ride(come, shape):
    parts = come[-16:].astype(jnp.float32)
    return come[:-16].reshape(shape), parts[0:2] + parts[2:4]


def gather_first(weights):
    half = weights.shape[0] // 2
    far = lax.ppermute(weights, ("x", "core"), [(0, 2)])
    rows = jnp.where(lax.axis_index("x") == 0, weights, far)
    come = swap(rows[half:], ("core", 0))
    return jnp.where(lax.axis_index("core") == 0, rows[:half], come), far


def gather_quarters(weights, first_far):
    half = weights.shape[0] // 2
    x_index, core = lax.axis_index("x"), lax.axis_index("core")
    far = lax.ppermute(weights, ("x", "core"), [(2, 0), (1, 3), (3, 1)])
    far = jnp.where((x_index == 1) & (core == 0), first_far, far)
    both = jnp.stack([jnp.where(x_index == 0, weights, far), jnp.where(x_index == 0, far, weights)])
    keep = jnp.where(core == 0, both[:, :half], both[:, half:])
    come = swap(jnp.where(core == 0, both[:, half:], both[:, :half]), ("core", 0))
    first = jnp.where(core == 0, keep, come)
    second = jnp.where(core == 0, come, keep)
    feed = jnp.stack([second[0], first[1], second[1]])
    return jnp.where(x_index == 0, feed[:, : half // 2], feed[:, half // 2 :])


def place_rows(own, far):
    tables = [rel_offsets(list(reversed(order))) for order in ctx_orders()]
    slots, width = own[0].shape[0], own[0].shape[2]
    lengths = [part.shape[1] for part in own]
    half = sum(lengths)

    def body(me_ref, *refs):
        out_ref = refs[-1]
        for core in range(2):

            @pl.when(me_ref[0] == core)
            def _(core=core):
                for source, base in ((0, core * half), (2, (1 - core) * half)):
                    out_ref[0, base : base + lengths[0]] = refs[source][0]
                    out_ref[0, base + lengths[0] : base + half] = refs[source + 1][0]

    specs = [
        pl.BlockSpec(
            (1, length, width),
            lambda step, me_ref, table=table: (find(step ^ me_ref[1], table), 0, 0),
        )
        for length, table in zip(lengths, tables)
    ]
    me = jnp.stack([lax.axis_index("core"), lax.axis_index("ctx")]).astype(jnp.int32)
    return pl.pallas_call(
        body,
        grid_spec=pltpu.PrefetchScalarGridSpec(
            num_scalar_prefetch=1,
            grid=(slots,),
            in_specs=specs * 2,
            out_specs=pl.BlockSpec((1, 2 * half, width), lambda step, me_ref: (step, 0, 0)),
        ),
        out_shape=jax.ShapeDtypeStruct((slots, 2 * half, width), own[0].dtype),
        cost_estimate=pl.CostEstimate(
            flops=0, bytes_accessed=8 * slots * half * width, transcendentals=0
        ),
        compiler_params=pltpu.CompilerParams(vmem_limit_bytes=VMEM_BYTES),
    )(me, *own, *far).reshape(slots * 2 * half, width)


def turned(values):
    return jnp.transpose(values)


def load_packed(ref, aligned):
    if not aligned:
        return ref[0, 0]
    half = ref.shape[1] // 2
    return jnp.concatenate(
        [
            ref[head * HD : (head + 1) * HD, side * half : (side + 1) * half]
            for side in range(2)
            for head in range(GROUP)
        ],
        axis=1,
    )


def store_packed(ref, values, aligned):
    if not aligned:
        ref[0, 0] = values
        return
    half = ref.shape[1] // 2
    for side in range(2):
        for head in range(GROUP):
            start = (side * GROUP + head) * half
            ref[head * HD : (head + 1) * HD, side * half : (side + 1) * half] = values[
                :, start : start + half
            ]


def load_tile(refs, side, tile):
    length = refs[0].shape[1] // 2
    if length >= KEY_TILE:
        start = side * length + tile * KEY_TILE
        return refs[0][:, start : start + KEY_TILE]
    many = KEY_TILE // length
    return jnp.concatenate(
        [
            ref[:, side * length : (side + 1) * length]
            for ref in refs[tile * many : (tile + 1) * many]
        ],
        axis=1,
    )


def attend_body(count, aligned, queries_ref, key_pos_ref, query_pos_ref, *refs):
    key_refs, value_refs = refs[:count], refs[count : 2 * count]
    out_ref, total_ref, work = refs[2 * count :]
    queries = load_packed(queries_ref, aligned)
    low_cols = queries.shape[1] // 2
    queries_high = queries[:, low_cols:]
    tiles = key_pos_ref.shape[1] // KEY_TILE
    largest = jnp.full((1, queries.shape[1]), HIDDEN, jnp.float32)
    largest_high = jnp.full((1, low_cols), HIDDEN, jnp.float32)
    for side in range(2):
        for tile in range(tiles):
            keys = turned(load_tile(key_refs, side, tile))
            row = (side * tiles + tile) * KEY_TILE
            key_places = key_pos_ref[side, tile * KEY_TILE : (tile + 1) * KEY_TILE]
            if side == 0:
                scores = matmul_n(keys, queries)
                scores = jnp.where(key_places <= query_pos_ref[...], scores, HIDDEN)
                work[row : row + KEY_TILE] = scores
                largest = jnp.maximum(largest, jnp.max(scores, axis=0, keepdims=True))
            else:
                scores = matmul_n(keys, queries_high)
                scores = jnp.where(key_places <= query_pos_ref[:, low_cols:], scores, HIDDEN)
                work[row : row + KEY_TILE, low_cols:] = scores
                largest_high = jnp.maximum(largest_high, jnp.max(scores, axis=0, keepdims=True))
    high_max = jnp.maximum(largest[:, low_cols:], largest_high)
    largest = jnp.concatenate([largest[:, :low_cols], high_max], axis=1)
    total = jnp.zeros_like(largest)
    mixed = jnp.zeros((HD, queries.shape[1]), jnp.float32)
    total_high = jnp.zeros_like(largest_high)
    mixed_high = jnp.zeros((HD, low_cols), jnp.float32)
    for side in range(2):
        for tile in range(tiles):
            values = load_tile(value_refs, side, tile)
            row = (side * tiles + tile) * KEY_TILE
            if side == 0:
                expos = jnp.exp(work[row : row + KEY_TILE] - largest)
                total = total + jnp.sum(expos, axis=0, keepdims=True)
                mixed = mixed + matmul_n(values, expos.astype(jnp.bfloat16))
            else:
                expos = jnp.exp(work[row : row + KEY_TILE, low_cols:] - high_max)
                total_high = total_high + jnp.sum(expos, axis=0, keepdims=True)
                mixed_high = mixed_high + matmul_n(values, expos.astype(jnp.bfloat16))
    total = jnp.concatenate([total[:, :low_cols], total[:, low_cols:] + total_high], axis=1)
    mixed = jnp.concatenate([mixed[:, :low_cols], mixed[:, low_cols:] + mixed_high], axis=1)
    store_packed(out_ref, (mixed / total).astype(jnp.bfloat16), aligned)
    total_ref[0, 0] = largest + jnp.log(total)


def attend_back_body(
    count, aligned, queries_ref, key_pos_ref, query_pos_ref, *refs
):
    key_refs, value_refs = refs[:count], refs[count : 2 * count]
    out_ref, total_ref, d_out_ref, cosine_ref, sine_ref = refs[2 * count : 2 * count + 5]
    d_queries_ref, pair_refs = refs[2 * count + 5], refs[2 * count + 6 :]
    all_queries, all_d_out = load_packed(queries_ref, aligned), load_packed(d_out_ref, aligned)
    low_cols = all_queries.shape[1] // 2
    tiles = key_pos_ref.shape[1] // KEY_TILE
    delta = jnp.sum(
        all_d_out.astype(jnp.float32) * load_packed(out_ref, aligned).astype(jnp.float32),
        axis=0,
        keepdims=True,
    )
    totals = total_ref[0, 0]
    parts = []
    for side in range(2):
        if side == 0:
            queries, d_out = all_queries, all_d_out
            query_places, log_total, row_delta = query_pos_ref[...], totals, delta
        else:
            queries, d_out = all_queries[:, low_cols:], all_d_out[:, low_cols:]
            query_places = query_pos_ref[:, low_cols:]
            log_total, row_delta = totals[:, low_cols:], delta[:, low_cols:]
        part = jnp.zeros((HD, queries.shape[1]), jnp.float32)
        for tile in range(tiles):
            keys_flat = load_tile(key_refs, side, tile)
            scores = matmul_n(turned(keys_flat), queries)
            seen = key_pos_ref[side, tile * KEY_TILE : (tile + 1) * KEY_TILE] <= query_places
            probs = jnp.where(seen, jnp.exp(scores - log_total), 0.0)
            d_probs = matmul_n(turned(load_tile(value_refs, side, tile)), d_out)
            d_scores = (probs * (d_probs - row_delta)).astype(jnp.bfloat16)
            part = part + matmul_n(keys_flat, d_scores)
            d_key = matmul_t(d_scores, queries).astype(jnp.bfloat16)
            d_value = matmul_t(probs.astype(jnp.bfloat16), d_out).astype(jnp.bfloat16)
            if aligned:
                length = key_refs[0].shape[1] // 2
                places_out = [(ref, slot) for ref in pair_refs for slot in range(ref.shape[0])]
                for piece in range(KEY_TILE // length):
                    ref, slot = places_out[tile * (KEY_TILE // length) + piece]
                    rows = slice(piece * length, (piece + 1) * length)
                    ref[slot, 0, side, :, :HD] = d_key[rows]
                    ref[slot, 0, side, :, HD:] = d_value[rows]
            else:
                rows = slice(tile * KEY_TILE, (tile + 1) * KEY_TILE)
                pair_refs[0][side, 0, rows, :HD] = d_key
                pair_refs[0][side, 0, rows, HD:] = d_value
        parts.append(part)
    d_queries = jnp.concatenate(
        [parts[0][:, :low_cols], parts[0][:, low_cols:] + parts[1]], axis=1
    )
    cosine, sine_part = cosine_ref[...], sine_ref[...]
    first_half, second_half = d_queries[: HD // 2], d_queries[HD // 2 :]
    turned_back = jnp.concatenate(
        [
            first_half * cosine + second_half * sine_part,
            second_half * cosine - first_half * sine_part,
        ],
        axis=0,
    )
    store_packed(d_queries_ref, (turned_back * SCALE_QK).astype(jnp.bfloat16), aligned)


def own_mask(rows, cols):
    return lax.broadcasted_iota(jnp.int32, (rows, cols), 0) <= (
        lax.broadcasted_iota(jnp.int32, (rows, cols), 1) % rows
    )


def slot_keys(ref, length):
    both = turned(ref[...])
    return both[:length], both[length:]


def attend_slots_body(count, flags_ref, queries_ref, *refs):
    key_refs, value_refs = refs[:count], refs[count : 2 * count]
    out_ref, total_ref, both_queries, work, largest, totals, mixed = refs[2 * count :]
    length = key_refs[0].shape[1] // 2
    cols = GROUP * length
    packed = load_packed(queries_ref, True)
    for side in range(2):
        both_queries[side] = packed[:, side * cols : (side + 1) * cols]
    visible = own_mask(length, cols)
    low_keys, high_keys = zip(*[slot_keys(ref, length) for ref in key_refs])
    row = 0

    def keep_scores(scores, row):
        work[row : row + scores.shape[0]] = scores
        return jnp.max(scores, axis=0, keepdims=True)

    for side, keys in ((0, low_keys[0]), (1, high_keys[0])):
        scores = jnp.where(visible, matmul_n(keys, both_queries[side]), HIDDEN)
        largest[side] = keep_scores(scores, row)
        row += length
    for slot in range(0, count, 2):
        keys = jnp.concatenate([low_keys[slot], low_keys[slot + 1]], axis=0)
        top = keep_scores(matmul_n(keys, both_queries[1]), row)
        largest[1] = jnp.maximum(largest[1], top)
        row += 2 * length
    for slot in range(1, count):
        side = flags_ref[slot]
        keys = jnp.where(side == 0, low_keys[slot], high_keys[slot])
        top = keep_scores(matmul_n(keys, both_queries[side]), row)
        largest[side] = jnp.maximum(largest[side], top)
        row += length
    row = 0
    for side in range(2):
        values = value_refs[0][:, side * length : (side + 1) * length]
        expos = jnp.exp(work[row : row + length] - largest[side])
        totals[side] = jnp.sum(expos, axis=0, keepdims=True)
        mixed[side] = matmul_n(values, expos.astype(jnp.bfloat16))
        row += length
    for slot in range(0, count, 2):
        values = jnp.concatenate(
            [value_refs[slot][:, :length], value_refs[slot + 1][:, :length]], axis=1
        )
        expos = jnp.exp(work[row : row + 2 * length] - largest[1])
        totals[1] += jnp.sum(expos, axis=0, keepdims=True)
        mixed[1] += matmul_n(values, expos.astype(jnp.bfloat16))
        row += 2 * length
    for slot in range(1, count):
        side = flags_ref[slot]
        values = jnp.where(side == 0, value_refs[slot][:, :length], value_refs[slot][:, length:])
        expos = jnp.exp(work[row : row + length] - largest[side])
        totals[side] += jnp.sum(expos, axis=0, keepdims=True)
        mixed[side] += matmul_n(values, expos.astype(jnp.bfloat16))
        row += length
    result = [(mixed[side] / totals[side]).astype(jnp.bfloat16) for side in range(2)]
    store_packed(out_ref, jnp.concatenate(result, axis=1), True)
    logs = [largest[side] + jnp.log(totals[side]) for side in range(2)]
    total_ref[0, 0] = jnp.concatenate(logs, axis=1)


def attend_slots_back_body(count, flags_ref, queries_ref, *refs):
    key_refs, value_refs = refs[:count], refs[count : 2 * count]
    out_ref, total_ref, d_out_ref, cosine_ref, sine_ref = refs[2 * count : 2 * count + 5]
    d_queries_ref = refs[2 * count + 5]
    pair_refs = refs[2 * count + 6 : -7]
    both_queries, both_d_out, turned_queries, turned_d_out, log_totals, deltas, sums = refs[-7:]
    length = key_refs[0].shape[1] // 2
    cols = GROUP * length
    queries, d_out = load_packed(queries_ref, True), load_packed(d_out_ref, True)
    delta = jnp.sum(
        d_out.astype(jnp.float32) * load_packed(out_ref, True).astype(jnp.float32),
        axis=0,
        keepdims=True,
    )
    for side in range(2):
        part = slice(side * cols, (side + 1) * cols)
        both_queries[side] = queries[:, part]
        both_d_out[side] = d_out[:, part]
        turned_queries[side] = turned(queries[:, part])
        turned_d_out[side] = turned(d_out[:, part])
        log_totals[side] = total_ref[0, 0, :, part]
        deltas[side] = delta[:, part]
    sums[...] = jnp.zeros_like(sums)
    visible = own_mask(length, cols)
    low_keys, high_keys = zip(*[slot_keys(ref, length) for ref in key_refs])
    low_values, high_values = zip(*[slot_keys(ref, length) for ref in value_refs])
    places_out = [(ref, slot) for ref in pair_refs for slot in range(ref.shape[0])]

    def block(keys, keys_flat, values, side, mask=None):
        probs = jnp.exp(matmul_n(keys, both_queries[side]) - log_totals[side])
        if mask is not None:
            probs = jnp.where(mask, probs, 0.0)
        d_probs = matmul_n(values, both_d_out[side])
        d_scores = (probs * (d_probs - deltas[side])).astype(jnp.bfloat16)
        sums[side] += matmul_n(keys_flat, d_scores)
        return jnp.concatenate(
            [
                matmul_n(d_scores, turned_queries[side]),
                matmul_n(probs.astype(jnp.bfloat16), turned_d_out[side]),
            ],
            axis=1,
        )

    low_terms = []
    for slot in range(0, count, 2):
        keys, values = [
            jnp.concatenate([part[slot], part[slot + 1]], axis=0) for part in (low_keys, low_values)
        ]
        flat = jnp.concatenate([key_refs[slot][:, :length], key_refs[slot + 1][:, :length]], axis=1)
        terms = block(keys, flat, values, 1)
        low_terms += [terms[:length], terms[length:]]
    ref, slot = places_out[0]
    own = [
        block(keys, key_refs[0][:, side * length : (side + 1) * length], values, side, visible)
        for side, (keys, values) in enumerate(
            ((low_keys[0], low_values[0]), (high_keys[0], high_values[0]))
        )
    ]
    ref[slot, 0, 0] = (low_terms[0] + own[0]).astype(jnp.bfloat16)
    ref[slot, 0, 1] = own[1].astype(jnp.bfloat16)
    for member in range(1, count):
        side = flags_ref[member]
        low = side == 0
        keys = jnp.where(low, low_keys[member], high_keys[member])
        flat = jnp.where(low, key_refs[member][:, :length], key_refs[member][:, length:])
        values = jnp.where(low, low_values[member], high_values[member])
        terms = block(keys, flat, values, side)
        ref, slot = places_out[member]
        ref[slot, 0, 0] = (low_terms[member] + jnp.where(low, terms, 0.0)).astype(jnp.bfloat16)
        ref[slot, 0, 1] = jnp.where(low, 0.0, terms).astype(jnp.bfloat16)
    d_queries = jnp.concatenate([sums[0], sums[1]], axis=1)
    store_packed(d_queries_ref, turn_queries_back(d_queries, cosine_ref, sine_ref), True)


def turn_queries_back(d_queries, cosine_ref, sine_ref):
    cosine, sine_part = cosine_ref[...], sine_ref[...]
    first_half, second_half = d_queries[: HD // 2], d_queries[HD // 2 :]
    turned_back = jnp.concatenate(
        [
            first_half * cosine + second_half * sine_part,
            second_half * cosine - first_half * sine_part,
        ],
        axis=0,
    )
    return (turned_back * SCALE_QK).astype(jnp.bfloat16)


def slot_specs(leads, local_rows, seq):
    specs = [
        pl.BlockSpec(memory_space=pltpu.SMEM),
        pl.BlockSpec((GROUP * HD, local_rows), lambda head: (head, seq)),
    ]
    for first in (0, KV):
        specs += [
            pl.BlockSpec(
                (None, HD, local_rows),
                lambda head, lead=lead, first=first: (lead, first + head, 0),
            )
            for lead in leads
        ]
    return specs


def attend_slots(queries, pairs, flags, local_rows, seq):
    count, cols = len(pairs), GROUP * local_rows // 2
    leads, arrays = [lead for _, lead in pairs], [array for array, _ in pairs]
    work = HEADS * local_rows * local_rows * count // 2
    return pl.pallas_call(
        lambda *refs: attend_slots_body(count, *refs),
        grid=(KV,),
        in_specs=slot_specs(leads, local_rows, seq),
        out_specs=[
            pl.BlockSpec((GROUP * HD, local_rows), lambda head: (head, 0)),
            pl.BlockSpec((1, 1, 1, 2 * cols), lambda head: (0, head, 0, 0)),
        ],
        out_shape=[
            jax.ShapeDtypeStruct((HEADS * HD, local_rows), jnp.bfloat16),
            jax.ShapeDtypeStruct((1, KV, 1, 2 * cols), jnp.float32),
        ],
        scratch_shapes=[
            pltpu.VMEM((2, HD, cols), jnp.bfloat16),
            pltpu.VMEM(((2 * count + 1) * local_rows // 2, cols), jnp.float32),
            pltpu.VMEM((2, 1, cols), jnp.float32),
            pltpu.VMEM((2, 1, cols), jnp.float32),
            pltpu.VMEM((2, HD, cols), jnp.float32),
        ],
        cost_estimate=pl.CostEstimate(
            flops=work * HD, bytes_accessed=1024 * 1024, transcendentals=0
        ),
        compiler_params=pltpu.CompilerParams(vmem_limit_bytes=VMEM_BYTES),
    )(flags, queries, *arrays, *arrays)


def attend_slots_back(
    queries, pairs, flags, mixed, log_total, d_mixed, tables, local_rows, seq, sets
):
    count, cols = len(pairs), GROUP * local_rows // 2
    leads, arrays = [lead for _, lead in pairs], [array for array, _ in pairs]
    work = HEADS * local_rows * local_rows * count // 2
    own = pl.BlockSpec((GROUP * HD, local_rows), lambda head: (head, 0))
    table_spec = pl.BlockSpec((HD // 2, 2 * cols), lambda head: (0, 0))
    length = local_rows // 2
    return pl.pallas_call(
        lambda *refs: attend_slots_back_body(count, *refs),
        grid=(KV,),
        in_specs=slot_specs(leads, local_rows, seq)
        + [
            own,
            pl.BlockSpec((1, 1, 1, 2 * cols), lambda head: (0, head, 0, 0)),
            pl.BlockSpec((GROUP * HD, local_rows), lambda head: (head, seq)),
            table_spec,
            table_spec,
        ],
        out_specs=[own]
        + [
            pl.BlockSpec((slots, 1, 2, length, 2 * HD), lambda head: (0, head, 0, 0, 0))
            for slots in sets
        ],
        out_shape=[jax.ShapeDtypeStruct((HEADS * HD, local_rows), jnp.bfloat16)]
        + [jax.ShapeDtypeStruct((slots, KV, 2, length, 2 * HD), jnp.bfloat16) for slots in sets],
        scratch_shapes=[
            pltpu.VMEM((2, HD, cols), jnp.bfloat16),
            pltpu.VMEM((2, HD, cols), jnp.bfloat16),
            pltpu.VMEM((2, cols, HD), jnp.bfloat16),
            pltpu.VMEM((2, cols, HD), jnp.bfloat16),
            pltpu.VMEM((2, 1, cols), jnp.float32),
            pltpu.VMEM((2, 1, cols), jnp.float32),
            pltpu.VMEM((2, HD, cols), jnp.float32),
        ],
        cost_estimate=pl.CostEstimate(
            flops=work * HD, bytes_accessed=1024 * 1024, transcendentals=0
        ),
        compiler_params=pltpu.CompilerParams(vmem_limit_bytes=VMEM_BYTES),
    )(flags, queries, *arrays, *arrays, mixed, log_total, d_mixed, *tables)


def head_specs(leads, aligned, cols, keys, local_rows, seq):
    count = len(leads)
    if aligned:
        packed = pl.BlockSpec((GROUP * HD, local_rows), lambda head: (head, seq))
    else:
        packed = pl.BlockSpec((1, 1, HD, cols), lambda head: (seq, head, 0, 0))
    specs = [
        packed,
        pl.BlockSpec((2, keys, 1), lambda head: (0, 0, 0)),
        pl.BlockSpec((1, cols), lambda head: (0, 0)),
    ]
    for first in (0, KV):
        specs += [
            pl.BlockSpec(
                (None, HD, 2 * keys // count),
                lambda head, lead=lead, first=first: (lead, first + head, seq),
            )
            for lead in leads
        ]
    return packed, specs


def attend(queries, pairs, key_pos, query_pos, local_rows, seq):
    aligned = queries.ndim == 2
    cols, keys, count = query_pos.shape[1], key_pos.shape[1], len(pairs)
    leads, arrays = [lead for _, lead in pairs], [array for array, _ in pairs]
    _, specs = head_specs(leads, aligned, cols, keys, local_rows, seq)
    work = HEADS * keys * cols // GROUP * 3 // 2
    if aligned:
        out_spec = pl.BlockSpec((GROUP * HD, local_rows), lambda head: (head, 0))
        out_shape = jax.ShapeDtypeStruct((HEADS * HD, local_rows), jnp.bfloat16)
    else:
        out_spec = pl.BlockSpec((1, 1, HD, cols), lambda head: (0, head, 0, 0))
        out_shape = jax.ShapeDtypeStruct((1, KV, HD, cols), jnp.bfloat16)
    return pl.pallas_call(
        lambda *refs: attend_body(count, aligned, *refs),
        grid=(KV,),
        in_specs=specs,
        out_specs=[out_spec, pl.BlockSpec((1, 1, 1, cols), lambda head: (0, head, 0, 0))],
        out_shape=[out_shape, jax.ShapeDtypeStruct((1, KV, 1, cols), jnp.float32)],
        scratch_shapes=[pltpu.VMEM((2 * keys, cols), jnp.float32)],
        cost_estimate=pl.CostEstimate(
            flops=work * HD, bytes_accessed=1024 * 1024, transcendentals=0
        ),
        compiler_params=pltpu.CompilerParams(vmem_limit_bytes=VMEM_BYTES),
    )(queries, key_pos, query_pos, *arrays, *arrays)


def attend_back(
    queries, pairs, key_pos, query_pos, mixed, log_total, d_mixed, tables, local_rows, seq, sets
):
    aligned = queries.ndim == 2
    cols, keys, count = query_pos.shape[1], key_pos.shape[1], len(pairs)
    leads, arrays = [lead for _, lead in pairs], [array for array, _ in pairs]
    packed, specs = head_specs(leads, aligned, cols, keys, local_rows, seq)
    work = HEADS * keys * cols // GROUP * 3 // 2
    if aligned:
        own = pl.BlockSpec((GROUP * HD, local_rows), lambda head: (head, 0))
        own_shape = jax.ShapeDtypeStruct((HEADS * HD, local_rows), jnp.bfloat16)
        length = keys // count
        pair_specs = [
            pl.BlockSpec((slots, 1, 2, length, 2 * HD), lambda head: (0, head, 0, 0, 0))
            for slots in sets
        ]
        pair_shapes = [
            jax.ShapeDtypeStruct((slots, KV, 2, length, 2 * HD), jnp.bfloat16) for slots in sets
        ]
    else:
        own = pl.BlockSpec((1, 1, HD, cols), lambda head: (0, head, 0, 0))
        own_shape = jax.ShapeDtypeStruct((1, KV, HD, cols), jnp.bfloat16)
        pair_specs = [pl.BlockSpec((2, 1, keys, 2 * HD), lambda head: (0, head, 0, 0))]
        pair_shapes = [jax.ShapeDtypeStruct((2, KV, keys, 2 * HD), jnp.bfloat16)]
    table_spec = pl.BlockSpec((HD // 2, cols), lambda head: (0, 0))
    return pl.pallas_call(
        lambda *refs: attend_back_body(count, aligned, *refs),
        grid=(KV,),
        in_specs=specs
        + [
            own,
            pl.BlockSpec((1, 1, 1, cols), lambda head: (0, head, 0, 0)),
            packed,
            table_spec,
            table_spec,
        ],
        out_specs=[own] + pair_specs,
        out_shape=[own_shape] + pair_shapes,
        cost_estimate=pl.CostEstimate(
            flops=work * HD, bytes_accessed=1024 * 1024, transcendentals=0
        ),
        compiler_params=pltpu.CompilerParams(vmem_limit_bytes=VMEM_BYTES),
    )(queries, key_pos, query_pos, *arrays, *arrays, mixed, log_total, d_mixed, *tables)


def put_rows(values, keep_ref, away_ref, place, core, x_index):
    quarter = values.shape[0] // 4
    for mine in range(4):

        @pl.when(2 * core + x_index == mine)
        def _(mine=mine):
            for ref, side in ((keep_ref, mine // 2), (away_ref, 1 - mine // 2)):
                for position, along_x in enumerate((mine % 2, 1 - mine % 2)):
                    start = (2 * side + along_x) * quarter
                    ref[place[0], place[1], position * quarter : (position + 1) * quarter] = values[
                        start : start + quarter
                    ]


def feed_body(
    parts, split, chained, me_ref, a_two_ref, dy_ref, *refs
):
    count = 4 if split else 6
    before, refs = (refs[:2], refs[2:]) if chained else (None, refs)
    weight_refs, (out_ref, d_two_ref), grad_refs = (
        refs[:count],
        refs[count : count + 2],
        refs[count + 2 :],
    )
    core, x_index = me_ref[0], me_ref[1]
    step = pl.program_id(0)

    @pl.when(step == 0)
    def _():
        for place, ref in enumerate((out_ref, d_two_ref)):
            ref[...] = before[place][...] if chained else jnp.zeros_like(ref)

    def rows_of(member):
        if split:
            rows_out = []
            for slot in range(weight_refs[0].shape[0]):
                parts_here = [ref[slot, member] for ref in weight_refs]
                for side in range(2):
                    for along_x in range(2):
                        near = jnp.where(x_index == along_x, parts_here[0], parts_here[1])
                        far = jnp.where(x_index == along_x, parts_here[2], parts_here[3])
                        rows_out.append(jnp.where(core == side, near, far))
            return jnp.concatenate(rows_out, axis=0)
        wanted = feed_core(member, step, parts)
        return jnp.where(wanted == core, weight_refs[2 * member][0], weight_refs[2 * member + 1][0])

    a_two, dy_low = a_two_ref[...], dy_ref[...]
    gate_rows, up_rows, down_rows = rows_of(0), rows_of(1), rows_of(2)
    gate_pre = matmul_t(gate_rows, a_two)
    up_pre = matmul_t(up_rows, a_two)
    d_hidden = matmul_t(down_rows, dy_low)
    sigma = jax.nn.sigmoid(gate_pre)
    gate_act = gate_pre * sigma
    hidden = (gate_act * up_pre).astype(jnp.bfloat16)
    d_gate = (d_hidden * up_pre * sigma * (1.0 + gate_pre * (1.0 - sigma))).astype(jnp.bfloat16)
    d_up = (d_hidden * gate_act).astype(jnp.bfloat16)
    out_ref[...] += matmul_c(hidden, down_rows)
    d_two_ref[...] += matmul_c(d_gate, gate_rows) + matmul_c(d_up, up_rows)
    for member, (left, right) in enumerate(((d_gate, a_two), (d_up, a_two), (hidden, dy_low))):
        grad = matmul_n(left, right).astype(jnp.bfloat16)
        if split:
            slots = grad_refs[0].shape[0]
            rows = grad.shape[0] // slots
            for slot in range(slots):
                put_rows(
                    grad[slot * rows : (slot + 1) * rows], *grad_refs, (slot, member), core, x_index
                )
        else:
            grad_refs[member][0] = grad


def feed_core(member, step, parts):
    ctx_count, single = parts
    return (member + 1) % 2 if single else step // ctx_count


def feed_forward(a_two, dy_low, mine, far, rows, before=()):
    tokens, width = a_two.shape
    ctx_count = lax.axis_size("ctx")
    blocks = FF // rows
    single = blocks == ctx_count
    split = mine[0].ndim == 4 if isinstance(mine, list) else False
    parts = (ctx_count, single)
    whole = pl.BlockSpec((tokens, width), lambda step, me_ref: (0, 0))

    def weight_spec(member, own):
        first = (member + 1) * blocks // ctx_count // 2 * ctx_count

        def index(step, me_ref):
            matches = (feed_core(member, step, parts) == me_ref[0]) == own
            return (first + jnp.where(matches, step % ctx_count, 0), 0, 0)

        return pl.BlockSpec((1, rows, width), index)

    if split:
        weight_specs = [
            pl.BlockSpec((2, 3, rows // 4, width), lambda step, me_ref: (step, 0, 0, 0))
        ] * 4
        weight_args = [*mine, *far]
        half = pl.BlockSpec((2, 3, rows // 2, width), lambda step, me_ref: (step, 0, 0, 0))
        grad_specs = [half, half]
        blocks = mine[0].shape[0]
        grad_shapes = [jax.ShapeDtypeStruct((blocks, 3, rows // 2, width), jnp.bfloat16)] * 2
    else:
        weight_specs = [weight_spec(member, own) for member in range(3) for own in (True, False)]
        weight_args = [mine, far] * 3
        grad_specs = [pl.BlockSpec((1, rows, width), lambda step, me_ref: (step, 0, 0))] * 3
        grad_shapes = [jax.ShapeDtypeStruct((blocks, rows, width), jnp.bfloat16)] * 3
    me = jnp.stack([lax.axis_index("core"), lax.axis_index("x")]).astype(jnp.int32)
    return pl.pallas_call(
        lambda *refs: feed_body(parts, split, bool(before), *refs),
        grid_spec=pltpu.PrefetchScalarGridSpec(
            num_scalar_prefetch=1,
            grid=(blocks // 2 if split else blocks,),
            in_specs=[whole] * (2 + len(before)) + weight_specs,
            out_specs=[whole, whole] + grad_specs,
        ),
        out_shape=[jax.ShapeDtypeStruct((tokens, width), jnp.float32)] * 2 + grad_shapes,
        cost_estimate=pl.CostEstimate(
            flops=18 * tokens * width * blocks * rows, bytes_accessed=12 * blocks * rows * width,
            transcendentals=0,
        ),
        compiler_params=pltpu.CompilerParams(vmem_limit_bytes=VMEM_BYTES),
    )(me, a_two, dy_low, *before, *weight_args)


def first_grads(d_qkv, attn_low, a_one, d_resid_low, rows, split):
    tokens, width = a_one.shape
    early = d_qkv.shape[0] // rows
    blocks = early + attn_low.shape[0] // rows

    def body(me_ref, qkv_ref, attn_ref, one_ref, resid_ref, *grad_refs):
        first = pl.program_id(0) < early
        left = jnp.where(first, qkv_ref[...], attn_ref[...])
        right = jnp.where(first, one_ref[...], resid_ref[...])
        grad = matmul_n(left, right).astype(jnp.bfloat16)
        if split:
            put_rows(grad, *grad_refs, (0, 0), me_ref[0], 0)
        else:
            grad_refs[0][0] = grad

    whole = pl.BlockSpec((tokens, width), lambda step, me_ref: (0, 0))
    if split:
        table = rel_offsets(slot_bits())
        half = pl.BlockSpec(
            (1, 1, rows // 2, width), lambda step, me_ref: (find(step ^ me_ref[1], table), 0, 0, 0)
        )
        grad_specs = [half, half]
        grad_shapes = [jax.ShapeDtypeStruct((blocks, 1, rows // 2, width), jnp.bfloat16)] * 2
    else:
        grad_specs = [pl.BlockSpec((1, rows, width), lambda step, me_ref: (step, 0, 0))]
        grad_shapes = [jax.ShapeDtypeStruct((blocks, rows, width), jnp.bfloat16)]
    me = jnp.stack([lax.axis_index(name) for name in ("core", "ctx")]).astype(jnp.int32)
    return pl.pallas_call(
        body,
        grid_spec=pltpu.PrefetchScalarGridSpec(
            num_scalar_prefetch=1,
            grid=(blocks,),
            in_specs=[
                pl.BlockSpec((rows, tokens), lambda step, me_ref: (jnp.minimum(step, early - 1), 0)),
                pl.BlockSpec((rows, tokens), lambda step, me_ref: (jnp.maximum(step - early, 0), 0)),
                whole,
                whole,
            ],
            out_specs=grad_specs,
        ),
        out_shape=grad_shapes,
        cost_estimate=pl.CostEstimate(
            flops=2 * tokens * width * blocks * rows, bytes_accessed=2 * blocks * rows * width, transcendentals=0
        ),
        compiler_params=pltpu.CompilerParams(vmem_limit_bytes=VMEM_BYTES),
    )(me, d_qkv, attn_low, a_one, d_resid_low)


def adam_update(param, grad, first, second, rate, decay, step_number):
    first_new = BETA_ONE * first + (1.0 - BETA_ONE) * grad
    second_new = BETA_TWO * second + (1.0 - BETA_TWO) * grad * grad
    fix_one = 1.0 - BETA_ONE**step_number
    fix_two = 1.0 - BETA_TWO**step_number
    update = first_new / fix_one / (jnp.sqrt(second_new / fix_two) + ADAM_EPS)
    return (first_new, second_new, param - rate * (update + decay * param))


def shards(inputs, cotangent, weights, gains, first_moment, second_moment, gain_first, gain_second):
    ctx_count = lax.axis_size("ctx")
    x_count = lax.axis_size("x")
    ctx_index, core, x_index = lax.axis_index("ctx"), lax.axis_index("core"), lax.axis_index("x")
    seqs, local_rows, model_width = inputs.shape
    half_rows = local_rows // 2
    tokens = seqs * local_rows
    weight_rows = weights.shape[0]
    q_cols = HEADS * HD
    kv_cols = KV * HD
    cut_o = q_cols + 2 * kv_cols
    slots = slot_bits()
    aligned = splits_rows(weight_rows) and half_rows % 128 == 0 and seqs == 2
    split = aligned
    local_index = jnp.arange(local_rows, dtype=jnp.int32)
    pos_here = places(ctx_index * local_rows + local_index, local_rows, ctx_count)
    cosine, sine_part = angle_tables(pos_here, 1.0)
    turn = (jnp.tile(cosine, (1, seqs)), jnp.tile(sine_part, (1, seqs)))

    turn_back = (turn[0], -turn[1])

    def pack(flat):
        if aligned:
            return flat
        return (
            flat.reshape(KV, GROUP, HD, -1, 2, half_rows)
            .transpose(3, 0, 2, 4, 1, 5)
            .reshape(-1, KV, HD, 2 * GROUP * half_rows)
        )

    def unpack(packed):
        if aligned:
            return packed
        return (
            packed.reshape(KV, HD, 2, GROUP, half_rows)
            .transpose(0, 3, 1, 2, 4)
            .reshape(q_cols, local_rows)
        )

    def by_columns(row):
        rows = row.shape[0]
        return jnp.broadcast_to(
            row.reshape(rows, 2, 1, half_rows), (rows, 2, GROUP, half_rows)
        ).reshape(rows, 2 * GROUP * half_rows)

    owners = ctx_index ^ jnp.asarray(rel_offsets(slots), jnp.int32)
    flags = (owners > ctx_index).astype(jnp.int32)
    inner = jnp.arange(half_rows, dtype=jnp.int32)
    key_pos = jnp.stack(
        [
            (owners[:, None] * half_rows + inner[None, :]).reshape(-1, 1),
            ((2 * ctx_count - 1 - owners[:, None]) * half_rows + inner[None, :]).reshape(-1, 1),
        ]
    )
    query_pos = by_columns(pos_here[None, :])
    packed_tables = (by_columns(cosine), by_columns(sine_part))

    tokens_in, cot_in = lax.optimization_barrier(
        (inputs.reshape(tokens, model_width), cotangent.reshape(tokens, model_width))
    )
    dy_low = cot_in.astype(jnp.bfloat16)
    a_one = (normalize(tokens_in) * gains[0]).astype(jnp.bfloat16)
    if split:
        first_half, first_far_x = gather_first(weights)
        cuts = row_cuts(weight_rows // 2)
        backward = [list(reversed(order)) for order in ctx_orders()]
        first_own = [
            double(first_half[None, low:high], order[0])
            for (low, high), order in zip(cuts, backward)
        ]
        later_weights, first_far_x, first_own = lax.optimization_barrier(
            (weights, first_far_x, first_own)
        )
        feed_quarter = gather_quarters(later_weights, first_far_x)
        first_own = [double(part, order[1]) for part, order in zip(first_own, backward)]
        first_own, a_one = lax.optimization_barrier((first_own, a_one))
        first_own = [double(part, order[2]) for part, order in zip(first_own, backward)]
        feed_quarter, first_own = lax.optimization_barrier((feed_quarter, first_own))
        feed_far_z = swap(feed_quarter[None], slots[0])
        first_far = [swap(part, ("core", 0)) for part in first_own]
        first_rows = place_rows(first_own, first_far)
    else:
        mine = lax.all_gather(weights, ("x", "ctx"), axis=0, tiled=True)
        mine = mine.reshape(x_count * ctx_count, weight_rows, model_width)
        far = swap(mine, ("core", 0))
        sides = [
            jnp.where(core == 0, mine[:ctx_count], far[:ctx_count]),
            jnp.where(core == 0, far[:ctx_count], mine[:ctx_count]),
        ]
        first_rows = jnp.concatenate(sides).reshape(-1, model_width)
    qkv_rows, o_rows = first_rows[:cut_o], first_rows[cut_o : cut_o + q_cols]

    pair_rows = matmul_t(qkv_rows[q_cols:], a_one)
    if split:
        pair_rows, feed_far_z = lax.optimization_barrier((pair_rows, feed_far_z))
    joined = jnp.concatenate(
        [rotate(pair_rows[:kv_cols], turn).astype(jnp.bfloat16), pair_rows[kv_cols:].astype(jnp.bfloat16)],
        axis=0,
    )
    if split:
        feed_own = jnp.concatenate([feed_quarter[None], feed_far_z], axis=0)
        joined, feed_own = lax.optimization_barrier((joined, feed_own))
    if aligned:
        mine_0, mine_1 = [
            joined[:, seq * local_rows : (seq + 1) * local_rows] for seq in range(2)
        ]
        far_0, own_y_0 = swap(mine_0, slots[0]), swap(mine_0, slots[2])
        feed_near, feed_y = swap(feed_own, slots[1]), swap(feed_own, slots[2])
        feed_x = swap(feed_own, ("x", 0))
        far_0, own_y_0, feed_near, feed_y, feed_x, mine_1 = lax.optimization_barrier(
            (far_0, own_y_0, feed_near, feed_y, feed_x, mine_1)
        )
        near_0, far_y_0 = swap(jnp.stack([mine_0, far_0]), slots[1]), swap(far_0, slots[2])
        far_1, own_y_1 = swap(mine_1, slots[0]), swap(mine_1, slots[2])
        near_x = swap(feed_near, ("x", 0))
        near_0, far_y_0, far_1, own_y_1, near_x, feed_y = lax.optimization_barrier(
            (near_0, far_y_0, far_1, own_y_1, near_x, feed_y)
        )
        near_y_0 = swap(near_0, slots[2])
        near_1, far_y_1 = swap(jnp.stack([mine_1, far_1]), slots[1]), swap(far_1, slots[2])
        y_x = swap(feed_y, ("x", 0))
        near_y_0, near_1, far_y_1, y_x, feed_near = lax.optimization_barrier(
            (near_y_0, near_1, far_y_1, y_x, feed_near)
        )
        near_y_1 = swap(near_1, slots[2])
        pairs = [
            [(own[None], 0), (far_z[None], 0), (near, 0), (near, 1)]
            + [(own_y[None], 0), (far_y[None], 0), (near_y, 0), (near_y, 1)]
            for own, far_z, near, own_y, far_y, near_y in (
                (mine_0, far_0, near_0, own_y_0, far_y_0, near_y_0),
                (mine_1, far_1, near_1, own_y_1, far_y_1, near_y_1),
            )
        ]
        feed_lower = [
            jnp.concatenate([feed_own, feed_near], axis=0),
            jnp.concatenate([feed_x, near_x], axis=0),
        ]
        feed_lower_far = [swap(part, ("core", 0)) for part in feed_lower]
    else:
        pairs = spread(joined, slots).reshape(ctx_count, 2 * kv_cols, seqs, 2, half_rows)
        pairs = [
            (
                pairs.transpose(1, 2, 3, 0, 4).reshape(
                    1, 2 * kv_cols, seqs * 2 * ctx_count * half_rows
                ),
                0,
            )
        ]
    q_rot = rotate(matmul_t(qkv_rows[:q_cols], a_one), turn).astype(jnp.bfloat16)
    queries = pack((q_rot * SCALE_QK).astype(jnp.bfloat16))
    attended = []
    for seq in range(seqs):
        if aligned:
            attended.append(attend_slots(queries, pairs[seq], flags, local_rows, seq))
            if seq == 0:
                attended, feed_near = lax.optimization_barrier((attended, feed_near))
                feed_near_y = swap(feed_near, slots[2])
        else:
            attended.append(attend(queries, pairs, key_pos, query_pos, local_rows, seq))
    attn_low = jnp.concatenate([unpack(mixed) for mixed, _ in attended], axis=1)
    resid = tokens_in + matmul_c(attn_low, o_rows)
    a_two = (normalize(resid) * gains[1]).astype(jnp.bfloat16)
    if aligned:
        a_two, feed_near_y = lax.optimization_barrier((a_two, feed_near_y))
        near_y_x = swap(feed_near_y, ("x", 0))
        upper_own = jnp.concatenate([feed_y, feed_near_y], axis=0)
        upper_far = swap(upper_own, ("core", 0))
        *sums_fed, keep_lower, away_lower = feed_forward(
            a_two, dy_low, feed_lower, feed_lower_far, weight_rows
        )
        sums_fed, near_y_x, upper_far = lax.optimization_barrier((sums_fed, near_y_x, upper_far))
        upper_x = jnp.concatenate([y_x, near_y_x], axis=0)
        come_lower = swap(away_lower, ("core", 0))
        fed, d_two, keep_upper, away_upper = feed_forward(
            a_two,
            dy_low,
            [upper_own, upper_x],
            [upper_far, swap(upper_x, ("core", 0))],
            weight_rows,
            sums_fed,
        )
        come_upper = swap(away_upper, ("core", 0))
    else:
        fed, d_two, *feed_grads = feed_forward(a_two, dy_low, mine, far, weight_rows)
    result = resid + fed
    d_norm_two, d_gain_two = norm_back(resid, d_two, gains[1])
    d_resid = cot_in + d_norm_two
    d_resid_low = d_resid.astype(jnp.bfloat16)
    d_attn = pack(matmul_t(o_rows, d_resid_low).astype(jnp.bfloat16))
    if aligned:
        quarter = weight_rows // 4
        held_upper, held_lower = [
            [(part[:, :, :quarter], part[:, :, quarter:]) for part in parts]
            for parts in ((keep_upper, come_upper), (keep_lower, come_lower))
        ]
        send_upper, send_lower = [
            total_low(*[far_part for _, far_part in parts]) for parts in (held_upper, held_lower)
        ]
        d_attn, send_upper = lax.optimization_barrier((d_attn, send_upper))
        x_upper = swap(send_upper, ("x", 0))
        x_lower = swap(send_lower, ("x", 0))
    d_q, d_pair = [], []
    for seq in range(seqs):
        mixed, log_total = attended[seq]
        if aligned:
            d_queries, *d_slots = attend_slots_back(
                queries, pairs[seq], flags, mixed, log_total, d_attn, packed_tables, local_rows, seq, (2, 2, 4)
            )
        else:
            d_queries, *d_slots = attend_back(
                queries, pairs, key_pos, query_pos, mixed, log_total, d_attn, packed_tables,
                local_rows, seq, (1,),
            )
        if aligned and seq == 1:
            d_slots, x_upper = lax.optimization_barrier((d_slots, x_upper))
            feed_y_come = swap(total_low(*[part for part, _ in held_upper], x_upper), slots[2])
        d_q.append(unpack(d_queries))
        if aligned:
            lower, near_part, upper = d_slots
            y_come = swap(upper, slots[2])
            near_come = swap(add_low(near_part, y_come[2:]), slots[1])
            if seq == 1:
                near_come, x_lower = lax.optimization_barrier((near_come, x_lower))
            far_come = swap(total_low(lower[1], y_come[1], near_come[1]), slots[0])
            if seq == 1:
                far_come, feed_y_come = lax.optimization_barrier((far_come, feed_y_come))
                rest = [part for part, _ in held_lower] + [x_lower, feed_y_come]
                feed_near_come = swap(total_low(*[part[2:] for part in rest]), slots[1])
            total = far_come.astype(jnp.float32)
            for part in (lower, y_come, near_come):
                total = total + part[0].astype(jnp.float32)
        else:
            total = collect(
                d_slots[0]
                .reshape(2, KV, ctx_count, half_rows, 2 * HD)
                .transpose(2, 1, 0, 3, 4),
                list(reversed(slots)),
            )
        d_pair.append(total)
    d_own = jnp.stack(d_pair).transpose(1, 4, 0, 2, 3).reshape(KV, 2 * HD, tokens)
    d_qkv = jnp.concatenate(
        [
            jnp.concatenate(d_q, axis=1),
            rotate(d_own[:, :HD].reshape(kv_cols, tokens), turn_back).astype(jnp.bfloat16),
            d_own[:, HD:].reshape(kv_cols, tokens).astype(jnp.bfloat16),
        ],
        axis=0,
    )
    d_one = matmul_c(d_qkv, qkv_rows)
    first_terms = first_grads(d_qkv, attn_low, a_one, d_resid_low, weight_rows, split)
    if split:
        first_terms, feed_near_come = lax.optimization_barrier((first_terms, feed_near_come))
        feed_rest = [part[:2] for part in rest] + [feed_near_come]
        far_send = total_low(*[part[1] for part in feed_rest])
        feed_later = {}

        def beside(step, value):
            if step == 0:
                value, sent = lax.optimization_barrier((value, far_send))
                feed_later["far"] = swap(sent, slots[0])
            if step == 1:
                value, far_come = lax.optimization_barrier((value, feed_later["far"]))
                sums = reduce_end(feed_rest, far_come)
                sent = jnp.where(
                    x_index == 0, sums[1:], jnp.broadcast_to(sums[:1], (2,) + sums.shape[1:])
                )
                feed_later["sums"] = sums
                feed_later["come"] = swap(sent.astype(jnp.bfloat16), ("x", 0))
            return value

    d_norm_one, d_gain_one = norm_back(tokens_in, d_one, gains[0])
    d_tokens = d_resid + d_norm_one
    gain_grad = jnp.stack([d_gain_one, d_gain_two], axis=0)
    if split:
        keep, away = [part[:, 0] for part in first_terms]
        first_half, gain_grad = reduce_halves(keep, away, gain_grad, beside)
        first_half, feed_come = lax.optimization_barrier((first_half, feed_later["come"]))
        feed_sums, feed_come = feed_later["sums"], feed_come.astype(jnp.float32)
        low_first = first_half.astype(jnp.bfloat16)
        first_come, gain_grad = swap_with(low_first, gain_grad, ("x", 0))
        first_half = first_half + first_come.astype(jnp.float32)
        halves = [
            jnp.where(x_index == 0, first_half, jnp.concatenate([feed_come[0], feed_sums[1]])),
            jnp.where(
                x_index == 0,
                jnp.concatenate([feed_sums[0], feed_come[0]]),
                jnp.concatenate([feed_come[1], feed_sums[2]]),
            ),
        ]
        own_half = jnp.where(core == 0, halves[0], halves[1])
        other_half = jnp.where(core == 0, halves[1], halves[0]).astype(jnp.bfloat16)
        come, gain_grad = swap_with(other_half, gain_grad, ("core", 0))
        come = come.astype(jnp.float32)
        weight_share = jnp.concatenate(
            [jnp.where(core == 0, own_half, come), jnp.where(core == 0, come, own_half)], axis=0
        )
    else:
        weight_share = scatter_whole([first_terms[0], *feed_grads])
        for where in [("core", 0)] + sum(bit_groups(), []):
            gain_grad = gain_grad + swap(gain_grad, where)
    weight_first, weight_second, weight_new = adam_update(
        weights.astype(jnp.float32), weight_share, first_moment, second_moment, RATE, DECAY, STEP
    )
    gain_first_new, gain_second_new, gain_new = adam_update(
        gains, gain_grad, gain_first, gain_second, GAIN_RATE, 0.0, STEP
    )
    return (
        result.reshape(inputs.shape),
        d_tokens.reshape(inputs.shape),
        weight_share,
        weight_second,
        weight_new,
        gain_grad,
        gain_second_new,
        gain_new,
    )


def solution(mesh):
    fine = Mesh(
        mesh.devices.reshape(mesh.shape["dp"] // 2, 2, mesh.shape["ctx"]), ("x", "core", "ctx")
    )
    rows = P(("x", "core"), "ctx", None)
    stacked = P(("x", "core", "ctx"), None)
    return jax.shard_map(
        shards,
        mesh=fine,
        in_specs=(rows, rows, stacked, P(), stacked, stacked, P(), P()),
        out_specs=(rows, rows, stacked, stacked, stacked, P(), P(), P()),
        check_vma=False,
    )
```

```python
import jax
import jax.numpy as jnp
import numpy as np
from jax import lax
from jax.experimental import pallas as pl
from jax.experimental.pallas import tpu as pltpu
from jax.sharding import Mesh
from jax.sharding import PartitionSpec as P

HEADS = 15
KV = 5
HD = 64
FF = 2560
STEP = 10


SCALE_QK = 0.125
THETA = 10000.0
EPSILON = 1e-05
BETA_ONE = 0.9
BETA_TWO = 0.95
ADAM_EPS = 1e-08
DECAY = 0.1
RATE = 0.02
GAIN_RATE = 0.2
GROUP = HEADS // KV
KEY_TILE = 256
HIDDEN = -1e30
VMEM_BYTES = 48 * 1024 * 1024


def places(row_index, local_rows, ctx_count):
    half_rows = local_rows // 2
    owner_index = row_index // local_rows
    inner_index = row_index % local_rows
    return jnp.where(
        inner_index < half_rows,
        owner_index * half_rows + inner_index,
        (2 * ctx_count - 1 - owner_index) * half_rows + inner_index - half_rows,
    )


def angle_tables(positions_in, sign):
    half_width = HD // 2
    frequency = THETA ** (-jnp.arange(half_width, dtype=jnp.float32) * 2.0 / HD)
    angles = frequency[:, None] * positions_in.astype(jnp.float32)[None, :]
    return jnp.cos(angles), sign * jnp.sin(angles)


def rotate(values, tables):
    cosine, sine_part = tables
    heads = values.reshape(-1, HD, values.shape[-1])
    first_half = heads[:, : HD // 2]
    second_half = heads[:, HD // 2 :]
    return jnp.concatenate(
        [
            first_half * cosine - second_half * sine_part,
            second_half * cosine + first_half * sine_part,
        ],
        axis=1,
    ).reshape(values.shape)


def normalize(values):
    return values * lax.rsqrt(jnp.mean(values * values, axis=-1, keepdims=True) + EPSILON)


def norm_back(values, grad_in, gain_row):
    inv_scale = lax.rsqrt(jnp.mean(values * values, axis=-1, keepdims=True) + EPSILON)
    unit_rows = values * inv_scale
    grad_unit = grad_in * gain_row
    grad_values = inv_scale * (
        grad_unit - unit_rows * jnp.mean(grad_unit * unit_rows, axis=-1, keepdims=True)
    )
    return (grad_values, jnp.sum(grad_in * unit_rows, axis=0))


def matmul_n(left, right):
    return jnp.dot(left, right, preferred_element_type=jnp.float32)


def matmul_t(left, right):
    return lax.dot_general(
        left, right, (((1,), (1,)), ((), ())), preferred_element_type=jnp.float32
    )


def matmul_c(left, right):
    return lax.dot_general(
        left, right, (((0,), (0,)), ((), ())), preferred_element_type=jnp.float32
    )


def bit_groups():
    x_bits = lax.axis_size("x").bit_length() - 1
    ctx_bits = lax.axis_size("ctx").bit_length() - 1
    low_ctx = ctx_bits // 2
    along_x = [("x", bit) for bit in range(x_bits)]
    along_y = [("ctx", bit) for bit in range(low_ctx)]
    along_z = [("ctx", bit) for bit in range(low_ctx, ctx_bits)]
    return along_x, along_y, along_z


def swap_by(values, axis, offset):
    size = lax.axis_size(axis)
    return lax.ppermute(values, axis, [(i, i ^ offset) for i in range(size)])


def swap(values, where):
    return swap_by(values, where[0], 1 << where[1])


def add_low(left, right):
    return (left.astype(jnp.float32) + right.astype(jnp.float32)).astype(jnp.bfloat16)


def rel_offsets(order):
    strides = {"x": 2 * lax.axis_size("ctx"), "ctx": 1}
    offsets = np.zeros((1,), np.int64)
    for axis, bit in order:
        offsets = np.concatenate([offsets, offsets ^ (strides[axis] << bit)])
    return offsets


def lookup(slot, offsets):
    total = jnp.int32(0)
    for bit in range(len(offsets).bit_length() - 1):
        total = total + ((slot >> bit) & 1) * int(offsets[1 << bit])
    return total


def find(offset, offsets):
    total = jnp.int32(0)
    for bit in range(len(offsets).bit_length() - 1):
        place = int(offsets[1 << bit]).bit_length() - 1
        total = total + (((offset >> place) & 1) << bit)
    return total


def collect(values, order):
    kept, arrived = values, None
    for where in order:
        half = kept.shape[0] // 2
        if arrived is None:
            away, kept_next = kept[half:], kept[:half]
        else:
            away = add_low(kept[half:], arrived[half:])
            kept_next = add_low(kept[:half], arrived[:half])
        arrived = swap(away, where)
        kept = kept_next
    return kept[0].astype(jnp.float32) + arrived[0].astype(jnp.float32)


def scatter_whole(terms):
    ctx_count = lax.axis_size("ctx")
    count = 2 * lax.axis_size("x") * ctx_count
    along_x, along_y, along_z = bit_groups()
    core = ("core", 0)
    me = device_index().reshape(1)
    blocks, rows, width = terms[0].shape
    first = -(-rows // 48) * 16
    groups = [(0, first), (first, 2 * first), (2 * first, rows)]
    orders = [
        along_x + along_y + along_z,
        along_y + along_z + along_x,
        along_z + along_x + along_y,
    ]
    tables = [rel_offsets(list(reversed(order))) for order in orders]

    def target(step, me_ref, flip):
        return lookup(step, tables[0]) ^ me_ref[0] ^ flip

    def sources(flip):
        def chosen(member):
            def index(step, me_ref):
                spot = target(step, me_ref, flip)
                return (jnp.where(spot // blocks == member, spot % blocks, 0), 0, 0)

            return pl.BlockSpec((1, rows, width), index)

        return [chosen(member) for member in range(len(terms))]

    def pick_body(me_ref, *refs):
        held = target(pl.program_id(0), me_ref, ctx_count) // blocks
        for member in range(len(terms)):

            @pl.when(held == member)
            def _(member=member):
                refs[-1][...] = refs[member][...]

    away = pl.pallas_call(
        pick_body,
        grid_spec=pltpu.PrefetchScalarGridSpec(
            num_scalar_prefetch=1,
            grid=(count // 2,),
            in_specs=sources(ctx_count),
            out_specs=pl.BlockSpec((1, rows, width), lambda step, me_ref: (step, 0, 0)),
        ),
        out_shape=jax.ShapeDtypeStruct((count // 2, rows, width), jnp.bfloat16),
        compiler_params=pltpu.CompilerParams(vmem_limit_bytes=VMEM_BYTES),
    )(me, *terms)
    arrived = swap(away, core)

    def merge_body(me_ref, *refs):
        held = target(pl.program_id(0), me_ref, 0) // blocks
        for member in range(len(terms)):

            @pl.when(held == member)
            def _(member=member):
                for (low, high), out in zip(groups, refs[-3:]):
                    out[0] = add_low(refs[member][0, low:high], refs[-4][0, low:high])

    parts = pl.pallas_call(
        merge_body,
        grid_spec=pltpu.PrefetchScalarGridSpec(
            num_scalar_prefetch=1,
            grid=(count // 2,),
            in_specs=sources(0)
            + [pl.BlockSpec((1, rows, width), lambda step, me_ref: (step, 0, 0))],
            out_specs=[
                pl.BlockSpec(
                    (1, high - low, width),
                    lambda step, me_ref, table=table: (
                        find(lookup(step, tables[0]), table),
                        0,
                        0,
                    ),
                )
                for (low, high), table in zip(groups, tables)
            ],
        ),
        out_shape=[
            jax.ShapeDtypeStruct((count // 2, high - low, width), jnp.bfloat16)
            for low, high in groups
        ],
        compiler_params=pltpu.CompilerParams(vmem_limit_bytes=VMEM_BYTES),
    )(me, *terms, arrived)
    return jnp.concatenate([collect(part, order) for part, order in zip(parts, orders)], axis=0)


def device_index():
    return (
        (lax.axis_index("x") * 2 + lax.axis_index("core")) * lax.axis_size("ctx")
        + lax.axis_index("ctx")
    ).astype(jnp.int32)


def splits_rows(rows):
    along_x, along_y, along_z = bit_groups()
    return (len(along_x), len(along_y), len(along_z)) == (1, 1, 2) and rows % 64 == 0


def spread(values, order):
    values = values[None]
    for where in order:
        values = double(values, where)
    return values


def double(values, where):
    return jnp.concatenate([values, swap(values, where)], axis=0)


def ctx_orders():
    along_x, along_y, along_z = bit_groups()
    return [along_y + along_z, along_z + along_y]


def row_cuts(rows):
    first = -(-rows * 3 // 80) * 16
    return [(0, first), (first, rows)]


def slot_bits():
    along_x, along_y, along_z = bit_groups()
    return list(reversed(along_z)) + along_y


def total_low(*terms):
    total = terms[0].astype(jnp.float32)
    for term in terms[1:]:
        total = total + term.astype(jnp.float32)
    return total.astype(jnp.bfloat16)


def reduce_end(rest, z_far):
    total = z_far.astype(jnp.float32)
    for part in rest:
        total = total + part[0].astype(jnp.float32)
    return total


def reduce_halves(keep, away, ride, beside):
    far_z, near_z, along_y = slot_bits()
    come = beside(0, swap(away, ("core", 0)))
    sums = []
    for (low, high), order in zip(
        row_cuts(keep.shape[1]), ([along_y, near_z, far_z], [near_z, far_z, along_y])
    ):
        shape = (2, 2, 2, high - low, keep.shape[2])
        terms = [keep[:, low:high].reshape(shape), come[:, low:high].reshape(shape)]
        left = [along_y, near_z, far_z]
        for position, where in enumerate(order):
            dim = left.index(where)
            left.remove(where)
            sent = total_low(*[lax.index_in_dim(term, 1, dim, False) for term in terms])
            if low == 0:
                arrived, ride = swap_with(sent, ride, where)
                arrived = beside(position + 1, arrived)
            else:
                arrived = swap(sent, where)
            terms = [lax.index_in_dim(term, 0, dim, False) for term in terms] + [arrived]
        total = terms[0].astype(jnp.float32)
        for term in terms[1:]:
            total = total + term.astype(jnp.float32)
        sums.append(total)
    return jnp.concatenate(sums, axis=0), ride


def ride_parts(ride):
    rounded = lax.reduce_precision(ride, 8, 7)
    return rounded, lax.reduce_precision(ride - rounded, 8, 7)


def with_ride(sent, parts):
    extra = jnp.concatenate([*parts, jnp.zeros((12, parts[0].shape[1]), jnp.float32)])
    return jnp.concatenate([sent.reshape(-1, sent.shape[-1]), extra.astype(jnp.bfloat16)], axis=0)


def swap_with(sent, ride, where):
    parts = ride_parts(ride)
    come, other = off_ride(swap(with_ride(sent, parts), where), sent.shape)
    return come, (parts[0] + parts[1]) + other


def off_ride(come, shape):
    parts = come[-16:].astype(jnp.float32)
    return come[:-16].reshape(shape), parts[0:2] + parts[2:4]


def gather_first(weights):
    half = weights.shape[0] // 2
    far = lax.ppermute(weights, ("x", "core"), [(0, 2)])
    rows = jnp.where(lax.axis_index("x") == 0, weights, far)
    come = swap(rows[half:], ("core", 0))
    return jnp.where(lax.axis_index("core") == 0, rows[:half], come), far


def gather_quarters(weights, first_far):
    half = weights.shape[0] // 2
    x_index, core = lax.axis_index("x"), lax.axis_index("core")
    far = lax.ppermute(weights, ("x", "core"), [(2, 0), (1, 3), (3, 1)])
    far = jnp.where((x_index == 1) & (core == 0), first_far, far)
    both = jnp.stack([jnp.where(x_index == 0, weights, far), jnp.where(x_index == 0, far, weights)])
    keep = jnp.where(core == 0, both[:, :half], both[:, half:])
    come = swap(jnp.where(core == 0, both[:, half:], both[:, :half]), ("core", 0))
    first = jnp.where(core == 0, keep, come)
    second = jnp.where(core == 0, come, keep)
    feed = jnp.stack([second[0], first[1], second[1]])
    return jnp.where(x_index == 0, feed[:, : half // 2], feed[:, half // 2 :])


def place_rows(own, far):
    tables = [rel_offsets(list(reversed(order))) for order in ctx_orders()]
    slots, width = own[0].shape[0], own[0].shape[2]
    lengths = [part.shape[1] for part in own]
    half = sum(lengths)

    def body(me_ref, *refs):
        out_ref = refs[-1]
        for core in range(2):

            @pl.when(me_ref[0] == core)
            def _(core=core):
                for source, base in ((0, core * half), (2, (1 - core) * half)):
                    out_ref[0, base : base + lengths[0]] = refs[source][0]
                    out_ref[0, base + lengths[0] : base + half] = refs[source + 1][0]

    specs = [
        pl.BlockSpec(
            (1, length, width),
            lambda step, me_ref, table=table: (find(step ^ me_ref[1], table), 0, 0),
        )
        for length, table in zip(lengths, tables)
    ]
    me = jnp.stack([lax.axis_index("core"), lax.axis_index("ctx")]).astype(jnp.int32)
    return pl.pallas_call(
        body,
        grid_spec=pltpu.PrefetchScalarGridSpec(
            num_scalar_prefetch=1,
            grid=(slots,),
            in_specs=specs * 2,
            out_specs=pl.BlockSpec((1, 2 * half, width), lambda step, me_ref: (step, 0, 0)),
        ),
        out_shape=jax.ShapeDtypeStruct((slots, 2 * half, width), own[0].dtype),
        cost_estimate=pl.CostEstimate(
            flops=0, bytes_accessed=8 * slots * half * width, transcendentals=0
        ),
        compiler_params=pltpu.CompilerParams(vmem_limit_bytes=VMEM_BYTES),
    )(me, *own, *far).reshape(slots * 2 * half, width)


def turned(values):
    return jnp.transpose(values)


def load_packed(ref, aligned):
    if not aligned:
        return ref[0, 0]
    half = ref.shape[1] // 2
    return jnp.concatenate(
        [
            ref[head * HD : (head + 1) * HD, side * half : (side + 1) * half]
            for side in range(2)
            for head in range(GROUP)
        ],
        axis=1,
    )


def store_packed(ref, values, aligned):
    if not aligned:
        ref[0, 0] = values
        return
    half = ref.shape[1] // 2
    for side in range(2):
        for head in range(GROUP):
            start = (side * GROUP + head) * half
            ref[head * HD : (head + 1) * HD, side * half : (side + 1) * half] = values[
                :, start : start + half
            ]


def load_tile(refs, side, tile):
    length = refs[0].shape[1] // 2
    if length >= KEY_TILE:
        start = side * length + tile * KEY_TILE
        return refs[0][:, start : start + KEY_TILE]
    many = KEY_TILE // length
    return jnp.concatenate(
        [
            ref[:, side * length : (side + 1) * length]
            for ref in refs[tile * many : (tile + 1) * many]
        ],
        axis=1,
    )


def attend_body(count, aligned, queries_ref, key_pos_ref, query_pos_ref, *refs):
    key_refs, value_refs = refs[:count], refs[count : 2 * count]
    out_ref, total_ref, work = refs[2 * count :]
    queries = load_packed(queries_ref, aligned)
    low_cols = queries.shape[1] // 2
    queries_high = queries[:, low_cols:]
    tiles = key_pos_ref.shape[1] // KEY_TILE
    largest = jnp.full((1, queries.shape[1]), HIDDEN, jnp.float32)
    largest_high = jnp.full((1, low_cols), HIDDEN, jnp.float32)
    for side in range(2):
        for tile in range(tiles):
            keys = turned(load_tile(key_refs, side, tile))
            row = (side * tiles + tile) * KEY_TILE
            key_places = key_pos_ref[side, tile * KEY_TILE : (tile + 1) * KEY_TILE]
            if side == 0:
                scores = matmul_n(keys, queries)
                scores = jnp.where(key_places <= query_pos_ref[...], scores, HIDDEN)
                work[row : row + KEY_TILE] = scores
                largest = jnp.maximum(largest, jnp.max(scores, axis=0, keepdims=True))
            else:
                scores = matmul_n(keys, queries_high)
                scores = jnp.where(key_places <= query_pos_ref[:, low_cols:], scores, HIDDEN)
                work[row : row + KEY_TILE, low_cols:] = scores
                largest_high = jnp.maximum(largest_high, jnp.max(scores, axis=0, keepdims=True))
    high_max = jnp.maximum(largest[:, low_cols:], largest_high)
    largest = jnp.concatenate([largest[:, :low_cols], high_max], axis=1)
    total = jnp.zeros_like(largest)
    mixed = jnp.zeros((HD, queries.shape[1]), jnp.float32)
    total_high = jnp.zeros_like(largest_high)
    mixed_high = jnp.zeros((HD, low_cols), jnp.float32)
    for side in range(2):
        for tile in range(tiles):
            values = load_tile(value_refs, side, tile)
            row = (side * tiles + tile) * KEY_TILE
            if side == 0:
                expos = jnp.exp(work[row : row + KEY_TILE] - largest)
                total = total + jnp.sum(expos, axis=0, keepdims=True)
                mixed = mixed + matmul_n(values, expos.astype(jnp.bfloat16))
            else:
                expos = jnp.exp(work[row : row + KEY_TILE, low_cols:] - high_max)
                total_high = total_high + jnp.sum(expos, axis=0, keepdims=True)
                mixed_high = mixed_high + matmul_n(values, expos.astype(jnp.bfloat16))
    total = jnp.concatenate([total[:, :low_cols], total[:, low_cols:] + total_high], axis=1)
    mixed = jnp.concatenate([mixed[:, :low_cols], mixed[:, low_cols:] + mixed_high], axis=1)
    store_packed(out_ref, (mixed / total).astype(jnp.bfloat16), aligned)
    total_ref[0, 0] = largest + jnp.log(total)


def attend_back_body(
    count, aligned, queries_ref, key_pos_ref, query_pos_ref, *refs
):
    key_refs, value_refs = refs[:count], refs[count : 2 * count]
    out_ref, total_ref, d_out_ref, cosine_ref, sine_ref = refs[2 * count : 2 * count + 5]
    d_queries_ref, pair_refs = refs[2 * count + 5], refs[2 * count + 6 :]
    all_queries, all_d_out = load_packed(queries_ref, aligned), load_packed(d_out_ref, aligned)
    low_cols = all_queries.shape[1] // 2
    tiles = key_pos_ref.shape[1] // KEY_TILE
    delta = jnp.sum(
        all_d_out.astype(jnp.float32) * load_packed(out_ref, aligned).astype(jnp.float32),
        axis=0,
        keepdims=True,
    )
    totals = total_ref[0, 0]
    parts = []
    for side in range(2):
        if side == 0:
            queries, d_out = all_queries, all_d_out
            query_places, log_total, row_delta = query_pos_ref[...], totals, delta
        else:
            queries, d_out = all_queries[:, low_cols:], all_d_out[:, low_cols:]
            query_places = query_pos_ref[:, low_cols:]
            log_total, row_delta = totals[:, low_cols:], delta[:, low_cols:]
        part = jnp.zeros((HD, queries.shape[1]), jnp.float32)
        for tile in range(tiles):
            keys_flat = load_tile(key_refs, side, tile)
            scores = matmul_n(turned(keys_flat), queries)
            seen = key_pos_ref[side, tile * KEY_TILE : (tile + 1) * KEY_TILE] <= query_places
            probs = jnp.where(seen, jnp.exp(scores - log_total), 0.0)
            d_probs = matmul_n(turned(load_tile(value_refs, side, tile)), d_out)
            d_scores = (probs * (d_probs - row_delta)).astype(jnp.bfloat16)
            part = part + matmul_n(keys_flat, d_scores)
            d_key = matmul_t(d_scores, queries).astype(jnp.bfloat16)
            d_value = matmul_t(probs.astype(jnp.bfloat16), d_out).astype(jnp.bfloat16)
            if aligned:
                length = key_refs[0].shape[1] // 2
                places_out = [(ref, slot) for ref in pair_refs for slot in range(ref.shape[0])]
                for piece in range(KEY_TILE // length):
                    ref, slot = places_out[tile * (KEY_TILE // length) + piece]
                    rows = slice(piece * length, (piece + 1) * length)
                    ref[slot, 0, side, :, :HD] = d_key[rows]
                    ref[slot, 0, side, :, HD:] = d_value[rows]
            else:
                rows = slice(tile * KEY_TILE, (tile + 1) * KEY_TILE)
                pair_refs[0][side, 0, rows, :HD] = d_key
                pair_refs[0][side, 0, rows, HD:] = d_value
        parts.append(part)
    d_queries = jnp.concatenate(
        [parts[0][:, :low_cols], parts[0][:, low_cols:] + parts[1]], axis=1
    )
    cosine, sine_part = cosine_ref[...], sine_ref[...]
    first_half, second_half = d_queries[: HD // 2], d_queries[HD // 2 :]
    turned_back = jnp.concatenate(
        [
            first_half * cosine + second_half * sine_part,
            second_half * cosine - first_half * sine_part,
        ],
        axis=0,
    )
    store_packed(d_queries_ref, (turned_back * SCALE_QK).astype(jnp.bfloat16), aligned)


def own_mask(rows, cols):
    return lax.broadcasted_iota(jnp.int32, (rows, cols), 0) <= (
        lax.broadcasted_iota(jnp.int32, (rows, cols), 1) % rows
    )


def slot_keys(ref, length):
    both = turned(ref[...])
    return both[:length], both[length:]


def attend_slots_body(count, flags_ref, queries_ref, *refs):
    key_refs, value_refs = refs[:count], refs[count : 2 * count]
    out_ref, total_ref, both_queries, work, largest, totals, mixed = refs[2 * count :]
    length = key_refs[0].shape[1] // 2
    cols = GROUP * length
    packed = load_packed(queries_ref, True)
    for side in range(2):
        both_queries[side] = packed[:, side * cols : (side + 1) * cols]
    visible = own_mask(length, cols)
    low_keys, high_keys = zip(*[slot_keys(ref, length) for ref in key_refs])
    row = 0

    def keep_scores(scores, row):
        work[row : row + scores.shape[0]] = scores
        return jnp.max(scores, axis=0, keepdims=True)

    for side, keys in ((0, low_keys[0]), (1, high_keys[0])):
        scores = jnp.where(visible, matmul_n(keys, both_queries[side]), HIDDEN)
        largest[side] = keep_scores(scores, row)
        row += length
    for slot in range(0, count, 2):
        keys = jnp.concatenate([low_keys[slot], low_keys[slot + 1]], axis=0)
        top = keep_scores(matmul_n(keys, both_queries[1]), row)
        largest[1] = jnp.maximum(largest[1], top)
        row += 2 * length
    for slot in range(1, count):
        side = flags_ref[slot]
        keys = jnp.where(side == 0, low_keys[slot], high_keys[slot])
        top = keep_scores(matmul_n(keys, both_queries[side]), row)
        largest[side] = jnp.maximum(largest[side], top)
        row += length
    row = 0
    for side in range(2):
        values = value_refs[0][:, side * length : (side + 1) * length]
        expos = jnp.exp(work[row : row + length] - largest[side])
        totals[side] = jnp.sum(expos, axis=0, keepdims=True)
        mixed[side] = matmul_n(values, expos.astype(jnp.bfloat16))
        row += length
    for slot in range(0, count, 2):
        values = jnp.concatenate(
            [value_refs[slot][:, :length], value_refs[slot + 1][:, :length]], axis=1
        )
        expos = jnp.exp(work[row : row + 2 * length] - largest[1])
        totals[1] += jnp.sum(expos, axis=0, keepdims=True)
        mixed[1] += matmul_n(values, expos.astype(jnp.bfloat16))
        row += 2 * length
    for slot in range(1, count):
        side = flags_ref[slot]
        values = jnp.where(side == 0, value_refs[slot][:, :length], value_refs[slot][:, length:])
        expos = jnp.exp(work[row : row + length] - largest[side])
        totals[side] += jnp.sum(expos, axis=0, keepdims=True)
        mixed[side] += matmul_n(values, expos.astype(jnp.bfloat16))
        row += length
    result = [(mixed[side] / totals[side]).astype(jnp.bfloat16) for side in range(2)]
    store_packed(out_ref, jnp.concatenate(result, axis=1), True)
    logs = [largest[side] + jnp.log(totals[side]) for side in range(2)]
    total_ref[0, 0] = jnp.concatenate(logs, axis=1)


def attend_slots_back_body(count, flags_ref, queries_ref, *refs):
    key_refs, value_refs = refs[:count], refs[count : 2 * count]
    out_ref, total_ref, d_out_ref, cosine_ref, sine_ref = refs[2 * count : 2 * count + 5]
    d_queries_ref = refs[2 * count + 5]
    pair_refs = refs[2 * count + 6 : -7]
    both_queries, both_d_out, turned_queries, turned_d_out, log_totals, deltas, sums = refs[-7:]
    length = key_refs[0].shape[1] // 2
    cols = GROUP * length
    queries, d_out = load_packed(queries_ref, True), load_packed(d_out_ref, True)
    delta = jnp.sum(
        d_out.astype(jnp.float32) * load_packed(out_ref, True).astype(jnp.float32),
        axis=0,
        keepdims=True,
    )
    for side in range(2):
        part = slice(side * cols, (side + 1) * cols)
        both_queries[side] = queries[:, part]
        both_d_out[side] = d_out[:, part]
        turned_queries[side] = turned(queries[:, part])
        turned_d_out[side] = turned(d_out[:, part])
        log_totals[side] = total_ref[0, 0, :, part]
        deltas[side] = delta[:, part]
    sums[...] = jnp.zeros_like(sums)
    visible = own_mask(length, cols)
    low_keys, high_keys = zip(*[slot_keys(ref, length) for ref in key_refs])
    low_values, high_values = zip(*[slot_keys(ref, length) for ref in value_refs])
    places_out = [(ref, slot) for ref in pair_refs for slot in range(ref.shape[0])]

    def block(keys, keys_flat, values, side, mask=None):
        probs = jnp.exp(matmul_n(keys, both_queries[side]) - log_totals[side])
        if mask is not None:
            probs = jnp.where(mask, probs, 0.0)
        d_probs = matmul_n(values, both_d_out[side])
        d_scores = (probs * (d_probs - deltas[side])).astype(jnp.bfloat16)
        sums[side] += matmul_n(keys_flat, d_scores)
        return jnp.concatenate(
            [
                matmul_n(d_scores, turned_queries[side]),
                matmul_n(probs.astype(jnp.bfloat16), turned_d_out[side]),
            ],
            axis=1,
        )

    low_terms = []
    for slot in range(0, count, 2):
        keys, values = [
            jnp.concatenate([part[slot], part[slot + 1]], axis=0) for part in (low_keys, low_values)
        ]
        flat = jnp.concatenate([key_refs[slot][:, :length], key_refs[slot + 1][:, :length]], axis=1)
        terms = block(keys, flat, values, 1)
        low_terms += [terms[:length], terms[length:]]
    ref, slot = places_out[0]
    own = [
        block(keys, key_refs[0][:, side * length : (side + 1) * length], values, side, visible)
        for side, (keys, values) in enumerate(
            ((low_keys[0], low_values[0]), (high_keys[0], high_values[0]))
        )
    ]
    ref[slot, 0, 0] = (low_terms[0] + own[0]).astype(jnp.bfloat16)
    ref[slot, 0, 1] = own[1].astype(jnp.bfloat16)
    for member in range(1, count):
        side = flags_ref[member]
        low = side == 0
        keys = jnp.where(low, low_keys[member], high_keys[member])
        flat = jnp.where(low, key_refs[member][:, :length], key_refs[member][:, length:])
        values = jnp.where(low, low_values[member], high_values[member])
        terms = block(keys, flat, values, side)
        ref, slot = places_out[member]
        ref[slot, 0, 0] = (low_terms[member] + jnp.where(low, terms, 0.0)).astype(jnp.bfloat16)
        ref[slot, 0, 1] = jnp.where(low, 0.0, terms).astype(jnp.bfloat16)
    d_queries = jnp.concatenate([sums[0], sums[1]], axis=1)
    store_packed(d_queries_ref, turn_queries_back(d_queries, cosine_ref, sine_ref), True)


def turn_queries_back(d_queries, cosine_ref, sine_ref):
    cosine, sine_part = cosine_ref[...], sine_ref[...]
    first_half, second_half = d_queries[: HD // 2], d_queries[HD // 2 :]
    turned_back = jnp.concatenate(
        [
            first_half * cosine + second_half * sine_part,
            second_half * cosine - first_half * sine_part,
        ],
        axis=0,
    )
    return (turned_back * SCALE_QK).astype(jnp.bfloat16)


def slot_specs(leads, local_rows, seq):
    specs = [
        pl.BlockSpec(memory_space=pltpu.SMEM),
        pl.BlockSpec((GROUP * HD, local_rows), lambda head: (head, seq)),
    ]
    for first in (0, KV):
        specs += [
            pl.BlockSpec(
                (None, HD, local_rows),
                lambda head, lead=lead, first=first: (lead, first + head, 0),
            )
            for lead in leads
        ]
    return specs


def attend_slots(queries, pairs, flags, local_rows, seq):
    count, cols = len(pairs), GROUP * local_rows // 2
    leads, arrays = [lead for _, lead in pairs], [array for array, _ in pairs]
    work = HEADS * local_rows * local_rows * count // 2
    return pl.pallas_call(
        lambda *refs: attend_slots_body(count, *refs),
        grid=(KV,),
        in_specs=slot_specs(leads, local_rows, seq),
        out_specs=[
            pl.BlockSpec((GROUP * HD, local_rows), lambda head: (head, 0)),
            pl.BlockSpec((1, 1, 1, 2 * cols), lambda head: (0, head, 0, 0)),
        ],
        out_shape=[
            jax.ShapeDtypeStruct((HEADS * HD, local_rows), jnp.bfloat16),
            jax.ShapeDtypeStruct((1, KV, 1, 2 * cols), jnp.float32),
        ],
        scratch_shapes=[
            pltpu.VMEM((2, HD, cols), jnp.bfloat16),
            pltpu.VMEM(((2 * count + 1) * local_rows // 2, cols), jnp.float32),
            pltpu.VMEM((2, 1, cols), jnp.float32),
            pltpu.VMEM((2, 1, cols), jnp.float32),
            pltpu.VMEM((2, HD, cols), jnp.float32),
        ],
        cost_estimate=pl.CostEstimate(
            flops=work * HD, bytes_accessed=1024 * 1024, transcendentals=0
        ),
        compiler_params=pltpu.CompilerParams(vmem_limit_bytes=VMEM_BYTES),
    )(flags, queries, *arrays, *arrays)


def attend_slots_back(
    queries, pairs, flags, mixed, log_total, d_mixed, tables, local_rows, seq, sets
):
    count, cols = len(pairs), GROUP * local_rows // 2
    leads, arrays = [lead for _, lead in pairs], [array for array, _ in pairs]
    work = HEADS * local_rows * local_rows * count // 2
    own = pl.BlockSpec((GROUP * HD, local_rows), lambda head: (head, 0))
    table_spec = pl.BlockSpec((HD // 2, 2 * cols), lambda head: (0, 0))
    length = local_rows // 2
    return pl.pallas_call(
        lambda *refs: attend_slots_back_body(count, *refs),
        grid=(KV,),
        in_specs=slot_specs(leads, local_rows, seq)
        + [
            own,
            pl.BlockSpec((1, 1, 1, 2 * cols), lambda head: (0, head, 0, 0)),
            pl.BlockSpec((GROUP * HD, local_rows), lambda head: (head, seq)),
            table_spec,
            table_spec,
        ],
        out_specs=[own]
        + [
            pl.BlockSpec((slots, 1, 2, length, 2 * HD), lambda head: (0, head, 0, 0, 0))
            for slots in sets
        ],
        out_shape=[jax.ShapeDtypeStruct((HEADS * HD, local_rows), jnp.bfloat16)]
        + [jax.ShapeDtypeStruct((slots, KV, 2, length, 2 * HD), jnp.bfloat16) for slots in sets],
        scratch_shapes=[
            pltpu.VMEM((2, HD, cols), jnp.bfloat16),
            pltpu.VMEM((2, HD, cols), jnp.bfloat16),
            pltpu.VMEM((2, cols, HD), jnp.bfloat16),
            pltpu.VMEM((2, cols, HD), jnp.bfloat16),
            pltpu.VMEM((2, 1, cols), jnp.float32),
            pltpu.VMEM((2, 1, cols), jnp.float32),
            pltpu.VMEM((2, HD, cols), jnp.float32),
        ],
        cost_estimate=pl.CostEstimate(
            flops=work * HD, bytes_accessed=1024 * 1024, transcendentals=0
        ),
        compiler_params=pltpu.CompilerParams(vmem_limit_bytes=VMEM_BYTES),
    )(flags, queries, *arrays, *arrays, mixed, log_total, d_mixed, *tables)


def head_specs(leads, aligned, cols, keys, local_rows, seq):
    count = len(leads)
    if aligned:
        packed = pl.BlockSpec((GROUP * HD, local_rows), lambda head: (head, seq))
    else:
        packed = pl.BlockSpec((1, 1, HD, cols), lambda head: (seq, head, 0, 0))
    specs = [
        packed,
        pl.BlockSpec((2, keys, 1), lambda head: (0, 0, 0)),
        pl.BlockSpec((1, cols), lambda head: (0, 0)),
    ]
    for first in (0, KV):
        specs += [
            pl.BlockSpec(
                (None, HD, 2 * keys // count),
                lambda head, lead=lead, first=first: (lead, first + head, seq),
            )
            for lead in leads
        ]
    return packed, specs


def attend(queries, pairs, key_pos, query_pos, local_rows, seq):
    aligned = queries.ndim == 2
    cols, keys, count = query_pos.shape[1], key_pos.shape[1], len(pairs)
    leads, arrays = [lead for _, lead in pairs], [array for array, _ in pairs]
    _, specs = head_specs(leads, aligned, cols, keys, local_rows, seq)
    work = HEADS * keys * cols // GROUP * 3 // 2
    if aligned:
        out_spec = pl.BlockSpec((GROUP * HD, local_rows), lambda head: (head, 0))
        out_shape = jax.ShapeDtypeStruct((HEADS * HD, local_rows), jnp.bfloat16)
    else:
        out_spec = pl.BlockSpec((1, 1, HD, cols), lambda head: (0, head, 0, 0))
        out_shape = jax.ShapeDtypeStruct((1, KV, HD, cols), jnp.bfloat16)
    return pl.pallas_call(
        lambda *refs: attend_body(count, aligned, *refs),
        grid=(KV,),
        in_specs=specs,
        out_specs=[out_spec, pl.BlockSpec((1, 1, 1, cols), lambda head: (0, head, 0, 0))],
        out_shape=[out_shape, jax.ShapeDtypeStruct((1, KV, 1, cols), jnp.float32)],
        scratch_shapes=[pltpu.VMEM((2 * keys, cols), jnp.float32)],
        cost_estimate=pl.CostEstimate(
            flops=work * HD, bytes_accessed=1024 * 1024, transcendentals=0
        ),
        compiler_params=pltpu.CompilerParams(vmem_limit_bytes=VMEM_BYTES),
    )(queries, key_pos, query_pos, *arrays, *arrays)


def attend_back(
    queries, pairs, key_pos, query_pos, mixed, log_total, d_mixed, tables, local_rows, seq, sets
):
    aligned = queries.ndim == 2
    cols, keys, count = query_pos.shape[1], key_pos.shape[1], len(pairs)
    leads, arrays = [lead for _, lead in pairs], [array for array, _ in pairs]
    packed, specs = head_specs(leads, aligned, cols, keys, local_rows, seq)
    work = HEADS * keys * cols // GROUP * 3 // 2
    if aligned:
        own = pl.BlockSpec((GROUP * HD, local_rows), lambda head: (head, 0))
        own_shape = jax.ShapeDtypeStruct((HEADS * HD, local_rows), jnp.bfloat16)
        length = keys // count
        pair_specs = [
            pl.BlockSpec((slots, 1, 2, length, 2 * HD), lambda head: (0, head, 0, 0, 0))
            for slots in sets
        ]
        pair_shapes = [
            jax.ShapeDtypeStruct((slots, KV, 2, length, 2 * HD), jnp.bfloat16) for slots in sets
        ]
    else:
        own = pl.BlockSpec((1, 1, HD, cols), lambda head: (0, head, 0, 0))
        own_shape = jax.ShapeDtypeStruct((1, KV, HD, cols), jnp.bfloat16)
        pair_specs = [pl.BlockSpec((2, 1, keys, 2 * HD), lambda head: (0, head, 0, 0))]
        pair_shapes = [jax.ShapeDtypeStruct((2, KV, keys, 2 * HD), jnp.bfloat16)]
    table_spec = pl.BlockSpec((HD // 2, cols), lambda head: (0, 0))
    return pl.pallas_call(
        lambda *refs: attend_back_body(count, aligned, *refs),
        grid=(KV,),
        in_specs=specs
        + [
            own,
            pl.BlockSpec((1, 1, 1, cols), lambda head: (0, head, 0, 0)),
            packed,
            table_spec,
            table_spec,
        ],
        out_specs=[own] + pair_specs,
        out_shape=[own_shape] + pair_shapes,
        cost_estimate=pl.CostEstimate(
            flops=work * HD, bytes_accessed=1024 * 1024, transcendentals=0
        ),
        compiler_params=pltpu.CompilerParams(vmem_limit_bytes=VMEM_BYTES),
    )(queries, key_pos, query_pos, *arrays, *arrays, mixed, log_total, d_mixed, *tables)


def put_rows(values, keep_ref, away_ref, place, core, x_index):
    quarter = values.shape[0] // 4
    for mine in range(4):

        @pl.when(2 * core + x_index == mine)
        def _(mine=mine):
            for ref, side in ((keep_ref, mine // 2), (away_ref, 1 - mine // 2)):
                for position, along_x in enumerate((mine % 2, 1 - mine % 2)):
                    start = (2 * side + along_x) * quarter
                    ref[place[0], place[1], position * quarter : (position + 1) * quarter] = values[
                        start : start + quarter
                    ]


def feed_body(
    parts, split, chained, me_ref, a_two_ref, dy_ref, *refs
):
    count = 4 if split else 6
    before, refs = (refs[:2], refs[2:]) if chained else (None, refs)
    weight_refs, (out_ref, d_two_ref), grad_refs = (
        refs[:count],
        refs[count : count + 2],
        refs[count + 2 :],
    )
    core, x_index = me_ref[0], me_ref[1]
    step = pl.program_id(0)

    @pl.when(step == 0)
    def _():
        for place, ref in enumerate((out_ref, d_two_ref)):
            ref[...] = before[place][...] if chained else jnp.zeros_like(ref)

    def rows_of(member):
        if split:
            rows_out = []
            for slot in range(weight_refs[0].shape[0]):
                parts_here = [ref[slot, member] for ref in weight_refs]
                for side in range(2):
                    for along_x in range(2):
                        near = jnp.where(x_index == along_x, parts_here[0], parts_here[1])
                        far = jnp.where(x_index == along_x, parts_here[2], parts_here[3])
                        rows_out.append(jnp.where(core == side, near, far))
            return jnp.concatenate(rows_out, axis=0)
        wanted = feed_core(member, step, parts)
        return jnp.where(wanted == core, weight_refs[2 * member][0], weight_refs[2 * member + 1][0])

    a_two, dy_low = a_two_ref[...], dy_ref[...]
    gate_rows, up_rows, down_rows = rows_of(0), rows_of(1), rows_of(2)
    gate_pre = matmul_t(gate_rows, a_two)
    up_pre = matmul_t(up_rows, a_two)
    d_hidden = matmul_t(down_rows, dy_low)
    sigma = jax.nn.sigmoid(gate_pre)
    gate_act = gate_pre * sigma
    hidden = (gate_act * up_pre).astype(jnp.bfloat16)
    d_gate = (d_hidden * up_pre * sigma * (1.0 + gate_pre * (1.0 - sigma))).astype(jnp.bfloat16)
    d_up = (d_hidden * gate_act).astype(jnp.bfloat16)
    out_ref[...] += matmul_c(hidden, down_rows)
    d_two_ref[...] += matmul_c(d_gate, gate_rows) + matmul_c(d_up, up_rows)
    for member, (left, right) in enumerate(((d_gate, a_two), (d_up, a_two), (hidden, dy_low))):
        grad = matmul_n(left, right).astype(jnp.bfloat16)
        if split:
            slots = grad_refs[0].shape[0]
            rows = grad.shape[0] // slots
            for slot in range(slots):
                put_rows(
                    grad[slot * rows : (slot + 1) * rows], *grad_refs, (slot, member), core, x_index
                )
        else:
            grad_refs[member][0] = grad


def feed_core(member, step, parts):
    ctx_count, single = parts
    return (member + 1) % 2 if single else step // ctx_count


def feed_forward(a_two, dy_low, mine, far, rows, before=()):
    tokens, width = a_two.shape
    ctx_count = lax.axis_size("ctx")
    blocks = FF // rows
    single = blocks == ctx_count
    split = mine[0].ndim == 4 if isinstance(mine, list) else False
    parts = (ctx_count, single)
    whole = pl.BlockSpec((tokens, width), lambda step, me_ref: (0, 0))

    def weight_spec(member, own):
        first = (member + 1) * blocks // ctx_count // 2 * ctx_count

        def index(step, me_ref):
            matches = (feed_core(member, step, parts) == me_ref[0]) == own
            return (first + jnp.where(matches, step % ctx_count, 0), 0, 0)

        return pl.BlockSpec((1, rows, width), index)

    if split:
        weight_specs = [
            pl.BlockSpec((2, 3, rows // 4, width), lambda step, me_ref: (step, 0, 0, 0))
        ] * 4
        weight_args = [*mine, *far]
        half = pl.BlockSpec((2, 3, rows // 2, width), lambda step, me_ref: (step, 0, 0, 0))
        grad_specs = [half, half]
        blocks = mine[0].shape[0]
        grad_shapes = [jax.ShapeDtypeStruct((blocks, 3, rows // 2, width), jnp.bfloat16)] * 2
    else:
        weight_specs = [weight_spec(member, own) for member in range(3) for own in (True, False)]
        weight_args = [mine, far] * 3
        grad_specs = [pl.BlockSpec((1, rows, width), lambda step, me_ref: (step, 0, 0))] * 3
        grad_shapes = [jax.ShapeDtypeStruct((blocks, rows, width), jnp.bfloat16)] * 3
    me = jnp.stack([lax.axis_index("core"), lax.axis_index("x")]).astype(jnp.int32)
    return pl.pallas_call(
        lambda *refs: feed_body(parts, split, bool(before), *refs),
        grid_spec=pltpu.PrefetchScalarGridSpec(
            num_scalar_prefetch=1,
            grid=(blocks // 2 if split else blocks,),
            in_specs=[whole] * (2 + len(before)) + weight_specs,
            out_specs=[whole, whole] + grad_specs,
        ),
        out_shape=[jax.ShapeDtypeStruct((tokens, width), jnp.float32)] * 2 + grad_shapes,
        cost_estimate=pl.CostEstimate(
            flops=18 * tokens * width * blocks * rows, bytes_accessed=12 * blocks * rows * width,
            transcendentals=0,
        ),
        compiler_params=pltpu.CompilerParams(vmem_limit_bytes=VMEM_BYTES),
    )(me, a_two, dy_low, *before, *weight_args)


def first_grads(d_qkv, attn_low, a_one, d_resid_low, rows, split):
    tokens, width = a_one.shape
    early = d_qkv.shape[0] // rows
    blocks = early + attn_low.shape[0] // rows

    def body(me_ref, qkv_ref, attn_ref, one_ref, resid_ref, *grad_refs):
        first = pl.program_id(0) < early
        left = jnp.where(first, qkv_ref[...], attn_ref[...])
        right = jnp.where(first, one_ref[...], resid_ref[...])
        grad = matmul_n(left, right).astype(jnp.bfloat16)
        if split:
            put_rows(grad, *grad_refs, (0, 0), me_ref[0], 0)
        else:
            grad_refs[0][0] = grad

    whole = pl.BlockSpec((tokens, width), lambda step, me_ref: (0, 0))
    if split:
        table = rel_offsets(slot_bits())
        half = pl.BlockSpec(
            (1, 1, rows // 2, width), lambda step, me_ref: (find(step ^ me_ref[1], table), 0, 0, 0)
        )
        grad_specs = [half, half]
        grad_shapes = [jax.ShapeDtypeStruct((blocks, 1, rows // 2, width), jnp.bfloat16)] * 2
    else:
        grad_specs = [pl.BlockSpec((1, rows, width), lambda step, me_ref: (step, 0, 0))]
        grad_shapes = [jax.ShapeDtypeStruct((blocks, rows, width), jnp.bfloat16)]
    me = jnp.stack([lax.axis_index(name) for name in ("core", "ctx")]).astype(jnp.int32)
    return pl.pallas_call(
        body,
        grid_spec=pltpu.PrefetchScalarGridSpec(
            num_scalar_prefetch=1,
            grid=(blocks,),
            in_specs=[
                pl.BlockSpec((rows, tokens), lambda step, me_ref: (jnp.minimum(step, early - 1), 0)),
                pl.BlockSpec((rows, tokens), lambda step, me_ref: (jnp.maximum(step - early, 0), 0)),
                whole,
                whole,
            ],
            out_specs=grad_specs,
        ),
        out_shape=grad_shapes,
        cost_estimate=pl.CostEstimate(
            flops=2 * tokens * width * blocks * rows, bytes_accessed=2 * blocks * rows * width, transcendentals=0
        ),
        compiler_params=pltpu.CompilerParams(vmem_limit_bytes=VMEM_BYTES),
    )(me, d_qkv, attn_low, a_one, d_resid_low)


def adam_update(param, grad, first, second, rate, decay, step_number):
    first_new = BETA_ONE * first + (1.0 - BETA_ONE) * grad
    second_new = BETA_TWO * second + (1.0 - BETA_TWO) * grad * grad
    fix_one = 1.0 - BETA_ONE**step_number
    fix_two = 1.0 - BETA_TWO**step_number
    update = first_new / fix_one / (jnp.sqrt(second_new / fix_two) + ADAM_EPS)
    return (first_new, second_new, param - rate * (update + decay * param))


def shards(inputs, cotangent, weights, gains, first_moment, second_moment, gain_first, gain_second):
    ctx_count = lax.axis_size("ctx")
    x_count = lax.axis_size("x")
    ctx_index, core, x_index = lax.axis_index("ctx"), lax.axis_index("core"), lax.axis_index("x")
    seqs, local_rows, model_width = inputs.shape
    half_rows = local_rows // 2
    tokens = seqs * local_rows
    weight_rows = weights.shape[0]
    q_cols = HEADS * HD
    kv_cols = KV * HD
    cut_o = q_cols + 2 * kv_cols
    slots = slot_bits()
    aligned = splits_rows(weight_rows) and half_rows % 128 == 0 and seqs == 2
    split = aligned
    local_index = jnp.arange(local_rows, dtype=jnp.int32)
    pos_here = places(ctx_index * local_rows + local_index, local_rows, ctx_count)
    cosine, sine_part = angle_tables(pos_here, 1.0)
    turn = (jnp.tile(cosine, (1, seqs)), jnp.tile(sine_part, (1, seqs)))

    turn_back = (turn[0], -turn[1])

    def pack(flat):
        if aligned:
            return flat
        return (
            flat.reshape(KV, GROUP, HD, -1, 2, half_rows)
            .transpose(3, 0, 2, 4, 1, 5)
            .reshape(-1, KV, HD, 2 * GROUP * half_rows)
        )

    def unpack(packed):
        if aligned:
            return packed
        return (
            packed.reshape(KV, HD, 2, GROUP, half_rows)
            .transpose(0, 3, 1, 2, 4)
            .reshape(q_cols, local_rows)
        )

    def by_columns(row):
        rows = row.shape[0]
        return jnp.broadcast_to(
            row.reshape(rows, 2, 1, half_rows), (rows, 2, GROUP, half_rows)
        ).reshape(rows, 2 * GROUP * half_rows)

    owners = ctx_index ^ jnp.asarray(rel_offsets(slots), jnp.int32)
    flags = (owners > ctx_index).astype(jnp.int32)
    inner = jnp.arange(half_rows, dtype=jnp.int32)
    key_pos = jnp.stack(
        [
            (owners[:, None] * half_rows + inner[None, :]).reshape(-1, 1),
            ((2 * ctx_count - 1 - owners[:, None]) * half_rows + inner[None, :]).reshape(-1, 1),
        ]
    )
    query_pos = by_columns(pos_here[None, :])
    packed_tables = (by_columns(cosine), by_columns(sine_part))

    tokens_in, cot_in = lax.optimization_barrier(
        (inputs.reshape(tokens, model_width), cotangent.reshape(tokens, model_width))
    )
    dy_low = cot_in.astype(jnp.bfloat16)
    a_one = (normalize(tokens_in) * gains[0]).astype(jnp.bfloat16)
    if split:
        first_half, first_far_x = gather_first(weights)
        cuts = row_cuts(weight_rows // 2)
        backward = [list(reversed(order)) for order in ctx_orders()]
        first_own = [
            double(first_half[None, low:high], order[0])
            for (low, high), order in zip(cuts, backward)
        ]
        later_weights, first_far_x, first_own = lax.optimization_barrier(
            (weights, first_far_x, first_own)
        )
        feed_quarter = gather_quarters(later_weights, first_far_x)
        first_own = [double(part, order[1]) for part, order in zip(first_own, backward)]
        first_own, a_one = lax.optimization_barrier((first_own, a_one))
        first_own = [double(part, order[2]) for part, order in zip(first_own, backward)]
        feed_quarter, first_own = lax.optimization_barrier((feed_quarter, first_own))
        feed_far_z = swap(feed_quarter[None], slots[0])
        first_far = [swap(part, ("core", 0)) for part in first_own]
        first_rows = place_rows(first_own, first_far)
    else:
        mine = lax.all_gather(weights, ("x", "ctx"), axis=0, tiled=True)
        mine = mine.reshape(x_count * ctx_count, weight_rows, model_width)
        far = swap(mine, ("core", 0))
        sides = [
            jnp.where(core == 0, mine[:ctx_count], far[:ctx_count]),
            jnp.where(core == 0, far[:ctx_count], mine[:ctx_count]),
        ]
        first_rows = jnp.concatenate(sides).reshape(-1, model_width)
    qkv_rows, o_rows = first_rows[:cut_o], first_rows[cut_o : cut_o + q_cols]

    pair_rows = matmul_t(qkv_rows[q_cols:], a_one)
    if split:
        pair_rows, feed_far_z = lax.optimization_barrier((pair_rows, feed_far_z))
    joined = jnp.concatenate(
        [rotate(pair_rows[:kv_cols], turn).astype(jnp.bfloat16), pair_rows[kv_cols:].astype(jnp.bfloat16)],
        axis=0,
    )
    if split:
        feed_own = jnp.concatenate([feed_quarter[None], feed_far_z], axis=0)
        joined, feed_own = lax.optimization_barrier((joined, feed_own))
    if aligned:
        mine_0, mine_1 = [
            joined[:, seq * local_rows : (seq + 1) * local_rows] for seq in range(2)
        ]
        far_0, own_y_0 = swap(mine_0, slots[0]), swap(mine_0, slots[2])
        feed_near, feed_y = swap(feed_own, slots[1]), swap(feed_own, slots[2])
        feed_x = swap(feed_own, ("x", 0))
        far_0, own_y_0, feed_near, feed_y, feed_x, mine_1 = lax.optimization_barrier(
            (far_0, own_y_0, feed_near, feed_y, feed_x, mine_1)
        )
        near_0, far_y_0 = swap(jnp.stack([mine_0, far_0]), slots[1]), swap(far_0, slots[2])
        far_1, own_y_1 = swap(mine_1, slots[0]), swap(mine_1, slots[2])
        near_x = swap(feed_near, ("x", 0))
        near_0, far_y_0, far_1, own_y_1, near_x, feed_y = lax.optimization_barrier(
            (near_0, far_y_0, far_1, own_y_1, near_x, feed_y)
        )
        near_y_0 = swap(near_0, slots[2])
        near_1, far_y_1 = swap(jnp.stack([mine_1, far_1]), slots[1]), swap(far_1, slots[2])
        y_x = swap(feed_y, ("x", 0))
        near_y_0, near_1, far_y_1, y_x, feed_near = lax.optimization_barrier(
            (near_y_0, near_1, far_y_1, y_x, feed_near)
        )
        near_y_1 = swap(near_1, slots[2])
        pairs = [
            [(own[None], 0), (far_z[None], 0), (near, 0), (near, 1)]
            + [(own_y[None], 0), (far_y[None], 0), (near_y, 0), (near_y, 1)]
            for own, far_z, near, own_y, far_y, near_y in (
                (mine_0, far_0, near_0, own_y_0, far_y_0, near_y_0),
                (mine_1, far_1, near_1, own_y_1, far_y_1, near_y_1),
            )
        ]
        feed_lower = [
            jnp.concatenate([feed_own, feed_near], axis=0),
            jnp.concatenate([feed_x, near_x], axis=0),
        ]
        feed_lower_far = [swap(part, ("core", 0)) for part in feed_lower]
    else:
        pairs = spread(joined, slots).reshape(ctx_count, 2 * kv_cols, seqs, 2, half_rows)
        pairs = [
            (
                pairs.transpose(1, 2, 3, 0, 4).reshape(
                    1, 2 * kv_cols, seqs * 2 * ctx_count * half_rows
                ),
                0,
            )
        ]
    q_rot = rotate(matmul_t(qkv_rows[:q_cols], a_one), turn).astype(jnp.bfloat16)
    queries = pack((q_rot * SCALE_QK).astype(jnp.bfloat16))
    attended = []
    for seq in range(seqs):
        if aligned:
            attended.append(attend_slots(queries, pairs[seq], flags, local_rows, seq))
            if seq == 0:
                attended, feed_near = lax.optimization_barrier((attended, feed_near))
                feed_near_y = swap(feed_near, slots[2])
        else:
            attended.append(attend(queries, pairs, key_pos, query_pos, local_rows, seq))
    attn_low = jnp.concatenate([unpack(mixed) for mixed, _ in attended], axis=1)
    resid = tokens_in + matmul_c(attn_low, o_rows)
    a_two = (normalize(resid) * gains[1]).astype(jnp.bfloat16)
    if aligned:
        a_two, feed_near_y = lax.optimization_barrier((a_two, feed_near_y))
        near_y_x = swap(feed_near_y, ("x", 0))
        upper_own = jnp.concatenate([feed_y, feed_near_y], axis=0)
        upper_far = swap(upper_own, ("core", 0))
        *sums_fed, keep_lower, away_lower = feed_forward(
            a_two, dy_low, feed_lower, feed_lower_far, weight_rows
        )
        sums_fed, near_y_x, upper_far = lax.optimization_barrier((sums_fed, near_y_x, upper_far))
        upper_x = jnp.concatenate([y_x, near_y_x], axis=0)
        come_lower = swap(away_lower, ("core", 0))
        fed, d_two, keep_upper, away_upper = feed_forward(
            a_two,
            dy_low,
            [upper_own, upper_x],
            [upper_far, swap(upper_x, ("core", 0))],
            weight_rows,
            sums_fed,
        )
        come_upper = swap(away_upper, ("core", 0))
    else:
        fed, d_two, *feed_grads = feed_forward(a_two, dy_low, mine, far, weight_rows)
    result = resid + fed
    d_norm_two, d_gain_two = norm_back(resid, d_two, gains[1])
    d_resid = cot_in + d_norm_two
    d_resid_low = d_resid.astype(jnp.bfloat16)
    d_attn = pack(matmul_t(o_rows, d_resid_low).astype(jnp.bfloat16))
    if aligned:
        quarter = weight_rows // 4
        held_upper, held_lower = [
            [(part[:, :, :quarter], part[:, :, quarter:]) for part in parts]
            for parts in ((keep_upper, come_upper), (keep_lower, come_lower))
        ]
        send_upper, send_lower = [
            total_low(*[far_part for _, far_part in parts]) for parts in (held_upper, held_lower)
        ]
        d_attn, send_upper = lax.optimization_barrier((d_attn, send_upper))
        x_upper = swap(send_upper, ("x", 0))
        x_lower = swap(send_lower, ("x", 0))
    d_q, d_pair = [], []
    for seq in range(seqs):
        mixed, log_total = attended[seq]
        if aligned:
            d_queries, *d_slots = attend_slots_back(
                queries, pairs[seq], flags, mixed, log_total, d_attn, packed_tables, local_rows, seq, (2, 2, 4)
            )
        else:
            d_queries, *d_slots = attend_back(
                queries, pairs, key_pos, query_pos, mixed, log_total, d_attn, packed_tables,
                local_rows, seq, (1,),
            )
        if aligned and seq == 1:
            d_slots, x_upper = lax.optimization_barrier((d_slots, x_upper))
            feed_y_come = swap(total_low(*[part for part, _ in held_upper], x_upper), slots[2])
        d_q.append(unpack(d_queries))
        if aligned:
            lower, near_part, upper = d_slots
            y_come = swap(upper, slots[2])
            near_come = swap(add_low(near_part, y_come[2:]), slots[1])
            if seq == 1:
                near_come, x_lower = lax.optimization_barrier((near_come, x_lower))
            far_come = swap(total_low(lower[1], y_come[1], near_come[1]), slots[0])
            if seq == 1:
                far_come, feed_y_come = lax.optimization_barrier((far_come, feed_y_come))
                rest = [part for part, _ in held_lower] + [x_lower, feed_y_come]
                feed_near_come = swap(total_low(*[part[2:] for part in rest]), slots[1])
            total = far_come.astype(jnp.float32)
            for part in (lower, y_come, near_come):
                total = total + part[0].astype(jnp.float32)
        else:
            total = collect(
                d_slots[0]
                .reshape(2, KV, ctx_count, half_rows, 2 * HD)
                .transpose(2, 1, 0, 3, 4),
                list(reversed(slots)),
            )
        d_pair.append(total)
    d_own = jnp.stack(d_pair).transpose(1, 4, 0, 2, 3).reshape(KV, 2 * HD, tokens)
    d_qkv = jnp.concatenate(
        [
            jnp.concatenate(d_q, axis=1),
            rotate(d_own[:, :HD].reshape(kv_cols, tokens), turn_back).astype(jnp.bfloat16),
            d_own[:, HD:].reshape(kv_cols, tokens).astype(jnp.bfloat16),
        ],
        axis=0,
    )
    d_one = matmul_c(d_qkv, qkv_rows)
    first_terms = first_grads(d_qkv, attn_low, a_one, d_resid_low, weight_rows, split)
    if split:
        first_terms, feed_near_come = lax.optimization_barrier((first_terms, feed_near_come))
        feed_rest = [part[:2] for part in rest] + [feed_near_come]
        far_send = total_low(*[part[1] for part in feed_rest])
        feed_later = {}

        def beside(step, value):
            if step == 0:
                value, sent = lax.optimization_barrier((value, far_send))
                feed_later["far"] = swap(sent, slots[0])
            if step == 1:
                value, far_come = lax.optimization_barrier((value, feed_later["far"]))
                sums = reduce_end(feed_rest, far_come)
                sent = jnp.where(
                    x_index == 0, sums[1:], jnp.broadcast_to(sums[:1], (2,) + sums.shape[1:])
                )
                feed_later["sums"] = sums
                feed_later["come"] = swap(sent.astype(jnp.bfloat16), ("x", 0))
            return value

    d_norm_one, d_gain_one = norm_back(tokens_in, d_one, gains[0])
    d_tokens = d_resid + d_norm_one
    gain_grad = jnp.stack([d_gain_one, d_gain_two], axis=0)
    if split:
        keep, away = [part[:, 0] for part in first_terms]
        first_half, gain_grad = reduce_halves(keep, away, gain_grad, beside)
        first_half, feed_come = lax.optimization_barrier((first_half, feed_later["come"]))
        feed_sums, feed_come = feed_later["sums"], feed_come.astype(jnp.float32)
        low_first = first_half.astype(jnp.bfloat16)
        first_come, gain_grad = swap_with(low_first, gain_grad, ("x", 0))
        first_half = first_half + first_come.astype(jnp.float32)
        halves = [
            jnp.where(x_index == 0, first_half, jnp.concatenate([feed_come[0], feed_sums[1]])),
            jnp.where(
                x_index == 0,
                jnp.concatenate([feed_sums[0], feed_come[0]]),
                jnp.concatenate([feed_come[1], feed_sums[2]]),
            ),
        ]
        own_half = jnp.where(core == 0, halves[0], halves[1])
        other_half = jnp.where(core == 0, halves[1], halves[0]).astype(jnp.bfloat16)
        come, gain_grad = swap_with(other_half, gain_grad, ("core", 0))
        come = come.astype(jnp.float32)
        weight_share = jnp.concatenate(
            [jnp.where(core == 0, own_half, come), jnp.where(core == 0, come, own_half)], axis=0
        )
    else:
        weight_share = scatter_whole([first_terms[0], *feed_grads])
        for where in [("core", 0)] + sum(bit_groups(), []):
            gain_grad = gain_grad + swap(gain_grad, where)
    weight_first, weight_second, weight_new = adam_update(
        weights.astype(jnp.float32), weight_share, first_moment, second_moment, RATE, DECAY, STEP
    )
    gain_first_new, gain_second_new, gain_new = adam_update(
        gains, gain_grad, gain_first, gain_second, GAIN_RATE, 0.0, STEP
    )
    return (
        result.reshape(inputs.shape),
        d_tokens.reshape(inputs.shape),
        weight_share,
        weight_second,
        weight_new,
        gain_grad,
        gain_second_new,
        gain_new,
    )


def solution(mesh):
    fine = Mesh(
        mesh.devices.reshape(mesh.shape["dp"] // 2, 2, mesh.shape["ctx"]), ("x", "core", "ctx")
    )
    rows = P(("x", "core"), "ctx", None)
    stacked = P(("x", "core", "ctx"), None)
    return jax.shard_map(
        shards,
        mesh=fine,
        in_specs=(rows, rows, stacked, P(), stacked, stacked, P(), P()),
        out_specs=(rows, rows, stacked, stacked, stacked, P(), P(), P()),
        check_vma=False,
    )
```
